32 devices in a mesh: groups: 2 (over x), wide: 16 (over z, y, core).
Axes of the slice: x: 2, y: 2, z: 4, core: 2. Of those that a mesh axis runs over, the one named last changes fastest.
Arguments:
- cell_index: int32 [3, 65536], P(None, 'wide'), may hold values from 0 to 127, as said below
- station_index: int32 [2, 1024], P(None, 'groups'), parts along dimension 1, may hold values from 0 to 127, as said below
- observed: float32 [5, 1024], P(None, 'groups'), parts along dimension 1, may hold values from -6 to 6
- comp_weight: float32 [5], replicated, may hold values from 0.25 to 4
- counts: int32 [16, 512], P('groups'), parts along dimension 0, may hold values from 0 to 3, as said below
Outputs:
- models: float32 [16, 65536], P('groups', 'wide'), parts along dimension 0
The draws below stay inside these ranges and needn't reach their ends.
There are 2 independent parts, one for each index of `groups`. The reference program is written for one: setup_inputs(seed, part) draws one part's arguments, and reference() takes and returns one part's arrays. A program takes and returns all parts, laid end to end along the dimension named above; an argument that names none is the same for every part. Nothing has to cross between parts.
Inputs may be any that keep to these rules, and one draw needn't show every extreme that they name: `cell_index`: each of the 128 x 32 x 16 grid places holds exactly one cell. Row 0 is below 128, row 1 below 32, row 2 below 16. `station_index`: row 0 is below 128, row 1 below 32. `counts`: bootstrap weights: row b holds how often each station is taken in resample b.
All inputs are finite; a program needn't handle non-finite values.
Results may differ from the reference program's by a relative error of at most 0.006.
Values may be sent and summed in bfloat16 or wider, within the bound.
No kernel may reach another device: no remote copies, remote signals or barrier semaphores. Data moves between devices by JAX's collectives and lax.ppermute only.
A program may use at most 64 MiB of HBM per device.

```python
import math
import jax
import jax.numpy as jnp
from jax import lax

C_DEV = 4096
STATIONS = 512
BOOT = 8
GRID = 128
IRLS = 2
CG_STEPS = 2
CELLS = 65536
GRID_Y = 32
ROWS = 2560


def draw_cell_index(key, part):
    key = jax.random.fold_in(key, 11)
    places = jax.random.permutation(key, CELLS).astype(jnp.int32)
    lateral_x = places % GRID
    lateral_y = places // GRID % GRID_Y
    depth_rows = places // (GRID * GRID_Y)
    return jnp.stack([lateral_x, lateral_y, depth_rows], axis=0).astype(jnp.int32)


def draw_station_index(key, part):
    key = jax.random.fold_in(key, 31)
    station_x = jax.random.randint(key, (1, STATIONS), 0, GRID)
    station_y = jax.random.randint(jax.random.fold_in(key, 32), (1, STATIONS), 0, GRID_Y)
    return jnp.concatenate([station_x, station_y], axis=0).astype(jnp.int32)


def draw_counts(key, part):
    key = jax.random.fold_in(key, 21)
    base_counts = jax.random.randint(key, (BOOT, STATIONS), 0, 4)
    top_station = jax.random.randint(jax.random.fold_in(key, 22), (BOOT, 1), 0, STATIONS)
    offset = jax.random.randint(jax.random.fold_in(key, 23), (BOOT, 1), 0, STATIONS - 1)
    empty_station = (top_station + 1 + offset) % STATIONS
    station_ids = jnp.arange(STATIONS, dtype=jnp.int32)[None, :]
    filled = jnp.where(station_ids == top_station, 3, base_counts)
    filled = jnp.where(station_ids == empty_station, 0, filled)
    return filled.astype(jnp.int32)


def gaussian(stream_key, shape, width, most, held_as=jnp.bfloat16):
    result = width * jax.random.normal(stream_key, shape, jnp.float32)
    return jnp.clip(result, min=-most, max=most).astype(held_as)


def setup_inputs(seed: int = 0, part: int = 0) -> dict:
    seeds = jax.random.split(jax.random.key(seed), 6)
    part_keys = jax.random.split(jax.random.fold_in(seeds[5], part), 6)
    return {
        "cell_index": draw_cell_index(jax.random.fold_in(seeds[5], 71), part),
        "station_index": draw_station_index(jax.random.fold_in(jax.random.fold_in(seeds[5], part), 71), part),
        "observed": gaussian(part_keys[2], (5, STATIONS), 1.0, 6.0, jnp.float32),
        "comp_weight": jnp.clip(jnp.exp(jax.random.uniform(seeds[3], (5,), jnp.float32, math.log(0.25), math.log(4.0))), 0.25, 4.0),
        "counts": draw_counts(jax.random.fold_in(jax.random.fold_in(seeds[5], part), 71), part),
    }


station_height = 2.0
focusing = 0.1
damping = 0.0002

def sensitivity(cell_block, station_index):
    cell_x = cell_block[0].astype(jnp.float32) + 0.5
    cell_y = cell_block[1].astype(jnp.float32) + 0.5
    cell_z = cell_block[2].astype(jnp.float32) + 0.5
    station_x = station_index[0].astype(jnp.float32) + 0.5
    station_y = station_index[1].astype(jnp.float32) + 0.5
    delta_x = cell_x[None, :] - station_x[:, None]
    delta_y = cell_y[None, :] - station_y[:, None]
    delta_z = jnp.broadcast_to(cell_z[None, :] + station_height, delta_x.shape)
    radius2 = delta_x * delta_x + delta_y * delta_y + delta_z * delta_z
    strength = 1.0 / (radius2 * radius2 * jnp.sqrt(radius2))
    components = [(3.0 * delta_x * delta_x - radius2) * strength, 3.0 * delta_x * delta_y * strength, 3.0 * delta_x * delta_z * strength, (3.0 * delta_y * delta_y - radius2) * strength, 3.0 * delta_y * delta_z * strength]
    return jnp.concatenate(components, axis=0).astype(jnp.bfloat16)

def reference(cell_index, station_index, observed, comp_weight, counts):
    block_count = CELLS // C_DEV
    blocks = cell_index.reshape(3, block_count, C_DEV).transpose(1, 0, 2)
    weights = (counts.astype(jnp.float32)[:, None, :] * comp_weight[None, :, None]).reshape(BOOT, ROWS)
    data_rows = observed.reshape(1, ROWS)
    depth_z = cell_index[2].astype(jnp.float32) + 0.5
    depth_weight = (station_height / (depth_z + station_height)) ** 3

    def forward(field):
        field_bf = field.astype(jnp.bfloat16).reshape(BOOT, block_count, C_DEV).transpose(1, 0, 2)

        def accumulate(running, paired):
            cell_block, shard_rows = paired
            sens_tile = sensitivity(cell_block, station_index)
            return (running + jnp.dot(shard_rows, sens_tile.T, preferred_element_type=jnp.float32), None)
        running, _ = lax.scan(accumulate, jnp.zeros((BOOT, ROWS), jnp.float32), (blocks, field_bf))
        return running

    def adjoint(values_bf):

        def per_block(cell_block):
            sens_tile = sensitivity(cell_block, station_index)
            return jnp.dot(values_bf, sens_tile, preferred_element_type=jnp.float32)
        pieces = lax.map(per_block, blocks)
        return pieces.transpose(1, 0, 2).reshape(BOOT, CELLS)
    models = jnp.zeros((BOOT, CELLS), jnp.float32)
    for outer_step in range(IRLS):
        penalty = damping * depth_weight[None, :] / (models * models + focusing * focusing)
        misfit = (weights * (data_rows - forward(models))).astype(jnp.bfloat16)
        residual = adjoint(misfit) - penalty * models
        direction = residual
        norm_now = lax.optimization_barrier(jnp.sum(residual * residual, axis=1))
        for inner_step in range(CG_STEPS):
            image_rows = forward(direction)
            weighted = weights * image_rows
            curvature = lax.optimization_barrier(jnp.sum(weighted * image_rows, axis=1)) + lax.optimization_barrier(jnp.sum(penalty * direction * direction, axis=1))
            step_size = norm_now / curvature
            applied = adjoint(weighted.astype(jnp.bfloat16)) + penalty * direction
            models = models + step_size[:, None] * direction
            residual = residual - step_size[:, None] * applied
            norm_next = lax.optimization_barrier(jnp.sum(residual * residual, axis=1))
            direction = residual + (norm_next / norm_now)[:, None] * direction
            norm_now = norm_next
    return models
```

```python
import functools

import jax
import jax.numpy as jnp
import ml_dtypes
import numpy as np
from jax import lax
from jax.experimental import pallas as pl
from jax.experimental.pallas import tpu as pltpu
from jax.sharding import PartitionSpec as P

IRLS = 2
CG_STEPS = 2
GRID = 128
DEPTHS = 16
LANES = 128
TEAM = 2

station_height = 2.0
focusing = 0.1
damping = 0.0002

PARITY = ((0, 0), (1, 1), (1, 0), (0, 0), (0, 1))
BF = jnp.bfloat16
F32 = jnp.float32


def offset_table(grid_y):
    one = np.float32
    dx = np.arange(GRID, dtype=one)[:, None, None]
    dy = np.arange(grid_y, dtype=one)[None, :, None]
    dz = (np.arange(DEPTHS, dtype=one) + one(0.5) + one(station_height))[None, None, :]
    radius2 = dx * dx + dy * dy + dz * dz
    strength = one(1) / (radius2 * radius2 * np.sqrt(radius2))
    three = one(3)
    kinds = [
        (three * dx * dx - radius2) * strength,
        three * dx * dy * strength,
        three * dx * dz * strength,
        (three * dy * dy - radius2) * strength,
        three * dy * dz * strength,
    ]
    return [k.astype(ml_dtypes.bfloat16).astype(np.float64) for k in kinds]


def angles(size):
    return 2 * np.pi * np.outer(np.arange(size), np.arange(size) + 0.5) / (2 * size)


def basis(size):
    return np.concatenate([np.cos(angles(size)), np.sin(angles(size))], axis=1)


def spectrum(values, odd, size):
    if odd:
        trig = 2 * np.sin(angles(size))
    else:
        trig = np.cos(angles(size)) * np.where(np.arange(size) == 0, 1, 2)[:, None]
    return np.tensordot(trig.T / size, values, axes=(1, 0))


def split(matrix):
    high = matrix.astype(ml_dtypes.bfloat16)
    low = (matrix - high.astype(np.float64)).astype(ml_dtypes.bfloat16)
    return high, low


@functools.lru_cache(maxsize=None)
def constants(grid_y):
    group = LANES // grid_y
    table = []
    for values, (odd_x, odd_y) in zip(offset_table(grid_y), PARITY):
        t = spectrum(values, odd_x, GRID)
        t = np.moveaxis(spectrum(np.moveaxis(t, 1, 0), odd_y, grid_y), 0, 1)
        table.append(np.moveaxis(t, 2, 0))
    table = np.tile(np.stack(table), (1, 1, 1, group)).astype(np.float32)

    base_x = basis(GRID)
    base_y = basis(grid_y)
    field_y = np.zeros((LANES, 2, LANES))
    station_y = np.zeros((grid_y, 2, LANES))
    for b in range(group):
        lanes = slice(b * grid_y, (b + 1) * grid_y)
        for half in range(2):
            part = base_y[:, half * grid_y : (half + 1) * grid_y]
            field_y[lanes, half, lanes] = part
            station_y[:, half, lanes] = part
    field_y = field_y.reshape(LANES, 2 * LANES)
    station_y = station_y.reshape(grid_y, 2 * LANES)
    spread = np.zeros((5, LANES, 2, LANES))
    for b in range(group):
        for c in range(5):
            spread[c, b * grid_y + c, :, b * grid_y : (b + 1) * grid_y] = 1
    spread = spread.reshape(5, LANES, 2 * LANES).astype(ml_dtypes.bfloat16)
    same = np.kron(np.eye(group), np.ones((grid_y, grid_y))).astype(np.float32)
    regroup = np.zeros((group, group, grid_y, group, group, grid_y))
    for b in range(group):
        for z in range(group):
            regroup[z, b, :, b, z, :] = np.eye(grid_y)
    regroup = regroup.reshape(group * LANES, group * LANES).astype(ml_dtypes.bfloat16)
    y_high, y_low = split(field_y)
    x_high, x_low = split(base_x.T)
    return dict(
        table=table,
        base_x=split(base_x)[0],
        base_xt2=np.concatenate([x_high, x_low], axis=1),
        field_y2=np.concatenate([y_high, y_low], axis=0),
        field_yt=split(field_y.T)[0],
        station_y2=np.stack(split(station_y)),
        spread=spread,
        gather_back=np.ascontiguousarray(spread.transpose(0, 2, 1)),
        same=same,
        regroup=regroup,
    )


def dot(a, b):
    return jnp.dot(a, b, preferred_element_type=F32)


def solve_kernel(
    grid_y,
    slot_ref,
    comp_ref,
    station_ref,
    observed_ref,
    counts_ref,
    table_ref,
    base_x_ref,
    base_xt2_ref,
    field_y2_ref,
    field_yt_ref,
    station_y2_ref,
    spread_ref,
    back_ref,
    same_ref,
    regroup_ref,
    out_ref,
    pick_x,
    pick_xt,
    pick_y,
    weights,
    data,
    pred,
    image,
    values,
    rows,
    spec_q,
    spec_f,
    spec_g,
    models,
    residual,
    direction,
    penalty,
    applied,
):
    group = LANES // grid_y
    stations = station_ref.shape[1]
    first = (slot_ref[0] * pl.num_programs(0) + pl.program_id(0)) * group

    station_x = station_ref[0:1, :]
    station_y = station_ref[1:2, :]
    place_x = (lax.broadcasted_iota(jnp.int32, (GRID, stations), 0) == station_x).astype(F32)
    place_y = (lax.broadcasted_iota(jnp.int32, (LANES, stations), 0) == station_y).astype(F32)
    pick_xt[...] = dot(base_xt2_ref[:, :GRID], place_x.astype(BF)).astype(BF)
    pick_x[...] = dot(jnp.transpose(place_x).astype(BF), base_x_ref[...]).astype(BF)
    place_yt = jnp.transpose(place_y)[:, :grid_y].astype(BF)
    pick_y[...] = dot(place_yt, station_y2_ref[0]) + dot(place_yt, station_y2_ref[1])

    rows[...] = jnp.zeros_like(rows)
    for b in range(group):
        count = counts_ref[pl.ds(first + b, 1), :].astype(F32)
        for c in range(5):
            rows[b * grid_y + c : b * grid_y + c + 1, :] = count * comp_ref[c]
    weights[...] = jnp.transpose(rows[...])
    for b in range(group):
        rows[b * grid_y : b * grid_y + 5, :] = observed_ref[...]
    data[...] = jnp.transpose(rows[...])

    def back_project():
        q = values[...]
        for c, (odd_x, odd_y) in enumerate(PARITY):
            v = (dot(q, spread_ref[c]) * pick_y[...]).astype(BF)
            spec = dot(pick_xt[...], v)
            for hx in range(2):
                for hy in range(2):
                    part = spec[hx * GRID : (hx + 1) * GRID, hy * LANES : (hy + 1) * LANES]
                    spec_q[c, hx, hy] = -part if (odd_x * hx + odd_y * hy) % 2 else part

        block = 4

        @pl.loop(0, DEPTHS // block)
        def _(zb):
            @pl.loop(0, GRID // 16)
            def _(tile):
                at = pl.ds(pl.multiple_of(tile * 16, 16), 16)
                q = [[[spec_q[c, hx, hy, at, :] for hy in range(2)] for hx in range(2)] for c in range(5)]
                for zi in range(block):
                    t = [table_ref[c, zb * block + zi, at, :] for c in range(5)]
                    for hx in range(2):
                        for hy in range(2):
                            total = None
                            for c, (odd_x, odd_y) in enumerate(PARITY):
                                term = t[c] * q[c][hx ^ odd_x][hy ^ odd_y]
                                total = term if total is None else total + term
                            spec_g[zi, pl.ds(pl.multiple_of(hx * GRID + tile * 16, 16), 16),
                                   hy * LANES : (hy + 1) * LANES] = total.astype(BF)

            for zi in range(block):
                along_x = dot(base_x_ref[...], spec_g[zi]).astype(BF)
                applied[zb * block + zi] = dot(along_x, field_yt_ref[...])

    def predict():
        @pl.loop(0, DEPTHS)
        def _(z):
            d = direction[z].astype(BF)
            y = dot(jnp.concatenate([d, d], axis=1), field_y2_ref[...]).astype(BF)
            spec_f[z] = dot(base_xt2_ref[...], jnp.concatenate([y, y], axis=0))

        @pl.loop(0, GRID // 8)
        def _(tile):
            at = [pl.ds(pl.multiple_of(hx * GRID + tile * 8, 8), 8) for hx in range(2)]
            total = [[[None] * 2 for _ in range(2)] for _ in range(5)]
            for z in range(DEPTHS):
                f = [[spec_f[z, at[hx], hy * LANES : (hy + 1) * LANES] for hy in range(2)] for hx in range(2)]
                for c, (odd_x, odd_y) in enumerate(PARITY):
                    t = table_ref[c, z, at[0], :]
                    for hx in range(2):
                        for hy in range(2):
                            term = t * f[hx ^ odd_x][hy ^ odd_y]
                            old = total[c][hx][hy]
                            total[c][hx][hy] = term if old is None else old + term
            for c, (odd_x, odd_y) in enumerate(PARITY):
                for hx in range(2):
                    for hy in range(2):
                        part = total[c][hx][hy]
                        part = -part if (odd_x * hx + odd_y * hy) % 2 else part
                        spec_q[c, hx, hy, pl.ds(pl.multiple_of(tile * 8, 8), 8), :] = part

        for c in range(5):
            q = jnp.concatenate(
                [jnp.concatenate([spec_q[c, hx, 0], spec_q[c, hx, 1]], axis=1) for hx in range(2)], axis=0
            ).astype(BF)
            part = (dot(pick_x[...], q) * pick_y[...]).astype(BF)
            part = dot(part, back_ref[c])
            if c == 0:
                image[...] = part
            else:
                image[...] += part

    def fold(a):
        return jnp.sum(a.reshape(a.shape[0] // 8, 8, LANES), axis=0)

    def total_of(partial):
        sums = jnp.dot(partial, same_ref[...], precision=lax.Precision.HIGHEST, preferred_element_type=F32)
        return jnp.sum(sums, axis=0, keepdims=True)

    def depth_weight(z):
        depth = z.astype(F32) + 0.5 + station_height
        ratio = station_height / jnp.full((1, LANES), depth, F32)
        return ratio * ratio * ratio

    zero = jnp.zeros((8, LANES), F32)

    @pl.loop(0, DEPTHS)
    def _(z):
        models[z] = jnp.zeros((GRID, LANES), F32)

    pred[...] = jnp.zeros_like(pred)

    def outer(_, carry):
        values[...] = (weights[...] * (data[...] - pred[...])).astype(BF)
        back_project()

        def start(z, carry):
            norm, cross = carry
            m = models[z]
            p = damping * depth_weight(z) / (m * m + focusing * focusing)
            penalty[z] = p
            r = applied[z] - p * m
            residual[z] = r
            direction[z] = r
            return norm + fold(r * r), cross + fold(p * r * r)

        norm, cross = lax.fori_loop(0, DEPTHS, start, (zero, zero))
        norm = total_of(norm)
        for inner in range(CG_STEPS):
            predict()
            weighted = weights[...] * image[...]
            step = norm / total_of(cross + fold(weighted * image[...]))
            pred[...] += step * image[...]
            if inner == CG_STEPS - 1:

                def last(z, carry):
                    models[z] += step * direction[z]
                    return carry

                lax.fori_loop(0, DEPTHS, last, 0)
                break
            values[...] = weighted.astype(BF)
            back_project()

            def update(z, carry):
                d = direction[z]
                models[z] += step * d
                r = residual[z] - step * (applied[z] + penalty[z] * d)
                residual[z] = r
                return carry + fold(r * r)

            new = total_of(lax.fori_loop(0, DEPTHS, update, zero))
            ratio = new / norm

            def turn(z, carry):
                d = residual[z] + ratio * direction[z]
                direction[z] = d
                return carry + fold(penalty[z] * d * d)

            cross = lax.fori_loop(0, DEPTHS, turn, zero)
            norm = new
        return carry

    lax.fori_loop(0, IRLS, outer, 0)

    for zq in range(DEPTHS // group):
        m = jnp.concatenate([models[zq * group + zi].astype(BF) for zi in range(group)], axis=1)
        m = dot(m, regroup_ref[...]).astype(BF)
        for b in range(group):
            out_ref[b, :, zq * LANES : (zq + 1) * LANES] = m[:, b * LANES : (b + 1) * LANES]


def solve(slot, comp_weight, station_index, observed, counts, boots, grid_y):
    group = LANES // grid_y
    stations = station_index.shape[1]
    consts = {k: jnp.asarray(v) for k, v in constants(grid_y).items()}
    vmem = pltpu.VMEM
    steps = boots // group
    whole = lambda a: pl.BlockSpec(a.shape, lambda i, n=a.ndim: (0,) * n)
    smem = pl.BlockSpec(memory_space=pltpu.SMEM)
    field = vmem((DEPTHS, GRID, LANES), F32)
    at_stations = vmem((stations, LANES), F32)
    arrays = [station_index, observed, counts] + list(consts.values())
    return pl.pallas_call(
        functools.partial(solve_kernel, grid_y),
        out_shape=jax.ShapeDtypeStruct((boots, GRID, DEPTHS * grid_y), BF),
        grid=(steps,),
        in_specs=[smem, smem] + [whole(a) for a in arrays],
        out_specs=pl.BlockSpec((group, GRID, DEPTHS * grid_y), lambda i: (i, 0, 0)),
        scratch_shapes=[
            vmem((stations, 2 * GRID), BF),
            vmem((2 * GRID, stations), BF),
            vmem((stations, 2 * LANES), F32),
            at_stations,
            at_stations,
            at_stations,
            at_stations,
            vmem((stations, LANES), BF),
            vmem((LANES, stations), F32),
            vmem((5, 2, 2, GRID, LANES), F32),
            vmem((DEPTHS, 2 * GRID, 2 * LANES), F32),
            vmem((4, 2 * GRID, 2 * LANES), BF),
            field,
            field,
            field,
            field,
            field,
        ],
        compiler_params=pltpu.CompilerParams(vmem_limit_bytes=48 * 1024 * 1024),
        cost_estimate=pl.CostEstimate(flops=10**10, bytes_accessed=10**7, transcendentals=0),
        name="solve",
    )(slot, comp_weight, *arrays)


def pick_kernel(grid_y, models_ref, cell_ref, out_ref):
    boots, _, depth_places = models_ref.shape
    cells = cell_ref.shape[1]
    cell_x = cell_ref[0:1, :]
    place = cell_ref[2:3, :] * grid_y + cell_ref[1:2, :]
    here = lax.broadcasted_iota(jnp.int32, (depth_places, cells), 0) == place
    chosen = jnp.where(here, 1.0, 0.0).astype(BF)
    at_x = lax.broadcasted_iota(jnp.int32, (GRID, cells), 0) == cell_x
    for b in range(boots):
        found = dot(models_ref[b], chosen)
        out_ref[b : b + 1, :] = jnp.sum(jnp.where(at_x, found, 0.0), axis=0, keepdims=True)


def pick(models, cells, grid_y):
    boots, _, depth_places = models.shape
    count = cells.shape[1]
    chunk = 512
    return pl.pallas_call(
        functools.partial(pick_kernel, grid_y),
        out_shape=jax.ShapeDtypeStruct((boots, count), F32),
        grid=(count // chunk,),
        in_specs=[
            pl.BlockSpec(models.shape, lambda i: (0, 0, 0)),
            pl.BlockSpec((3, chunk), lambda i: (0, i)),
        ],
        out_specs=pl.BlockSpec((boots, chunk), lambda i: (0, i)),
        compiler_params=pltpu.CompilerParams(vmem_limit_bytes=48 * 1024 * 1024),
        cost_estimate=pl.CostEstimate(
            flops=2 * boots * GRID * depth_places * count, bytes_accessed=10**6, transcendentals=0
        ),
        name="pick",
    )(models, cells)


def local(wide, cell_index, station_index, observed, comp_weight, counts):
    boots = counts.shape[0]
    grid_y = cell_index.shape[1] * wide // (GRID * DEPTHS)
    group = LANES // grid_y
    team = TEAM if wide % TEAM == 0 and boots % (TEAM * group) == 0 else 1
    mine = boots // team
    slot = lax.axis_index("wide") % team
    models = solve(
        slot.astype(jnp.int32).reshape(1), comp_weight, station_index, observed, counts, mine, grid_y
    )
    own = pick(models, cell_index, grid_y)
    if team == 1:
        return own
    pairs = [(i, i ^ 1) for i in range(wide)]
    theirs = pick(models, lax.ppermute(cell_index, "wide", pairs), grid_y)
    other = lax.ppermute(theirs, "wide", pairs)
    return jnp.concatenate(
        [jnp.where(slot == 0, own, other), jnp.where(slot == 0, other, own)], axis=0
    )


def solution(mesh):
    in_specs = (P(None, "wide"), P(None, "groups"), P(None, "groups"), P(), P("groups", None))
    out_specs = P("groups", "wide")
    fn = functools.partial(local, mesh.shape["wide"])
    return jax.shard_map(fn, mesh=mesh, in_specs=in_specs, out_specs=out_specs, check_vma=False)
```

```python
import functools

import jax
import jax.numpy as jnp
import ml_dtypes
import numpy as np
from jax import lax
from jax.experimental import pallas as pl
from jax.experimental.pallas import tpu as pltpu
from jax.sharding import PartitionSpec as P

IRLS = 2
CG_STEPS = 2
GRID = 128
DEPTHS = 16
LANES = 128
TEAM = 4

station_height = 2.0
focusing = 0.1
damping = 0.0002

PARITY = ((0, 0), (1, 1), (1, 0), (0, 0), (0, 1))
BF = jnp.bfloat16
F32 = jnp.float32


def offset_table(grid_y):
    one = np.float32
    dx = np.arange(GRID, dtype=one)[:, None, None]
    dy = np.arange(grid_y, dtype=one)[None, :, None]
    dz = (np.arange(DEPTHS, dtype=one) + one(0.5) + one(station_height))[None, None, :]
    radius2 = dx * dx + dy * dy + dz * dz
    strength = one(1) / (radius2 * radius2 * np.sqrt(radius2))
    three = one(3)
    kinds = [
        (three * dx * dx - radius2) * strength,
        three * dx * dy * strength,
        three * dx * dz * strength,
        (three * dy * dy - radius2) * strength,
        three * dy * dz * strength,
    ]
    return [k.astype(ml_dtypes.bfloat16).astype(np.float64) for k in kinds]


def angles(size):
    return 2 * np.pi * np.outer(np.arange(size), np.arange(size) + 0.5) / (2 * size)


def basis(size):
    return np.concatenate([np.cos(angles(size)), np.sin(angles(size))], axis=1)


def spectrum(values, odd, size):
    if odd:
        trig = 2 * np.sin(angles(size))
    else:
        trig = np.cos(angles(size)) * np.where(np.arange(size) == 0, 1, 2)[:, None]
    return np.tensordot(trig.T / size, values, axes=(1, 0))


def split(matrix):
    high = matrix.astype(ml_dtypes.bfloat16)
    low = (matrix - high.astype(np.float64)).astype(ml_dtypes.bfloat16)
    return high, low


@functools.lru_cache(maxsize=None)
def constants(grid_y, boots):
    deep = LANES // grid_y // boots
    slabs = DEPTHS // deep
    table = []
    for values, (odd_x, odd_y) in zip(offset_table(grid_y), PARITY):
        t = spectrum(values, odd_x, GRID)
        t = np.moveaxis(spectrum(np.moveaxis(t, 1, 0), odd_y, grid_y), 0, 1)
        t = np.moveaxis(t, 2, 0).reshape(slabs, deep, GRID, 1, grid_y).transpose(0, 2, 1, 3, 4)
        table.append(np.tile(t, (1, 1, 1, boots, 1)).reshape(slabs, GRID, LANES))
    table = np.stack(table).astype(np.float32)

    base_x = basis(GRID)
    base_y = basis(grid_y).reshape(grid_y, 2, grid_y)
    copies = deep * boots
    field_y = np.einsum("ab,yhl->ayhbl", np.eye(copies), base_y).reshape(LANES, 2 * LANES)
    station_y = np.einsum("b,yhl->yhbl", np.ones(copies), base_y).reshape(grid_y, 2 * LANES)
    spread = np.zeros((6, deep, boots, grid_y, deep, boots, grid_y))
    for c in range(5):
        for b in range(boots):
            spread[c, 0, b, c, :, b, :] = 1
    spread = spread.reshape(3, 2, LANES, LANES)
    back = spread.transpose(0, 1, 3, 2).reshape(3, 2 * LANES, LANES)
    spread = spread.transpose(0, 2, 1, 3).reshape(3, LANES, 2 * LANES)
    same = np.einsum("ab,dc,yz->dayczb", np.eye(boots), np.ones((deep, deep)), np.ones((grid_y, grid_y)))
    same = same.transpose(0, 1, 2, 3, 5, 4).reshape(LANES, LANES)
    regroup = np.einsum("st,de,ab,yz->sdaybtez", *[np.eye(n) for n in (boots, deep, boots, grid_y)])
    regroup = regroup.reshape(boots * LANES, boots * LANES)
    y_high, y_low = split(field_y)
    x_high, x_low = split(base_x.T)
    half = lambda a: a.astype(ml_dtypes.bfloat16)
    return dict(
        table=table,
        base_x=half(base_x),
        base_xt2=np.concatenate([x_high, x_low], axis=1),
        field_y2=np.concatenate([y_high, y_low], axis=0),
        field_yt=half(field_y.T),
        station_y2=np.stack(split(station_y)),
        spread=half(spread),
        back=half(back),
        same=same.astype(np.float32),
        regroup=half(regroup),
    )


def dot(a, b):
    return jnp.dot(a, b, preferred_element_type=F32)


def solve_kernel(grid_y, boots, n_const, slot_ref, comp_ref, station_ref, observed_ref, counts_ref, *refs):
    sources, out_ref = refs[:n_const], refs[n_const]
    held = refs[n_const + 1 : 2 * n_const + 1]
    (
        copied,
        pick_x,
        pick_xt,
        pick_y,
        weights,
        data,
        pred,
        image,
        values,
        rows,
        spec_q,
        spec_i,
        spec_f,
        spec_g,
        models,
        residual,
        direction,
        penalty,
        applied,
    ) = refs[2 * n_const + 1 :]
    copies = [pltpu.make_async_copy(s, h, copied.at[i]) for i, (s, h) in enumerate(zip(sources, held))]
    first_step = pl.program_id(0) == 0

    @pl.when(first_step)
    def _():
        for copy in copies:
            copy.start()

    (table_ref, base_x_ref, base_xt2_ref, field_y2_ref, field_yt_ref) = held[:5]
    (station_y2_ref, spread_ref, back_ref, same_ref, regroup_ref) = held[5:]
    deep = LANES // grid_y // boots
    slabs = DEPTHS // deep
    stations = station_ref.shape[1]
    first = (slot_ref[0] * pl.num_programs(0) + pl.program_id(0)) * boots

    rows[...] = jnp.zeros_like(rows)
    for b in range(boots):
        rows[b * grid_y : b * grid_y + 5, :] = observed_ref[...]
    data[...] = jnp.transpose(rows[...])
    for b in range(boots):
        count = counts_ref[pl.ds(first + b, 1), :].astype(F32)
        for c in range(5):
            rows[b * grid_y + c : b * grid_y + c + 1, :] = count * comp_ref[c]
    weights[...] = jnp.transpose(rows[...])

    station_x = station_ref[0:1, :]
    station_y = station_ref[1:2, :]
    place_x = (lax.broadcasted_iota(jnp.int32, (GRID, stations), 0) == station_x).astype(F32)
    place_y = (lax.broadcasted_iota(jnp.int32, (LANES, stations), 0) == station_y).astype(F32)
    place_xt = jnp.transpose(place_x).astype(BF)
    place_yt = jnp.transpose(place_y)[:, :grid_y].astype(BF)

    @pl.when(first_step)
    def _():
        for copy in copies[1:]:
            copy.wait()

    pick_xt[...] = dot(base_xt2_ref[:, :GRID], place_x.astype(BF)).astype(BF)
    pick_x[...] = dot(place_xt, base_x_ref[...]).astype(BF)
    pick_y[...] = dot(place_yt, station_y2_ref[0]) + dot(place_yt, station_y2_ref[1])

    @pl.when(first_step)
    def _():
        copies[0].wait()

    def back_project():
        q = values[...]
        for c, (odd_x, odd_y) in enumerate(PARITY):
            if c % 2 == 0:
                spreads = dot(q, spread_ref[c // 2])
            e = spreads[:, c % 2 * LANES : (c % 2 + 1) * LANES]
            v = jnp.concatenate([e * pick_y[:, :LANES], e * pick_y[:, LANES:]], axis=1).astype(BF)
            spec = dot(pick_xt[...], v)
            for hx in range(2):
                for hy in range(2):
                    part = spec[hx * GRID : (hx + 1) * GRID, hy * LANES : (hy + 1) * LANES]
                    spec_q[c, hx, hy] = -part if (odd_x * hx + odd_y * hy) % 2 else part

        @pl.loop(0, GRID // 16)
        def _(tile):
            at = pl.ds(pl.multiple_of(tile * 16, 16), 16)
            for hx in range(2):
                q = [[spec_q[c, hx ^ PARITY[c][0], hy, at, :] for hy in range(2)] for c in range(5)]
                to = pl.ds(pl.multiple_of(hx * GRID + tile * 16, 16), 16)
                for z in range(slabs):
                    t = [table_ref[c, z, at, :] for c in range(5)]
                    for hy in range(2):
                        total = None
                        for c in range(5):
                            term = t[c] * q[c][hy ^ PARITY[c][1]]
                            total = term if total is None else total + term
                        spec_g[z, to, hy * LANES : (hy + 1) * LANES] = total.astype(BF)

        for z in range(slabs):
            along_x = dot(base_x_ref[...], spec_g[z]).astype(BF)
            applied[z] = dot(along_x, field_yt_ref[...])

    def predict():
        d = direction[...].reshape(slabs * GRID, LANES).astype(BF)
        y = dot(jnp.concatenate([d, d], axis=1), field_y2_ref[...]).astype(BF)
        for z in range(slabs):
            part = y[z * GRID : (z + 1) * GRID]
            spec_f[z] = dot(base_xt2_ref[...], jnp.concatenate([part, part], axis=0))

        @pl.loop(0, GRID // 16)
        def _(tile):
            done = []
            for sub in range(2):
                at = [pl.ds(pl.multiple_of(hx * GRID + tile * 16 + sub * 8, 8), 8) for hx in range(2)]
                total = [[[None] * 2 for _ in range(2)] for _ in range(5)]
                for z in range(slabs):
                    f = [[spec_f[z, at[hx], hy * LANES : (hy + 1) * LANES] for hy in range(2)] for hx in range(2)]
                    for c, (odd_x, odd_y) in enumerate(PARITY):
                        t = table_ref[c, z, at[0], :]
                        for hx in range(2):
                            for hy in range(2):
                                term = t * f[hx ^ odd_x][hy ^ odd_y]
                                old = total[c][hx][hy]
                                total[c][hx][hy] = term if old is None else old + term
                done.append(total)
            for c, (odd_x, odd_y) in enumerate(PARITY):
                for hx in range(2):
                    to = pl.ds(pl.multiple_of(hx * GRID + tile * 16, 16), 16)
                    for hy in range(2):
                        part = jnp.concatenate([done[sub][c][hx][hy] for sub in range(2)], axis=0)
                        part = -part if (odd_x * hx + odd_y * hy) % 2 else part
                        spec_i[c, to, hy * LANES : (hy + 1) * LANES] = part.astype(BF)

        total = None
        pair = []
        for c in range(5):
            part = dot(pick_x[...], spec_i[c]) * pick_y[...]
            pair.append((part[:, :LANES] + part[:, LANES:]).astype(BF))
            if c % 2 or c == 4:
                if c == 4:
                    part = dot(pair[0], back_ref[2, :LANES, :])
                else:
                    part = dot(jnp.concatenate(pair, axis=1), back_ref[c // 2])
                total = part if total is None else total + part
                pair = []
        image[...] = total

    def fold(a):
        return jnp.sum(a.reshape(a.shape[0] // 8, 8, LANES), axis=0)

    def total_of(partial):
        if boots == 1:
            return jnp.broadcast_to(jnp.sum(partial, keepdims=True), (1, LANES))
        sums = jnp.dot(partial, same_ref[...], precision=lax.Precision.HIGHEST, preferred_element_type=F32)
        return jnp.sum(sums, axis=0, keepdims=True)

    def depth_weight(z):
        within = lax.broadcasted_iota(jnp.int32, (1, LANES), 1) // (boots * grid_y)
        depth = (within + z * deep).astype(F32) + 0.5 + station_height
        ratio = station_height / depth
        return ratio * ratio * ratio

    models[...] = jnp.zeros_like(models)
    pred[...] = jnp.zeros_like(pred)

    def outer(_, carry):
        values[...] = (weights[...] * (data[...] - pred[...])).astype(BF)
        back_project()
        norm = cross = jnp.zeros((8, LANES), F32)
        for z in range(slabs):
            m = models[z]
            p = damping * depth_weight(z) / (m * m + focusing * focusing)
            penalty[z] = p
            r = applied[z] - p * m
            residual[z] = r
            direction[z] = r
            norm += fold(r * r)
            cross += fold(p * r * r)
        norm = total_of(norm)
        for inner in range(CG_STEPS):
            predict()
            weighted = weights[...] * image[...]
            step = norm / total_of(cross + fold(weighted * image[...]))
            pred[...] += step * image[...]
            if inner == CG_STEPS - 1:
                for z in range(slabs):
                    models[z] += step * direction[z]
                break
            values[...] = weighted.astype(BF)
            back_project()
            new = jnp.zeros((8, LANES), F32)
            for z in range(slabs):
                d = direction[z]
                models[z] += step * d
                r = residual[z] - step * (applied[z] + penalty[z] * d)
                residual[z] = r
                new += fold(r * r)
            new = total_of(new)
            ratio = new / norm
            cross = jnp.zeros((8, LANES), F32)
            for z in range(slabs):
                d = residual[z] + ratio * direction[z]
                direction[z] = d
                cross += fold(penalty[z] * d * d)
            norm = new
        return carry

    lax.fori_loop(0, IRLS, outer, 0)

    for group in range(slabs // boots):
        m = jnp.concatenate([models[group * boots + i].astype(BF) for i in range(boots)], axis=1)
        if boots > 1:
            m = dot(m, regroup_ref[...]).astype(BF)
        for b in range(boots):
            out_ref[b, :, group * LANES : (group + 1) * LANES] = m[:, b * LANES : (b + 1) * LANES]


def solve(slot, comp_weight, station_index, observed, counts, mine, grid_y):
    boots = min(mine, LANES // grid_y)
    slabs = DEPTHS * grid_y * boots // LANES
    stations = station_index.shape[1]
    consts = [jnp.asarray(v) for v in constants(grid_y, boots).values()]
    vmem = pltpu.VMEM
    whole = lambda a: pl.BlockSpec(a.shape, lambda i, n=a.ndim: (0,) * n)
    smem = pl.BlockSpec(memory_space=pltpu.SMEM)
    field = vmem((slabs, GRID, LANES), F32)
    at_stations = vmem((stations, LANES), F32)
    inputs = [station_index, observed, counts]
    return pl.pallas_call(
        functools.partial(solve_kernel, grid_y, boots, len(consts)),
        out_shape=jax.ShapeDtypeStruct((mine, GRID, DEPTHS * grid_y), BF),
        grid=(mine // boots,),
        in_specs=[smem, smem]
        + [whole(a) for a in inputs]
        + [pl.BlockSpec(memory_space=pl.ANY) for _ in consts],
        out_specs=pl.BlockSpec((boots, GRID, DEPTHS * grid_y), lambda i: (i, 0, 0)),
        scratch_shapes=[vmem(a.shape, a.dtype) for a in consts]
        + [
            pltpu.SemaphoreType.DMA((len(consts),)),
            vmem((stations, 2 * GRID), BF),
            vmem((2 * GRID, stations), BF),
            vmem((stations, 2 * LANES), F32),
            at_stations,
            at_stations,
            at_stations,
            at_stations,
            vmem((stations, LANES), BF),
            vmem((LANES, stations), F32),
            vmem((5, 2, 2, GRID, LANES), F32),
            vmem((5, 2 * GRID, 2 * LANES), BF),
            vmem((slabs, 2 * GRID, 2 * LANES), F32),
            vmem((slabs, 2 * GRID, 2 * LANES), BF),
            field,
            field,
            field,
            field,
            field,
        ],
        compiler_params=pltpu.CompilerParams(vmem_limit_bytes=60 * 1024 * 1024),
        cost_estimate=pl.CostEstimate(flops=10**10, bytes_accessed=10**7, transcendentals=0),
        name="solve",
    )(slot, comp_weight, *inputs, *consts)


def pick_kernel(grid_y, count, models_ref, *refs):
    boots = models_ref.shape[0]
    for cell_ref, out_ref in zip(refs[:count], refs[count:]):
        cells = cell_ref.shape[1]
        place = cell_ref[...].astype(F32)
        wide = lambda row, rows: jnp.broadcast_to(row, (rows, cells)).astype(BF)
        y_row = wide(place[1:2], grid_y)
        z_row = wide(place[2:3], grid_y)
        here_y = lax.broadcasted_iota(jnp.int32, (grid_y, cells), 0).astype(F32).astype(BF) == y_row
        here_y = jnp.where(here_y, jnp.ones_like(y_row), jnp.zeros_like(y_row))
        chosen = jnp.concatenate(
            [jnp.where(z_row == jnp.full_like(z_row, z), here_y, jnp.zeros_like(here_y)) for z in range(DEPTHS)],
            axis=0,
        )
        at_x = lax.broadcasted_iota(jnp.int32, (GRID, cells), 0) == cell_ref[0:1, :]
        for b in range(boots):
            found = dot(models_ref[b], chosen)
            out_ref[b : b + 1, :] = jnp.sum(jnp.where(at_x, found, 0.0), axis=0, keepdims=True)


def pick(models, cells, grid_y):
    boots, _, depth_places = models.shape
    count = cells[0].shape[1]
    chunk = 512
    return pl.pallas_call(
        functools.partial(pick_kernel, grid_y, len(cells)),
        out_shape=[jax.ShapeDtypeStruct((boots, count), F32)] * len(cells),
        grid=(count // chunk,),
        in_specs=[pl.BlockSpec(models.shape, lambda i: (0, 0, 0))]
        + [pl.BlockSpec((3, chunk), lambda i: (0, i))] * len(cells),
        out_specs=[pl.BlockSpec((boots, chunk), lambda i: (0, i))] * len(cells),
        compiler_params=pltpu.CompilerParams(vmem_limit_bytes=48 * 1024 * 1024),
        cost_estimate=pl.CostEstimate(
            flops=2 * boots * GRID * depth_places * count * len(cells), bytes_accessed=10**6, transcendentals=0
        ),
        name="pick",
    )(models, *cells)


def local(wide, cell_index, station_index, observed, comp_weight, counts):
    boots = counts.shape[0]
    grid_y = cell_index.shape[1] * wide // (GRID * DEPTHS)
    team = TEAM if wide % TEAM == 0 and boots % TEAM == 0 else 1
    slot = lax.axis_index("wide").astype(jnp.int32) & (team - 1)

    def swap(a, k):
        return lax.ppermute(a, "wide", [(i, i ^ k) for i in range(wide)])

    theirs = [swap(cell_index, k) for k in range(1, team)]
    models = solve(slot.reshape(1), comp_weight, station_index, observed, counts, boots // team, grid_y)
    sent = [swap(a, k + 1) for k, a in enumerate(pick(models, theirs, grid_y))] if theirs else []
    got = jnp.stack([*pick(models, [cell_index], grid_y), *sent])
    bit = 1
    while bit < team:
        pairs = got.reshape((team // (2 * bit), 2, bit) + got.shape[1:])
        got = jnp.where(slot & bit != 0, pairs[:, ::-1], pairs).reshape(got.shape)
        bit *= 2
    return got.reshape(boots, -1)


def solution(mesh):
    in_specs = (P(None, "wide"), P(None, "groups"), P(None, "groups"), P(), P("groups", None))
    out_specs = P("groups", "wide")
    fn = functools.partial(local, mesh.shape["wide"])
    return jax.shard_map(fn, mesh=mesh, in_specs=in_specs, out_specs=out_specs, check_vma=False)
```

```python
import functools

import jax
import jax.numpy as jnp
import ml_dtypes
import numpy as np
from jax import lax
from jax.experimental import pallas as pl
from jax.experimental.pallas import tpu as pltpu
from jax.sharding import PartitionSpec as P

IRLS = 2
CG_STEPS = 2
GRID = 128
DEPTHS = 16
LANES = 128
TEAM = 8

station_height = 2.0
focusing = 0.1
damping = 0.0002

PARITY = ((0, 0), (1, 1), (1, 0), (0, 0), (0, 1))
BF = jnp.bfloat16
F32 = jnp.float32


def offset_table(grid_y):
    one = np.float32
    dx = np.arange(GRID, dtype=one)[:, None, None]
    dy = np.arange(grid_y, dtype=one)[None, :, None]
    dz = (np.arange(DEPTHS, dtype=one) + one(0.5) + one(station_height))[None, None, :]
    radius2 = dx * dx + dy * dy + dz * dz
    strength = one(1) / (radius2 * radius2 * np.sqrt(radius2))
    three = one(3)
    kinds = [
        (three * dx * dx - radius2) * strength,
        three * dx * dy * strength,
        three * dx * dz * strength,
        (three * dy * dy - radius2) * strength,
        three * dy * dz * strength,
    ]
    return [k.astype(ml_dtypes.bfloat16).astype(np.float64) for k in kinds]


def angles(size):
    return 2 * np.pi * np.outer(np.arange(size), np.arange(size) + 0.5) / (2 * size)


def basis(size):
    return np.concatenate([np.cos(angles(size)), np.sin(angles(size))], axis=1)


def spectrum(values, odd, size):
    if odd:
        trig = 2 * np.sin(angles(size))
    else:
        trig = np.cos(angles(size)) * np.where(np.arange(size) == 0, 1, 2)[:, None]
    return np.tensordot(trig.T / size, values, axes=(1, 0))


def split(matrix):
    high = matrix.astype(ml_dtypes.bfloat16)
    low = (matrix - high.astype(np.float64)).astype(ml_dtypes.bfloat16)
    return high, low


@functools.lru_cache(maxsize=None)
def constants(grid_y, boots):
    deep = LANES // grid_y // boots
    slabs = DEPTHS // deep
    table = []
    for values, (odd_x, odd_y) in zip(offset_table(grid_y), PARITY):
        t = spectrum(values, odd_x, GRID)
        t = np.moveaxis(spectrum(np.moveaxis(t, 1, 0), odd_y, grid_y), 0, 1)
        t = np.moveaxis(t, 2, 0).reshape(slabs, deep, GRID, 1, grid_y).transpose(0, 2, 1, 3, 4)
        table.append(np.tile(t, (1, 1, 1, boots, 1)).reshape(slabs, GRID, LANES))
    table = np.stack(table).astype(np.float32)

    base_x = basis(GRID)
    base_y = basis(grid_y).reshape(grid_y, 2, grid_y)
    copies = deep * boots
    field_y = np.einsum("ab,yhl->ayhbl", np.eye(copies), base_y).reshape(LANES, 2 * LANES)
    station_y = np.einsum("b,yhl->yhbl", np.ones(copies), base_y).reshape(grid_y, 2 * LANES)
    spread = np.zeros((6, deep, boots, grid_y, deep, boots, grid_y))
    for c in range(5):
        for b in range(boots):
            spread[c, 0, b, c, :, b, :] = 1
    spread = spread.reshape(3, 2, LANES, LANES)
    back = spread.transpose(0, 1, 3, 2).reshape(3, 2 * LANES, LANES)
    spread = spread.transpose(0, 2, 1, 3).reshape(3, LANES, 2 * LANES)
    same = np.einsum("ab,dc,yz->dayczb", np.eye(boots), np.ones((deep, deep)), np.ones((grid_y, grid_y)))
    same = same.transpose(0, 1, 2, 3, 5, 4).reshape(LANES, LANES)
    regroup = np.einsum("st,de,ab,yz->sdaybtez", *[np.eye(n) for n in (boots, deep, boots, grid_y)])
    regroup = regroup.reshape(boots * LANES, boots * LANES)
    y_high, y_low = split(field_y)
    x_high, x_low = split(base_x.T)
    half = lambda a: a.astype(ml_dtypes.bfloat16)
    return dict(
        table=table,
        base_x=half(base_x),
        base_xt2=np.concatenate([x_high, x_low], axis=1),
        field_y2=np.concatenate([y_high, y_low], axis=0),
        field_yt=half(field_y.T),
        station_y2=np.stack(split(station_y)),
        spread=half(spread),
        back=half(back),
        same=same.astype(np.float32),
        regroup=half(regroup),
    )


def dot(a, b):
    return jnp.dot(a, b, preferred_element_type=F32)


def solve_kernel(grid_y, boots, n_const, slot_ref, comp_ref, station_ref, observed_ref, counts_ref, *refs):
    sources, out_ref = refs[:n_const], refs[n_const]
    held = refs[n_const + 1 : 2 * n_const + 1]
    (
        copied,
        pick_x,
        pick_xt,
        pick_y,
        weights,
        data,
        pred,
        image,
        values,
        rows,
        spec_q,
        spec_i,
        spec_f,
        spec_g,
        models,
        residual,
        direction,
        penalty,
        applied,
    ) = refs[2 * n_const + 1 :]
    copies = [pltpu.make_async_copy(s, h, copied.at[i]) for i, (s, h) in enumerate(zip(sources, held))]
    first_step = pl.program_id(0) == 0

    @pl.when(first_step)
    def _():
        for copy in copies:
            copy.start()

    (table_ref, base_x_ref, base_xt2_ref, field_y2_ref, field_yt_ref) = held[:5]
    (station_y2_ref, spread_ref, back_ref, same_ref, regroup_ref) = held[5:]
    deep = LANES // grid_y // boots
    slabs = DEPTHS // deep
    stations = station_ref.shape[1]
    first = (slot_ref[0] * pl.num_programs(0) + pl.program_id(0)) * boots

    rows[...] = jnp.zeros_like(rows)
    for b in range(boots):
        rows[b * grid_y : b * grid_y + 5, :] = observed_ref[...]
    data[...] = jnp.transpose(rows[...])
    for b in range(boots):
        count = counts_ref[pl.ds(first + b, 1), :].astype(F32)
        for c in range(5):
            rows[b * grid_y + c : b * grid_y + c + 1, :] = count * comp_ref[c]
    weights[...] = jnp.transpose(rows[...])

    station_x = station_ref[0:1, :]
    station_y = station_ref[1:2, :]
    place_x = (lax.broadcasted_iota(jnp.int32, (GRID, stations), 0) == station_x).astype(F32)
    place_y = (lax.broadcasted_iota(jnp.int32, (LANES, stations), 0) == station_y).astype(F32)
    place_xt = jnp.transpose(place_x).astype(BF)
    place_yt = jnp.transpose(place_y)[:, :grid_y].astype(BF)

    @pl.when(first_step)
    def _():
        for copy in copies[1:]:
            copy.wait()

    pick_xt[...] = dot(base_xt2_ref[:, :GRID], place_x.astype(BF)).astype(BF)
    pick_x[...] = dot(place_xt, base_x_ref[...]).astype(BF)
    pick_y[...] = dot(place_yt, station_y2_ref[0]) + dot(place_yt, station_y2_ref[1])

    @pl.when(first_step)
    def _():
        copies[0].wait()

    def back_project():
        q = values[...]
        for c, (odd_x, odd_y) in enumerate(PARITY):
            if c % 2 == 0:
                spreads = dot(q, spread_ref[c // 2])
            e = spreads[:, c % 2 * LANES : (c % 2 + 1) * LANES]
            v = jnp.concatenate([e * pick_y[:, :LANES], e * pick_y[:, LANES:]], axis=1).astype(BF)
            spec = dot(pick_xt[...], v)
            for hx in range(2):
                for hy in range(2):
                    part = spec[hx * GRID : (hx + 1) * GRID, hy * LANES : (hy + 1) * LANES]
                    spec_q[c, hx, hy] = -part if (odd_x * hx + odd_y * hy) % 2 else part

        @pl.loop(0, GRID // 16)
        def _(tile):
            at = pl.ds(pl.multiple_of(tile * 16, 16), 16)
            for hx in range(2):
                q = [[spec_q[c, hx ^ PARITY[c][0], hy, at, :] for hy in range(2)] for c in range(5)]
                to = pl.ds(pl.multiple_of(hx * GRID + tile * 16, 16), 16)
                for z in range(slabs):
                    t = [table_ref[c, z, at, :] for c in range(5)]
                    for hy in range(2):
                        total = None
                        for c in range(5):
                            term = t[c] * q[c][hy ^ PARITY[c][1]]
                            total = term if total is None else total + term
                        spec_g[z, to, hy * LANES : (hy + 1) * LANES] = total.astype(BF)

        for z in range(slabs):
            along_x = dot(base_x_ref[...], spec_g[z]).astype(BF)
            applied[z] = dot(along_x, field_yt_ref[...])

    def predict():
        d = direction[...].reshape(slabs * GRID, LANES).astype(BF)
        y = dot(jnp.concatenate([d, d], axis=1), field_y2_ref[...]).astype(BF)
        for z in range(slabs):
            part = y[z * GRID : (z + 1) * GRID]
            spec_f[z] = dot(base_xt2_ref[...], jnp.concatenate([part, part], axis=0))

        @pl.loop(0, GRID // 16)
        def _(tile):
            done = []
            for sub in range(2):
                at = [pl.ds(pl.multiple_of(hx * GRID + tile * 16 + sub * 8, 8), 8) for hx in range(2)]
                total = [[[None] * 2 for _ in range(2)] for _ in range(5)]
                for z in range(slabs):
                    f = [[spec_f[z, at[hx], hy * LANES : (hy + 1) * LANES] for hy in range(2)] for hx in range(2)]
                    for c, (odd_x, odd_y) in enumerate(PARITY):
                        t = table_ref[c, z, at[0], :]
                        for hx in range(2):
                            for hy in range(2):
                                term = t * f[hx ^ odd_x][hy ^ odd_y]
                                old = total[c][hx][hy]
                                total[c][hx][hy] = term if old is None else old + term
                done.append(total)
            for c, (odd_x, odd_y) in enumerate(PARITY):
                for hx in range(2):
                    to = pl.ds(pl.multiple_of(hx * GRID + tile * 16, 16), 16)
                    for hy in range(2):
                        part = jnp.concatenate([done[sub][c][hx][hy] for sub in range(2)], axis=0)
                        part = -part if (odd_x * hx + odd_y * hy) % 2 else part
                        spec_i[c, to, hy * LANES : (hy + 1) * LANES] = part.astype(BF)

        total = None
        pair = []
        for c in range(5):
            part = dot(pick_x[...], spec_i[c]) * pick_y[...]
            pair.append((part[:, :LANES] + part[:, LANES:]).astype(BF))
            if c % 2 or c == 4:
                if c == 4:
                    part = dot(pair[0], back_ref[2, :LANES, :])
                else:
                    part = dot(jnp.concatenate(pair, axis=1), back_ref[c // 2])
                total = part if total is None else total + part
                pair = []
        image[...] = total

    def fold(a):
        return jnp.sum(a.reshape(a.shape[0] // 8, 8, LANES), axis=0)

    def total_of(partial):
        if boots == 1:
            return jnp.broadcast_to(jnp.sum(partial, keepdims=True), (1, LANES))
        sums = jnp.dot(partial, same_ref[...], precision=lax.Precision.HIGHEST, preferred_element_type=F32)
        return jnp.sum(sums, axis=0, keepdims=True)

    def depth_weight(z):
        within = lax.broadcasted_iota(jnp.int32, (1, LANES), 1) // (boots * grid_y)
        depth = (within + z * deep).astype(F32) + 0.5 + station_height
        ratio = station_height / depth
        return ratio * ratio * ratio

    models[...] = jnp.zeros_like(models)
    pred[...] = jnp.zeros_like(pred)

    def outer(_, carry):
        values[...] = (weights[...] * (data[...] - pred[...])).astype(BF)
        back_project()
        norm = cross = jnp.zeros((8, LANES), F32)
        for z in range(slabs):
            m = models[z]
            p = damping * depth_weight(z) / (m * m + focusing * focusing)
            penalty[z] = p
            r = applied[z] - p * m
            residual[z] = r
            direction[z] = r
            norm += fold(r * r)
            cross += fold(p * r * r)
        norm = total_of(norm)
        for inner in range(CG_STEPS):
            predict()
            weighted = weights[...] * image[...]
            step = norm / total_of(cross + fold(weighted * image[...]))
            pred[...] += step * image[...]
            if inner == CG_STEPS - 1:
                for z in range(slabs):
                    models[z] += step * direction[z]
                break
            values[...] = weighted.astype(BF)
            back_project()
            new = jnp.zeros((8, LANES), F32)
            for z in range(slabs):
                d = direction[z]
                models[z] += step * d
                r = residual[z] - step * (applied[z] + penalty[z] * d)
                residual[z] = r
                new += fold(r * r)
            new = total_of(new)
            ratio = new / norm
            cross = jnp.zeros((8, LANES), F32)
            for z in range(slabs):
                d = residual[z] + ratio * direction[z]
                direction[z] = d
                cross += fold(penalty[z] * d * d)
            norm = new
        return carry

    lax.fori_loop(0, IRLS, outer, 0)

    for group in range(slabs // boots):
        m = jnp.concatenate([models[group * boots + i].astype(BF) for i in range(boots)], axis=1)
        if boots > 1:
            m = dot(m, regroup_ref[...]).astype(BF)
        for b in range(boots):
            out_ref[b, :, group * LANES : (group + 1) * LANES] = m[:, b * LANES : (b + 1) * LANES]


def solve(slot, comp_weight, station_index, observed, counts, mine, grid_y):
    boots = min(mine, LANES // grid_y)
    slabs = DEPTHS * grid_y * boots // LANES
    stations = station_index.shape[1]
    consts = [jnp.asarray(v) for v in constants(grid_y, boots).values()]
    vmem = pltpu.VMEM
    whole = lambda a: pl.BlockSpec(a.shape, lambda i, n=a.ndim: (0,) * n)
    smem = pl.BlockSpec(memory_space=pltpu.SMEM)
    field = vmem((slabs, GRID, LANES), F32)
    at_stations = vmem((stations, LANES), F32)
    inputs = [station_index, observed, counts]
    return pl.pallas_call(
        functools.partial(solve_kernel, grid_y, boots, len(consts)),
        out_shape=jax.ShapeDtypeStruct((mine, GRID, DEPTHS * grid_y), BF),
        grid=(mine // boots,),
        in_specs=[smem, smem]
        + [whole(a) for a in inputs]
        + [pl.BlockSpec(memory_space=pl.ANY) for _ in consts],
        out_specs=pl.BlockSpec((boots, GRID, DEPTHS * grid_y), lambda i: (i, 0, 0)),
        scratch_shapes=[vmem(a.shape, a.dtype) for a in consts]
        + [
            pltpu.SemaphoreType.DMA((len(consts),)),
            vmem((stations, 2 * GRID), BF),
            vmem((2 * GRID, stations), BF),
            vmem((stations, 2 * LANES), F32),
            at_stations,
            at_stations,
            at_stations,
            at_stations,
            vmem((stations, LANES), BF),
            vmem((LANES, stations), F32),
            vmem((5, 2, 2, GRID, LANES), F32),
            vmem((5, 2 * GRID, 2 * LANES), BF),
            vmem((slabs, 2 * GRID, 2 * LANES), F32),
            vmem((slabs, 2 * GRID, 2 * LANES), BF),
            field,
            field,
            field,
            field,
            field,
        ],
        compiler_params=pltpu.CompilerParams(vmem_limit_bytes=60 * 1024 * 1024),
        cost_estimate=pl.CostEstimate(flops=10**10, bytes_accessed=10**7, transcendentals=0),
        name="solve",
    )(slot, comp_weight, *inputs, *consts)


def pick_kernel(grid_y, count, models_ref, *refs):
    boots = models_ref.shape[0]
    for cell_ref, out_ref in zip(refs[:count], refs[count:]):
        cells = cell_ref.shape[1]
        place = cell_ref[...].astype(F32)
        wide = lambda row, rows: jnp.broadcast_to(row, (rows, cells)).astype(BF)
        y_row = wide(place[1:2], grid_y)
        z_row = wide(place[2:3], grid_y)
        here_y = lax.broadcasted_iota(jnp.int32, (grid_y, cells), 0).astype(F32).astype(BF) == y_row
        here_y = jnp.where(here_y, jnp.ones_like(y_row), jnp.zeros_like(y_row))
        chosen = jnp.concatenate(
            [jnp.where(z_row == jnp.full_like(z_row, z), here_y, jnp.zeros_like(here_y)) for z in range(DEPTHS)],
            axis=0,
        )
        at_x = lax.broadcasted_iota(jnp.int32, (GRID, cells), 0) == cell_ref[0:1, :]
        for b in range(boots):
            found = dot(models_ref[b], chosen)
            out_ref[b : b + 1, :] = jnp.sum(jnp.where(at_x, found, 0.0), axis=0, keepdims=True)


def pick(models, cells, grid_y):
    boots, _, depth_places = models.shape
    count = cells[0].shape[1]
    chunk = 512
    return pl.pallas_call(
        functools.partial(pick_kernel, grid_y, len(cells)),
        out_shape=[jax.ShapeDtypeStruct((boots, count), F32)] * len(cells),
        grid=(count // chunk,),
        in_specs=[pl.BlockSpec(models.shape, lambda i: (0, 0, 0))]
        + [pl.BlockSpec((3, chunk), lambda i: (0, i))] * len(cells),
        out_specs=[pl.BlockSpec((boots, chunk), lambda i: (0, i))] * len(cells),
        compiler_params=pltpu.CompilerParams(vmem_limit_bytes=48 * 1024 * 1024),
        cost_estimate=pl.CostEstimate(
            flops=2 * boots * GRID * depth_places * count * len(cells), bytes_accessed=10**6, transcendentals=0
        ),
        name="pick",
    )(models, *cells)


def local(wide, cell_index, station_index, observed, comp_weight, counts):
    boots = counts.shape[0]
    grid_y = cell_index.shape[1] * wide // (GRID * DEPTHS)
    team = TEAM if wide % TEAM == 0 and boots % TEAM == 0 else 1
    slot = lax.axis_index("wide").astype(jnp.int32) & (team - 1)

    def swap(a, k):
        return lax.ppermute(a, "wide", [(i, i ^ k) for i in range(wide)])

    theirs = [swap(cell_index, k) for k in range(1, team)]
    models = solve(slot.reshape(1), comp_weight, station_index, observed, counts, boots // team, grid_y)
    sent = [swap(a, k + 1) for k, a in enumerate(pick(models, theirs, grid_y))] if theirs else []
    got = jnp.stack([*pick(models, [cell_index], grid_y), *sent])
    bit = 1
    while bit < team:
        pairs = got.reshape((team // (2 * bit), 2, bit) + got.shape[1:])
        got = jnp.where(slot & bit != 0, pairs[:, ::-1], pairs).reshape(got.shape)
        bit *= 2
    return got.reshape(boots, -1)


def solution(mesh):
    in_specs = (P(None, "wide"), P(None, "groups"), P(None, "groups"), P(), P("groups", None))
    out_specs = P("groups", "wide")
    fn = functools.partial(local, mesh.shape["wide"])
    return jax.shard_map(fn, mesh=mesh, in_specs=in_specs, out_specs=out_specs, check_vma=False)
```

```python
import functools

import jax
import jax.numpy as jnp
import ml_dtypes
import numpy as np
from jax import lax
from jax.experimental import pallas as pl
from jax.experimental.pallas import tpu as pltpu
from jax.sharding import PartitionSpec as P

IRLS = 2
CG_STEPS = 2
GRID = 128
DEPTHS = 16
LANES = 128
TEAM = 4
BLOCK = 4

station_height = 2.0
focusing = 0.1
damping = 0.0002

PARITY = ((0, 0), (1, 1), (1, 0), (0, 0), (0, 1))
BF = jnp.bfloat16
F32 = jnp.float32


def offset_table(grid_y):
    one = np.float32
    dx = np.arange(GRID, dtype=one)[:, None, None]
    dy = np.arange(grid_y, dtype=one)[None, :, None]
    dz = (np.arange(DEPTHS, dtype=one) + one(0.5) + one(station_height))[None, None, :]
    radius2 = dx * dx + dy * dy + dz * dz
    strength = one(1) / (radius2 * radius2 * np.sqrt(radius2))
    three = one(3)
    kinds = [
        (three * dx * dx - radius2) * strength,
        three * dx * dy * strength,
        three * dx * dz * strength,
        (three * dy * dy - radius2) * strength,
        three * dy * dz * strength,
    ]
    return [k.astype(ml_dtypes.bfloat16).astype(np.float64) for k in kinds]


def angles(size):
    return 2 * np.pi * np.outer(np.arange(size), np.arange(size) + 0.5) / (2 * size)


def basis(size):
    return np.concatenate([np.cos(angles(size)), np.sin(angles(size))], axis=1)


def spectrum(values, odd, size):
    if odd:
        trig = 2 * np.sin(angles(size))
    else:
        trig = np.cos(angles(size)) * np.where(np.arange(size) == 0, 1, 2)[:, None]
    return np.tensordot(trig.T / size, values, axes=(1, 0))


def split(matrix):
    high = matrix.astype(ml_dtypes.bfloat16)
    low = (matrix - high.astype(np.float64)).astype(ml_dtypes.bfloat16)
    return high, low


@functools.lru_cache(maxsize=None)
def constants(grid_y, boots):
    deep = LANES // grid_y // boots
    slabs = DEPTHS // deep
    table = []
    for values, (odd_x, odd_y) in zip(offset_table(grid_y), PARITY):
        t = spectrum(values, odd_x, GRID)
        t = np.moveaxis(spectrum(np.moveaxis(t, 1, 0), odd_y, grid_y), 0, 1)
        t = np.moveaxis(t, 2, 0).reshape(slabs, deep, GRID, 1, grid_y).transpose(0, 2, 1, 3, 4)
        table.append(np.tile(t, (1, 1, 1, boots, 1)).reshape(slabs, GRID, LANES))
    table = np.stack(table).astype(np.float32)

    base_x = basis(GRID)
    base_y = basis(grid_y).reshape(grid_y, 2, grid_y)
    copies = deep * boots
    field_y = np.einsum("ab,yhl->ayhbl", np.eye(copies), base_y).reshape(LANES, 2 * LANES)
    station_y = np.einsum("b,yhl->yhbl", np.ones(copies), base_y).reshape(grid_y, 2 * LANES)
    spread = np.zeros((6, deep, boots, grid_y, deep, boots, grid_y))
    for c in range(5):
        for b in range(boots):
            spread[c, 0, b, c, :, b, :] = 1
    spread = spread.reshape(3, 2, LANES, LANES)
    back = spread.transpose(0, 1, 3, 2).reshape(3, 2 * LANES, LANES)
    spread = spread.transpose(0, 2, 1, 3).reshape(3, LANES, 2 * LANES)
    same = np.einsum("ab,dc,yz->dayczb", np.eye(boots), np.ones((deep, deep)), np.ones((grid_y, grid_y)))
    same = same.transpose(0, 1, 2, 3, 5, 4).reshape(LANES, LANES)
    regroup = np.einsum("st,de,ab,yz->sdaybtez", *[np.eye(n) for n in (boots, deep, boots, grid_y)])
    regroup = regroup.reshape(boots * LANES, boots * LANES)
    y_high, y_low = split(field_y)
    x_high, x_low = split(base_x.T)
    half = lambda a: a.astype(ml_dtypes.bfloat16)
    return dict(
        table=table,
        base_x=half(base_x),
        base_xt2=np.concatenate([x_high, x_low], axis=1),
        field_y2=np.concatenate([y_high, y_low], axis=0),
        field_yt=half(field_y.T),
        station_y2=np.stack(split(station_y)),
        spread=half(spread),
        back=half(back),
        same=same.astype(np.float32),
        regroup=half(regroup),
    )


def dot(a, b):
    return jnp.dot(a, b, preferred_element_type=F32)


def solve_kernel(grid_y, boots, n_const, slot_ref, comp_ref, station_ref, observed_ref, counts_ref, *refs):
    sources, out_ref = refs[:n_const], refs[n_const]
    held = refs[n_const + 1 : 2 * n_const + 1]
    (
        copied,
        pick_x,
        pick_xt,
        pick_y,
        weights,
        data,
        pred,
        image,
        values,
        rows,
        sums,
        spec_q,
        spec_i,
        spec_f,
        spec_g,
        models,
        residual,
        direction,
        penalty,
        applied,
    ) = refs[2 * n_const + 1 :]
    copies = [pltpu.make_async_copy(s, h, copied.at[i]) for i, (s, h) in enumerate(zip(sources, held))]
    first_step = pl.program_id(0) == 0

    @pl.when(first_step)
    def _():
        for copy in copies:
            copy.start()

    (table_ref, base_x_ref, base_xt2_ref, field_y2_ref, field_yt_ref) = held[:5]
    (station_y2_ref, spread_ref, back_ref, same_ref, regroup_ref) = held[5:]
    deep = LANES // grid_y // boots
    slabs = DEPTHS // deep
    stations = station_ref.shape[1]
    first = (slot_ref[0] * pl.num_programs(0) + pl.program_id(0)) * boots
    blocks = [list(range(z, z + BLOCK)) for z in range(0, slabs, BLOCK)]

    rows[...] = jnp.zeros_like(rows)
    for b in range(boots):
        rows[b * grid_y : b * grid_y + 5, :] = observed_ref[...]
    data[...] = jnp.transpose(rows[...])
    for b in range(boots):
        count = counts_ref[pl.ds(first + b, 1), :].astype(F32)
        for c in range(5):
            rows[b * grid_y + c : b * grid_y + c + 1, :] = count * comp_ref[c]
    weights[...] = jnp.transpose(rows[...])
    values[...] = (weights[...] * data[...]).astype(BF)

    station_x = station_ref[0:1, :]
    station_y = station_ref[1:2, :]
    place_x = (lax.broadcasted_iota(jnp.int32, (GRID, stations), 0) == station_x).astype(F32)
    place_y = (lax.broadcasted_iota(jnp.int32, (LANES, stations), 0) == station_y).astype(F32)
    place_xt = jnp.transpose(place_x).astype(BF)
    place_yt = jnp.transpose(place_y)[:, :grid_y].astype(BF)

    @pl.when(first_step)
    def _():
        for copy in copies[1:]:
            copy.wait()

    pick_xt[...] = dot(base_xt2_ref[:, :GRID], place_x.astype(BF)).astype(BF)
    pick_x[...] = dot(place_xt, base_x_ref[...]).astype(BF)
    pick_y[...] = dot(place_yt, station_y2_ref[0]) + dot(place_yt, station_y2_ref[1])

    @pl.when(first_step)
    def _():
        copies[0].wait()

    def back_project():
        q = values[...]
        for c, (odd_x, odd_y) in enumerate(PARITY):
            if c % 2 == 0:
                spreads = dot(q, spread_ref[c // 2])
            e = spreads[:, c % 2 * LANES : (c % 2 + 1) * LANES]
            v = jnp.concatenate([e * pick_y[:, :LANES], e * pick_y[:, LANES:]], axis=1).astype(BF)
            spec = dot(pick_xt[...], v)
            for hx in range(2):
                for hy in range(2):
                    part = spec[hx * GRID : (hx + 1) * GRID, hy * LANES : (hy + 1) * LANES]
                    spec_q[c, hx, hy] = -part if (odd_x * hx + odd_y * hy) % 2 else part

        for block in blocks:
            for row in range(0, GRID, 16):
                at = slice(row, row + 16)
                for hx in range(2):
                    q = [[spec_q[c, hx ^ PARITY[c][0], hy, at, :] for hy in range(2)] for c in range(5)]
                    to = slice(hx * GRID + row, hx * GRID + row + 16)
                    for z in block:
                        t = [table_ref[c, z, at, :] for c in range(5)]
                        for hy in range(2):
                            total = None
                            for c in range(5):
                                term = t[c] * q[c][hy ^ PARITY[c][1]]
                                total = term if total is None else total + term
                            spec_g[z, to, hy * LANES : (hy + 1) * LANES] = total.astype(BF)
            for z in block:
                along_x = dot(base_x_ref[...], spec_g[z]).astype(BF)
                applied[z] = dot(along_x, field_yt_ref[...])

    def predict():
        for block in blocks:
            r = residual[block[0] : block[-1] + 1].reshape(BLOCK * GRID, LANES).astype(BF)
            y = dot(jnp.concatenate([r, r], axis=1), field_y2_ref[...]).astype(BF)
            for i, z in enumerate(block):
                part = y[i * GRID : (i + 1) * GRID]
                spec_f[z] = dot(base_xt2_ref[...], jnp.concatenate([part, part], axis=0))
            for row in range(0, GRID, 16):
                done = []
                for sub in range(row, row + 16, 8):
                    at = [slice(hx * GRID + sub, hx * GRID + sub + 8) for hx in range(2)]
                    total = [[[None] * 2 for _ in range(2)] for _ in range(5)]
                    if block is not blocks[0]:
                        total = [
                            [[spec_q[c, hx, hy, at[0], :] for hy in range(2)] for hx in range(2)] for c in range(5)
                        ]
                    for z in block:
                        f = [[spec_f[z, at[hx], hy * LANES : (hy + 1) * LANES] for hy in range(2)] for hx in range(2)]
                        for c, (odd_x, odd_y) in enumerate(PARITY):
                            t = table_ref[c, z, at[0], :]
                            for hx in range(2):
                                for hy in range(2):
                                    term = t * f[hx ^ odd_x][hy ^ odd_y]
                                    old = total[c][hx][hy]
                                    total[c][hx][hy] = term if old is None else old + term
                    if block is not blocks[-1]:
                        for c in range(5):
                            for hx in range(2):
                                for hy in range(2):
                                    spec_q[c, hx, hy, at[0], :] = total[c][hx][hy]
                    done.append(total)
                if block is not blocks[-1]:
                    continue
                for c, (odd_x, odd_y) in enumerate(PARITY):
                    for hx in range(2):
                        for hy in range(2):
                            part = jnp.concatenate([done[sub][c][hx][hy] for sub in range(2)], axis=0)
                            part = -part if (odd_x * hx + odd_y * hy) % 2 else part
                            spec_i[c, hx * GRID + row : hx * GRID + row + 16, hy * LANES : (hy + 1) * LANES] = (
                                part.astype(BF)
                            )

        total = None
        pair = []
        for c in range(5):
            part = dot(pick_x[...], spec_i[c]) * pick_y[...]
            pair.append((part[:, :LANES] + part[:, LANES:]).astype(BF))
            if c % 2 or c == 4:
                if c == 4:
                    part = dot(pair[0], back_ref[2, :LANES, :])
                else:
                    part = dot(jnp.concatenate(pair, axis=1), back_ref[c // 2])
                total = part if total is None else total + part
                pair = []
        return total

    def fold(a):
        return jnp.sum(a.reshape(a.shape[0] // 8, 8, LANES), axis=0)

    def total_of(partial):
        if boots == 1:
            return jnp.broadcast_to(jnp.sum(partial, keepdims=True), (1, LANES))
        sums = jnp.dot(partial, same_ref[...], precision=lax.Precision.HIGHEST, preferred_element_type=F32)
        return jnp.sum(sums, axis=0, keepdims=True)

    def depth_weight(z):
        within = lax.broadcasted_iota(jnp.int32, (1, LANES), 1) // (boots * grid_y)
        depth = (within + z * deep).astype(F32) + 0.5 + station_height
        ratio = station_height / depth
        return ratio * ratio * ratio

    models[...] = jnp.zeros_like(models)
    direction[...] = jnp.zeros_like(direction)
    pred[...] = jnp.zeros_like(pred)
    image[...] = jnp.zeros_like(image)

    def round_of(index, carry):
        old_norm, old_step = carry
        fresh = index % CG_STEPS == 0
        back_project()

        @pl.when(fresh)
        def _():
            norm = jnp.zeros((8, LANES), F32)
            for z in range(slabs):
                m = models[z]
                p = damping * depth_weight(z) / (m * m + focusing * focusing)
                penalty[z] = p
                r = applied[z] - p * m
                residual[z] = r
                norm += fold(r * r)
            sums[...] = norm

        @pl.when(jnp.logical_not(fresh))
        def _():
            norm = jnp.zeros((8, LANES), F32)
            for z in range(slabs):
                r = residual[z] - old_step * (applied[z] + penalty[z] * direction[z])
                residual[z] = r
                norm += fold(r * r)
            sums[...] = norm

        norm = total_of(sums[...])
        ratio = jnp.where(fresh, 0.0, norm / old_norm)
        cross = jnp.zeros((8, LANES), F32)
        for z in range(slabs):
            d = residual[z] + ratio * direction[z]
            direction[z] = d
            cross += fold(penalty[z] * d * d)
        here = predict() + ratio * image[...]
        image[...] = here
        step = norm / total_of(cross + fold(weights[...] * here * here))
        for z in range(slabs):
            models[z] += step * direction[z]
        now = pred[...] + step * here
        pred[...] = now
        values[...] = (weights[...] * jnp.where(fresh, here, data[...] - now)).astype(BF)
        return norm, step

    one = jnp.ones((1, LANES), F32)
    lax.fori_loop(0, IRLS * CG_STEPS, round_of, (one, one))

    for group in range(slabs // boots):
        m = jnp.concatenate([models[group * boots + i].astype(BF) for i in range(boots)], axis=1)
        if boots > 1:
            m = dot(m, regroup_ref[...]).astype(BF)
        for b in range(boots):
            out_ref[b * GRID : (b + 1) * GRID, group * LANES : (group + 1) * LANES] = (
                m[:, b * LANES : (b + 1) * LANES]
            )


def solve(slot, comp_weight, station_index, observed, counts, mine, grid_y):
    boots = min(mine, LANES // grid_y)
    slabs = DEPTHS * grid_y * boots // LANES
    stations = station_index.shape[1]
    consts = [jnp.asarray(v) for v in constants(grid_y, boots).values()]
    vmem = pltpu.VMEM
    whole = lambda a: pl.BlockSpec(a.shape, lambda i, n=a.ndim: (0,) * n)
    smem = pl.BlockSpec(memory_space=pltpu.SMEM)
    field = vmem((slabs, GRID, LANES), F32)
    at_stations = vmem((stations, LANES), F32)
    inputs = [station_index, observed, counts]
    return pl.pallas_call(
        functools.partial(solve_kernel, grid_y, boots, len(consts)),
        out_shape=jax.ShapeDtypeStruct((mine * GRID, DEPTHS * grid_y), BF),
        grid=(mine // boots,),
        in_specs=[smem, smem]
        + [whole(a) for a in inputs]
        + [pl.BlockSpec(memory_space=pltpu.HBM) for _ in consts],
        out_specs=pl.BlockSpec((boots * GRID, DEPTHS * grid_y), lambda i: (i, 0)),
        scratch_shapes=[vmem(a.shape, a.dtype) for a in consts]
        + [
            pltpu.SemaphoreType.DMA((len(consts),)),
            vmem((stations, 2 * GRID), BF),
            vmem((2 * GRID, stations), BF),
            vmem((stations, 2 * LANES), F32),
            at_stations,
            at_stations,
            at_stations,
            at_stations,
            vmem((stations, LANES), BF),
            vmem((LANES, stations), F32),
            vmem((8, LANES), F32),
            vmem((5, 2, 2, GRID, LANES), F32),
            vmem((5, 2 * GRID, 2 * LANES), BF),
            vmem((slabs, 2 * GRID, 2 * LANES), F32),
            vmem((slabs, 2 * GRID, 2 * LANES), BF),
            field,
            field,
            field,
            field,
            field,
        ],
        compiler_params=pltpu.CompilerParams(vmem_limit_bytes=40 * 1024 * 1024),
        cost_estimate=pl.CostEstimate(flops=10**10, bytes_accessed=10**7, transcendentals=0),
        name="solve",
    )(slot, comp_weight, *inputs, *consts)


def pick_kernel(grid_y, boots, count, models_ref, *refs):
    chunk = 512

    def pick_chunk(cell_ref, out_ref, at):
        cells = cell_ref[:, at]
        place = cells.astype(F32)
        wide = lambda row, rows: jnp.broadcast_to(row, (rows, chunk)).astype(BF)
        y_row = wide(place[1:2], grid_y)
        z_row = wide(place[2:3], grid_y)
        here_y = lax.broadcasted_iota(jnp.int32, (grid_y, chunk), 0).astype(F32).astype(BF) == y_row
        here_y = jnp.where(here_y, jnp.ones_like(y_row), jnp.zeros_like(y_row))
        chosen = jnp.concatenate(
            [jnp.where(z_row == jnp.full_like(z_row, z), here_y, jnp.zeros_like(here_y)) for z in range(DEPTHS)],
            axis=0,
        )
        at_x = lax.broadcasted_iota(jnp.int32, (GRID, chunk), 0) == cells[0:1]
        found = dot(models_ref[...], chosen)
        for b in range(boots):
            part = jnp.where(at_x, found[b * GRID : (b + 1) * GRID], 0.0)
            out_ref[b : b + 1, at] = jnp.sum(part, axis=0, keepdims=True)

    per = max(1, 4 // count)

    @pl.loop(0, refs[0].shape[1] // (per * chunk))
    def _(step):
        for i in range(per):
            at = pl.ds(pl.multiple_of((step * per + i) * chunk, chunk), chunk)
            for cell_ref, out_ref in zip(refs[:count], refs[count:]):
                pick_chunk(cell_ref, out_ref, at)


def pick(models, cells, grid_y):
    boots = models.shape[0] // GRID
    count = cells[0].shape[1]
    vmem = pl.BlockSpec(memory_space=pltpu.VMEM)
    return pl.pallas_call(
        functools.partial(pick_kernel, grid_y, boots, len(cells)),
        out_shape=[jax.ShapeDtypeStruct((boots, count), F32)] * len(cells),
        in_specs=[vmem] * (1 + len(cells)),
        out_specs=[vmem] * len(cells),
        compiler_params=pltpu.CompilerParams(vmem_limit_bytes=40 * 1024 * 1024),
        cost_estimate=pl.CostEstimate(
            flops=2 * models.size * count * len(cells), bytes_accessed=10**6, transcendentals=0
        ),
        name="pick",
    )(models, *cells)


def local(wide, cell_index, station_index, observed, comp_weight, counts):
    boots = counts.shape[0]
    grid_y = cell_index.shape[1] * wide // (GRID * DEPTHS)
    team = TEAM if wide % TEAM == 0 and boots % TEAM == 0 else 1
    slot = lax.axis_index("wide").astype(jnp.int32) & (team - 1)

    def swap(a, k):
        return lax.ppermute(a, "wide", [(i, i ^ k) for i in range(wide)])

    theirs = [swap(cell_index, k) for k in range(1, team)]
    models = solve(slot.reshape(1), comp_weight, station_index, observed, counts, boots // team, grid_y)
    sent = [swap(a, k + 1) for k, a in enumerate(pick(models, theirs, grid_y))] if theirs else []
    got = [*pick(models, [cell_index], grid_y), *sent]
    blocks = []
    for member in range(team):
        block = got[member]
        for other in range(1, team):
            block = jnp.where(slot == other, got[member ^ other], block)
        blocks.append(block)
    return jnp.concatenate(blocks, axis=0)


def solution(mesh):
    in_specs = (P(None, "wide"), P(None, "groups"), P(None, "groups"), P(), P("groups", None))
    out_specs = P("groups", "wide")
    fn = functools.partial(local, mesh.shape["wide"])
    return jax.shard_map(fn, mesh=mesh, in_specs=in_specs, out_specs=out_specs, check_vma=False)
```

```python
import functools

import jax
import jax.numpy as jnp
import ml_dtypes
import numpy as np
from jax import lax
from jax.experimental import pallas as pl
from jax.experimental.pallas import tpu as pltpu
from jax.sharding import PartitionSpec as P

IRLS = 2
CG_STEPS = 2
GRID = 128
DEPTHS = 16
LANES = 128
TEAM = 4
BLOCK = 4
CHUNK = 512

station_height = 2.0
focusing = 0.1
damping = 0.0002

PARITY = ((0, 0), (1, 1), (1, 0), (0, 0), (0, 1))
BF = jnp.bfloat16
F32 = jnp.float32


def offset_table(grid_y):
    one = np.float32
    dx = np.arange(GRID, dtype=one)[:, None, None]
    dy = np.arange(grid_y, dtype=one)[None, :, None]
    dz = (np.arange(DEPTHS, dtype=one) + one(0.5) + one(station_height))[None, None, :]
    radius2 = dx * dx + dy * dy + dz * dz
    strength = one(1) / (radius2 * radius2 * np.sqrt(radius2))
    three = one(3)
    kinds = [
        (three * dx * dx - radius2) * strength,
        three * dx * dy * strength,
        three * dx * dz * strength,
        (three * dy * dy - radius2) * strength,
        three * dy * dz * strength,
    ]
    return [k.astype(ml_dtypes.bfloat16).astype(np.float64) for k in kinds]


def angles(size):
    return 2 * np.pi * np.outer(np.arange(size), np.arange(size) + 0.5) / (2 * size)


def basis(size):
    return np.concatenate([np.cos(angles(size)), np.sin(angles(size))], axis=1)


def spectrum(values, odd, size):
    if odd:
        trig = 2 * np.sin(angles(size))
    else:
        trig = np.cos(angles(size)) * np.where(np.arange(size) == 0, 1, 2)[:, None]
    return np.tensordot(trig.T / size, values, axes=(1, 0))


def split(matrix):
    high = matrix.astype(ml_dtypes.bfloat16)
    low = (matrix - high.astype(np.float64)).astype(ml_dtypes.bfloat16)
    return high, low


@functools.lru_cache(maxsize=None)
def constants(grid_y, boots):
    deep = LANES // grid_y // boots
    slabs = DEPTHS // deep
    table = []
    for values, (odd_x, odd_y) in zip(offset_table(grid_y), PARITY):
        t = spectrum(values, odd_x, GRID)
        t = np.moveaxis(spectrum(np.moveaxis(t, 1, 0), odd_y, grid_y), 0, 1)
        t = np.moveaxis(t, 2, 0).reshape(slabs, deep, GRID, 1, grid_y).transpose(0, 2, 1, 3, 4)
        table.append(np.tile(t, (1, 1, 1, boots, 1)).reshape(slabs, GRID, LANES))
    table = np.stack(table).astype(np.float32)

    base_x = basis(GRID)
    base_y = basis(grid_y).reshape(grid_y, 2, grid_y)
    copies = deep * boots
    field_y = np.einsum("ab,yhl->ayhbl", np.eye(copies), base_y).reshape(LANES, 2 * LANES)
    station_y = np.einsum("b,yhl->yhbl", np.ones(copies), base_y).reshape(grid_y, 2 * LANES)
    spread = np.zeros((5, deep, boots, grid_y, deep, boots, grid_y))
    for c in range(5):
        for b in range(boots):
            spread[c, 0, b, c, :, b, :] = 1
    spread = spread.reshape(5, LANES, LANES)
    back = spread.transpose(0, 2, 1).reshape(5 * LANES, LANES)
    spread = spread.transpose(1, 0, 2).reshape(LANES, 5 * LANES)
    same = np.einsum("ab,dc,yz->dayczb", np.eye(boots), np.ones((deep, deep)), np.ones((grid_y, grid_y)))
    same = same.transpose(0, 1, 2, 3, 5, 4).reshape(LANES, LANES)
    regroup = np.einsum("st,de,ab,yz->sdaybtez", *[np.eye(n) for n in (boots, deep, boots, grid_y)])
    regroup = regroup.reshape(boots * LANES, boots * LANES)
    y_high, y_low = split(field_y)
    x_high, x_low = split(base_x.T)
    half = lambda a: a.astype(ml_dtypes.bfloat16)
    return dict(
        table=table,
        base_x=half(base_x),
        base_xt2=np.concatenate([x_high, x_low], axis=1),
        field_y2=np.concatenate([y_high, y_low], axis=0),
        field_yt=half(field_y.T),
        station_y2=np.stack(split(station_y)),
        spread=half(spread),
        back=half(back),
        same=same.astype(np.float32),
        regroup=half(regroup),
    )


def dot(a, b):
    return jnp.dot(a, b, preferred_element_type=F32)


def solve_kernel(grid_y, boots, n_const, team, slot_ref, comp_ref, station_ref, observed_ref, counts_ref, *refs):
    cell_refs, refs = refs[:team], refs[team:]
    sources, refs = refs[:n_const], refs[n_const:]
    out_refs, refs = refs[:team], refs[team:]
    held, refs = refs[:n_const], refs[n_const:]
    (
        copied,
        pick_x,
        pick_xt,
        pick_y,
        weights,
        data,
        pred,
        image,
        values,
        rows,
        sums,
        spec_q,
        spec_i,
        spec_f,
        spec_g,
        models,
        residual,
        direction,
        penalty,
        applied,
        found_in,
    ) = refs
    copies = [pltpu.make_async_copy(s, h, copied.at[i]) for i, (s, h) in enumerate(zip(sources, held))]
    first_step = pl.program_id(0) == 0

    @pl.when(first_step)
    def _():
        for copy in copies:
            copy.start()

    (table_ref, base_x_ref, base_xt2_ref, field_y2_ref, field_yt_ref) = held[:5]
    (station_y2_ref, spread_ref, back_ref, same_ref, regroup_ref) = held[5:]
    deep = LANES // grid_y // boots
    slabs = DEPTHS // deep
    stations = station_ref.shape[1]
    first = (slot_ref[0] * pl.num_programs(0) + pl.program_id(0)) * boots
    blocks = [list(range(z, z + BLOCK)) for z in range(0, slabs, BLOCK)]

    rows[...] = jnp.zeros_like(rows)
    for b in range(boots):
        rows[b * grid_y : b * grid_y + 5, :] = observed_ref[...]
    data[...] = jnp.transpose(rows[...])
    for b in range(boots):
        count = counts_ref[pl.ds(first + b, 1), :].astype(F32)
        for c in range(5):
            rows[b * grid_y + c : b * grid_y + c + 1, :] = count * comp_ref[c]
    weights[...] = jnp.transpose(rows[...])
    values[...] = (weights[...] * data[...]).astype(BF)

    station_x = station_ref[0:1, :]
    station_y = station_ref[1:2, :]
    place_x = (lax.broadcasted_iota(jnp.int32, (GRID, stations), 0) == station_x).astype(F32)
    place_y = (lax.broadcasted_iota(jnp.int32, (LANES, stations), 0) == station_y).astype(F32)
    place_xt = jnp.transpose(place_x).astype(BF)
    place_yt = jnp.transpose(place_y)[:, :grid_y].astype(BF)

    @pl.when(first_step)
    def _():
        for copy in copies[1:]:
            copy.wait()

    pick_xt[...] = dot(base_xt2_ref[:, :GRID], place_x.astype(BF)).astype(BF)
    pick_x[...] = dot(place_xt, base_x_ref[...]).astype(BF)
    pick_y[...] = dot(place_yt, station_y2_ref[0]) + dot(place_yt, station_y2_ref[1])

    @pl.when(first_step)
    def _():
        copies[0].wait()

    def back_project():
        spreads = dot(values[...], spread_ref[...])
        parts = []
        for c in range(5):
            e = spreads[:, c * LANES : (c + 1) * LANES]
            parts += [e * pick_y[:, :LANES], e * pick_y[:, LANES:]]
        spec = dot(pick_xt[...], jnp.concatenate(parts, axis=1).astype(BF))
        for c, (odd_x, odd_y) in enumerate(PARITY):
            for hx in range(2):
                for hy in range(2):
                    lane = (2 * c + hy) * LANES
                    part = spec[hx * GRID : (hx + 1) * GRID, lane : lane + LANES]
                    spec_q[c, hx, hy] = -part if (odd_x * hx + odd_y * hy) % 2 else part

        for block in blocks:
            for row in range(0, GRID, 16):
                at = slice(row, row + 16)
                for hx in range(2):
                    q = [[spec_q[c, hx ^ PARITY[c][0], hy, at, :] for hy in range(2)] for c in range(5)]
                    to = slice(hx * GRID + row, hx * GRID + row + 16)
                    for z in block:
                        t = [table_ref[c, z, at, :] for c in range(5)]
                        for hy in range(2):
                            total = None
                            for c in range(5):
                                term = t[c] * q[c][hy ^ PARITY[c][1]]
                                total = term if total is None else total + term
                            lane = (2 * z + hy) * LANES
                            spec_g[to, lane : lane + LANES] = total.astype(BF)
            along_x = dot(base_x_ref[...], spec_g[:, block[0] * 2 * LANES : (block[-1] + 1) * 2 * LANES]).astype(BF)
            along_x = jnp.concatenate([along_x[:, i * 2 * LANES : (i + 1) * 2 * LANES] for i in range(BLOCK)], axis=0)
            applied[block[0] : block[-1] + 1] = dot(along_x, field_yt_ref[...]).reshape(BLOCK, GRID, LANES)

    def predict():
        for block in blocks:
            r = residual[block[0] : block[-1] + 1].reshape(BLOCK * GRID, LANES).astype(BF)
            y = dot(jnp.concatenate([r, r], axis=1), field_y2_ref[...]).astype(BF)
            y = jnp.concatenate([y[i * GRID : (i + 1) * GRID] for i in range(BLOCK)], axis=1)
            spec_f[:, block[0] * 2 * LANES : (block[-1] + 1) * 2 * LANES] = dot(
                base_xt2_ref[...], jnp.concatenate([y, y], axis=0)
            )
            for row in range(0, GRID, 16):
                done = []
                for sub in range(row, row + 16, 8):
                    at = [slice(hx * GRID + sub, hx * GRID + sub + 8) for hx in range(2)]
                    total = [[[None] * 2 for _ in range(2)] for _ in range(5)]
                    if block is not blocks[0]:
                        total = [
                            [[spec_q[c, hx, hy, at[0], :] for hy in range(2)] for hx in range(2)] for c in range(5)
                        ]
                    for z in block:
                        lane = 2 * z * LANES
                        f = [[spec_f[at[hx], lane + hy * LANES : lane + (hy + 1) * LANES] for hy in range(2)] for hx in range(2)]
                        for c, (odd_x, odd_y) in enumerate(PARITY):
                            t = table_ref[c, z, at[0], :]
                            for hx in range(2):
                                for hy in range(2):
                                    term = t * f[hx ^ odd_x][hy ^ odd_y]
                                    old = total[c][hx][hy]
                                    total[c][hx][hy] = term if old is None else old + term
                    if block is not blocks[-1]:
                        for c in range(5):
                            for hx in range(2):
                                for hy in range(2):
                                    spec_q[c, hx, hy, at[0], :] = total[c][hx][hy]
                    done.append(total)
                if block is not blocks[-1]:
                    continue
                for c, (odd_x, odd_y) in enumerate(PARITY):
                    for hx in range(2):
                        for hy in range(2):
                            part = jnp.concatenate([done[sub][c][hx][hy] for sub in range(2)], axis=0)
                            part = -part if (odd_x * hx + odd_y * hy) % 2 else part
                            lane = (2 * c + hy) * LANES
                            spec_i[hx * GRID + row : hx * GRID + row + 16, lane : lane + LANES] = part.astype(BF)

        picked = dot(pick_x[...], spec_i[...])
        parts = []
        for c in range(5):
            lane = 2 * c * LANES
            cosines = picked[:, lane : lane + LANES] * pick_y[:, :LANES]
            sines = picked[:, lane + LANES : lane + 2 * LANES] * pick_y[:, LANES:]
            parts.append((cosines + sines).astype(BF))
        return dot(jnp.concatenate(parts, axis=1), back_ref[...])

    def fold(a):
        return jnp.sum(a.reshape(a.shape[0] // 8, 8, LANES), axis=0)

    def total_of(partial):
        if boots == 1:
            return jnp.broadcast_to(jnp.sum(partial, keepdims=True), (1, LANES))
        sums = jnp.dot(partial, same_ref[...], precision=lax.Precision.HIGHEST, preferred_element_type=F32)
        return jnp.sum(sums, axis=0, keepdims=True)

    def depth_weight(z):
        within = lax.broadcasted_iota(jnp.int32, (1, LANES), 1) // (boots * grid_y)
        depth = (within + z * deep).astype(F32) + 0.5 + station_height
        ratio = station_height / depth
        return ratio * ratio * ratio

    models[...] = jnp.zeros_like(models)
    direction[...] = jnp.zeros_like(direction)
    pred[...] = jnp.zeros_like(pred)
    image[...] = jnp.zeros_like(image)

    def round_of(index, carry):
        old_norm, old_step = carry
        fresh = index % CG_STEPS == 0
        back_project()

        @pl.when(fresh)
        def _():
            norm = jnp.zeros((8, LANES), F32)
            for z in range(slabs):
                m = models[z]
                p = damping * depth_weight(z) / (m * m + focusing * focusing)
                penalty[z] = p
                r = applied[z] - p * m
                residual[z] = r
                norm += fold(r * r)
            sums[...] = norm

        @pl.when(jnp.logical_not(fresh))
        def _():
            norm = jnp.zeros((8, LANES), F32)
            for z in range(slabs):
                r = residual[z] - old_step * (applied[z] + penalty[z] * direction[z])
                residual[z] = r
                norm += fold(r * r)
            sums[...] = norm

        norm = total_of(sums[...])
        ratio = jnp.where(fresh, 0.0, norm / old_norm)
        cross = jnp.zeros((8, LANES), F32)
        for z in range(slabs):
            d = residual[z] + ratio * direction[z]
            direction[z] = d
            cross += fold(penalty[z] * d * d)
        here = predict() + ratio * image[...]
        image[...] = here
        step = norm / total_of(cross + fold(weights[...] * here * here))
        for z in range(slabs):
            models[z] += step * direction[z]
        now = pred[...] + step * here
        pred[...] = now
        values[...] = (weights[...] * jnp.where(fresh, here, data[...] - now)).astype(BF)
        return norm, step

    one = jnp.ones((1, LANES), F32)
    lax.fori_loop(0, IRLS * CG_STEPS, round_of, (one, one))

    for group in range(slabs // boots):
        m = jnp.concatenate([models[group * boots + i].astype(BF) for i in range(boots)], axis=1)
        if boots > 1:
            m = dot(m, regroup_ref[...]).astype(BF)
        for b in range(boots):
            found_in[b * GRID : (b + 1) * GRID, group * LANES : (group + 1) * LANES] = (
                m[:, b * LANES : (b + 1) * LANES]
            )

    @pl.loop(0, cell_refs[0].shape[1] // CHUNK)
    def _(step):
        at = pl.ds(pl.multiple_of(step * CHUNK, CHUNK), CHUNK)
        for cell_ref, out_ref in zip(cell_refs, out_refs):
            cells = cell_ref[:, at]
            place = cells.astype(F32)
            wide = lambda row, rows: jnp.broadcast_to(row, (rows, CHUNK)).astype(BF)
            y_row = wide(place[1:2], grid_y)
            z_row = wide(place[2:3], grid_y)
            here_y = lax.broadcasted_iota(jnp.int32, (grid_y, CHUNK), 0).astype(F32).astype(BF) == y_row
            here_y = jnp.where(here_y, jnp.ones_like(y_row), jnp.zeros_like(y_row))
            chosen = jnp.concatenate(
                [jnp.where(z_row == jnp.full_like(z_row, z), here_y, jnp.zeros_like(here_y)) for z in range(DEPTHS)],
                axis=0,
            )
            at_x = lax.broadcasted_iota(jnp.int32, (GRID, CHUNK), 0) == cells[0:1]
            found = dot(found_in[...], chosen)
            parts = [
                jnp.sum(jnp.where(at_x, found[b * GRID : (b + 1) * GRID], 0.0), axis=0, keepdims=True)
                for b in range(boots)
            ]
            out_ref[0, :, at] = jnp.concatenate(parts, axis=0).astype(BF)


def solve(slot, comp_weight, station_index, observed, counts, cells, mine, grid_y):
    boots = min(mine, LANES // grid_y)
    slabs = DEPTHS * grid_y * boots // LANES
    stations = station_index.shape[1]
    count = cells[0].shape[1]
    consts = [jnp.asarray(v) for v in constants(grid_y, boots).values()]
    vmem = pltpu.VMEM
    whole = lambda a: pl.BlockSpec(a.shape, lambda i, n=a.ndim: (0,) * n)
    smem = pl.BlockSpec(memory_space=pltpu.SMEM)
    field = vmem((slabs, GRID, LANES), F32)
    at_stations = vmem((stations, LANES), F32)
    inputs = [station_index, observed, counts, *cells]
    return pl.pallas_call(
        functools.partial(solve_kernel, grid_y, boots, len(consts), len(cells)),
        out_shape=[jax.ShapeDtypeStruct((mine // boots, boots, count), BF)] * len(cells),
        grid=(mine // boots,),
        in_specs=[smem, smem]
        + [whole(a) for a in inputs]
        + [pl.BlockSpec(memory_space=pl.ANY) for _ in consts],
        out_specs=[pl.BlockSpec((1, boots, count), lambda i: (i, 0, 0))] * len(cells),
        scratch_shapes=[vmem(a.shape, a.dtype) for a in consts]
        + [
            pltpu.SemaphoreType.DMA((len(consts),)),
            vmem((stations, 2 * GRID), BF),
            vmem((2 * GRID, stations), BF),
            vmem((stations, 2 * LANES), F32),
            at_stations,
            at_stations,
            at_stations,
            at_stations,
            vmem((stations, LANES), BF),
            vmem((LANES, stations), F32),
            vmem((8, LANES), F32),
            vmem((5, 2, 2, GRID, LANES), F32),
            vmem((2 * GRID, 10 * LANES), BF),
            vmem((2 * GRID, slabs * 2 * LANES), F32),
            vmem((2 * GRID, slabs * 2 * LANES), BF),
            field,
            field,
            field,
            field,
            field,
            vmem((boots * GRID, DEPTHS * grid_y), BF),
        ],
        compiler_params=pltpu.CompilerParams(vmem_limit_bytes=60 * 1024 * 1024),
        cost_estimate=pl.CostEstimate(flops=10**10, bytes_accessed=10**7, transcendentals=0),
        name="solve",
    )(slot, comp_weight, *inputs, *consts)


def local(wide, cell_index, station_index, observed, comp_weight, counts):
    boots = counts.shape[0]
    grid_y = cell_index.shape[1] * wide // (GRID * DEPTHS)
    team = TEAM if wide % TEAM == 0 and boots % TEAM == 0 else 1
    slot = lax.axis_index("wide").astype(jnp.int32) & (team - 1)

    def swap(a, k):
        return lax.ppermute(a, "wide", [(i, i ^ k) for i in range(wide)])

    cells = [cell_index] + [swap(cell_index, k) for k in range(1, team)]
    found = solve(slot.reshape(1), comp_weight, station_index, observed, counts, cells, boots // team, grid_y)
    got = [found[0]] + [swap(found[k], k) for k in range(1, team)]
    blocks = []
    for member in range(team):
        block = got[member]
        for other in range(1, team):
            block = jnp.where(slot == other, got[member ^ other], block)
        blocks.append(block)
    return jnp.concatenate(blocks, axis=0).reshape(boots, -1).astype(F32)


def solution(mesh):
    in_specs = (P(None, "wide"), P(None, "groups"), P(None, "groups"), P(), P("groups", None))
    out_specs = P("groups", "wide")
    fn = functools.partial(local, mesh.shape["wide"])
    return jax.shard_map(fn, mesh=mesh, in_specs=in_specs, out_specs=out_specs, check_vma=False)
```

```python
import functools

import jax
import jax.numpy as jnp
import ml_dtypes
import numpy as np
from jax import lax
from jax.experimental import pallas as pl
from jax.experimental.pallas import tpu as pltpu
from jax.sharding import PartitionSpec as P

IRLS = 2
CG_STEPS = 2
GRID = 128
DEPTHS = 16
LANES = 128
TEAM = 4
BLOCK = 4
CHUNK = 512
ROWS = 32

station_height = 2.0
focusing = 0.1
damping = 0.0002

PARITY = ((0, 0), (1, 1), (1, 0), (0, 0), (0, 1))
BF = jnp.bfloat16
F32 = jnp.float32


def offset_table(grid_y):
    one = np.float32
    dx = np.arange(GRID, dtype=one)[:, None, None]
    dy = np.arange(grid_y, dtype=one)[None, :, None]
    dz = (np.arange(DEPTHS, dtype=one) + one(0.5) + one(station_height))[None, None, :]
    radius2 = dx * dx + dy * dy + dz * dz
    strength = one(1) / (radius2 * radius2 * np.sqrt(radius2))
    three = one(3)
    kinds = [
        (three * dx * dx - radius2) * strength,
        three * dx * dy * strength,
        three * dx * dz * strength,
        (three * dy * dy - radius2) * strength,
        three * dy * dz * strength,
    ]
    return [k.astype(ml_dtypes.bfloat16).astype(np.float64) for k in kinds]


def angles(size):
    return 2 * np.pi * np.outer(np.arange(size), np.arange(size) + 0.5) / (2 * size)


def basis(size):
    return np.concatenate([np.cos(angles(size)), np.sin(angles(size))], axis=1)


def spectrum(values, odd, size):
    if odd:
        trig = 2 * np.sin(angles(size))
    else:
        trig = np.cos(angles(size)) * np.where(np.arange(size) == 0, 1, 2)[:, None]
    return np.tensordot(trig.T / size, values, axes=(1, 0))


def split(matrix):
    high = matrix.astype(ml_dtypes.bfloat16)
    low = (matrix - high.astype(np.float64)).astype(ml_dtypes.bfloat16)
    return high, low


class Layout:
    def __init__(self, parts):
        self.at = {}
        row = 0
        for name, rows in parts:
            self.at[name] = (row, rows)
            row += rows
        self.rows = row


def layout(grid_y, boots):
    slabs = DEPTHS * grid_y * boots // LANES
    return Layout(
        [
            ("base_x", GRID),
            ("base_xt2", 2 * GRID),
            ("field_y2", 2 * LANES),
            ("field_yt", 2 * LANES),
            ("station_y2", 2 * grid_y),
            ("spread", 3 * LANES),
            ("back", 5 * LANES),
            ("same", LANES),
            ("regroup", boots * LANES * max(1, boots // 2)),
            ("table", 5 * slabs // 2 * GRID),
        ]
    )


@functools.lru_cache(maxsize=None)
def constants(grid_y, boots):
    deep = LANES // grid_y // boots
    slabs = DEPTHS // deep
    table = []
    for values, (odd_x, odd_y) in zip(offset_table(grid_y), PARITY):
        t = spectrum(values, odd_x, GRID)
        t = np.moveaxis(spectrum(np.moveaxis(t, 1, 0), odd_y, grid_y), 0, 1)
        t = np.moveaxis(t, 2, 0).reshape(slabs, deep, GRID, 1, grid_y).transpose(0, 2, 1, 3, 4)
        table.append(np.tile(t, (1, 1, 1, boots, 1)).reshape(slabs, GRID, LANES))
    table = np.stack(table).reshape(5, slabs // 2, 2, GRID, LANES).transpose(0, 1, 3, 2, 4)

    base_x = basis(GRID)
    base_y = basis(grid_y).reshape(grid_y, 2, grid_y)
    copies = deep * boots
    field_y = np.einsum("ab,yhl->ayhbl", np.eye(copies), base_y).reshape(LANES, 2 * LANES)
    station_y = np.einsum("b,yhl->yhbl", np.ones(copies), base_y).reshape(grid_y, 2 * LANES)
    spread = np.zeros((6, deep, boots, grid_y, deep, boots, grid_y))
    for c in range(5):
        for b in range(boots):
            spread[c, 0, b, c, :, b, :] = 1
    spread = spread.reshape(6, LANES, LANES)
    back = spread[:5].transpose(0, 2, 1).reshape(5 * LANES, LANES)
    spread = spread.reshape(3, 2, LANES, LANES).transpose(0, 2, 1, 3)
    same = np.einsum("ab,dc,yz->daycbz", np.eye(boots), np.ones((deep, deep)), np.ones((grid_y, grid_y)))
    same = same.reshape(LANES, LANES)
    regroup = np.einsum("st,de,ab,yz->sdaybtez", *[np.eye(n) for n in (boots, deep, boots, grid_y)])
    regroup = regroup.reshape(boots * LANES, boots * LANES)
    if boots > 2:
        regroup = np.concatenate(np.split(regroup, boots // 2, axis=1), axis=0)
    y_high, y_low = split(field_y)
    x_high, x_low = split(base_x.T)
    parts = dict(
        base_x=base_x,
        base_xt2=np.concatenate([x_high, x_low], axis=1),
        field_y2=np.concatenate([y_high, y_low], axis=0),
        field_yt=field_y.T,
        station_y2=np.concatenate(split(station_y)),
        spread=spread.reshape(3 * LANES, 2 * LANES),
        back=back,
        same=same,
        regroup=regroup,
        table=table.reshape(-1, 2 * LANES),
    )
    where = layout(grid_y, boots)
    whole = np.zeros((max(where.rows, 1 << 14), 2 * LANES), ml_dtypes.bfloat16)
    for name, (row, rows) in where.at.items():
        part = parts[name].astype(ml_dtypes.bfloat16)
        assert part.shape[0] == rows
        whole[row : row + rows, : part.shape[1]] = part
    return whole


def dot(a, b):
    return jnp.dot(a, b, preferred_element_type=F32)


def solve_kernel(
    grid_y,
    boots,
    slot_ref,
    comp_ref,
    station_ref,
    observed_ref,
    counts_ref,
    source,
    out_ref,
    const,
    copied,
    pick_x,
    pick_xt,
    pick_y,
    weights,
    data,
    pred,
    image,
    values,
    rows,
    sums,
    spread_out,
    spec_q,
    spec_i,
    spec_f,
    spec_g,
    picked_in,
    models,
    residual,
    direction,
    penalty,
    applied,
):
    deep = LANES // grid_y // boots
    slabs = DEPTHS // deep
    where = layout(grid_y, boots)
    split_row = where.at["table"][0]
    copies = [
        pltpu.make_async_copy(source.at[a:b], const.at[a:b], copied.at[i])
        for i, (a, b) in enumerate([(0, split_row), (split_row, where.rows)])
    ]
    first_step = pl.program_id(0) == 0

    @pl.when(first_step)
    def _():
        for copy in copies:
            copy.start()

    def held(name, width=2 * LANES):
        row, count = where.at[name]
        return const[row : row + count, :width]

    def table(c, z, at):
        row = split_row + (c * (slabs // 2) + z // 2) * GRID
        return const[row + at.start : row + at.stop, z % 2 * LANES : (z % 2 + 1) * LANES]

    stations = station_ref.shape[1]
    first = (slot_ref[0] * pl.num_programs(0) + pl.program_id(0)) * boots
    blocks = [list(range(z, z + BLOCK)) for z in range(0, slabs, BLOCK)]
    pieces = [(z, slice(row, row + ROWS)) for z in range(slabs) for row in range(0, GRID, ROWS)]

    rows[...] = jnp.zeros_like(rows)
    for b in range(boots):
        rows[b * grid_y : b * grid_y + 5, :] = observed_ref[...]
    data[...] = jnp.transpose(rows[...])
    for b in range(boots):
        count = counts_ref[pl.ds(first + b, 1), :].astype(F32)
        for c in range(5):
            rows[b * grid_y + c : b * grid_y + c + 1, :] = count * comp_ref[c]
    weights[...] = jnp.transpose(rows[...])
    values[...] = (weights[...] * data[...]).astype(BF)

    station_x = station_ref[0:1, :]
    station_y = station_ref[1:2, :]
    place_x = (lax.broadcasted_iota(jnp.int32, (GRID, stations), 0) == station_x).astype(F32)
    place_y = (lax.broadcasted_iota(jnp.int32, (LANES, stations), 0) == station_y).astype(F32)
    place_xt = jnp.transpose(place_x).astype(BF)
    place_yt = jnp.transpose(place_y)[:, :grid_y].astype(BF)

    @pl.when(first_step)
    def _():
        copies[0].wait()

    pick_xt[...] = dot(held("base_xt2", GRID), place_x.astype(BF)).astype(BF)
    pick_x[...] = dot(place_xt, held("base_x")).astype(BF)
    station_y2 = held("station_y2")
    pick_y[...] = dot(place_yt, station_y2[:grid_y]) + dot(place_yt, station_y2[grid_y:])

    @pl.when(first_step)
    def _():
        copies[1].wait()

    def back_project():
        spread = held("spread")
        spread = jnp.concatenate([spread[i * LANES : (i + 1) * LANES] for i in range(3)], axis=1)
        spreads = dot(values[...], spread[:, : 5 * LANES])
        for row in range(0, stations, ROWS):
            at = slice(row, row + ROWS)
            cosines, sines = pick_y[at, :LANES], pick_y[at, LANES:]
            for c in range(5):
                e = spreads[at, c * LANES : (c + 1) * LANES]
                spread_out[at, 2 * c * LANES : (2 * c + 1) * LANES] = (e * cosines).astype(BF)
                spread_out[at, (2 * c + 1) * LANES : (2 * c + 2) * LANES] = (e * sines).astype(BF)
        spec = dot(pick_xt[...], spread_out[...])
        for c, (odd_x, odd_y) in enumerate(PARITY):
            for hx in range(2):
                for hy in range(2):
                    lane = (2 * c + hy) * LANES
                    part = spec[hx * GRID : (hx + 1) * GRID, lane : lane + LANES]
                    spec_q[c, hx, hy] = -part if (odd_x * hx + odd_y * hy) % 2 else part

        for row in range(0, GRID, 16):
            at = slice(row, row + 16)
            for hx in range(2):
                q = [[spec_q[c, hx ^ PARITY[c][0], hy, at, :] for hy in range(2)] for c in range(5)]
                to = slice(hx * GRID + row, hx * GRID + row + 16)
                for z in range(slabs):
                    t = [table(c, z, at).astype(F32) for c in range(5)]
                    for hy in range(2):
                        total = None
                        for c in range(5):
                            term = t[c] * q[c][hy ^ PARITY[c][1]]
                            total = term if total is None else total + term
                        lane = (2 * z + hy) * LANES
                        spec_g[to, lane : lane + LANES] = total.astype(BF)
        for block in blocks:
            along_x = dot(held("base_x"), spec_g[:, block[0] * 2 * LANES : (block[-1] + 1) * 2 * LANES]).astype(BF)
            along_x = jnp.concatenate([along_x[:, i * 2 * LANES : (i + 1) * 2 * LANES] for i in range(BLOCK)], axis=0)
            applied[block[0] : block[-1] + 1] = dot(along_x, held("field_yt", LANES)).reshape(BLOCK, GRID, LANES)

    def predict():
        for block in blocks:
            r = residual[block[0] : block[-1] + 1].reshape(BLOCK * GRID, LANES).astype(BF)
            y = dot(jnp.concatenate([r, r], axis=1), held("field_y2")).astype(BF)
            y = jnp.concatenate([y[i * GRID : (i + 1) * GRID] for i in range(BLOCK)], axis=1)
            spec_f[:, block[0] * 2 * LANES : (block[-1] + 1) * 2 * LANES] = dot(
                held("base_xt2"), jnp.concatenate([y, y], axis=0)
            ).astype(BF)

        for row in range(0, GRID, 16):
            at = [slice(hx * GRID + row, hx * GRID + row + 16) for hx in range(2)]
            total = [[[None] * 2 for _ in range(2)] for _ in range(5)]
            for eight in range(0, slabs, 8):
                part = [[[None] * 2 for _ in range(2)] for _ in range(5)]
                for z in range(eight, min(slabs, eight + 8)):
                    lane = 2 * z * LANES
                    f = [
                        [spec_f[at[hx], lane + hy * LANES : lane + (hy + 1) * LANES] for hy in range(2)]
                        for hx in range(2)
                    ]
                    for c, (odd_x, odd_y) in enumerate(PARITY):
                        t = table(c, z, at[0])
                        for hx in range(2):
                            for hy in range(2):
                                term = t * f[hx ^ odd_x][hy ^ odd_y]
                                old = part[c][hx][hy]
                                part[c][hx][hy] = term if old is None else old + term
                for c in range(5):
                    for hx in range(2):
                        for hy in range(2):
                            old = total[c][hx][hy]
                            new = part[c][hx][hy]
                            total[c][hx][hy] = new if old is None else old.astype(F32) + new.astype(F32)
            for c, (odd_x, odd_y) in enumerate(PARITY):
                for hx in range(2):
                    for hy in range(2):
                        part = total[c][hx][hy].astype(BF)
                        part = -part if (odd_x * hx + odd_y * hy) % 2 else part
                        lane = (2 * c + hy) * LANES
                        spec_i[at[hx], lane : lane + LANES] = part

        picked = dot(pick_x[...], spec_i[...])
        for row in range(0, stations, ROWS):
            at = slice(row, row + ROWS)
            cosines, sines = pick_y[at, :LANES], pick_y[at, LANES:]
            for c in range(5):
                lane = 2 * c * LANES
                part = picked[at, lane : lane + LANES] * cosines + picked[at, lane + LANES : lane + 2 * LANES] * sines
                picked_in[at, c * LANES : (c + 1) * LANES] = part.astype(BF)
        return dot(picked_in[...], held("back", LANES))

    def fold(a):
        return jnp.sum(a.reshape(a.shape[0] // 8, 8, LANES), axis=0)

    def total_of(partial):
        if boots == 1:
            return jnp.broadcast_to(jnp.sum(partial, keepdims=True), (1, LANES))
        sums = jnp.dot(
            partial, held("same", LANES).astype(F32), precision=lax.Precision.HIGHEST, preferred_element_type=F32
        )
        return jnp.sum(sums, axis=0, keepdims=True)

    def depth_weight(z):
        within = lax.broadcasted_iota(jnp.int32, (1, LANES), 1) // (boots * grid_y)
        depth = (within + z * deep).astype(F32) + 0.5 + station_height
        ratio = station_height / depth
        return ratio * ratio * ratio

    models[...] = jnp.zeros_like(models)
    direction[...] = jnp.zeros_like(direction)
    pred[...] = jnp.zeros_like(pred)
    image[...] = jnp.zeros_like(image)
    no_sum = jnp.zeros((8, LANES), F32)

    def round_of(index, carry):
        old_norm, old_step = carry
        fresh = index % CG_STEPS == 0
        back_project()

        @pl.when(fresh)
        def _():
            norm = no_sum
            for z, at in pieces:
                m = models[z, at]
                p = damping * depth_weight(z) / (m * m + focusing * focusing)
                penalty[z, at] = p
                r = applied[z, at] - p * m
                residual[z, at] = r
                norm += fold(r * r)
            sums[...] = norm

        @pl.when(jnp.logical_not(fresh))
        def _():
            norm = no_sum
            for z, at in pieces:
                r = residual[z, at] - old_step * (applied[z, at] + penalty[z, at] * direction[z, at])
                residual[z, at] = r
                norm += fold(r * r)
            sums[...] = norm

        norm = total_of(sums[...])
        ratio = jnp.where(fresh, 0.0, norm / old_norm)
        cross = no_sum
        for z, at in pieces:
            d = residual[z, at] + ratio * direction[z, at]
            direction[z, at] = d
            cross += fold(penalty[z, at] * d * d)
        here = predict() + ratio * image[...]
        image[...] = here
        step = norm / total_of(cross + fold(weights[...] * here * here))
        for z, at in pieces:
            models[z, at] += step * direction[z, at]
        now = pred[...] + step * here
        pred[...] = now
        values[...] = (weights[...] * jnp.where(fresh, here, data[...] - now)).astype(BF)
        return norm, step

    one = jnp.ones((1, LANES), F32)
    lax.fori_loop(0, IRLS * CG_STEPS, round_of, (one, one))

    for group in range(slabs // boots):
        m = jnp.concatenate([models[group * boots + i].astype(BF) for i in range(boots)], axis=1)
        if boots > 1:
            regroup = held("regroup")
            regroup = [regroup[i * boots * LANES : (i + 1) * boots * LANES] for i in range(boots // 2)]
            m = dot(m, jnp.concatenate(regroup, axis=1)).astype(BF)
        for b in range(boots):
            out_ref[b * GRID : (b + 1) * GRID, group * LANES : (group + 1) * LANES] = (
                m[:, b * LANES : (b + 1) * LANES]
            )


def solve(slot, comp_weight, station_index, observed, counts, mine, grid_y):
    boots = min(mine, LANES // grid_y)
    slabs = DEPTHS * grid_y * boots // LANES
    stations = station_index.shape[1]
    const = jnp.asarray(constants(grid_y, boots))
    vmem = pltpu.VMEM
    whole = lambda a: pl.BlockSpec(a.shape, lambda i, n=a.ndim: (0,) * n)
    smem = pl.BlockSpec(memory_space=pltpu.SMEM)
    field = vmem((slabs, GRID, LANES), F32)
    at_stations = vmem((stations, LANES), F32)
    inputs = [station_index, observed, counts]
    return pl.pallas_call(
        functools.partial(solve_kernel, grid_y, boots),
        out_shape=jax.ShapeDtypeStruct((mine * GRID, DEPTHS * grid_y), BF),
        grid=(mine // boots,),
        in_specs=[smem, smem] + [whole(a) for a in inputs] + [pl.BlockSpec(memory_space=pl.ANY)],
        out_specs=pl.BlockSpec((boots * GRID, DEPTHS * grid_y), lambda i: (i, 0)),
        scratch_shapes=[
            vmem((layout(grid_y, boots).rows, 2 * LANES), BF),
            pltpu.SemaphoreType.DMA((2,)),
            vmem((stations, 2 * GRID), BF),
            vmem((2 * GRID, stations), BF),
            vmem((stations, 2 * LANES), F32),
            at_stations,
            at_stations,
            at_stations,
            at_stations,
            vmem((stations, LANES), BF),
            vmem((LANES, stations), F32),
            vmem((8, LANES), F32),
            vmem((stations, 10 * LANES), BF),
            vmem((5, 2, 2, GRID, LANES), F32),
            vmem((2 * GRID, 10 * LANES), BF),
            vmem((2 * GRID, slabs * 2 * LANES), BF),
            vmem((2 * GRID, slabs * 2 * LANES), BF),
            vmem((stations, 5 * LANES), BF),
            field,
            field,
            field,
            field,
            field,
        ],
        compiler_params=pltpu.CompilerParams(vmem_limit_bytes=56 * 1024 * 1024),
        cost_estimate=pl.CostEstimate(flops=10**10, bytes_accessed=10**7, transcendentals=0),
        name="solve",
    )(slot, comp_weight, *inputs, const)


def pick_kernel(grid_y, boots, count, models_ref, *refs):
    def pick_chunk(cell_ref, out_ref, at):
        cells = cell_ref[:, at]
        place = cells.astype(F32)
        wide = lambda row, rows: jnp.broadcast_to(row, (rows, CHUNK)).astype(BF)
        y_row = wide(place[1:2], grid_y)
        z_row = wide(place[2:3], grid_y)
        here_y = lax.broadcasted_iota(jnp.int32, (grid_y, CHUNK), 0).astype(F32).astype(BF) == y_row
        here_y = jnp.where(here_y, jnp.ones_like(y_row), jnp.zeros_like(y_row))
        chosen = jnp.concatenate(
            [jnp.where(z_row == jnp.full_like(z_row, z), here_y, jnp.zeros_like(here_y)) for z in range(DEPTHS)],
            axis=0,
        )
        at_x = lax.broadcasted_iota(jnp.int32, (GRID, CHUNK), 0) == cells[0:1]
        found = dot(models_ref[...], chosen)
        parts = [
            jnp.sum(jnp.where(at_x, found[b * GRID : (b + 1) * GRID], 0.0), axis=0, keepdims=True)
            for b in range(boots)
        ]
        out_ref[:, at] = jnp.concatenate(parts, axis=0).astype(BF)

    per = max(1, 4 // count)

    @pl.loop(0, refs[0].shape[1] // (per * CHUNK))
    def _(step):
        for i in range(per):
            at = pl.ds(pl.multiple_of((step * per + i) * CHUNK, CHUNK), CHUNK)
            for cell_ref, out_ref in zip(refs[:count], refs[count:]):
                pick_chunk(cell_ref, out_ref, at)


def pick(models, cells, grid_y):
    boots = models.shape[0] // GRID
    count = cells[0].shape[1]
    vmem = pl.BlockSpec(memory_space=pltpu.VMEM)
    return pl.pallas_call(
        functools.partial(pick_kernel, grid_y, boots, len(cells)),
        out_shape=[jax.ShapeDtypeStruct((boots, count), BF)] * len(cells),
        in_specs=[vmem] * (1 + len(cells)),
        out_specs=[vmem] * len(cells),
        compiler_params=pltpu.CompilerParams(vmem_limit_bytes=40 * 1024 * 1024),
        cost_estimate=pl.CostEstimate(
            flops=2 * models.size * count * len(cells), bytes_accessed=10**6, transcendentals=0
        ),
        name="pick",
    )(models, *cells)


def local(wide, cell_index, station_index, observed, comp_weight, counts):
    boots = counts.shape[0]
    grid_y = cell_index.shape[1] * wide // (GRID * DEPTHS)
    team = TEAM if wide % TEAM == 0 and boots % TEAM == 0 else 1
    slot = lax.axis_index("wide").astype(jnp.int32) & (team - 1)

    def swap(a, k):
        return lax.ppermute(a, "wide", [(i, i ^ k) for i in range(wide)])

    theirs = [swap(cell_index, k) for k in range(1, team)]
    models = solve(slot.reshape(1), comp_weight, station_index, observed, counts, boots // team, grid_y)
    sent = [swap(a, k + 1) for k, a in enumerate(pick(models, theirs, grid_y))] if theirs else []
    got = [*pick(models, [cell_index], grid_y), *sent]
    blocks = []
    for member in range(team):
        block = got[member]
        for other in range(1, team):
            block = jnp.where(slot == other, got[member ^ other], block)
        blocks.append(block.astype(F32))
    return jnp.concatenate(blocks, axis=0)


def solution(mesh):
    in_specs = (P(None, "wide"), P(None, "groups"), P(None, "groups"), P(), P("groups", None))
    out_specs = P("groups", "wide")
    fn = functools.partial(local, mesh.shape["wide"])
    return jax.shard_map(fn, mesh=mesh, in_specs=in_specs, out_specs=out_specs, check_vma=False)
```

```python
import functools

import jax
import jax.numpy as jnp
import ml_dtypes
import numpy as np
from jax import lax
from jax.experimental import pallas as pl
from jax.experimental.pallas import tpu as pltpu
from jax.sharding import PartitionSpec as P

IRLS = 2
CG_STEPS = 2
GRID = 128
DEPTHS = 16
LANES = 128
TEAM = 4
BLOCK = 2
CHUNK = 512
ROWS = 32

station_height = 2.0
focusing = 0.1
damping = 0.0002

PARITY = ((0, 0), (1, 1), (1, 0), (0, 0), (0, 1))
BF = jnp.bfloat16
F32 = jnp.float32


def offset_table(grid_y):
    one = np.float32
    dx = np.arange(GRID, dtype=one)[:, None, None]
    dy = np.arange(grid_y, dtype=one)[None, :, None]
    dz = (np.arange(DEPTHS, dtype=one) + one(0.5) + one(station_height))[None, None, :]
    radius2 = dx * dx + dy * dy + dz * dz
    strength = one(1) / (radius2 * radius2 * np.sqrt(radius2))
    three = one(3)
    kinds = [
        (three * dx * dx - radius2) * strength,
        three * dx * dy * strength,
        three * dx * dz * strength,
        (three * dy * dy - radius2) * strength,
        three * dy * dz * strength,
    ]
    return [k.astype(ml_dtypes.bfloat16).astype(np.float64) for k in kinds]


def angles(size):
    return 2 * np.pi * np.outer(np.arange(size), np.arange(size) + 0.5) / (2 * size)


def basis(size):
    return np.concatenate([np.cos(angles(size)), np.sin(angles(size))], axis=1)


def spectrum(values, odd, size):
    if odd:
        trig = 2 * np.sin(angles(size))
    else:
        trig = np.cos(angles(size)) * np.where(np.arange(size) == 0, 1, 2)[:, None]
    return np.tensordot(trig.T / size, values, axes=(1, 0))


def split(matrix):
    high = matrix.astype(ml_dtypes.bfloat16)
    low = (matrix - high.astype(np.float64)).astype(ml_dtypes.bfloat16)
    return high, low


class Layout:
    def __init__(self, parts):
        self.at = {}
        row = 0
        for name, rows in parts:
            self.at[name] = (row, rows)
            row += rows
        self.rows = row


def layout(grid_y, boots):
    slabs = DEPTHS * grid_y * boots // LANES
    return Layout(
        [
            ("base_x", GRID),
            ("base_xt2", 2 * GRID),
            ("field_y2", 2 * LANES),
            ("field_yt", 2 * LANES),
            ("station_y2", 2 * grid_y),
            ("spread", 3 * LANES),
            ("back", 5 * LANES),
            ("same", LANES),
            ("regroup", boots * LANES * max(1, boots // 2)),
            ("table", 5 * slabs // 2 * GRID),
        ]
    )


@functools.lru_cache(maxsize=None)
def constants(grid_y, boots):
    deep = LANES // grid_y // boots
    slabs = DEPTHS // deep
    table = []
    for values, (odd_x, odd_y) in zip(offset_table(grid_y), PARITY):
        t = spectrum(values, odd_x, GRID)
        t = np.moveaxis(spectrum(np.moveaxis(t, 1, 0), odd_y, grid_y), 0, 1)
        t = np.moveaxis(t, 2, 0).reshape(slabs, deep, GRID, 1, grid_y).transpose(0, 2, 1, 3, 4)
        table.append(np.tile(t, (1, 1, 1, boots, 1)).reshape(slabs, GRID, LANES))
    table = np.stack(table).reshape(5, slabs // 2, 2, GRID, LANES).transpose(0, 1, 3, 2, 4)

    base_x = basis(GRID)
    base_y = basis(grid_y).reshape(grid_y, 2, grid_y)
    copies = deep * boots
    field_y = np.einsum("ab,yhl->ayhbl", np.eye(copies), base_y).reshape(LANES, 2 * LANES)
    compact = deep == 2
    near = 1 if compact else deep
    station_y = np.einsum("b,yhl->yhbl", np.ones(near * boots), base_y).reshape(grid_y, -1)
    halves = 2 if compact else 1
    spread = np.zeros((5, deep, boots, grid_y, halves, near, boots, grid_y))
    for c in range(5):
        for b in range(boots):
            spread[c, 0, b, c, :, :, b, :] = 1
    spread = spread.reshape(5, LANES, LANES)
    back = spread.transpose(0, 2, 1).reshape(5 * LANES, LANES)
    spread = np.concatenate([spread, np.zeros((1, LANES, LANES))])
    spread = spread.reshape(3, 2, LANES, LANES).transpose(0, 2, 1, 3)
    same = np.einsum("ab,dc,yz->daycbz", np.eye(boots), np.ones((deep, deep)), np.ones((grid_y, grid_y)))
    same = same.reshape(LANES, LANES)
    regroup = np.einsum("st,de,ab,yz->sdaybtez", *[np.eye(n) for n in (boots, deep, boots, grid_y)])
    regroup = regroup.reshape(boots * LANES, boots * LANES)
    if boots > 2:
        regroup = np.concatenate(np.split(regroup, boots // 2, axis=1), axis=0)
    y_high, y_low = split(field_y)
    x_high, x_low = split(base_x.T)
    parts = dict(
        base_x=base_x,
        base_xt2=np.concatenate([x_high, x_low], axis=1),
        field_y2=np.concatenate([y_high, y_low], axis=0),
        field_yt=field_y.T,
        station_y2=np.concatenate(split(station_y)),
        spread=spread.reshape(3 * LANES, 2 * LANES),
        back=back,
        same=same,
        regroup=regroup,
        table=table.reshape(-1, 2 * LANES),
    )
    where = layout(grid_y, boots)
    whole = np.zeros((max(where.rows, 1 << 14), 2 * LANES), ml_dtypes.bfloat16)
    for name, (row, rows) in where.at.items():
        part = parts[name].astype(ml_dtypes.bfloat16)
        assert part.shape[0] == rows
        whole[row : row + rows, : part.shape[1]] = part
    return whole


def dot(a, b):
    return jnp.dot(a, b, preferred_element_type=F32)


def interleave(ahead, behind):
    for stage in range(len(ahead) + 1):
        first = ahead[stage] if stage < len(ahead) else []
        second = behind[stage - 1] if stage else []
        done = 0
        for i, step in enumerate(first):
            step()
            upto = (i + 1) * len(second) // len(first)
            for other in second[done:upto]:
                other()
            done = upto
        for other in second[done:]:
            other()


def solve_kernel(
    grid_y,
    boots,
    slot_ref,
    comp_ref,
    station_ref,
    observed_ref,
    counts_ref,
    source,
    out_ref,
    const,
    copied,
    pick_x,
    pick_xt,
    pick_y,
    weights,
    data,
    pred,
    image,
    values,
    rows,
    sums,
    spread_out,
    spec_q,
    spec_i,
    spec_f,
    spec_g,
    spec_a,
    picked_in,
    models,
    residual,
    direction,
    penalty,
    applied,
):
    deep = LANES // grid_y // boots
    slabs = DEPTHS // deep
    where = layout(grid_y, boots)
    split_row = where.at["table"][0]
    compact = deep == 2
    wide = LANES if compact else 2 * LANES
    low_lanes = lax.broadcasted_iota(jnp.int32, (1, LANES), 1) < LANES // 2
    copies = [
        pltpu.make_async_copy(source.at[a:b], const.at[a:b], copied.at[i])
        for i, (a, b) in enumerate([(0, split_row), (split_row, where.rows)])
    ]
    first_step = pl.program_id(0) == 0

    @pl.when(first_step)
    def _():
        for copy in copies:
            copy.start()

    def held(name, width=2 * LANES):
        row, count = where.at[name]
        return const[row : row + count, :width]

    def table(c, z, at):
        row = split_row + (c * (slabs // 2) + z // 2) * GRID
        return const[row + at.start : row + at.stop, z % 2 * LANES : (z % 2 + 1) * LANES]

    stations = station_ref.shape[1]
    first = (slot_ref[0] * pl.num_programs(0) + pl.program_id(0)) * boots
    blocks = [list(range(z, z + BLOCK)) for z in range(0, slabs, BLOCK)]
    pieces = [(z, slice(row, row + ROWS)) for z in range(slabs) for row in range(0, GRID, ROWS)]

    rows[...] = jnp.zeros_like(rows)
    for b in range(boots):
        rows[b * grid_y : b * grid_y + 5, :] = observed_ref[...]
    data[...] = jnp.transpose(rows[...])
    for b in range(boots):
        count = counts_ref[pl.ds(first + b, 1), :].astype(F32)
        for c in range(5):
            rows[b * grid_y + c : b * grid_y + c + 1, :] = count * comp_ref[c]
    weights[...] = jnp.transpose(rows[...])
    values[...] = (weights[...] * data[...]).astype(BF)

    station_x = station_ref[0:1, :]
    station_y = station_ref[1:2, :]
    place_x = (lax.broadcasted_iota(jnp.int32, (GRID, stations), 0) == station_x).astype(F32)
    place_y = (lax.broadcasted_iota(jnp.int32, (LANES, stations), 0) == station_y).astype(F32)
    place_xt = jnp.transpose(place_x).astype(BF)
    place_yt = jnp.transpose(place_y)[:, :grid_y].astype(BF)

    @pl.when(first_step)
    def _():
        copies[0].wait()

    pick_xt[...] = dot(held("base_xt2", GRID), place_x.astype(BF)).astype(BF)
    pick_x[...] = dot(place_xt, held("base_x")).astype(BF)
    station_y2 = held("station_y2", wide)
    pick_y[...] = dot(place_yt, station_y2[:grid_y]) + dot(place_yt, station_y2[grid_y:])

    @pl.when(first_step)
    def _():
        copies[1].wait()

    no_sum = jnp.zeros((8, LANES), F32)

    def back_project():
        spread = held("spread")
        spread = jnp.concatenate([spread[i * LANES : (i + 1) * LANES] for i in range(3)], axis=1)
        spreads = dot(values[...], spread[:, : 5 * LANES])
        for row in range(0, stations, ROWS):
            at = slice(row, row + ROWS)
            trig = [pick_y[at, lane : lane + LANES] for lane in range(0, wide, LANES)]
            for c in range(5):
                e = spreads[at, c * LANES : (c + 1) * LANES]
                for i, part in enumerate(trig):
                    lane = c * wide + i * LANES
                    spread_out[at, lane : lane + LANES] = (e * part).astype(BF)
        spec = dot(pick_xt[...], spread_out[...])
        for c, (odd_x, odd_y) in enumerate(PARITY):
            for hx in range(2):
                for row in range(0, GRID, ROWS):
                    at = slice(hx * GRID + row, hx * GRID + row + ROWS)
                    if compact:
                        part = spec[at, c * LANES : (c + 1) * LANES]
                        turned = pltpu.roll(part, LANES // 2, 1)
                        parts = [jnp.where(low_lanes, part, turned), jnp.where(low_lanes, turned, part)]
                    else:
                        parts = [spec[at, lane : lane + LANES] for lane in (c * wide, c * wide + LANES)]
                    for hy, part in enumerate(parts):
                        spec_q[c, hx, hy, row : row + ROWS, :] = -part if (odd_x * hx + odd_y * hy) % 2 else part

        def products(block, row):
            at = slice(row, row + 16)
            t = [[table(c, z, at).astype(F32) for c in range(5)] for z in block]
            for hx in range(2):
                to = slice(hx * GRID + row, hx * GRID + row + 16)
                for hy in range(2):
                    q = [spec_q[c, hx ^ PARITY[c][0], hy ^ PARITY[c][1], at, :] for c in range(5)]
                    for z, tz in zip(block, t):
                        total = tz[0] * q[0]
                        for c in range(1, 5):
                            total = total + tz[c] * q[c]
                        lane = (2 * z + hy) * LANES
                        spec_g[to, lane : lane + LANES] = total.astype(BF)

        along = {}

        def inverse_x(z):
            along[z] = dot(held("base_x"), spec_g[:, 2 * z * LANES : (2 * z + 2) * LANES]).astype(BF)

        def inverse_y(z):
            applied[z] = dot(along[z], held("field_yt", LANES))

        interleave(
            [[functools.partial(products, block, row) for row in range(0, GRID, 16)] for block in blocks],
            [[functools.partial(f, z) for f in (inverse_x, inverse_y) for z in block] for block in blocks],
        )

    def predict():
        along = {}

        def forward_y(block):
            r = residual[block[0] : block[-1] + 1].reshape(BLOCK * GRID, LANES).astype(BF)
            y = dot(jnp.concatenate([r, r], axis=1), held("field_y2")).astype(BF)
            for i, z in enumerate(block):
                along[z] = jnp.concatenate([y[i * GRID : (i + 1) * GRID]] * 2, axis=0)

        def forward_x(z):
            spec_f[:, 2 * z * LANES : (2 * z + 2) * LANES] = dot(held("base_xt2"), along[z]).astype(BF)

        def products(block, row):
            at = [slice(hx * GRID + row, hx * GRID + row + 16) for hx in range(2)]
            begin = block[0] % 8 == 0
            f = {
                (z, hx, hy): spec_f[at[hx], (2 * z + hy) * LANES : (2 * z + hy + 1) * LANES]
                for z in block
                for hx in range(2)
                for hy in range(2)
            }
            for c, (odd_x, odd_y) in enumerate(PARITY):
                t = [table(c, z, at[0]) for z in block]
                for hx in range(2):
                    parts = []
                    for hy in range(2):
                        total = None if begin else spec_a[c, hx, hy, at[0], :]
                        for z, tz in zip(block, t):
                            term = tz * f[z, hx ^ odd_x, hy ^ odd_y]
                            total = term if total is None else total + term
                        if block[-1] % 8 != 7 and block is not blocks[-1]:
                            spec_a[c, hx, hy, at[0], :] = total
                            continue
                        total = total.astype(F32)
                        if block[-1] >= 8:
                            total = total + spec_q[c, hx, hy, at[0], :]
                        if block is not blocks[-1]:
                            spec_q[c, hx, hy, at[0], :] = total
                            continue
                        parts.append(-total if (odd_x * hx + odd_y * hy) % 2 else total)
                    if not parts:
                        continue
                    if compact:
                        low, high = parts
                        parts = [
                            jnp.where(low_lanes, low, high)
                            + pltpu.roll(jnp.where(low_lanes, high, low), LANES // 2, 1)
                        ]
                    for i, part in enumerate(parts):
                        lane = c * wide + i * LANES
                        spec_i[at[hx], lane : lane + LANES] = part.astype(BF)

        interleave(
            [
                [functools.partial(forward_y, block)] + [functools.partial(forward_x, z) for z in block]
                for block in blocks
            ],
            [[functools.partial(products, block, row) for row in range(0, GRID, 16)] for block in blocks],
        )

        picked = dot(pick_x[...], spec_i[...])
        for row in range(0, stations, ROWS):
            at = slice(row, row + ROWS)
            for c in range(5):
                part = None
                for lane in range(0, wide, LANES):
                    term = picked[at, c * wide + lane : c * wide + lane + LANES] * pick_y[at, lane : lane + LANES]
                    part = term if part is None else part + term
                picked_in[at, c * LANES : (c + 1) * LANES] = part.astype(BF)
        return dot(picked_in[...], held("back", LANES))

    def fold(a):
        return jnp.sum(a.reshape(a.shape[0] // 8, 8, LANES), axis=0)

    def total_of(partial):
        if boots == 1:
            return jnp.broadcast_to(jnp.sum(partial, keepdims=True), (1, LANES))
        parts = []
        for _ in range(3):
            part = partial.astype(BF).astype(F32)
            parts.append(part)
            partial = partial - part
        parts.append(no_sum)
        sums = dot(jnp.concatenate(parts, axis=0).astype(BF), held("same", LANES))
        return jnp.sum(sums, axis=0, keepdims=True)

    def depth_weight(z):
        within = lax.broadcasted_iota(jnp.int32, (1, LANES), 1) // (boots * grid_y)
        depth = (within + z * deep).astype(F32) + 0.5 + station_height
        ratio = station_height / depth
        return ratio * ratio * ratio

    models[...] = jnp.zeros_like(models)
    direction[...] = jnp.zeros_like(direction)
    pred[...] = jnp.zeros_like(pred)
    image[...] = jnp.zeros_like(image)

    def round_of(index, carry):
        old_norm, old_step = carry
        fresh = index % CG_STEPS == 0
        back_project()

        @pl.when(fresh)
        def _():
            norm = no_sum
            for z, at in pieces:
                m = models[z, at]
                p = damping * depth_weight(z) / (m * m + focusing * focusing)
                penalty[z, at] = p
                r = applied[z, at] - p * m
                residual[z, at] = r
                norm += fold(r * r)
            sums[...] = norm

        @pl.when(jnp.logical_not(fresh))
        def _():
            norm = no_sum
            for z, at in pieces:
                r = residual[z, at] - old_step * (applied[z, at] + penalty[z, at] * direction[z, at])
                residual[z, at] = r
                norm += fold(r * r)
            sums[...] = norm

        norm = total_of(sums[...])
        ratio = jnp.where(fresh, 0.0, norm / old_norm)
        cross = no_sum
        for z, at in pieces:
            d = residual[z, at] + ratio * direction[z, at]
            direction[z, at] = d
            cross += fold(penalty[z, at] * d * d)
        here = predict() + ratio * image[...]
        image[...] = here
        step = norm / total_of(cross + fold(weights[...] * here * here))
        for z, at in pieces:
            models[z, at] += step * direction[z, at]
        now = pred[...] + step * here
        pred[...] = now
        values[...] = (weights[...] * jnp.where(fresh, here, data[...] - now)).astype(BF)
        return norm, step

    one = jnp.ones((1, LANES), F32)
    lax.fori_loop(0, IRLS * CG_STEPS, round_of, (one, one))

    for group in range(slabs // boots):
        m = jnp.concatenate([models[group * boots + i].astype(BF) for i in range(boots)], axis=1)
        if boots > 1:
            regroup = held("regroup")
            regroup = [regroup[i * boots * LANES : (i + 1) * boots * LANES] for i in range(boots // 2)]
            m = dot(m, jnp.concatenate(regroup, axis=1)).astype(BF)
        for b in range(boots):
            out_ref[b * GRID : (b + 1) * GRID, group * LANES : (group + 1) * LANES] = (
                m[:, b * LANES : (b + 1) * LANES]
            )


def solve(slot, comp_weight, station_index, observed, counts, mine, grid_y):
    boots = min(mine, LANES // grid_y)
    slabs = DEPTHS * grid_y * boots // LANES
    stations = station_index.shape[1]
    const = jnp.asarray(constants(grid_y, boots))
    vmem = pltpu.VMEM
    whole = lambda a: pl.BlockSpec(a.shape, lambda i, n=a.ndim: (0,) * n)
    smem = pl.BlockSpec(memory_space=pltpu.SMEM)
    field = vmem((slabs, GRID, LANES), F32)
    at_stations = vmem((stations, LANES), F32)
    wide = LANES if 2 * slabs == DEPTHS else 2 * LANES
    inputs = [station_index, observed, counts]
    return pl.pallas_call(
        functools.partial(solve_kernel, grid_y, boots),
        out_shape=jax.ShapeDtypeStruct((mine * GRID, DEPTHS * grid_y), BF),
        grid=(mine // boots,),
        in_specs=[smem, smem] + [whole(a) for a in inputs] + [pl.BlockSpec(memory_space=pl.ANY)],
        out_specs=pl.BlockSpec((boots * GRID, DEPTHS * grid_y), lambda i: (i, 0)),
        scratch_shapes=[
            vmem((layout(grid_y, boots).rows, 2 * LANES), BF),
            pltpu.SemaphoreType.DMA((2,)),
            vmem((stations, 2 * GRID), BF),
            vmem((2 * GRID, stations), BF),
            vmem((stations, wide), F32),
            at_stations,
            at_stations,
            at_stations,
            at_stations,
            vmem((stations, LANES), BF),
            vmem((LANES, stations), F32),
            vmem((8, LANES), F32),
            vmem((stations, 5 * wide), BF),
            vmem((5, 2, 2, GRID, LANES), F32),
            vmem((2 * GRID, 5 * wide), BF),
            vmem((2 * GRID, slabs * 2 * LANES), BF),
            vmem((2 * GRID, slabs * 2 * LANES), BF),
            vmem((5, 2, 2, GRID, LANES), BF),
            vmem((stations, 5 * LANES), BF),
            field,
            field,
            field,
            field,
            field,
        ],
        compiler_params=pltpu.CompilerParams(vmem_limit_bytes=56 * 1024 * 1024),
        cost_estimate=pl.CostEstimate(flops=10**10, bytes_accessed=10**7, transcendentals=0),
        name="solve",
    )(slot, comp_weight, *inputs, const)


def pick_kernel(grid_y, boots, count, models_ref, *refs):
    def pick_chunk(cell_ref, out_ref, at):
        cells = cell_ref[:, at]
        place = cells.astype(F32)
        wide = lambda row, rows: jnp.broadcast_to(row, (rows, CHUNK)).astype(BF)
        y_row = wide(place[1:2], grid_y)
        z_row = wide(place[2:3], grid_y)
        here_y = lax.broadcasted_iota(jnp.int32, (grid_y, CHUNK), 0).astype(F32).astype(BF) == y_row
        here_y = jnp.where(here_y, jnp.ones_like(y_row), jnp.zeros_like(y_row))
        chosen = jnp.concatenate(
            [jnp.where(z_row == jnp.full_like(z_row, z), here_y, jnp.zeros_like(here_y)) for z in range(DEPTHS)],
            axis=0,
        )
        at_x = lax.broadcasted_iota(jnp.int32, (GRID, CHUNK), 0) == cells[0:1]
        found = dot(models_ref[...], chosen)
        parts = [
            jnp.sum(jnp.where(at_x, found[b * GRID : (b + 1) * GRID], 0.0), axis=0, keepdims=True)
            for b in range(boots)
        ]
        out_ref[:, at] = jnp.concatenate(parts, axis=0).astype(BF)

    per = max(1, 4 // count)

    @pl.loop(0, refs[0].shape[1] // (per * CHUNK))
    def _(step):
        for i in range(per):
            at = pl.ds(pl.multiple_of((step * per + i) * CHUNK, CHUNK), CHUNK)
            for cell_ref, out_ref in zip(refs[:count], refs[count:]):
                pick_chunk(cell_ref, out_ref, at)


def pick(models, cells, grid_y):
    boots = models.shape[0] // GRID
    count = cells[0].shape[1]
    vmem = pl.BlockSpec(memory_space=pltpu.VMEM)
    return pl.pallas_call(
        functools.partial(pick_kernel, grid_y, boots, len(cells)),
        out_shape=[jax.ShapeDtypeStruct((boots, count), BF)] * len(cells),
        in_specs=[vmem] * (1 + len(cells)),
        out_specs=[vmem] * len(cells),
        compiler_params=pltpu.CompilerParams(vmem_limit_bytes=40 * 1024 * 1024),
        cost_estimate=pl.CostEstimate(
            flops=2 * models.size * count * len(cells), bytes_accessed=10**6, transcendentals=0
        ),
        name="pick",
    )(models, *cells)


def local(wide, cell_index, station_index, observed, comp_weight, counts):
    boots = counts.shape[0]
    grid_y = cell_index.shape[1] * wide // (GRID * DEPTHS)
    team = TEAM if wide % TEAM == 0 and boots % TEAM == 0 else 1
    slot = lax.axis_index("wide").astype(jnp.int32) & (team - 1)

    def swap(a, k):
        return lax.ppermute(a, "wide", [(i, i ^ k) for i in range(wide)])

    theirs = [swap(cell_index, k) for k in range(1, team)]
    models = solve(slot.reshape(1), comp_weight, station_index, observed, counts, boots // team, grid_y)
    far = [swap(a, k + 2) for k, a in enumerate(pick(models, theirs[1:], grid_y))] if team > 2 else []
    near = pick(models, [cell_index] + theirs[:1], grid_y)
    got = [near[0]] + [swap(a, 1) for a in near[1:]] + far
    blocks = []
    for member in range(team):
        block = got[member]
        for other in range(1, team):
            block = jnp.where(slot == other, got[member ^ other], block)
        blocks.append(block.astype(F32))
    return jnp.concatenate(blocks, axis=0)


def solution(mesh):
    in_specs = (P(None, "wide"), P(None, "groups"), P(None, "groups"), P(), P("groups", None))
    out_specs = P("groups", "wide")
    fn = functools.partial(local, mesh.shape["wide"])
    return jax.shard_map(fn, mesh=mesh, in_specs=in_specs, out_specs=out_specs, check_vma=False)
```

```python
import functools

import jax
import jax.numpy as jnp
import ml_dtypes
import numpy as np
from jax import lax
from jax.experimental import pallas as pl
from jax.experimental.pallas import tpu as pltpu
from jax.sharding import PartitionSpec as P

IRLS = 2
CG_STEPS = 2
GRID = 128
DEPTHS = 16
LANES = 128
TEAM = 4
CHUNK = 2048
ROWS = 32

station_height = 2.0
focusing = 0.1
damping = 0.0002

PARITY = ((0, 0), (1, 1), (1, 0), (0, 0), (0, 1))
BF = jnp.bfloat16
F32 = jnp.float32


def offset_table(grid_y):
    one = np.float32
    dx = np.arange(GRID, dtype=one)[:, None, None]
    dy = np.arange(grid_y, dtype=one)[None, :, None]
    dz = (np.arange(DEPTHS, dtype=one) + one(0.5) + one(station_height))[None, None, :]
    radius2 = dx * dx + dy * dy + dz * dz
    strength = one(1) / (radius2 * radius2 * np.sqrt(radius2))
    three = one(3)
    kinds = [
        (three * dx * dx - radius2) * strength,
        three * dx * dy * strength,
        three * dx * dz * strength,
        (three * dy * dy - radius2) * strength,
        three * dy * dz * strength,
    ]
    return [k.astype(ml_dtypes.bfloat16).astype(np.float64) for k in kinds]


def angles(size):
    return 2 * np.pi * np.outer(np.arange(size), np.arange(size) + 0.5) / (2 * size)


def basis(size):
    return np.concatenate([np.cos(angles(size)), np.sin(angles(size))], axis=1)


def spectrum(values, odd, size):
    if odd:
        trig = 2 * np.sin(angles(size))
    else:
        trig = np.cos(angles(size)) * np.where(np.arange(size) == 0, 1, 2)[:, None]
    return np.tensordot(trig.T / size, values, axes=(1, 0))


def split(matrix):
    high = matrix.astype(ml_dtypes.bfloat16)
    low = (matrix - high.astype(np.float64)).astype(ml_dtypes.bfloat16)
    return high, low


class Layout:
    def __init__(self, parts):
        self.at = {}
        row = 0
        for name, rows in parts:
            self.at[name] = (row, rows)
            row += rows
        self.rows = row


def layout(grid_y, boots):
    slabs = DEPTHS * grid_y * boots // LANES
    return Layout(
        [
            ("base_x", GRID),
            ("base_xt2", 2 * GRID),
            ("field_y2", 2 * LANES),
            ("field_yt", 2 * LANES),
            ("station_y2", 2 * grid_y),
            ("back", 5 * LANES),
            ("same", LANES),
            ("regroup", boots * LANES * max(1, boots // 2)),
            ("table", 5 * slabs // 2 * GRID),
        ]
    )


@functools.lru_cache(maxsize=None)
def constants(grid_y, boots):
    deep = LANES // grid_y // boots
    slabs = DEPTHS // deep
    table = []
    for values, (odd_x, odd_y) in zip(offset_table(grid_y), PARITY):
        t = spectrum(values, odd_x, GRID)
        t = np.moveaxis(spectrum(np.moveaxis(t, 1, 0), odd_y, grid_y), 0, 1)
        t = np.moveaxis(t, 2, 0).reshape(slabs, deep, GRID, 1, grid_y).transpose(0, 2, 1, 3, 4)
        table.append(np.tile(t, (1, 1, 1, boots, 1)).reshape(slabs, GRID, LANES))
    table = np.stack(table).reshape(5, slabs // 2, 2, GRID, LANES).transpose(0, 1, 3, 2, 4)

    base_x = basis(GRID)
    base_y = basis(grid_y).reshape(grid_y, 2, grid_y)
    copies = deep * boots
    field_y = np.einsum("ab,yhl->ayhbl", np.eye(copies), base_y).reshape(LANES, 2 * LANES)
    compact = deep == 2
    near = 1 if compact else deep
    station_y = np.einsum("b,yhl->yhbl", np.ones(near * boots), base_y).reshape(grid_y, -1)
    halves = 2 if compact else 1
    spread = np.zeros((5, deep, boots, grid_y, halves, near, boots, grid_y))
    for c in range(5):
        for b in range(boots):
            spread[c, 0, b, c, :, :, b, :] = 1
    spread = spread.reshape(5, LANES, LANES)
    back = spread.transpose(0, 2, 1).reshape(5 * LANES, LANES)
    same = np.einsum("ab,dc,yz->daycbz", np.eye(boots), np.ones((deep, deep)), np.ones((grid_y, grid_y)))
    same = same.reshape(LANES, LANES)
    regroup = np.einsum("st,de,ab,yz->sdaybtez", *[np.eye(n) for n in (boots, deep, boots, grid_y)])
    regroup = regroup.reshape(boots * LANES, boots * LANES)
    if boots > 2:
        regroup = np.concatenate(np.split(regroup, boots // 2, axis=1), axis=0)
    y_high, y_low = split(field_y)
    x_high, x_low = split(base_x.T)
    parts = dict(
        base_x=base_x,
        base_xt2=np.concatenate([x_high, x_low], axis=1),
        field_y2=np.concatenate([y_high, y_low], axis=0),
        field_yt=field_y.T,
        station_y2=np.concatenate(split(station_y)),
        back=back,
        same=same,
        regroup=regroup,
        table=table.reshape(-1, 2 * LANES),
    )
    where = layout(grid_y, boots)
    whole = np.zeros((max(where.rows, 1 << 14), 2 * LANES), ml_dtypes.bfloat16)
    for name, (row, rows) in where.at.items():
        part = parts[name].astype(ml_dtypes.bfloat16)
        assert part.shape[0] == rows
        whole[row : row + rows, : part.shape[1]] = part
    return whole


def dot(a, b):
    return jnp.dot(a, b, preferred_element_type=F32)


def solve_kernel(
    grid_y,
    boots,
    slot_ref,
    comp_ref,
    station_ref,
    observed_ref,
    counts_ref,
    source,
    out_ref,
    const,
    copied,
    pick_x,
    pick_xt,
    pick_y,
    weights,
    data,
    pred,
    image,
    values,
    rows,
    table_wide,
    sums,
    spread_out,
    spec_q,
    spec_i,
    spec_f,
    spec_g,
    picked_in,
    models,
    residual,
    direction,
    penalty,
    applied,
):
    deep = LANES // grid_y // boots
    slabs = DEPTHS // deep
    where = layout(grid_y, boots)
    split_row = where.at["table"][0]
    compact = deep == 2
    wide = LANES if compact else 2 * LANES
    low_lanes = lax.broadcasted_iota(jnp.int32, (1, LANES), 1) < LANES // 2
    copies = [
        pltpu.make_async_copy(source.at[a:b], const.at[a:b], copied.at[i])
        for i, (a, b) in enumerate([(0, split_row), (split_row, where.rows)])
    ]
    first_step = pl.program_id(0) == 0

    @pl.when(first_step)
    def _():
        for copy in copies:
            copy.start()

    def held(name, width=2 * LANES):
        row, count = where.at[name]
        return const[row : row + count, :width]

    def table(c, z, at):
        row = split_row + (c * (slabs // 2) + z // 2) * GRID
        return const[row + at.start : row + at.stop, z % 2 * LANES : (z % 2 + 1) * LANES]

    stations = station_ref.shape[1]
    first = (slot_ref[0] * pl.num_programs(0) + pl.program_id(0)) * boots
    pieces = [(z, slice(row, row + ROWS)) for z in range(slabs) for row in range(0, GRID, ROWS)]

    rows[...] = jnp.zeros_like(rows)
    for b in range(boots):
        row = b * grid_y
        rows[row : row + 5, :] = observed_ref[...]
        count = counts_ref[pl.ds(first + b, 1), :].astype(F32)
        for c in range(5):
            rows[row + 8 + c : row + 9 + c, :] = count * comp_ref[c]
    rows[16:18, :] = station_ref[...].astype(F32)
    turned = jnp.transpose(rows[...])
    lane = lax.broadcasted_iota(jnp.int32, (1, LANES), 1)
    used = lane % grid_y < 5
    data[...] = jnp.where(used, turned, 0.0)
    weights[...] = jnp.where(used, pltpu.roll(turned, LANES - 8, 1), 0.0)
    values[...] = (weights[...] * data[...]).astype(BF).astype(F32)

    place_x = (lax.broadcasted_iota(jnp.int32, (GRID, stations), 0) == station_ref[0:1, :]).astype(F32).astype(BF)
    place_xt = (turned[:, 16:17] == lane.astype(F32)).astype(F32).astype(BF)
    place_yt = (turned[:, 17:18] == lane.astype(F32)).astype(F32)[:, :grid_y].astype(BF)

    @pl.when(first_step)
    def _():
        copies[0].wait()

    pick_xt[...] = dot(held("base_xt2", GRID), place_x).astype(BF)
    pick_x[...] = dot(place_xt, held("base_x")).astype(BF)
    station_y2 = held("station_y2", wide)
    pick_y[...] = dot(place_yt, station_y2[:grid_y]) + dot(place_yt, station_y2[grid_y:])

    @pl.when(first_step)
    def _():
        copies[1].wait()
        for c in range(5):
            for z in range(slabs):
                table_wide[c, z] = table(c, z, slice(0, GRID)).astype(F32)

    no_sum = jnp.zeros((8, LANES), F32)

    def back_project():
        owner = lane // grid_y % boots * grid_y
        for row in range(0, stations, ROWS):
            at = slice(row, row + ROWS)
            trig = [pick_y[at, lane : lane + LANES] for lane in range(0, wide, LANES)]
            for c in range(5):
                e = jnp.take_along_axis(values[at, :], jnp.broadcast_to(owner + c, (ROWS, LANES)), axis=1)
                for i, part in enumerate(trig):
                    to = c * wide + i * LANES
                    spread_out[at, to : to + LANES] = (e * part).astype(BF)
        spec = dot(pick_xt[...], spread_out[...])
        for c, (odd_x, odd_y) in enumerate(PARITY):
            for hx in range(2):
                for row in range(0, GRID, ROWS):
                    at = slice(hx * GRID + row, hx * GRID + row + ROWS)
                    if compact:
                        part = spec[at, c * LANES : (c + 1) * LANES]
                        turned = pltpu.roll(part, LANES // 2, 1)
                        parts = [jnp.where(low_lanes, part, turned), jnp.where(low_lanes, turned, part)]
                    else:
                        parts = [spec[at, lane : lane + LANES] for lane in (c * wide, c * wide + LANES)]
                    for hy, part in enumerate(parts):
                        spec_q[c, hx, hy, row : row + ROWS, :] = -part if (odd_x * hx + odd_y * hy) % 2 else part

        for row in range(0, GRID, 16):
            at = slice(row, row + 16)
            for hx in range(2):
                q = [[spec_q[c, hx ^ PARITY[c][0], hy, at, :] for hy in range(2)] for c in range(5)]
                to = slice(hx * GRID + row, hx * GRID + row + 16)
                for z in range(slabs):
                    t = [table_wide[c, z, at, :] for c in range(5)]
                    for hy in range(2):
                        total = t[0] * q[0][hy]
                        for c in range(1, 5):
                            total = total + t[c] * q[c][hy ^ PARITY[c][1]]
                        spec_g[to, (2 * z + hy) * LANES : (2 * z + hy + 1) * LANES] = total.astype(BF)
        along_x = dot(held("base_x"), spec_g[...]).astype(BF)
        along_x = jnp.concatenate([along_x[:, 2 * z * LANES : (2 * z + 2) * LANES] for z in range(slabs)], axis=0)
        applied[...] = dot(along_x, held("field_yt", LANES)).reshape(slabs, GRID, LANES)

    def predict():
        r = residual[...].reshape(slabs * GRID, LANES).astype(BF)
        y = dot(jnp.concatenate([r, r], axis=1), held("field_y2")).astype(BF)
        y = jnp.concatenate([y[z * GRID : (z + 1) * GRID] for z in range(slabs)], axis=1)
        spec_f[...] = dot(held("base_xt2"), jnp.concatenate([y, y], axis=0)).astype(BF)

        for row in range(0, GRID, 16):
            at = [slice(hx * GRID + row, hx * GRID + row + 16) for hx in range(2)]
            total = [[[None] * 2 for _ in range(2)] for _ in range(5)]
            for eight in range(0, slabs, 8):
                part = [[[None] * 2 for _ in range(2)] for _ in range(5)]
                for z in range(eight, min(slabs, eight + 8)):
                    f = [
                        [spec_f[at[hx], (2 * z + hy) * LANES : (2 * z + hy + 1) * LANES] for hy in range(2)]
                        for hx in range(2)
                    ]
                    for c, (odd_x, odd_y) in enumerate(PARITY):
                        t = table(c, z, at[0])
                        for hx in range(2):
                            for hy in range(2):
                                term = t * f[hx ^ odd_x][hy ^ odd_y]
                                old = part[c][hx][hy]
                                part[c][hx][hy] = term if old is None else old + term
                for c in range(5):
                    for hx in range(2):
                        for hy in range(2):
                            new = part[c][hx][hy].astype(F32)
                            total[c][hx][hy] = total[c][hx][hy] + new if eight else new
            for c, (odd_x, odd_y) in enumerate(PARITY):
                for hx in range(2):
                    parts = [-total[c][hx][hy] if (odd_x * hx + odd_y * hy) % 2 else total[c][hx][hy] for hy in range(2)]
                    if compact:
                        low, high = parts
                        parts = [
                            jnp.where(low_lanes, low, high)
                            + pltpu.roll(jnp.where(low_lanes, high, low), LANES // 2, 1)
                        ]
                    for i, part in enumerate(parts):
                        to = c * wide + i * LANES
                        spec_i[at[hx], to : to + LANES] = part.astype(BF)

        picked = dot(pick_x[...], spec_i[...])
        for row in range(0, stations, ROWS):
            at = slice(row, row + ROWS)
            for c in range(5):
                part = None
                for lane in range(0, wide, LANES):
                    term = picked[at, c * wide + lane : c * wide + lane + LANES] * pick_y[at, lane : lane + LANES]
                    part = term if part is None else part + term
                picked_in[at, c * LANES : (c + 1) * LANES] = part.astype(BF)
        return dot(picked_in[...], held("back", LANES))

    def fold(a):
        return jnp.sum(a.reshape(a.shape[0] // 8, 8, LANES), axis=0)

    def total_of(partial):
        if boots == 1:
            return jnp.broadcast_to(jnp.sum(partial, keepdims=True), (1, LANES))
        parts = []
        for _ in range(3):
            part = partial.astype(BF).astype(F32)
            parts.append(part)
            partial = partial - part
        parts.append(no_sum)
        sums = dot(jnp.concatenate(parts, axis=0).astype(BF), held("same", LANES))
        return jnp.sum(sums, axis=0, keepdims=True)

    def depth_weight(z):
        within = lax.broadcasted_iota(jnp.int32, (1, LANES), 1) // (boots * grid_y)
        depth = (within + z * deep).astype(F32) + 0.5 + station_height
        ratio = station_height / depth
        return ratio * ratio * ratio

    models[...] = jnp.zeros_like(models)
    direction[...] = jnp.zeros_like(direction)
    pred[...] = jnp.zeros_like(pred)
    image[...] = jnp.zeros_like(image)

    def round_of(index, carry):
        old_norm, old_step = carry
        fresh = index % CG_STEPS == 0
        back_project()

        @pl.when(fresh)
        def _():
            norm = no_sum
            for z, at in pieces:
                m = models[z, at]
                p = damping * depth_weight(z) / (m * m + focusing * focusing)
                penalty[z, at] = p
                r = applied[z, at] - p * m
                residual[z, at] = r
                norm += fold(r * r)
            sums[...] = norm

        @pl.when(jnp.logical_not(fresh))
        def _():
            norm = no_sum
            for z, at in pieces:
                r = residual[z, at] - old_step * (applied[z, at] + penalty[z, at] * direction[z, at])
                residual[z, at] = r
                norm += fold(r * r)
            sums[...] = norm

        norm = total_of(sums[...])
        ratio = jnp.where(fresh, 0.0, norm / old_norm)
        cross = no_sum
        for z, at in pieces:
            d = residual[z, at] + ratio * direction[z, at]
            direction[z, at] = d
            cross += fold(penalty[z, at] * d * d)
        here = predict() + ratio * image[...]
        image[...] = here
        step = norm / total_of(cross + fold(weights[...] * here * here))
        for z, at in pieces:
            models[z, at] += step * direction[z, at]
        now = pred[...] + step * here
        pred[...] = now
        values[...] = (weights[...] * jnp.where(fresh, here, data[...] - now)).astype(BF).astype(F32)
        return norm, step

    one = jnp.ones((1, LANES), F32)
    lax.fori_loop(0, IRLS * CG_STEPS, round_of, (one, one))

    for group in range(slabs // boots):
        m = jnp.concatenate([models[group * boots + i].astype(BF) for i in range(boots)], axis=1)
        if boots > 1:
            regroup = held("regroup")
            regroup = [regroup[i * boots * LANES : (i + 1) * boots * LANES] for i in range(boots // 2)]
            m = dot(m, jnp.concatenate(regroup, axis=1)).astype(BF)
        for b in range(boots):
            out_ref[b * GRID : (b + 1) * GRID, group * LANES : (group + 1) * LANES] = (
                m[:, b * LANES : (b + 1) * LANES]
            )


def solve(slot, comp_weight, station_index, observed, counts, mine, grid_y):
    boots = min(mine, LANES // grid_y)
    slabs = DEPTHS * grid_y * boots // LANES
    stations = station_index.shape[1]
    const = jnp.asarray(constants(grid_y, boots))
    vmem = pltpu.VMEM
    whole = lambda a: pl.BlockSpec(a.shape, lambda i, n=a.ndim: (0,) * n)
    smem = pl.BlockSpec(memory_space=pltpu.SMEM)
    field = vmem((slabs, GRID, LANES), F32)
    at_stations = vmem((stations, LANES), F32)
    wide = LANES if 2 * slabs == DEPTHS else 2 * LANES
    inputs = [station_index, observed, counts]
    return pl.pallas_call(
        functools.partial(solve_kernel, grid_y, boots),
        out_shape=jax.ShapeDtypeStruct((mine * GRID, DEPTHS * grid_y), BF),
        grid=(mine // boots,),
        in_specs=[smem, smem] + [whole(a) for a in inputs] + [pl.BlockSpec(memory_space=pl.ANY)],
        out_specs=pl.BlockSpec((boots * GRID, DEPTHS * grid_y), lambda i: (i, 0)),
        scratch_shapes=[
            vmem((layout(grid_y, boots).rows, 2 * LANES), BF),
            pltpu.SemaphoreType.DMA((2,)),
            vmem((stations, 2 * GRID), BF),
            vmem((2 * GRID, stations), BF),
            vmem((stations, wide), F32),
            at_stations,
            at_stations,
            at_stations,
            at_stations,
            at_stations,
            vmem((LANES, stations), F32),
            vmem((5, slabs, GRID, LANES), F32),
            vmem((8, LANES), F32),
            vmem((stations, 5 * wide), BF),
            vmem((5, 2, 2, GRID, LANES), F32),
            vmem((2 * GRID, 5 * wide), BF),
            vmem((2 * GRID, slabs * 2 * LANES), BF),
            vmem((2 * GRID, slabs * 2 * LANES), BF),
            vmem((stations, 5 * LANES), BF),
            field,
            field,
            field,
            field,
            field,
        ],
        compiler_params=pltpu.CompilerParams(vmem_limit_bytes=56 * 1024 * 1024),
        cost_estimate=pl.CostEstimate(flops=10**10, bytes_accessed=10**7, transcendentals=0),
        name="solve",
    )(slot, comp_weight, *inputs, const)


def pick_kernel(grid_y, boots, count, models_ref, *refs):
    def pick_chunk(cell_ref, out_ref, at):
        cells = cell_ref[:, at]
        place = cells.astype(F32)
        wide = lambda row, rows: jnp.broadcast_to(row, (rows, CHUNK)).astype(BF)
        count_up = lambda rows: lax.broadcasted_iota(jnp.int32, (rows, CHUNK), 0).astype(F32).astype(BF)
        here_y = count_up(grid_y) == wide(place[1:2], grid_y)
        here_y = jnp.where(here_y, jnp.ones((grid_y, CHUNK), BF), jnp.zeros((grid_y, CHUNK), BF))
        z_row = wide(place[2:3], 16)
        none = jnp.zeros((16, CHUNK), BF)
        chosen = []
        for z in range(DEPTHS):
            here_z = z_row == jnp.full((16, CHUNK), z, BF)
            chosen += [jnp.where(here_z, here_y[i : i + 16], none) for i in range(0, grid_y, 16)]
        found = dot(models_ref[...], jnp.concatenate(chosen, axis=0)).astype(BF)
        at_x = count_up(GRID) == wide(place[0:1], GRID)
        parts = []
        for b in range(boots):
            part = jnp.where(at_x, found[b * GRID : (b + 1) * GRID], jnp.zeros((GRID, CHUNK), BF))
            while part.shape[0] > 16:
                half = part.shape[0] // 2
                part = part[:half] + part[half:]
            parts.append(jnp.sum(part.astype(F32), axis=0, keepdims=True))
        out_ref[:, at] = jnp.concatenate(parts, axis=0).astype(BF)

    @pl.loop(0, refs[0].shape[1] // CHUNK)
    def _(step):
        at = pl.ds(pl.multiple_of(step * CHUNK, CHUNK), CHUNK)
        for cell_ref, out_ref in zip(refs[:count], refs[count:]):
            pick_chunk(cell_ref, out_ref, at)


def pick(models, cells, grid_y):
    boots = models.shape[0] // GRID
    count = cells[0].shape[1]
    vmem = pl.BlockSpec(memory_space=pltpu.VMEM)
    return pl.pallas_call(
        functools.partial(pick_kernel, grid_y, boots, len(cells)),
        out_shape=[jax.ShapeDtypeStruct((boots, count), BF)] * len(cells),
        in_specs=[vmem] * (1 + len(cells)),
        out_specs=[vmem] * len(cells),
        compiler_params=pltpu.CompilerParams(vmem_limit_bytes=40 * 1024 * 1024),
        cost_estimate=pl.CostEstimate(
            flops=2 * models.size * count * len(cells), bytes_accessed=10**6, transcendentals=0
        ),
        name="pick",
    )(models, *cells)


def local(wide, cell_index, station_index, observed, comp_weight, counts):
    boots = counts.shape[0]
    grid_y = cell_index.shape[1] * wide // (GRID * DEPTHS)
    team = TEAM if wide % TEAM == 0 and boots % TEAM == 0 else 1
    slot = lax.axis_index("wide").astype(jnp.int32) & (team - 1)

    def swap(a, k):
        return lax.ppermute(a, "wide", [(i, i ^ k) for i in range(wide)])

    theirs = [swap(cell_index, k) for k in range(1, team)]
    models = solve(slot.reshape(1), comp_weight, station_index, observed, counts, boots // team, grid_y)
    far = [swap(a, k + 2) for k, a in enumerate(pick(models, theirs[1:], grid_y))] if team > 2 else []
    near = pick(models, [cell_index] + theirs[:1], grid_y)
    got = [near[0]] + [swap(a, 1) for a in near[1:]] + far
    blocks = []
    for member in range(team):
        block = got[member]
        for other in range(1, team):
            block = jnp.where(slot == other, got[member ^ other], block)
        blocks.append(block.astype(F32))
    return jnp.concatenate(blocks, axis=0)


def solution(mesh):
    in_specs = (P(None, "wide"), P(None, "groups"), P(None, "groups"), P(), P("groups", None))
    out_specs = P("groups", "wide")
    fn = functools.partial(local, mesh.shape["wide"])
    return jax.shard_map(fn, mesh=mesh, in_specs=in_specs, out_specs=out_specs, check_vma=False)
```

```python
import functools

import jax
import jax.numpy as jnp
import ml_dtypes
import numpy as np
from jax import lax
from jax.experimental import pallas as pl
from jax.experimental.pallas import tpu as pltpu
from jax.sharding import PartitionSpec as P

IRLS = 2
CG_STEPS = 2
GRID = 128
DEPTHS = 16
LANES = 128
TEAM = 4
CHUNK = 2048
ROWS = 32

station_height = 2.0
focusing = 0.1
damping = 0.0002

PARITY = ((0, 0), (1, 1), (1, 0), (0, 0), (0, 1))
BF = jnp.bfloat16
F32 = jnp.float32


def offset_table(grid_y):
    one = np.float32
    dx = np.arange(GRID, dtype=one)[:, None, None]
    dy = np.arange(grid_y, dtype=one)[None, :, None]
    dz = (np.arange(DEPTHS, dtype=one) + one(0.5) + one(station_height))[None, None, :]
    radius2 = dx * dx + dy * dy + dz * dz
    strength = one(1) / (radius2 * radius2 * np.sqrt(radius2))
    three = one(3)
    kinds = [
        (three * dx * dx - radius2) * strength,
        three * dx * dy * strength,
        three * dx * dz * strength,
        (three * dy * dy - radius2) * strength,
        three * dy * dz * strength,
    ]
    return [k.astype(ml_dtypes.bfloat16).astype(np.float64) for k in kinds]


def angles(size):
    return 2 * np.pi * np.outer(np.arange(size), np.arange(size) + 0.5) / (2 * size)


def basis(size):
    return np.concatenate([np.cos(angles(size)), np.sin(angles(size))], axis=1)


def spectrum(values, odd, size):
    if odd:
        trig = 2 * np.sin(angles(size))
    else:
        trig = np.cos(angles(size)) * np.where(np.arange(size) == 0, 1, 2)[:, None]
    return np.tensordot(trig.T / size, values, axes=(1, 0))


def split(matrix):
    high = matrix.astype(ml_dtypes.bfloat16)
    low = (matrix - high.astype(np.float64)).astype(ml_dtypes.bfloat16)
    return high, low


class Layout:
    def __init__(self, parts):
        self.at = {}
        row = 0
        for name, rows in parts:
            self.at[name] = (row, rows)
            row += rows
        self.rows = row


def layout(grid_y, boots):
    slabs = DEPTHS * grid_y * boots // LANES
    return Layout(
        [
            ("base_x", GRID),
            ("base_xt2", 2 * GRID),
            ("field_y2", 2 * LANES),
            ("field_yt", 2 * LANES),
            ("station_y2", 2 * grid_y),
            ("spread", 3 * LANES),
            ("back", 5 * LANES),
            ("same", LANES),
            ("regroup", boots * LANES * max(1, boots // 2)),
            ("table", 5 * slabs // 2 * GRID),
        ]
    )


@functools.lru_cache(maxsize=None)
def constants(grid_y, boots):
    deep = LANES // grid_y // boots
    slabs = DEPTHS // deep
    table = []
    for values, (odd_x, odd_y) in zip(offset_table(grid_y), PARITY):
        t = spectrum(values, odd_x, GRID)
        t = np.moveaxis(spectrum(np.moveaxis(t, 1, 0), odd_y, grid_y), 0, 1)
        t = np.moveaxis(t, 2, 0).reshape(slabs, deep, GRID, 1, grid_y).transpose(0, 2, 1, 3, 4)
        table.append(np.tile(t, (1, 1, 1, boots, 1)).reshape(slabs, GRID, LANES))
    table = np.stack(table).reshape(5, slabs // 2, 2, GRID, LANES).transpose(0, 1, 3, 2, 4)

    base_x = basis(GRID)
    base_y = basis(grid_y).reshape(grid_y, 2, grid_y)
    copies = deep * boots
    field_y = np.einsum("ab,yhl->ayhbl", np.eye(copies), base_y).reshape(LANES, 2 * LANES)
    compact = deep == 2
    near = 1 if compact else deep
    station_y = np.einsum("b,yhl->yhbl", np.ones(near * boots), base_y).reshape(grid_y, -1)
    halves = 2 if compact else 1
    spread = np.zeros((5, deep, boots, grid_y, halves, near, boots, grid_y))
    for c in range(5):
        for b in range(boots):
            spread[c, 0, b, c, :, :, b, :] = 1
    spread = spread.reshape(5, LANES, LANES)
    back = spread.transpose(0, 2, 1).reshape(5 * LANES, LANES)
    spread = np.concatenate([spread, np.zeros((1, LANES, LANES))])
    spread = spread.reshape(3, 2, LANES, LANES).transpose(0, 2, 1, 3)
    same = np.einsum("ab,dc,yz->daycbz", np.eye(boots), np.ones((deep, deep)), np.ones((grid_y, grid_y)))
    same = same.reshape(LANES, LANES)
    regroup = np.einsum("st,de,ab,yz->sdaybtez", *[np.eye(n) for n in (boots, deep, boots, grid_y)])
    regroup = regroup.reshape(boots * LANES, boots * LANES)
    if boots > 2:
        regroup = np.concatenate(np.split(regroup, boots // 2, axis=1), axis=0)
    y_high, y_low = split(field_y)
    x_high, x_low = split(base_x.T)
    parts = dict(
        base_x=base_x,
        base_xt2=np.concatenate([x_high, x_low], axis=1),
        field_y2=np.concatenate([y_high, y_low], axis=0),
        field_yt=field_y.T,
        station_y2=np.concatenate(split(station_y)),
        spread=spread.reshape(3 * LANES, 2 * LANES),
        back=back,
        same=same,
        regroup=regroup,
        table=table.reshape(-1, 2 * LANES),
    )
    where = layout(grid_y, boots)
    whole = np.zeros((max(where.rows, 1 << 14), 2 * LANES), ml_dtypes.bfloat16)
    for name, (row, rows) in where.at.items():
        part = parts[name].astype(ml_dtypes.bfloat16)
        assert part.shape[0] == rows
        whole[row : row + rows, : part.shape[1]] = part
    return whole


def dot(a, b):
    return jnp.dot(a, b, preferred_element_type=F32)


def solve_kernel(
    grid_y,
    boots,
    slot_ref,
    comp_ref,
    station_ref,
    observed_ref,
    counts_ref,
    source,
    out_ref,
    const,
    copied,
    pick_x,
    pick_xt,
    pick_y,
    weights,
    data,
    pred,
    image,
    values,
    rows,
    table_wide,
    sums,
    spread_out,
    spec_q,
    spec_i,
    spec_f,
    spec_g,
    picked_in,
    models,
    residual,
    direction,
    penalty,
    applied,
):
    deep = LANES // grid_y // boots
    slabs = DEPTHS // deep
    where = layout(grid_y, boots)
    split_row = where.at["table"][0]
    compact = deep == 2
    wide = LANES if compact else 2 * LANES
    low_lanes = lax.broadcasted_iota(jnp.int32, (1, LANES), 1) < LANES // 2
    copies = [
        pltpu.make_async_copy(source.at[a:b], const.at[a:b], copied.at[i])
        for i, (a, b) in enumerate([(0, split_row), (split_row, where.rows)])
    ]
    first_step = pl.program_id(0) == 0

    @pl.when(first_step)
    def _():
        for copy in copies:
            copy.start()

    def held(name, width=2 * LANES):
        row, count = where.at[name]
        return const[row : row + count, :width]

    def table(c, z, at):
        row = split_row + (c * (slabs // 2) + z // 2) * GRID
        return const[row + at.start : row + at.stop, z % 2 * LANES : (z % 2 + 1) * LANES]

    stations = station_ref.shape[1]
    first = (slot_ref[0] * pl.num_programs(0) + pl.program_id(0)) * boots
    pieces = [(z, slice(row, row + ROWS)) for z in range(slabs) for row in range(0, GRID, ROWS)]

    rows[...] = jnp.zeros_like(rows)
    for b in range(boots):
        row = b * grid_y
        rows[row : row + 5, :] = observed_ref[...]
        count = counts_ref[pl.ds(first + b, 1), :].astype(F32)
        for c in range(5):
            rows[row + 8 + c : row + 9 + c, :] = count * comp_ref[c]
    rows[16:18, :] = station_ref[...].astype(F32)
    turned = jnp.transpose(rows[...])
    lane = lax.broadcasted_iota(jnp.int32, (1, LANES), 1)
    used = lane % grid_y < 5
    data[...] = jnp.where(used, turned, 0.0)
    weights[...] = jnp.where(used, pltpu.roll(turned, LANES - 8, 1), 0.0)
    values[...] = (weights[...] * data[...]).astype(BF)

    place_x = (lax.broadcasted_iota(jnp.int32, (GRID, stations), 0) == station_ref[0:1, :]).astype(F32).astype(BF)
    place_xt = (turned[:, 16:17] == lane.astype(F32)).astype(F32).astype(BF)
    place_yt = (turned[:, 17:18] == lane.astype(F32)).astype(F32)[:, :grid_y].astype(BF)

    @pl.when(first_step)
    def _():
        copies[0].wait()

    pick_xt[...] = dot(held("base_xt2", GRID), place_x).astype(BF)
    pick_x[...] = dot(place_xt, held("base_x")).astype(BF)
    station_y2 = held("station_y2", wide)
    pick_y[...] = dot(place_yt, station_y2[:grid_y]) + dot(place_yt, station_y2[grid_y:])

    @pl.when(first_step)
    def _():
        copies[1].wait()
        for c in range(5):
            for z in range(slabs):
                table_wide[c, z] = table(c, z, slice(0, GRID)).astype(F32)

    no_sum = jnp.zeros((8, LANES), F32)

    def back_project():
        spread = held("spread")
        spread = jnp.concatenate([spread[i * LANES : (i + 1) * LANES] for i in range(3)], axis=1)
        spreads = dot(values[...], spread[:, : 5 * LANES])
        for row in range(0, stations, ROWS):
            at = slice(row, row + ROWS)
            trig = [pick_y[at, lane : lane + LANES] for lane in range(0, wide, LANES)]
            for c in range(5):
                e = spreads[at, c * LANES : (c + 1) * LANES]
                for i, part in enumerate(trig):
                    to = c * wide + i * LANES
                    spread_out[at, to : to + LANES] = (e * part).astype(BF)
        spec = dot(pick_xt[...], spread_out[...])
        for c, (odd_x, odd_y) in enumerate(PARITY):
            for hx in range(2):
                for row in range(0, GRID, ROWS):
                    at = slice(hx * GRID + row, hx * GRID + row + ROWS)
                    if compact:
                        part = spec[at, c * LANES : (c + 1) * LANES]
                        turned = pltpu.roll(part, LANES // 2, 1)
                        parts = [jnp.where(low_lanes, part, turned), jnp.where(low_lanes, turned, part)]
                    else:
                        parts = [spec[at, lane : lane + LANES] for lane in (c * wide, c * wide + LANES)]
                    for hy, part in enumerate(parts):
                        spec_q[c, hx, hy, row : row + ROWS, :] = -part if (odd_x * hx + odd_y * hy) % 2 else part

        for row in range(0, GRID, 16):
            at = slice(row, row + 16)
            for hx in range(2):
                q = [[spec_q[c, hx ^ PARITY[c][0], hy, at, :] for hy in range(2)] for c in range(5)]
                to = slice(hx * GRID + row, hx * GRID + row + 16)
                for z in range(slabs):
                    t = [table_wide[c, z, at, :] for c in range(5)]
                    for hy in range(2):
                        total = t[0] * q[0][hy]
                        for c in range(1, 5):
                            total = total + t[c] * q[c][hy ^ PARITY[c][1]]
                        spec_g[to, (2 * z + hy) * LANES : (2 * z + hy + 1) * LANES] = total.astype(BF)
        along_x = dot(held("base_x"), spec_g[...]).astype(BF)
        along_x = jnp.concatenate([along_x[:, 2 * z * LANES : (2 * z + 2) * LANES] for z in range(slabs)], axis=0)
        applied[...] = dot(along_x, held("field_yt", LANES)).reshape(slabs, GRID, LANES)

    def predict():
        r = residual[...].reshape(slabs * GRID, LANES).astype(BF)
        y = dot(jnp.concatenate([r, r], axis=1), held("field_y2")).astype(BF)
        y = jnp.concatenate([y[z * GRID : (z + 1) * GRID] for z in range(slabs)], axis=1)
        spec_f[...] = dot(held("base_xt2"), jnp.concatenate([y, y], axis=0)).astype(BF)

        for row in range(0, GRID, 16):
            at = [slice(hx * GRID + row, hx * GRID + row + 16) for hx in range(2)]
            total = [[[None] * 2 for _ in range(2)] for _ in range(5)]
            for eight in range(0, slabs, 8):
                part = [[[None] * 2 for _ in range(2)] for _ in range(5)]
                for z in range(eight, min(slabs, eight + 8)):
                    f = [
                        [spec_f[at[hx], (2 * z + hy) * LANES : (2 * z + hy + 1) * LANES] for hy in range(2)]
                        for hx in range(2)
                    ]
                    for c, (odd_x, odd_y) in enumerate(PARITY):
                        t = table(c, z, at[0])
                        for hx in range(2):
                            for hy in range(2):
                                term = t * f[hx ^ odd_x][hy ^ odd_y]
                                old = part[c][hx][hy]
                                part[c][hx][hy] = term if old is None else old + term
                for c in range(5):
                    for hx in range(2):
                        for hy in range(2):
                            new = part[c][hx][hy].astype(F32)
                            total[c][hx][hy] = total[c][hx][hy] + new if eight else new
            for c, (odd_x, odd_y) in enumerate(PARITY):
                for hx in range(2):
                    parts = [-total[c][hx][hy] if (odd_x * hx + odd_y * hy) % 2 else total[c][hx][hy] for hy in range(2)]
                    if compact:
                        low, high = parts
                        parts = [
                            jnp.where(low_lanes, low, high)
                            + pltpu.roll(jnp.where(low_lanes, high, low), LANES // 2, 1)
                        ]
                    for i, part in enumerate(parts):
                        to = c * wide + i * LANES
                        spec_i[at[hx], to : to + LANES] = part.astype(BF)

        picked = dot(pick_x[...], spec_i[...])
        for row in range(0, stations, ROWS):
            at = slice(row, row + ROWS)
            for c in range(5):
                part = None
                for lane in range(0, wide, LANES):
                    term = picked[at, c * wide + lane : c * wide + lane + LANES] * pick_y[at, lane : lane + LANES]
                    part = term if part is None else part + term
                picked_in[at, c * LANES : (c + 1) * LANES] = part.astype(BF)
        return dot(picked_in[...], held("back", LANES))

    def fold(a):
        return jnp.sum(a.reshape(a.shape[0] // 8, 8, LANES), axis=0)

    def total_of(partial):
        if boots == 1:
            return jnp.broadcast_to(jnp.sum(partial, keepdims=True), (1, LANES))
        parts = []
        for _ in range(3):
            part = partial.astype(BF).astype(F32)
            parts.append(part)
            partial = partial - part
        parts.append(no_sum)
        sums = dot(jnp.concatenate(parts, axis=0).astype(BF), held("same", LANES))
        return jnp.sum(sums, axis=0, keepdims=True)

    def depth_weight(z):
        within = lax.broadcasted_iota(jnp.int32, (1, LANES), 1) // (boots * grid_y)
        depth = (within + z * deep).astype(F32) + 0.5 + station_height
        ratio = station_height / depth
        return ratio * ratio * ratio

    models[...] = jnp.zeros_like(models)
    direction[...] = jnp.zeros_like(direction)
    pred[...] = jnp.zeros_like(pred)
    image[...] = jnp.zeros_like(image)

    def round_of(index, carry):
        old_norm, old_step = carry
        fresh = index % CG_STEPS == 0
        back_project()

        @pl.when(fresh)
        def _():
            norm = no_sum
            for z, at in pieces:
                m = models[z, at]
                p = damping * depth_weight(z) / (m * m + focusing * focusing)
                penalty[z, at] = p
                r = applied[z, at] - p * m
                residual[z, at] = r
                norm += fold(r * r)
            sums[...] = norm

        @pl.when(jnp.logical_not(fresh))
        def _():
            norm = no_sum
            for z, at in pieces:
                r = residual[z, at] - old_step * (applied[z, at] + penalty[z, at] * direction[z, at])
                residual[z, at] = r
                norm += fold(r * r)
            sums[...] = norm

        norm = total_of(sums[...])
        ratio = jnp.where(fresh, 0.0, norm / old_norm)
        cross = no_sum
        for z, at in pieces:
            d = residual[z, at] + ratio * direction[z, at]
            direction[z, at] = d
            cross += fold(penalty[z, at] * d * d)
        here = predict() + ratio * image[...]
        image[...] = here
        step = norm / total_of(cross + fold(weights[...] * here * here))
        for z, at in pieces:
            models[z, at] += step * direction[z, at]
        now = pred[...] + step * here
        pred[...] = now
        values[...] = (weights[...] * jnp.where(fresh, here, data[...] - now)).astype(BF)
        return norm, step

    one = jnp.ones((1, LANES), F32)
    lax.fori_loop(0, IRLS * CG_STEPS, round_of, (one, one))

    for group in range(slabs // boots):
        m = jnp.concatenate([models[group * boots + i].astype(BF) for i in range(boots)], axis=1)
        if boots > 1:
            regroup = held("regroup")
            regroup = [regroup[i * boots * LANES : (i + 1) * boots * LANES] for i in range(boots // 2)]
            m = dot(m, jnp.concatenate(regroup, axis=1)).astype(BF)
        for b in range(boots):
            out_ref[b * GRID : (b + 1) * GRID, group * LANES : (group + 1) * LANES] = (
                m[:, b * LANES : (b + 1) * LANES]
            )


def solve(slot, comp_weight, station_index, observed, counts, mine, grid_y):
    boots = min(mine, LANES // grid_y)
    slabs = DEPTHS * grid_y * boots // LANES
    stations = station_index.shape[1]
    const = jnp.asarray(constants(grid_y, boots))
    vmem = pltpu.VMEM
    whole = lambda a: pl.BlockSpec(a.shape, lambda i, n=a.ndim: (0,) * n)
    smem = pl.BlockSpec(memory_space=pltpu.SMEM)
    field = vmem((slabs, GRID, LANES), F32)
    at_stations = vmem((stations, LANES), F32)
    wide = LANES if 2 * slabs == DEPTHS else 2 * LANES
    inputs = [station_index, observed, counts]
    return pl.pallas_call(
        functools.partial(solve_kernel, grid_y, boots),
        out_shape=jax.ShapeDtypeStruct((mine * GRID, DEPTHS * grid_y), BF),
        grid=(mine // boots,),
        in_specs=[smem, smem] + [whole(a) for a in inputs] + [pl.BlockSpec(memory_space=pl.ANY)],
        out_specs=pl.BlockSpec((boots * GRID, DEPTHS * grid_y), lambda i: (i, 0)),
        scratch_shapes=[
            vmem((layout(grid_y, boots).rows, 2 * LANES), BF),
            pltpu.SemaphoreType.DMA((2,)),
            vmem((stations, 2 * GRID), BF),
            vmem((2 * GRID, stations), BF),
            vmem((stations, wide), F32),
            at_stations,
            at_stations,
            at_stations,
            at_stations,
            vmem((stations, LANES), BF),
            vmem((LANES, stations), F32),
            vmem((5, slabs, GRID, LANES), F32),
            vmem((8, LANES), F32),
            vmem((stations, 5 * wide), BF),
            vmem((5, 2, 2, GRID, LANES), F32),
            vmem((2 * GRID, 5 * wide), BF),
            vmem((2 * GRID, slabs * 2 * LANES), BF),
            vmem((2 * GRID, slabs * 2 * LANES), BF),
            vmem((stations, 5 * LANES), BF),
            field,
            field,
            field,
            field,
            field,
        ],
        compiler_params=pltpu.CompilerParams(vmem_limit_bytes=56 * 1024 * 1024),
        cost_estimate=pl.CostEstimate(flops=10**10, bytes_accessed=10**7, transcendentals=0),
        name="solve",
    )(slot, comp_weight, *inputs, const)


def pick_kernel(grid_y, boots, count, models_ref, *refs):
    def pick_chunk(cell_ref, out_ref, at):
        cells = cell_ref[:, at]
        place = cells.astype(F32)
        wide = lambda row, rows: jnp.broadcast_to(row, (rows, CHUNK)).astype(BF)
        count_up = lambda rows: lax.broadcasted_iota(jnp.int32, (rows, CHUNK), 0).astype(F32).astype(BF)
        here_y = count_up(grid_y) == wide(place[1:2], grid_y)
        here_y = jnp.where(here_y, jnp.ones((grid_y, CHUNK), BF), jnp.zeros((grid_y, CHUNK), BF))
        z_row = wide(place[2:3], 16)
        none = jnp.zeros((16, CHUNK), BF)
        chosen = []
        for z in range(DEPTHS):
            here_z = z_row == jnp.full((16, CHUNK), z, BF)
            chosen += [jnp.where(here_z, here_y[i : i + 16], none) for i in range(0, grid_y, 16)]
        found = dot(models_ref[...], jnp.concatenate(chosen, axis=0)).astype(BF)
        at_x = count_up(GRID) == wide(place[0:1], GRID)
        parts = []
        for b in range(boots):
            part = jnp.where(at_x, found[b * GRID : (b + 1) * GRID], jnp.zeros((GRID, CHUNK), BF))
            while part.shape[0] > 16:
                half = part.shape[0] // 2
                part = part[:half] + part[half:]
            parts.append(jnp.sum(part.astype(F32), axis=0, keepdims=True))
        out_ref[:, at] = jnp.concatenate(parts, axis=0).astype(BF)

    @pl.loop(0, refs[0].shape[1] // CHUNK)
    def _(step):
        at = pl.ds(pl.multiple_of(step * CHUNK, CHUNK), CHUNK)
        for cell_ref, out_ref in zip(refs[:count], refs[count:]):
            pick_chunk(cell_ref, out_ref, at)


def pick(models, cells, grid_y):
    boots = models.shape[0] // GRID
    count = cells[0].shape[1]
    vmem = pl.BlockSpec(memory_space=pltpu.VMEM)
    return pl.pallas_call(
        functools.partial(pick_kernel, grid_y, boots, len(cells)),
        out_shape=[jax.ShapeDtypeStruct((boots, count), BF)] * len(cells),
        in_specs=[vmem] * (1 + len(cells)),
        out_specs=[vmem] * len(cells),
        compiler_params=pltpu.CompilerParams(vmem_limit_bytes=40 * 1024 * 1024),
        cost_estimate=pl.CostEstimate(
            flops=2 * models.size * count * len(cells), bytes_accessed=10**6, transcendentals=0
        ),
        name="pick",
    )(models, *cells)


def local(wide, cell_index, station_index, observed, comp_weight, counts):
    boots = counts.shape[0]
    grid_y = cell_index.shape[1] * wide // (GRID * DEPTHS)
    team = TEAM if wide % TEAM == 0 and boots % TEAM == 0 else 1
    slot = lax.axis_index("wide").astype(jnp.int32) & (team - 1)

    def swap(a, k):
        return lax.ppermute(a, "wide", [(i, i ^ k) for i in range(wide)])

    theirs = [swap(cell_index, k) for k in range(1, team)]
    models = solve(slot.reshape(1), comp_weight, station_index, observed, counts, boots // team, grid_y)
    far = [swap(a, k + 2) for k, a in enumerate(pick(models, theirs[1:], grid_y))] if team > 2 else []
    near = pick(models, [cell_index] + theirs[:1], grid_y)
    got = [near[0]] + [swap(a, 1) for a in near[1:]] + far
    blocks = []
    for member in range(team):
        block = got[member]
        for other in range(1, team):
            block = jnp.where(slot == other, got[member ^ other], block)
        blocks.append(block.astype(F32))
    return jnp.concatenate(blocks, axis=0)


def solution(mesh):
    in_specs = (P(None, "wide"), P(None, "groups"), P(None, "groups"), P(), P("groups", None))
    out_specs = P("groups", "wide")
    fn = functools.partial(local, mesh.shape["wide"])
    return jax.shard_map(fn, mesh=mesh, in_specs=in_specs, out_specs=out_specs, check_vma=False)
```

```python
import functools

import jax
import jax.numpy as jnp
import ml_dtypes
import numpy as np
from jax import lax
from jax.experimental import pallas as pl
from jax.experimental.pallas import tpu as pltpu
from jax.sharding import PartitionSpec as P

IRLS = 2
CG_STEPS = 2
GRID = 128
DEPTHS = 16
LANES = 128
TEAM = 4
CHUNK = 2048
ROWS = 32

station_height = 2.0
focusing = 0.1
damping = 0.0002

PARITY = ((0, 0), (1, 1), (1, 0), (0, 0), (0, 1))
BF = jnp.bfloat16
F32 = jnp.float32


def offset_table(grid_y):
    one = np.float32
    dx = np.arange(GRID, dtype=one)[:, None, None]
    dy = np.arange(grid_y, dtype=one)[None, :, None]
    dz = (np.arange(DEPTHS, dtype=one) + one(0.5) + one(station_height))[None, None, :]
    radius2 = dx * dx + dy * dy + dz * dz
    strength = one(1) / (radius2 * radius2 * np.sqrt(radius2))
    three = one(3)
    kinds = [
        (three * dx * dx - radius2) * strength,
        three * dx * dy * strength,
        three * dx * dz * strength,
        (three * dy * dy - radius2) * strength,
        three * dy * dz * strength,
    ]
    return [k.astype(ml_dtypes.bfloat16).astype(np.float64) for k in kinds]


def angles(size):
    return 2 * np.pi * np.outer(np.arange(size), np.arange(size) + 0.5) / (2 * size)


def basis(size):
    return np.concatenate([np.cos(angles(size)), np.sin(angles(size))], axis=1)


def spectrum(values, odd, size):
    if odd:
        trig = 2 * np.sin(angles(size))
    else:
        trig = np.cos(angles(size)) * np.where(np.arange(size) == 0, 1, 2)[:, None]
    return np.tensordot(trig.T / size, values, axes=(1, 0))


def split(matrix):
    high = matrix.astype(ml_dtypes.bfloat16)
    low = (matrix - high.astype(np.float64)).astype(ml_dtypes.bfloat16)
    return high, low


class Layout:
    def __init__(self, parts):
        self.at = {}
        row = 0
        for name, rows in parts:
            self.at[name] = (row, rows)
            row += rows
        self.rows = row


def layout(grid_y, boots):
    slabs = DEPTHS * grid_y * boots // LANES
    return Layout(
        [
            ("base_x", GRID),
            ("base_xt2", 2 * GRID),
            ("field_y2", 2 * LANES),
            ("field_yt", 2 * LANES),
            ("station_y2", 2 * grid_y),
            ("spread", 3 * LANES),
            ("back", 5 * LANES),
            ("same", LANES),
            ("regroup", boots * LANES * max(1, boots // 2)),
            ("table", 5 * slabs // 2 * GRID),
        ]
    )


@functools.lru_cache(maxsize=None)
def constants(grid_y, boots):
    deep = LANES // grid_y // boots
    slabs = DEPTHS // deep
    table = []
    for values, (odd_x, odd_y) in zip(offset_table(grid_y), PARITY):
        t = spectrum(values, odd_x, GRID)
        t = np.moveaxis(spectrum(np.moveaxis(t, 1, 0), odd_y, grid_y), 0, 1)
        t = np.moveaxis(t, 2, 0).reshape(slabs, deep, GRID, 1, grid_y).transpose(0, 2, 1, 3, 4)
        table.append(np.tile(t, (1, 1, 1, boots, 1)).reshape(slabs, GRID, LANES))
    table = np.stack(table).reshape(5, slabs // 2, 2, GRID, LANES).transpose(0, 1, 3, 2, 4)

    base_x = basis(GRID)
    base_y = basis(grid_y).reshape(grid_y, 2, grid_y)
    copies = deep * boots
    field_y = np.einsum("ab,yhl->ayhbl", np.eye(copies), base_y).reshape(LANES, 2 * LANES)
    station_y = np.einsum("b,yhl->yhbl", np.ones(copies), base_y).reshape(grid_y, 2 * LANES)
    spread = np.zeros((5, deep, boots, grid_y, deep, boots, grid_y))
    for c in range(5):
        for b in range(boots):
            spread[c, 0, b, c, :, b, :] = 1
    spread = spread.reshape(5, LANES, LANES)
    back = spread.transpose(0, 2, 1).reshape(5 * LANES, LANES)
    spread = np.concatenate([spread, np.zeros((1, LANES, LANES))])
    spread = spread.reshape(3, 2, LANES, LANES).transpose(0, 2, 1, 3)
    same = np.einsum("ab,dc,yz->daycbz", np.eye(boots), np.ones((deep, deep)), np.ones((grid_y, grid_y)))
    same = same.reshape(LANES, LANES)
    regroup = np.einsum("st,de,ab,yz->sdaybtez", *[np.eye(n) for n in (boots, deep, boots, grid_y)])
    regroup = regroup.reshape(boots * LANES, boots * LANES)
    if boots > 2:
        regroup = np.concatenate(np.split(regroup, boots // 2, axis=1), axis=0)
    y_high, y_low = split(field_y)
    x_high, x_low = split(base_x.T)
    parts = dict(
        base_x=base_x,
        base_xt2=np.concatenate([x_high, x_low], axis=1),
        field_y2=np.concatenate([y_high, y_low], axis=0),
        field_yt=field_y.T,
        station_y2=np.concatenate(split(station_y)),
        spread=spread.reshape(3 * LANES, 2 * LANES),
        back=back,
        same=same,
        regroup=regroup,
        table=table.reshape(-1, 2 * LANES),
    )
    where = layout(grid_y, boots)
    whole = np.zeros((max(where.rows, 1 << 14), 2 * LANES), ml_dtypes.bfloat16)
    for name, (row, rows) in where.at.items():
        part = parts[name].astype(ml_dtypes.bfloat16)
        assert part.shape[0] == rows
        whole[row : row + rows, : part.shape[1]] = part
    return whole


def dot(a, b):
    return jnp.dot(a, b, preferred_element_type=F32)


def solve_kernel(
    grid_y,
    boots,
    slot_ref,
    comp_ref,
    station_ref,
    observed_ref,
    counts_ref,
    source,
    out_ref,
    const,
    copied,
    pick_x,
    pick_xt,
    pick_y,
    weights,
    data,
    pred,
    image,
    values,
    rows,
    table_wide,
    sums,
    spread_out,
    spec_q,
    spec_i,
    spec_f,
    spec_g,
    picked_in,
    models,
    residual,
    direction,
    penalty,
    applied,
):
    deep = LANES // grid_y // boots
    slabs = DEPTHS // deep
    where = layout(grid_y, boots)
    split_row = where.at["table"][0]
    wide = 2 * LANES
    copies = [
        pltpu.make_async_copy(source.at[a:b], const.at[a:b], copied.at[i])
        for i, (a, b) in enumerate([(0, split_row), (split_row, where.rows)])
    ]
    first_step = pl.program_id(0) == 0

    @pl.when(first_step)
    def _():
        for copy in copies:
            copy.start()

    def held(name, width=2 * LANES):
        row, count = where.at[name]
        return const[row : row + count, :width]

    def table(c, z, at):
        row = split_row + (c * (slabs // 2) + z // 2) * GRID
        return const[row + at.start : row + at.stop, z % 2 * LANES : (z % 2 + 1) * LANES]

    stations = station_ref.shape[1]
    first = (slot_ref[0] * pl.num_programs(0) + pl.program_id(0)) * boots
    pieces = [(z, slice(row, row + ROWS)) for z in range(slabs) for row in range(0, GRID, ROWS)]

    rows[...] = jnp.zeros_like(rows)
    for b in range(boots):
        row = b * grid_y
        rows[row : row + 5, :] = observed_ref[...]
        count = counts_ref[pl.ds(first + b, 1), :].astype(F32)
        for c in range(5):
            rows[row + 8 + c : row + 9 + c, :] = count * comp_ref[c]
    rows[16:18, :] = station_ref[...].astype(F32)
    turned = jnp.transpose(rows[...])
    lane = lax.broadcasted_iota(jnp.int32, (1, LANES), 1)
    used = lane % grid_y < 5
    data[...] = jnp.where(used, turned, 0.0)
    weights[...] = jnp.where(used, pltpu.roll(turned, LANES - 8, 1), 0.0)
    values[...] = (weights[...] * data[...]).astype(BF)

    place_x = (lax.broadcasted_iota(jnp.int32, (GRID, stations), 0) == station_ref[0:1, :]).astype(F32).astype(BF)
    place_xt = (turned[:, 16:17] == lane.astype(F32)).astype(F32).astype(BF)
    place_yt = (turned[:, 17:18] == lane.astype(F32)).astype(F32)[:, :grid_y].astype(BF)

    @pl.when(first_step)
    def _():
        copies[0].wait()

    pick_xt[...] = dot(held("base_xt2", GRID), place_x).astype(BF)
    pick_x[...] = dot(place_xt, held("base_x")).astype(BF)
    station_y2 = held("station_y2")
    pick_y[...] = dot(place_yt, station_y2[:grid_y]) + dot(place_yt, station_y2[grid_y:])

    @pl.when(first_step)
    def _():
        copies[1].wait()
        for c in range(5):
            for z in range(slabs):
                table_wide[c, z] = table(c, z, slice(0, GRID)).astype(F32)

    no_sum = jnp.zeros((8, LANES), F32)

    def back_project():
        spread = held("spread")
        spread = jnp.concatenate([spread[i * LANES : (i + 1) * LANES] for i in range(3)], axis=1)
        spreads = dot(values[...], spread[:, : 5 * LANES])
        for row in range(0, stations, ROWS):
            at = slice(row, row + ROWS)
            trig = [pick_y[at, lane : lane + LANES] for lane in range(0, wide, LANES)]
            for c in range(5):
                e = spreads[at, c * LANES : (c + 1) * LANES]
                for i, part in enumerate(trig):
                    to = c * wide + i * LANES
                    spread_out[at, to : to + LANES] = (e * part).astype(BF)
        spec = dot(pick_xt[...], spread_out[...])
        for c, (odd_x, odd_y) in enumerate(PARITY):
            for hx in range(2):
                for hy in range(2):
                    part = spec[hx * GRID : (hx + 1) * GRID, c * wide + hy * LANES : c * wide + (hy + 1) * LANES]
                    spec_q[c, hx, hy] = -part if (odd_x * hx + odd_y * hy) % 2 else part

        for row in range(0, GRID, 16):
            at = slice(row, row + 16)
            for hx in range(2):
                q = [[spec_q[c, hx ^ PARITY[c][0], hy, at, :] for hy in range(2)] for c in range(5)]
                to = slice(hx * GRID + row, hx * GRID + row + 16)
                for z in range(slabs):
                    t = [table_wide[c, z, at, :] for c in range(5)]
                    for hy in range(2):
                        total = t[0] * q[0][hy]
                        for c in range(1, 5):
                            total = total + t[c] * q[c][hy ^ PARITY[c][1]]
                        spec_g[to, (2 * z + hy) * LANES : (2 * z + hy + 1) * LANES] = total.astype(BF)
        along_x = dot(held("base_x"), spec_g[...]).astype(BF)
        along_x = jnp.concatenate([along_x[:, 2 * z * LANES : (2 * z + 2) * LANES] for z in range(slabs)], axis=0)
        applied[...] = dot(along_x, held("field_yt", LANES)).reshape(slabs, GRID, LANES)

    def predict():
        r = residual[...].reshape(slabs * GRID, LANES).astype(BF)
        y = dot(jnp.concatenate([r, r], axis=1), held("field_y2")).astype(BF)
        y = jnp.concatenate([y[z * GRID : (z + 1) * GRID] for z in range(slabs)], axis=1)
        spec_f[...] = dot(held("base_xt2"), jnp.concatenate([y, y], axis=0)).astype(BF)

        for row in range(0, GRID, 16):
            at = [slice(hx * GRID + row, hx * GRID + row + 16) for hx in range(2)]
            total = [[[None] * 2 for _ in range(2)] for _ in range(5)]
            for eight in range(0, slabs, 8):
                part = [[[None] * 2 for _ in range(2)] for _ in range(5)]
                for z in range(eight, min(slabs, eight + 8)):
                    f = [
                        [spec_f[at[hx], (2 * z + hy) * LANES : (2 * z + hy + 1) * LANES] for hy in range(2)]
                        for hx in range(2)
                    ]
                    for c, (odd_x, odd_y) in enumerate(PARITY):
                        t = table(c, z, at[0])
                        for hx in range(2):
                            for hy in range(2):
                                term = t * f[hx ^ odd_x][hy ^ odd_y]
                                old = part[c][hx][hy]
                                part[c][hx][hy] = term if old is None else old + term
                for c in range(5):
                    for hx in range(2):
                        for hy in range(2):
                            new = part[c][hx][hy]
                            total[c][hx][hy] = total[c][hx][hy].astype(F32) + new.astype(F32) if eight else new
            for c, (odd_x, odd_y) in enumerate(PARITY):
                for hx in range(2):
                    for hy in range(2):
                        part = total[c][hx][hy].astype(BF)
                        part = -part if (odd_x * hx + odd_y * hy) % 2 else part
                        spec_i[at[hx], c * wide + hy * LANES : c * wide + (hy + 1) * LANES] = part

        picked = dot(pick_x[...], spec_i[...])
        for row in range(0, stations, ROWS):
            at = slice(row, row + ROWS)
            for c in range(5):
                part = None
                for lane in range(0, wide, LANES):
                    term = picked[at, c * wide + lane : c * wide + lane + LANES] * pick_y[at, lane : lane + LANES]
                    part = term if part is None else part + term
                picked_in[at, c * LANES : (c + 1) * LANES] = part.astype(BF)
        return dot(picked_in[...], held("back", LANES))

    def fold(a):
        return jnp.sum(a.reshape(a.shape[0] // 8, 8, LANES), axis=0)

    def total_of(partial):
        if boots == 1:
            return jnp.broadcast_to(jnp.sum(partial, keepdims=True), (1, LANES))
        parts = []
        for _ in range(3):
            part = partial.astype(BF).astype(F32)
            parts.append(part)
            partial = partial - part
        parts.append(no_sum)
        sums = dot(jnp.concatenate(parts, axis=0).astype(BF), held("same", LANES))
        return jnp.sum(sums, axis=0, keepdims=True)

    def depth_weight(z):
        within = lax.broadcasted_iota(jnp.int32, (1, LANES), 1) // (boots * grid_y)
        depth = (within + z * deep).astype(F32) + 0.5 + station_height
        ratio = station_height / depth
        return ratio * ratio * ratio

    models[...] = jnp.zeros_like(models)
    direction[...] = jnp.zeros_like(direction)
    pred[...] = jnp.zeros_like(pred)
    image[...] = jnp.zeros_like(image)

    def round_of(index, carry):
        old_norm, old_step = carry
        fresh = index % CG_STEPS == 0
        back_project()

        @pl.when(fresh)
        def _():
            norm = no_sum
            for z, at in pieces:
                m = models[z, at]
                p = damping * depth_weight(z) / (m * m + focusing * focusing)
                penalty[z, at] = p
                r = applied[z, at] - p * m
                residual[z, at] = r
                norm += fold(r * r)
            sums[...] = norm

        @pl.when(jnp.logical_not(fresh))
        def _():
            norm = no_sum
            for z, at in pieces:
                r = residual[z, at] - old_step * (applied[z, at] + penalty[z, at] * direction[z, at])
                residual[z, at] = r
                norm += fold(r * r)
            sums[...] = norm

        norm = total_of(sums[...])
        ratio = jnp.where(fresh, 0.0, norm / old_norm)
        cross = no_sum
        for z, at in pieces:
            d = residual[z, at] + ratio * direction[z, at]
            direction[z, at] = d
            cross += fold(penalty[z, at] * d * d)
        here = predict() + ratio * image[...]
        image[...] = here
        step = norm / total_of(cross + fold(weights[...] * here * here))
        for z, at in pieces:
            models[z, at] += step * direction[z, at]
        now = pred[...] + step * here
        pred[...] = now
        values[...] = (weights[...] * jnp.where(fresh, here, data[...] - now)).astype(BF)
        return norm, step

    one = jnp.ones((1, LANES), F32)
    lax.fori_loop(0, IRLS * CG_STEPS, round_of, (one, one))

    for group in range(slabs // boots):
        m = jnp.concatenate([models[group * boots + i].astype(BF) for i in range(boots)], axis=1)
        if boots > 1:
            regroup = held("regroup")
            regroup = [regroup[i * boots * LANES : (i + 1) * boots * LANES] for i in range(boots // 2)]
            m = dot(m, jnp.concatenate(regroup, axis=1)).astype(BF)
        for b in range(boots):
            out_ref[b * GRID : (b + 1) * GRID, group * LANES : (group + 1) * LANES] = (
                m[:, b * LANES : (b + 1) * LANES]
            )


def solve(slot, comp_weight, station_index, observed, counts, mine, grid_y):
    boots = min(mine, LANES // grid_y)
    slabs = DEPTHS * grid_y * boots // LANES
    stations = station_index.shape[1]
    const = jnp.asarray(constants(grid_y, boots))
    vmem = pltpu.VMEM
    whole = lambda a: pl.BlockSpec(a.shape, lambda i, n=a.ndim: (0,) * n)
    smem = pl.BlockSpec(memory_space=pltpu.SMEM)
    field = vmem((slabs, GRID, LANES), F32)
    at_stations = vmem((stations, LANES), F32)
    wide = 2 * LANES
    inputs = [station_index, observed, counts]
    return pl.pallas_call(
        functools.partial(solve_kernel, grid_y, boots),
        out_shape=jax.ShapeDtypeStruct((mine * GRID, DEPTHS * grid_y), BF),
        grid=(mine // boots,),
        in_specs=[smem, smem] + [whole(a) for a in inputs] + [pl.BlockSpec(memory_space=pl.ANY)],
        out_specs=pl.BlockSpec((boots * GRID, DEPTHS * grid_y), lambda i: (i, 0)),
        scratch_shapes=[
            vmem((layout(grid_y, boots).rows, 2 * LANES), BF),
            pltpu.SemaphoreType.DMA((2,)),
            vmem((stations, 2 * GRID), BF),
            vmem((2 * GRID, stations), BF),
            vmem((stations, wide), F32),
            at_stations,
            at_stations,
            at_stations,
            at_stations,
            vmem((stations, LANES), BF),
            vmem((LANES, stations), F32),
            vmem((5, slabs, GRID, LANES), F32),
            vmem((8, LANES), F32),
            vmem((stations, 5 * wide), BF),
            vmem((5, 2, 2, GRID, LANES), F32),
            vmem((2 * GRID, 5 * wide), BF),
            vmem((2 * GRID, slabs * 2 * LANES), BF),
            vmem((2 * GRID, slabs * 2 * LANES), BF),
            vmem((stations, 5 * LANES), BF),
            field,
            field,
            field,
            field,
            field,
        ],
        compiler_params=pltpu.CompilerParams(vmem_limit_bytes=56 * 1024 * 1024),
        cost_estimate=pl.CostEstimate(flops=10**10, bytes_accessed=10**7, transcendentals=0),
        name="solve",
    )(slot, comp_weight, *inputs, const)


def pick_kernel(grid_y, boots, count, models_ref, *refs):
    def pick_chunk(cell_ref, out_ref, at):
        cells = cell_ref[:, at]
        place = cells.astype(F32)
        wide = lambda row, rows: jnp.broadcast_to(row, (rows, CHUNK)).astype(BF)
        count_up = lambda rows: lax.broadcasted_iota(jnp.int32, (rows, CHUNK), 0).astype(F32).astype(BF)
        here_y = count_up(grid_y) == wide(place[1:2], grid_y)
        here_y = jnp.where(here_y, jnp.ones((grid_y, CHUNK), BF), jnp.zeros((grid_y, CHUNK), BF))
        z_row = wide(place[2:3], 16)
        none = jnp.zeros((16, CHUNK), BF)
        chosen = []
        for z in range(DEPTHS):
            here_z = z_row == jnp.full((16, CHUNK), z, BF)
            chosen += [jnp.where(here_z, here_y[i : i + 16], none) for i in range(0, grid_y, 16)]
        found = dot(models_ref[...], jnp.concatenate(chosen, axis=0)).astype(BF)
        at_x = count_up(GRID) == wide(place[0:1], GRID)
        none = jnp.zeros((GRID, CHUNK), BF)
        parts = [jnp.where(at_x, found[b * GRID : (b + 1) * GRID], none) for b in range(boots)]
        owner = lax.broadcasted_iota(jnp.int32, (16, boots * GRID), 1) // GRID
        owner = (owner == lax.broadcasted_iota(jnp.int32, (16, boots * GRID), 0)).astype(F32).astype(BF)
        out_ref[:, at] = dot(owner, jnp.concatenate(parts, axis=0))[:boots].astype(BF)

    @pl.loop(0, refs[0].shape[1] // CHUNK)
    def _(step):
        at = pl.ds(pl.multiple_of(step * CHUNK, CHUNK), CHUNK)
        for cell_ref, out_ref in zip(refs[:count], refs[count:]):
            pick_chunk(cell_ref, out_ref, at)


def pick(models, cells, grid_y):
    boots = models.shape[0] // GRID
    count = cells[0].shape[1]
    vmem = pl.BlockSpec(memory_space=pltpu.VMEM)
    return pl.pallas_call(
        functools.partial(pick_kernel, grid_y, boots, len(cells)),
        out_shape=[jax.ShapeDtypeStruct((boots, count), BF)] * len(cells),
        in_specs=[vmem] * (1 + len(cells)),
        out_specs=[vmem] * len(cells),
        compiler_params=pltpu.CompilerParams(vmem_limit_bytes=40 * 1024 * 1024),
        cost_estimate=pl.CostEstimate(
            flops=2 * models.size * count * len(cells), bytes_accessed=10**6, transcendentals=0
        ),
        name="pick",
    )(models, *cells)


def local(wide, cell_index, station_index, observed, comp_weight, counts):
    boots = counts.shape[0]
    grid_y = cell_index.shape[1] * wide // (GRID * DEPTHS)
    team = TEAM if wide % TEAM == 0 and boots % TEAM == 0 else 1
    slot = lax.axis_index("wide").astype(jnp.int32) & (team - 1)

    def swap(a, k):
        return lax.ppermute(a, "wide", [(i, i ^ k) for i in range(wide)])

    theirs = [swap(cell_index, k) for k in range(1, team)]
    models = solve(slot.reshape(1), comp_weight, station_index, observed, counts, boots // team, grid_y)
    far = [swap(a, k + 2) for k, a in enumerate(pick(models, theirs[1:], grid_y))] if team > 2 else []
    near = pick(models, [cell_index] + theirs[:1], grid_y)
    got = [near[0]] + [swap(a, 1) for a in near[1:]] + far
    blocks = []
    for member in range(team):
        block = got[member]
        for other in range(1, team):
            block = jnp.where(slot == other, got[member ^ other], block)
        blocks.append(block.astype(F32))
    return jnp.concatenate(blocks, axis=0)


def solution(mesh):
    in_specs = (P(None, "wide"), P(None, "groups"), P(None, "groups"), P(), P("groups", None))
    out_specs = P("groups", "wide")
    fn = functools.partial(local, mesh.shape["wide"])
    return jax.shard_map(fn, mesh=mesh, in_specs=in_specs, out_specs=out_specs, check_vma=False)
```

```python
import functools

import jax
import jax.numpy as jnp
import ml_dtypes
import numpy as np
from jax import lax
from jax.experimental import pallas as pl
from jax.experimental.pallas import tpu as pltpu
from jax.sharding import PartitionSpec as P

IRLS = 2
CG_STEPS = 2
GRID = 128
DEPTHS = 16
LANES = 128
TEAM = 4
CHUNK = 2048
ROWS = 32

station_height = 2.0
focusing = 0.1
damping = 0.0002

PARITY = ((0, 0), (1, 1), (1, 0), (0, 0), (0, 1))
BF = jnp.bfloat16
F32 = jnp.float32


def offset_table(grid_y):
    one = np.float32
    dx = np.arange(GRID, dtype=one)[:, None, None]
    dy = np.arange(grid_y, dtype=one)[None, :, None]
    dz = (np.arange(DEPTHS, dtype=one) + one(0.5) + one(station_height))[None, None, :]
    radius2 = dx * dx + dy * dy + dz * dz
    strength = one(1) / (radius2 * radius2 * np.sqrt(radius2))
    three = one(3)
    kinds = [
        (three * dx * dx - radius2) * strength,
        three * dx * dy * strength,
        three * dx * dz * strength,
        (three * dy * dy - radius2) * strength,
        three * dy * dz * strength,
    ]
    return [k.astype(ml_dtypes.bfloat16).astype(np.float64) for k in kinds]


def angles(size):
    return 2 * np.pi * np.outer(np.arange(size), np.arange(size) + 0.5) / (2 * size)


def basis(size):
    return np.concatenate([np.cos(angles(size)), np.sin(angles(size))], axis=1)


def spectrum(values, odd, size):
    if odd:
        trig = 2 * np.sin(angles(size))
    else:
        trig = np.cos(angles(size)) * np.where(np.arange(size) == 0, 1, 2)[:, None]
    return np.tensordot(trig.T / size, values, axes=(1, 0))


def split(matrix):
    high = matrix.astype(ml_dtypes.bfloat16)
    low = (matrix - high.astype(np.float64)).astype(ml_dtypes.bfloat16)
    return high, low


class Layout:
    def __init__(self, parts):
        self.at = {}
        row = 0
        for name, rows in parts:
            self.at[name] = (row, rows)
            row += rows
        self.rows = row


def layout(grid_y, boots):
    return Layout(
        [
            ("base_x", GRID),
            ("base_xt2", 2 * GRID),
            ("station_y2", 4 * grid_y),
            ("spread", 3 * LANES),
            ("table", 5 * DEPTHS // 2 * GRID),
            ("field_y2", 2 * LANES),
            ("field_yt", 2 * LANES),
            ("back", 5 * LANES),
            ("same", LANES),
            ("regroup", boots * LANES * max(1, boots // 2)),
        ]
    )


@functools.lru_cache(maxsize=None)
def constants(grid_y, boots):
    deep = LANES // grid_y // boots
    copies = LANES // grid_y
    table = []
    for values, (odd_x, odd_y) in zip(offset_table(grid_y), PARITY):
        t = spectrum(values, odd_x, GRID)
        t = np.moveaxis(spectrum(np.moveaxis(t, 1, 0), odd_y, grid_y), 0, 1)
        table.append(np.tile(np.moveaxis(t, 2, 0), (1, 1, copies)))
    table = np.stack(table).reshape(5, DEPTHS // 2, 2, GRID, LANES).transpose(0, 1, 3, 2, 4)

    base_x = basis(GRID)
    base_y = basis(grid_y).reshape(grid_y, 2, grid_y)
    field_y = np.einsum("de,ab,yhl->dayehbl", np.eye(deep), np.eye(boots), base_y).reshape(LANES, 2 * LANES)
    odd_y = np.stack([-base_y[:, 1], base_y[:, 0]], axis=1)
    station_y = [np.tile(b[:, :, None], (1, 1, boots, 1)).reshape(grid_y, -1) for b in (base_y, odd_y)]
    spread = np.zeros((5, deep, boots, grid_y, copies, grid_y))
    for c in range(5):
        for copy in range(copies):
            spread[c, 0, copy % boots, c, copy, :] = 1
    spread = spread.reshape(5, LANES, LANES)
    back = spread.transpose(0, 2, 1).reshape(5 * LANES, LANES)
    spread = np.concatenate([spread, np.zeros((1, LANES, LANES))])
    spread = spread.reshape(3, 2, LANES, LANES).transpose(0, 2, 1, 3)
    same = np.einsum("ab,dc,yz->daycbz", np.eye(boots), np.ones((deep, deep)), np.ones((grid_y, grid_y)))
    same = same.reshape(LANES, LANES)
    regroup = np.einsum("st,de,ab,yz->sdaybtez", *[np.eye(n) for n in (boots, deep, boots, grid_y)])
    regroup = regroup.reshape(boots * LANES, boots * LANES)
    if boots > 2:
        regroup = np.concatenate(np.split(regroup, boots // 2, axis=1), axis=0)
    y_high, y_low = split(field_y)
    x_high, x_low = split(base_x.T)
    parts = dict(
        base_x=base_x,
        base_xt2=np.concatenate([x_high, x_low], axis=1),
        field_y2=np.concatenate([y_high, y_low], axis=0),
        field_yt=field_y.T,
        station_y2=np.concatenate([part for b in station_y for part in split(b)]),
        spread=spread.reshape(3 * LANES, 2 * LANES),
        back=back,
        same=same,
        regroup=regroup,
        table=table.reshape(-1, 2 * LANES),
    )
    where = layout(grid_y, boots)
    whole = np.zeros((max(where.rows, 1 << 14), 2 * LANES), ml_dtypes.bfloat16)
    for name, (row, rows) in where.at.items():
        part = parts[name].astype(ml_dtypes.bfloat16)
        assert part.shape[0] == rows
        whole[row : row + rows, : part.shape[1]] = part
    return whole


def dot(a, b):
    return jnp.dot(a, b, preferred_element_type=F32)


def solve_kernel(
    grid_y,
    boots,
    slot_ref,
    comp_ref,
    station_ref,
    observed_ref,
    counts_ref,
    source,
    out_ref,
    const,
    copied,
    pick_x,
    pick_xt,
    pick_y,
    weights,
    data,
    pred,
    image,
    values,
    rows,
    table_wide,
    sums,
    spread_out,
    spec_q,
    spec_i,
    spec_f,
    spec_g,
    picked_in,
    models,
    residual,
    direction,
    penalty,
    applied,
):
    deep = LANES // grid_y // boots
    slabs = DEPTHS // deep
    where = layout(grid_y, boots)
    table_row, table_rows = where.at["table"]
    wide = 2 * boots * grid_y
    chunks = range(wide // LANES)
    bounds = [0, table_row, table_row + table_rows, where.rows]
    copies = [
        pltpu.make_async_copy(source.at[a:b], const.at[a:b], copied.at[i])
        for i, (a, b) in enumerate(zip(bounds[:-1], bounds[1:]))
    ]
    first_step = pl.program_id(0) == 0

    @pl.when(first_step)
    def _():
        for copy in copies:
            copy.start()

    def held(name, width=2 * LANES):
        row, count = where.at[name]
        return const[row : row + count, :width]

    def table(c, z, at):
        row = table_row + (c * (DEPTHS // 2) + z // 2) * GRID
        return const[row + at.start : row + at.stop, z % 2 * LANES : (z % 2 + 1) * LANES]

    stations = station_ref.shape[1]
    first = (slot_ref[0] * pl.num_programs(0) + pl.program_id(0)) * boots
    pieces = [(z, slice(row, row + ROWS)) for z in range(slabs) for row in range(0, GRID, ROWS)]

    rows[...] = jnp.zeros_like(rows)
    for b in range(boots):
        row = b * grid_y
        rows[row : row + 5, :] = observed_ref[...]
        count = counts_ref[pl.ds(first + b, 1), :].astype(F32)
        for c in range(5):
            rows[row + 8 + c : row + 9 + c, :] = count * comp_ref[c]
    rows[16:18, :] = station_ref[...].astype(F32)
    turned = jnp.transpose(rows[...])
    lane = lax.broadcasted_iota(jnp.int32, (1, LANES), 1)
    used = lane % grid_y < 5
    data[...] = jnp.where(used, turned, 0.0)
    weights[...] = jnp.where(used, pltpu.roll(turned, LANES - 8, 1), 0.0)
    values[...] = (weights[...] * data[...]).astype(BF)

    place_x = (lax.broadcasted_iota(jnp.int32, (GRID, stations), 0) == station_ref[0:1, :]).astype(F32).astype(BF)
    place_xt = (turned[:, 16:17] == lane.astype(F32)).astype(F32).astype(BF)
    place_yt = (turned[:, 17:18] == lane.astype(F32)).astype(F32)[:, :grid_y].astype(BF)

    @pl.when(first_step)
    def _():
        copies[0].wait()

    pick_xt[...] = dot(held("base_xt2", GRID), place_x).astype(BF)
    pick_x[...] = dot(place_xt, held("base_x")).astype(BF)
    station_y2 = held("station_y2", wide)
    for odd in range(2):
        high, low = [station_y2[(2 * odd + i) * grid_y : (2 * odd + i + 1) * grid_y] for i in range(2)]
        pick_y[:, odd * wide : (odd + 1) * wide] = dot(place_yt, high) + dot(place_yt, low)
    no_sum = jnp.zeros((8, LANES), F32)

    def trig(at, odd, chunk):
        lane = odd * wide + chunk * LANES
        return pick_y[at, lane : lane + LANES]

    def back_project(index):
        spread = held("spread")
        spread = jnp.concatenate([spread[i * LANES : (i + 1) * LANES] for i in range(3)], axis=1)
        spreads = dot(values[...], spread[:, : 5 * LANES])
        for row in range(0, stations, ROWS):
            at = slice(row, row + ROWS)
            for c, (_, odd_y) in enumerate(PARITY):
                e = spreads[at, c * LANES : (c + 1) * LANES]
                for chunk in chunks:
                    to = c * wide + chunk * LANES
                    spread_out[at, to : to + LANES] = (e * trig(at, odd_y, chunk)).astype(BF)
        spec = dot(pick_xt[...], spread_out[...])
        for c, (odd_x, _) in enumerate(PARITY):
            for hx in range(2):
                for chunk in chunks:
                    lane = c * wide + chunk * LANES
                    part = spec[hx * GRID : (hx + 1) * GRID, lane : lane + LANES]
                    spec_q[c, hx, chunk] = -part if odd_x * hx else part

        @pl.when(jnp.logical_and(first_step, index == 0))
        def _():
            copies[1].wait()
            copies[2].wait()
            for c in range(5):
                for z in range(DEPTHS):
                    table_wide[c, z] = table(c, z, slice(0, GRID)).astype(F32)

        for row in range(0, GRID, 16):
            at = slice(row, row + 16)
            for chunk in chunks:
                q = [[spec_q[c, hx, chunk, at, :] for hx in range(2)] for c in range(5)]
                for z in range(DEPTHS):
                    t = [table_wide[c, z, at, :] for c in range(5)]
                    lane = z * wide + chunk * LANES
                    for hx in range(2):
                        total = t[0] * q[0][hx]
                        for c in range(1, 5):
                            total = total + t[c] * q[c][hx ^ PARITY[c][0]]
                        spec_g[hx * GRID + row : hx * GRID + row + 16, lane : lane + LANES] = total.astype(BF)
        along_x = dot(held("base_x"), spec_g[...]).astype(BF)
        along_x = jnp.concatenate([along_x[:, 2 * z * LANES : (2 * z + 2) * LANES] for z in range(slabs)], axis=0)
        applied[...] = dot(along_x, held("field_yt", LANES)).reshape(slabs, GRID, LANES)

    def predict():
        r = residual[...].reshape(slabs * GRID, LANES).astype(BF)
        y = dot(jnp.concatenate([r, r], axis=1), held("field_y2")).astype(BF)
        y = jnp.concatenate([y[z * GRID : (z + 1) * GRID] for z in range(slabs)], axis=1)
        spec_f[...] = dot(held("base_xt2"), jnp.concatenate([y, y], axis=0)).astype(BF)

        for row in range(0, GRID, 16):
            at = [slice(hx * GRID + row, hx * GRID + row + 16) for hx in range(2)]
            for chunk in chunks:
                total = [[None] * 2 for _ in range(5)]
                for eight in range(0, DEPTHS, 8):
                    part = [[None] * 2 for _ in range(5)]
                    for z in range(eight, eight + 8):
                        lane = z * wide + chunk * LANES
                        f = [spec_f[at[hx], lane : lane + LANES] for hx in range(2)]
                        for c, (odd_x, _) in enumerate(PARITY):
                            t = table(c, z, at[0])
                            for hx in range(2):
                                term = t * f[hx ^ odd_x]
                                part[c][hx] = part[c][hx] + term if z > eight else term
                    for c in range(5):
                        for hx in range(2):
                            total[c][hx] = total[c][hx] + part[c][hx] if eight else part[c][hx]
                for c, (odd_x, _) in enumerate(PARITY):
                    lane = c * wide + chunk * LANES
                    for hx in range(2):
                        part = -total[c][hx] if odd_x * hx else total[c][hx]
                        spec_i[at[hx], lane : lane + LANES] = part

        picked = dot(pick_x[...], spec_i[...])
        for row in range(0, stations, ROWS):
            at = slice(row, row + ROWS)
            for c, (_, odd_y) in enumerate(PARITY):
                part = None
                for chunk in chunks:
                    lane = c * wide + chunk * LANES
                    term = picked[at, lane : lane + LANES] * trig(at, odd_y, chunk)
                    part = term if part is None else part + term
                picked_in[at, c * LANES : (c + 1) * LANES] = part.astype(BF)
        return dot(picked_in[...], held("back", LANES))

    def fold(a):
        return jnp.sum(a.reshape(a.shape[0] // 8, 8, LANES), axis=0)

    def totals_of(partials):
        rows_of = []
        for partial in partials:
            for _ in range(3):
                part = partial.astype(BF).astype(F32)
                rows_of.append(part)
                partial = partial - part
        if len(rows_of) % 2:
            rows_of.append(no_sum)
        sums = dot(jnp.concatenate(rows_of, axis=0).astype(BF), held("same", LANES))
        return [jnp.sum(sums[i * 24 : (i + 1) * 24], axis=0, keepdims=True) for i in range(len(partials))]

    def depth_weight(z):
        within = lax.broadcasted_iota(jnp.int32, (1, LANES), 1) // (boots * grid_y)
        depth = (within + z * deep).astype(F32) + 0.5 + station_height
        ratio = station_height / depth
        return ratio * ratio * ratio

    models[...] = jnp.zeros_like(models)
    direction[...] = jnp.zeros_like(direction)
    pred[...] = jnp.zeros_like(pred)
    image[...] = jnp.zeros_like(image)

    def round_of(index, carry):
        old_norm, old_step, old_curve = carry
        fresh = index % CG_STEPS == 0
        back_project(index)

        @pl.when(fresh)
        def _():
            norm = bend = no_sum
            for z, at in pieces:
                m = models[z, at]
                p = damping * depth_weight(z) / (m * m + focusing * focusing)
                penalty[z, at] = p
                r = applied[z, at] - p * m
                residual[z, at] = r
                square = r * r
                norm += fold(square)
                bend += fold(p * square)
            sums[0] = norm
            sums[1] = bend
            sums[2] = no_sum

        @pl.when(jnp.logical_not(fresh))
        def _():
            norm = bend = cross = no_sum
            for z, at in pieces:
                d = direction[z, at]
                p = penalty[z, at]
                pd = p * d
                r = residual[z, at] - old_step * (applied[z, at] + pd)
                residual[z, at] = r
                square = r * r
                norm += fold(square)
                bend += fold(p * square)
                cross += fold(pd * r)
            sums[0] = norm
            sums[1] = bend
            sums[2] = cross

        here = predict()
        weighted = weights[...] * here
        norm, bend, cross = totals_of(
            [sums[0], sums[1] + fold(weighted * here), sums[2] + fold(weighted * image[...])]
        )
        ratio = jnp.where(fresh, 0.0, norm / old_norm)
        curve = bend + ratio * (2.0 * cross + ratio * old_curve)
        step = norm / curve
        here = here + ratio * image[...]
        image[...] = here
        now = pred[...] + step * here
        pred[...] = now
        values[...] = (weights[...] * jnp.where(fresh, here, data[...] - now)).astype(BF)
        for z, at in pieces:
            d = residual[z, at] + ratio * direction[z, at]
            direction[z, at] = d
            models[z, at] += step * d
        return norm, step, curve

    one = jnp.ones((1, LANES), F32)
    lax.fori_loop(0, IRLS * CG_STEPS, round_of, (one, one, one))

    for group in range(slabs // boots):
        m = jnp.concatenate([models[group * boots + i].astype(BF) for i in range(boots)], axis=1)
        if boots > 1:
            regroup = held("regroup")
            regroup = [regroup[i * boots * LANES : (i + 1) * boots * LANES] for i in range(boots // 2)]
            m = dot(m, jnp.concatenate(regroup, axis=1)).astype(BF)
        for b in range(boots):
            out_ref[b * GRID : (b + 1) * GRID, group * LANES : (group + 1) * LANES] = (
                m[:, b * LANES : (b + 1) * LANES]
            )


def solve(slot, comp_weight, station_index, observed, counts, mine, grid_y):
    boots = min(mine, LANES // grid_y)
    slabs = DEPTHS * grid_y * boots // LANES
    stations = station_index.shape[1]
    const = jnp.asarray(constants(grid_y, boots))
    vmem = pltpu.VMEM
    whole = lambda a: pl.BlockSpec(a.shape, lambda i, n=a.ndim: (0,) * n)
    smem = pl.BlockSpec(memory_space=pltpu.SMEM)
    field = vmem((slabs, GRID, LANES), F32)
    at_stations = vmem((stations, LANES), F32)
    wide = 2 * boots * grid_y
    inputs = [station_index, observed, counts]
    return pl.pallas_call(
        functools.partial(solve_kernel, grid_y, boots),
        out_shape=jax.ShapeDtypeStruct((mine * GRID, DEPTHS * grid_y), BF),
        grid=(mine // boots,),
        in_specs=[smem, smem] + [whole(a) for a in inputs] + [pl.BlockSpec(memory_space=pl.ANY)],
        out_specs=pl.BlockSpec((boots * GRID, DEPTHS * grid_y), lambda i: (i, 0)),
        scratch_shapes=[
            vmem((layout(grid_y, boots).rows, 2 * LANES), BF),
            pltpu.SemaphoreType.DMA((3,)),
            vmem((stations, 2 * GRID), BF),
            vmem((2 * GRID, stations), BF),
            vmem((stations, 2 * wide), F32),
            at_stations,
            at_stations,
            at_stations,
            at_stations,
            vmem((stations, LANES), BF),
            vmem((LANES, stations), F32),
            vmem((5, DEPTHS, GRID, LANES), F32),
            vmem((3, 8, LANES), F32),
            vmem((stations, 5 * wide), BF),
            vmem((5, 2, wide // LANES, GRID, LANES), F32),
            vmem((2 * GRID, 5 * wide), BF),
            vmem((2 * GRID, slabs * 2 * LANES), BF),
            vmem((2 * GRID, slabs * 2 * LANES), BF),
            vmem((stations, 5 * LANES), BF),
            field,
            field,
            field,
            field,
            field,
        ],
        compiler_params=pltpu.CompilerParams(vmem_limit_bytes=56 * 1024 * 1024),
        cost_estimate=pl.CostEstimate(flops=10**10, bytes_accessed=10**7, transcendentals=0),
        name="solve",
    )(slot, comp_weight, *inputs, const)


def pick_kernel(grid_y, boots, count, models_ref, *refs):
    def pick_chunk(cell_ref, out_ref, at):
        cells = cell_ref[:, at]
        place = cells.astype(F32)
        wide = lambda row, rows: jnp.broadcast_to(row, (rows, CHUNK)).astype(BF)
        count_up = lambda rows: lax.broadcasted_iota(jnp.int32, (rows, CHUNK), 0).astype(F32).astype(BF)
        here_y = count_up(grid_y) == wide(place[1:2], grid_y)
        here_y = jnp.where(here_y, jnp.ones((grid_y, CHUNK), BF), jnp.zeros((grid_y, CHUNK), BF))
        z_row = wide(place[2:3], 16)
        none = jnp.zeros((16, CHUNK), BF)
        chosen = []
        for z in range(DEPTHS):
            here_z = z_row == jnp.full((16, CHUNK), z, BF)
            chosen += [jnp.where(here_z, here_y[i : i + 16], none) for i in range(0, grid_y, 16)]
        found = dot(models_ref[...], jnp.concatenate(chosen, axis=0)).astype(BF)
        at_x = count_up(GRID) == wide(place[0:1], GRID)
        parts = []
        for b in range(boots):
            part = jnp.where(at_x, found[b * GRID : (b + 1) * GRID], jnp.zeros((GRID, CHUNK), BF))
            while part.shape[0] > 16:
                half = part.shape[0] // 2
                part = part[:half] + part[half:]
            parts.append(jnp.sum(part.astype(F32), axis=0, keepdims=True))
        out_ref[:, at] = jnp.concatenate(parts, axis=0).astype(BF)

    @pl.loop(0, refs[0].shape[1] // CHUNK)
    def _(step):
        at = pl.ds(pl.multiple_of(step * CHUNK, CHUNK), CHUNK)
        for cell_ref, out_ref in zip(refs[:count], refs[count:]):
            pick_chunk(cell_ref, out_ref, at)


def pick(models, cells, grid_y):
    boots = models.shape[0] // GRID
    count = cells[0].shape[1]
    vmem = pl.BlockSpec(memory_space=pltpu.VMEM)
    return pl.pallas_call(
        functools.partial(pick_kernel, grid_y, boots, len(cells)),
        out_shape=[jax.ShapeDtypeStruct((boots, count), BF)] * len(cells),
        in_specs=[vmem] * (1 + len(cells)),
        out_specs=[vmem] * len(cells),
        compiler_params=pltpu.CompilerParams(vmem_limit_bytes=40 * 1024 * 1024),
        cost_estimate=pl.CostEstimate(
            flops=2 * models.size * count * len(cells), bytes_accessed=10**6, transcendentals=0
        ),
        name="pick",
    )(models, *cells)


def local(wide, cell_index, station_index, observed, comp_weight, counts):
    boots = counts.shape[0]
    grid_y = cell_index.shape[1] * wide // (GRID * DEPTHS)
    team = TEAM if wide % TEAM == 0 and boots % TEAM == 0 else 1
    while 4 * boots * grid_y < team * 2 * LANES:
        team //= 2
    slot = lax.axis_index("wide").astype(jnp.int32) & (team - 1)

    def swap(a, k):
        return lax.ppermute(a, "wide", [(i, i ^ k) for i in range(wide)])

    theirs = [swap(cell_index, k) for k in range(1, team)]
    models = solve(slot.reshape(1), comp_weight, station_index, observed, counts, boots // team, grid_y)
    far = [swap(a, k + 2) for k, a in enumerate(pick(models, theirs[1:], grid_y))] if team > 2 else []
    near = pick(models, [cell_index] + theirs[:1], grid_y)
    got = [near[0]] + [swap(a, 1) for a in near[1:]] + far
    blocks = []
    for member in range(team):
        block = got[member]
        for other in range(1, team):
            block = jnp.where(slot == other, got[member ^ other], block)
        blocks.append(block.astype(F32))
    return jnp.concatenate(blocks, axis=0)


def solution(mesh):
    in_specs = (P(None, "wide"), P(None, "groups"), P(None, "groups"), P(), P("groups", None))
    out_specs = P("groups", "wide")
    fn = functools.partial(local, mesh.shape["wide"])
    return jax.shard_map(fn, mesh=mesh, in_specs=in_specs, out_specs=out_specs, check_vma=False)
```

```python
import functools

import jax
import jax.numpy as jnp
import ml_dtypes
import numpy as np
from jax import lax
from jax.experimental import pallas as pl
from jax.experimental.pallas import tpu as pltpu
from jax.sharding import PartitionSpec as P

IRLS = 2
CG_STEPS = 2
GRID = 128
DEPTHS = 16
LANES = 128
TEAM = 4
CHUNK = 2048
ROWS = 32

station_height = 2.0
focusing = 0.1
damping = 0.0002

PARITY = ((0, 0), (1, 1), (1, 0), (0, 0), (0, 1))
BF = jnp.bfloat16
F32 = jnp.float32


def offset_table(grid_y):
    one = np.float32
    dx = np.arange(GRID, dtype=one)[:, None, None]
    dy = np.arange(grid_y, dtype=one)[None, :, None]
    dz = (np.arange(DEPTHS, dtype=one) + one(0.5) + one(station_height))[None, None, :]
    radius2 = dx * dx + dy * dy + dz * dz
    strength = one(1) / (radius2 * radius2 * np.sqrt(radius2))
    three = one(3)
    kinds = [
        (three * dx * dx - radius2) * strength,
        three * dx * dy * strength,
        three * dx * dz * strength,
        (three * dy * dy - radius2) * strength,
        three * dy * dz * strength,
    ]
    return [k.astype(ml_dtypes.bfloat16).astype(np.float64) for k in kinds]


def angles(size):
    return 2 * np.pi * np.outer(np.arange(size), np.arange(size) + 0.5) / (2 * size)


def basis(size):
    return np.concatenate([np.cos(angles(size)), np.sin(angles(size))], axis=1)


def spectrum(values, odd, size):
    if odd:
        trig = 2 * np.sin(angles(size))
    else:
        trig = np.cos(angles(size)) * np.where(np.arange(size) == 0, 1, 2)[:, None]
    return np.tensordot(trig.T / size, values, axes=(1, 0))


def split(matrix):
    high = matrix.astype(ml_dtypes.bfloat16)
    low = (matrix - high.astype(np.float64)).astype(ml_dtypes.bfloat16)
    return high, low


class Layout:
    def __init__(self, parts):
        self.at = {}
        row = 0
        for name, rows in parts:
            self.at[name] = (row, rows)
            row += rows
        self.rows = row


def layout(grid_y, boots):
    return Layout(
        [
            ("base_x", GRID),
            ("base_xt2", 2 * GRID),
            ("station_y2", 4 * grid_y),
            ("spread", 3 * LANES),
            ("table", 5 * DEPTHS // 2 * GRID),
            ("field_y2", 2 * LANES),
            ("field_yt", 2 * LANES),
            ("back", 5 * LANES),
            ("same", LANES),
            ("regroup", boots * LANES * max(1, boots // 2)),
        ]
    )


@functools.lru_cache(maxsize=None)
def constants(grid_y, boots):
    deep = LANES // grid_y // boots
    copies = LANES // grid_y
    table = []
    for values, (odd_x, odd_y) in zip(offset_table(grid_y), PARITY):
        t = spectrum(values, odd_x, GRID)
        t = np.moveaxis(spectrum(np.moveaxis(t, 1, 0), odd_y, grid_y), 0, 1)
        table.append(np.tile(np.moveaxis(t, 2, 0), (1, 1, copies)))
    table = np.stack(table).reshape(5, DEPTHS // 2, 2, GRID, LANES).transpose(0, 1, 3, 2, 4)

    base_x = basis(GRID)
    base_y = basis(grid_y).reshape(grid_y, 2, grid_y)
    field_y = np.einsum("de,ab,yhl->dayehbl", np.eye(deep), np.eye(boots), base_y).reshape(LANES, 2 * LANES)
    odd_y = np.stack([-base_y[:, 1], base_y[:, 0]], axis=1)
    station_y = [np.tile(b[:, :, None], (1, 1, boots, 1)).reshape(grid_y, -1) for b in (base_y, odd_y)]
    spread = np.zeros((5, deep, boots, grid_y, copies, grid_y))
    for c in range(5):
        for copy in range(copies):
            spread[c, 0, copy % boots, c, copy, :] = 1
    spread = spread.reshape(5, LANES, LANES)
    back = spread.transpose(0, 2, 1).reshape(5 * LANES, LANES)
    spread = np.concatenate([spread, np.zeros((1, LANES, LANES))])
    spread = spread.reshape(3, 2, LANES, LANES).transpose(0, 2, 1, 3)
    same = np.einsum("ab,dc,yz->daycbz", np.eye(boots), np.ones((deep, deep)), np.ones((grid_y, grid_y)))
    same = same.reshape(LANES, LANES)
    regroup = np.einsum("st,de,ab,yz->sdaybtez", *[np.eye(n) for n in (boots, deep, boots, grid_y)])
    regroup = regroup.reshape(boots * LANES, boots * LANES)
    if boots > 2:
        regroup = np.concatenate(np.split(regroup, boots // 2, axis=1), axis=0)
    y_high, y_low = split(field_y)
    x_high, x_low = split(base_x.T)
    parts = dict(
        base_x=base_x,
        base_xt2=np.concatenate([x_high, x_low], axis=1),
        field_y2=np.concatenate([y_high, y_low], axis=0),
        field_yt=field_y.T,
        station_y2=np.concatenate([part for b in station_y for part in split(b)]),
        spread=spread.reshape(3 * LANES, 2 * LANES),
        back=back,
        same=same,
        regroup=regroup,
        table=table.reshape(-1, 2 * LANES),
    )
    where = layout(grid_y, boots)
    whole = np.zeros((max(where.rows, 1 << 14), 2 * LANES), ml_dtypes.bfloat16)
    for name, (row, rows) in where.at.items():
        part = parts[name].astype(ml_dtypes.bfloat16)
        assert part.shape[0] == rows
        whole[row : row + rows, : part.shape[1]] = part
    return whole


def dot(a, b):
    return jnp.dot(a, b, preferred_element_type=F32)


def solve_kernel(
    grid_y,
    boots,
    slot_ref,
    comp_ref,
    station_ref,
    observed_ref,
    counts_ref,
    source,
    out_ref,
    const,
    copied,
    pick_x,
    pick_xt,
    pick_y,
    weights,
    data,
    pred,
    image,
    values,
    rows,
    table_wide,
    spread_out,
    spec_q,
    spec_i,
    spec_f,
    spec_g,
    picked_in,
    models,
    residual,
    direction,
    penalty,
):
    deep = LANES // grid_y // boots
    slabs = DEPTHS // deep
    where = layout(grid_y, boots)
    table_row, table_rows = where.at["table"]
    wide = 2 * boots * grid_y
    chunks = range(wide // LANES)
    bounds = [0, table_row, table_row + table_rows, where.rows]
    copies = [
        pltpu.make_async_copy(source.at[a:b], const.at[a:b], copied.at[i])
        for i, (a, b) in enumerate(zip(bounds[:-1], bounds[1:]))
    ]
    first_step = pl.program_id(0) == 0

    @pl.when(first_step)
    def _():
        for copy in copies:
            copy.start()

    def held(name, width=2 * LANES):
        row, count = where.at[name]
        return const[row : row + count, :width]

    def table(c, z, at):
        row = table_row + (c * (DEPTHS // 2) + z // 2) * GRID
        return const[row + at.start : row + at.stop, z % 2 * LANES : (z % 2 + 1) * LANES]

    stations = station_ref.shape[1]
    first = (slot_ref[0] * pl.num_programs(0) + pl.program_id(0)) * boots
    halves = [range(half, half + slabs // 2) for half in (0, slabs // 2)]
    half_lanes = slabs // 2 * 2 * LANES

    def pieces(half):
        return [(slab, slice(row, row + ROWS)) for slab in half for row in range(0, GRID, ROWS)]


    rows[...] = jnp.zeros_like(rows)
    for b in range(boots):
        row = b * grid_y
        rows[row : row + 5, :] = observed_ref[...]
        count = counts_ref[pl.ds(first + b, 1), :].astype(F32)
        for c in range(5):
            rows[row + 8 + c : row + 9 + c, :] = count * comp_ref[c]
    rows[16:18, :] = station_ref[...].astype(F32)
    turned = jnp.transpose(rows[...])
    lane = lax.broadcasted_iota(jnp.int32, (1, LANES), 1)
    used = lane % grid_y < 5
    data[...] = jnp.where(used, turned, 0.0)
    weights[...] = jnp.where(used, pltpu.roll(turned, LANES - 8, 1), 0.0)
    values[...] = (weights[...] * data[...]).astype(BF)

    place_x = (lax.broadcasted_iota(jnp.int32, (GRID, stations), 0) == station_ref[0:1, :]).astype(F32).astype(BF)
    place_xt = (turned[:, 16:17] == lane.astype(F32)).astype(F32).astype(BF)
    place_yt = (turned[:, 17:18] == lane.astype(F32)).astype(F32)[:, :grid_y].astype(BF)

    @pl.when(first_step)
    def _():
        copies[0].wait()

    pick_xt[...] = dot(held("base_xt2", GRID), place_x).astype(BF)
    pick_x[...] = dot(place_xt, held("base_x")).astype(BF)
    station_y2 = held("station_y2", wide)
    for odd in range(2):
        high, low = [station_y2[(2 * odd + i) * grid_y : (2 * odd + i + 1) * grid_y] for i in range(2)]
        pick_y[:, odd * wide : (odd + 1) * wide] = dot(place_yt, high) + dot(place_yt, low)
    no_sum = jnp.zeros((8, LANES), F32)

    @pl.when(first_step)
    def _():
        copies[1].wait()
        copies[2].wait()
        for c in range(5):
            for z in range(DEPTHS):
                table_wide[c, z] = table(c, z, slice(0, GRID)).astype(F32)

    def trig(at, odd, chunk):
        lane = odd * wide + chunk * LANES
        return pick_y[at, lane : lane + LANES]

    def back_project(receive):
        spread = held("spread")
        spread = jnp.concatenate([spread[i * LANES : (i + 1) * LANES] for i in range(3)], axis=1)
        spreads = dot(values[...], spread[:, : 5 * LANES])
        for row in range(0, stations, ROWS):
            at = slice(row, row + ROWS)
            for c, (_, odd_y) in enumerate(PARITY):
                e = spreads[at, c * LANES : (c + 1) * LANES]
                for chunk in chunks:
                    to = c * wide + chunk * LANES
                    spread_out[at, to : to + LANES] = (e * trig(at, odd_y, chunk)).astype(BF)
        spec = dot(pick_xt[...], spread_out[...])
        for c, (odd_x, _) in enumerate(PARITY):
            for hx in range(2):
                for chunk in chunks:
                    lane = c * wide + chunk * LANES
                    part = spec[hx * GRID : (hx + 1) * GRID, lane : lane + LANES]
                    spec_q[c, hx, chunk] = -part if odd_x * hx else part

        for half in halves:
            for row in range(0, GRID, 16):
                at = slice(row, row + 16)
                for chunk in chunks:
                    q = [[spec_q[c, hx, chunk, at, :] for hx in range(2)] for c in range(5)]
                    for z in range(half.start * deep, half.stop * deep):
                        t = [table_wide[c, z, at, :] for c in range(5)]
                        lane = z * wide + chunk * LANES
                        for hx in range(2):
                            total = t[0] * q[0][hx]
                            for c in range(1, 5):
                                total = total + t[c] * q[c][hx ^ PARITY[c][0]]
                            spec_g[hx * GRID + row : hx * GRID + row + 16, lane : lane + LANES] = total.astype(BF)
            lane = half.start * 2 * LANES
            along_x = dot(held("base_x"), spec_g[:, lane : lane + half_lanes]).astype(BF)
            along_x = [along_x[:, lane : lane + 2 * LANES] for lane in range(0, half_lanes, 2 * LANES)]
            receive(half, dot(jnp.concatenate(along_x, axis=0), held("field_yt", LANES)))

    def predict():
        for half in halves:
            r = residual[half.start : half.stop].reshape(len(half) * GRID, LANES).astype(BF)
            y = dot(jnp.concatenate([r, r], axis=1), held("field_y2")).astype(BF)
            y = jnp.concatenate([y[i * GRID : (i + 1) * GRID] for i in range(len(half))], axis=1)
            lane = half.start * 2 * LANES
            spec_f[:, lane : lane + half_lanes] = dot(held("base_xt2"), jnp.concatenate([y, y], axis=0)).astype(BF)

            for row in range(0, GRID, 16):
                at = [slice(hx * GRID + row, hx * GRID + row + 16) for hx in range(2)]
                for chunk in chunks:
                    total = [[None] * 2 for _ in range(5)]
                    for z in range(half.start * deep, half.stop * deep):
                        lane = z * wide + chunk * LANES
                        f = [spec_f[at[hx], lane : lane + LANES] for hx in range(2)]
                        for c, (odd_x, _) in enumerate(PARITY):
                            t = table(c, z, at[0])
                            for hx in range(2):
                                term = t * f[hx ^ odd_x]
                                total[c][hx] = term if total[c][hx] is None else total[c][hx] + term
                    for c, (odd_x, _) in enumerate(PARITY):
                        lane = c * wide + chunk * LANES
                        for hx in range(2):
                            part = total[c][hx]
                            if half is not halves[0]:
                                part = part + spec_i[at[hx], lane : lane + LANES]
                                part = -part if odd_x * hx else part
                            spec_i[at[hx], lane : lane + LANES] = part

        picked = dot(pick_x[...], spec_i[...])
        for row in range(0, stations, ROWS):
            at = slice(row, row + ROWS)
            for c, (_, odd_y) in enumerate(PARITY):
                part = None
                for chunk in chunks:
                    lane = c * wide + chunk * LANES
                    term = picked[at, lane : lane + LANES] * trig(at, odd_y, chunk)
                    part = term if part is None else part + term
                picked_in[at, c * LANES : (c + 1) * LANES] = part.astype(BF)
        return dot(picked_in[...], held("back", LANES))

    def fold(a):
        return jnp.sum(a.reshape(a.shape[0] // 8, 8, LANES), axis=0)

    def totals_of(partials):
        rows_of = []
        for partial in partials:
            for _ in range(3):
                part = partial.astype(BF).astype(F32)
                rows_of.append(part)
                partial = partial - part
        if len(rows_of) % 2:
            rows_of.append(no_sum)
        sums = dot(jnp.concatenate(rows_of, axis=0).astype(BF), held("same", LANES))
        return [jnp.sum(sums[i * 24 : (i + 1) * 24], axis=0, keepdims=True) for i in range(len(partials))]

    def depth_weight(z):
        within = lax.broadcasted_iota(jnp.int32, (1, LANES), 1) // (boots * grid_y)
        depth = (within + z * deep).astype(F32) + 0.5 + station_height
        ratio = station_height / depth
        return ratio * ratio * ratio

    models[...] = jnp.zeros_like(models)
    pred[...] = jnp.zeros_like(pred)

    def round_of(fresh, carry):
        old_norm, old_step, old_curve = carry
        sums = [no_sum] * 3

        def receive(half, applied):
            norm, bend, cross = sums
            for slab, at in pieces(half):
                row = (slab - half.start) * GRID + at.start
                g = applied[row : row + ROWS]
                if fresh:
                    m = models[slab, at]
                    p = damping * depth_weight(slab) / (m * m + focusing * focusing)
                    penalty[slab, at] = p
                    r = g - p * m
                else:
                    p = penalty[slab, at]
                    pd = p * direction[slab, at]
                    r = residual[slab, at] - old_step * (g + pd)
                    cross += fold(pd * r)
                residual[slab, at] = r
                square = r * r
                norm += fold(square)
                bend += fold(p * square)
            sums[:] = [norm, bend, cross]

        back_project(receive)
        here = predict()
        weighted = weights[...] * here
        norm, bend, cross = sums
        if fresh:
            norm, curve = totals_of([norm, bend + fold(weighted * here)])
        else:
            norm, bend, cross = totals_of(
                [norm, bend + fold(weighted * here), cross + fold(weighted * image[...])]
            )
            ratio = norm / old_norm
            curve = bend + ratio * (2.0 * cross + ratio * old_curve)
            here = here + ratio * image[...]
        step = norm / curve
        now = pred[...] + step * here
        pred[...] = now
        if fresh:
            image[...] = here
            values[...] = (weights[...] * here).astype(BF)
        else:
            values[...] = (weights[...] * (data[...] - now)).astype(BF)
        for half in halves:
            for slab, at in pieces(half):
                d = residual[slab, at]
                if not fresh:
                    d = d + ratio * direction[slab, at]
                direction[slab, at] = d
                models[slab, at] += step * d
        return norm, step, curve

    def outer(_, carry):
        for inner in range(CG_STEPS):
            carry = round_of(inner == 0, carry)
        return carry

    one = jnp.ones((1, LANES), F32)
    lax.fori_loop(0, IRLS, outer, (one, one, one))

    for group in range(slabs // boots):
        m = jnp.concatenate([models[group * boots + i].astype(BF) for i in range(boots)], axis=1)
        if boots > 1:
            regroup = held("regroup")
            regroup = [regroup[i * boots * LANES : (i + 1) * boots * LANES] for i in range(boots // 2)]
            m = dot(m, jnp.concatenate(regroup, axis=1)).astype(BF)
        for b in range(boots):
            out_ref[b * GRID : (b + 1) * GRID, group * LANES : (group + 1) * LANES] = (
                m[:, b * LANES : (b + 1) * LANES]
            )


def solve(slot, comp_weight, station_index, observed, counts, mine, grid_y):
    boots = min(mine, LANES // grid_y)
    slabs = DEPTHS * grid_y * boots // LANES
    stations = station_index.shape[1]
    const = jnp.asarray(constants(grid_y, boots))
    vmem = pltpu.VMEM
    whole = lambda a: pl.BlockSpec(a.shape, lambda i, n=a.ndim: (0,) * n)
    smem = pl.BlockSpec(memory_space=pltpu.SMEM)
    field = vmem((slabs, GRID, LANES), F32)
    at_stations = vmem((stations, LANES), F32)
    wide = 2 * boots * grid_y
    inputs = [station_index, observed, counts]
    return pl.pallas_call(
        functools.partial(solve_kernel, grid_y, boots),
        out_shape=jax.ShapeDtypeStruct((mine * GRID, DEPTHS * grid_y), BF),
        grid=(mine // boots,),
        in_specs=[smem, smem] + [whole(a) for a in inputs] + [pl.BlockSpec(memory_space=pl.ANY)],
        out_specs=pl.BlockSpec((boots * GRID, DEPTHS * grid_y), lambda i: (i, 0)),
        scratch_shapes=[
            vmem((layout(grid_y, boots).rows, 2 * LANES), BF),
            pltpu.SemaphoreType.DMA((3,)),
            vmem((stations, 2 * GRID), BF),
            vmem((2 * GRID, stations), BF),
            vmem((stations, 2 * wide), F32),
            at_stations,
            at_stations,
            at_stations,
            at_stations,
            vmem((stations, LANES), BF),
            vmem((LANES, stations), F32),
            vmem((5, DEPTHS, GRID, LANES), F32),
            vmem((stations, 5 * wide), BF),
            vmem((5, 2, wide // LANES, GRID, LANES), F32),
            vmem((2 * GRID, 5 * wide), BF),
            vmem((2 * GRID, slabs * 2 * LANES), BF),
            vmem((2 * GRID, slabs * 2 * LANES), BF),
            vmem((stations, 5 * LANES), BF),
            field,
            field,
            field,
            field,
        ],
        compiler_params=pltpu.CompilerParams(vmem_limit_bytes=56 * 1024 * 1024),
        cost_estimate=pl.CostEstimate(flops=10**10, bytes_accessed=10**7, transcendentals=0),
        name="solve",
    )(slot, comp_weight, *inputs, const)


def pick_kernel(grid_y, boots, count, models_ref, *refs):
    def pick_chunk(cell_ref, out_ref, at):
        cells = cell_ref[:, at]
        place = cells.astype(F32)
        wide = lambda row, rows: jnp.broadcast_to(row, (rows, CHUNK)).astype(BF)
        count_up = lambda rows: lax.broadcasted_iota(jnp.int32, (rows, CHUNK), 0).astype(F32).astype(BF)
        here_y = count_up(grid_y) == wide(place[1:2], grid_y)
        here_y = jnp.where(here_y, jnp.ones((grid_y, CHUNK), BF), jnp.zeros((grid_y, CHUNK), BF))
        z_row = wide(place[2:3], 16)
        none = jnp.zeros((16, CHUNK), BF)
        chosen = []
        for z in range(DEPTHS):
            here_z = z_row == jnp.full((16, CHUNK), z, BF)
            chosen += [jnp.where(here_z, here_y[i : i + 16], none) for i in range(0, grid_y, 16)]
        found = dot(models_ref[...], jnp.concatenate(chosen, axis=0)).astype(BF)
        at_x = count_up(GRID) == wide(place[0:1], GRID)
        parts = []
        for b in range(boots):
            part = jnp.where(at_x, found[b * GRID : (b + 1) * GRID], jnp.zeros((GRID, CHUNK), BF))
            while part.shape[0] > 16:
                half = part.shape[0] // 2
                part = part[:half] + part[half:]
            parts.append(jnp.sum(part.astype(F32), axis=0, keepdims=True))
        out_ref[:, at] = jnp.concatenate(parts, axis=0).astype(BF)

    @pl.loop(0, refs[0].shape[1] // CHUNK)
    def _(step):
        at = pl.ds(pl.multiple_of(step * CHUNK, CHUNK), CHUNK)
        for cell_ref, out_ref in zip(refs[:count], refs[count:]):
            pick_chunk(cell_ref, out_ref, at)


def pick(models, cells, grid_y):
    boots = models.shape[0] // GRID
    count = cells[0].shape[1]
    vmem = pl.BlockSpec(memory_space=pltpu.VMEM)
    return pl.pallas_call(
        functools.partial(pick_kernel, grid_y, boots, len(cells)),
        out_shape=[jax.ShapeDtypeStruct((boots, count), BF)] * len(cells),
        in_specs=[vmem] * (1 + len(cells)),
        out_specs=[vmem] * len(cells),
        compiler_params=pltpu.CompilerParams(vmem_limit_bytes=40 * 1024 * 1024),
        cost_estimate=pl.CostEstimate(
            flops=2 * models.size * count * len(cells), bytes_accessed=10**6, transcendentals=0
        ),
        name="pick",
    )(models, *cells)


def local(wide, cell_index, station_index, observed, comp_weight, counts):
    boots = counts.shape[0]
    grid_y = cell_index.shape[1] * wide // (GRID * DEPTHS)
    team = TEAM if wide % TEAM == 0 and boots % TEAM == 0 else 1
    while 4 * boots * grid_y < team * 2 * LANES:
        team //= 2
    slot = lax.axis_index("wide").astype(jnp.int32) & (team - 1)

    def swap(a, k):
        return lax.ppermute(a, "wide", [(i, i ^ k) for i in range(wide)])

    theirs = [swap(cell_index, k) for k in range(1, team)]
    models = solve(slot.reshape(1), comp_weight, station_index, observed, counts, boots // team, grid_y)
    far = [swap(a, k + 2) for k, a in enumerate(pick(models, theirs[1:], grid_y))] if team > 2 else []
    near = pick(models, [cell_index] + theirs[:1], grid_y)
    got = [near[0]] + [swap(a, 1) for a in near[1:]] + far
    blocks = []
    for member in range(team):
        block = got[member]
        for other in range(1, team):
            block = jnp.where(slot == other, got[member ^ other], block)
        blocks.append(block.astype(F32))
    return jnp.concatenate(blocks, axis=0)


def solution(mesh):
    in_specs = (P(None, "wide"), P(None, "groups"), P(None, "groups"), P(), P("groups", None))
    out_specs = P("groups", "wide")
    fn = functools.partial(local, mesh.shape["wide"])
    return jax.shard_map(fn, mesh=mesh, in_specs=in_specs, out_specs=out_specs, check_vma=False)
```

```python
import functools

import jax
import jax.numpy as jnp
import ml_dtypes
import numpy as np
from jax import lax
from jax.experimental import pallas as pl
from jax.experimental.pallas import tpu as pltpu
from jax.sharding import PartitionSpec as P

IRLS = 2
CG_STEPS = 2
GRID = 128
DEPTHS = 16
LANES = 128
TEAM = 4
CHUNK = 2048
ROWS = 32

station_height = 2.0
focusing = 0.1
damping = 0.0002

PARITY = ((0, 0), (1, 1), (1, 0), (0, 0), (0, 1))
BF = jnp.bfloat16
F32 = jnp.float32


def offset_table(grid_y):
    one = np.float32
    dx = np.arange(GRID, dtype=one)[:, None, None]
    dy = np.arange(grid_y, dtype=one)[None, :, None]
    dz = (np.arange(DEPTHS, dtype=one) + one(0.5) + one(station_height))[None, None, :]
    radius2 = dx * dx + dy * dy + dz * dz
    strength = one(1) / (radius2 * radius2 * np.sqrt(radius2))
    three = one(3)
    kinds = [
        (three * dx * dx - radius2) * strength,
        three * dx * dy * strength,
        three * dx * dz * strength,
        (three * dy * dy - radius2) * strength,
        three * dy * dz * strength,
    ]
    return [k.astype(ml_dtypes.bfloat16).astype(np.float64) for k in kinds]


def angles(size):
    return 2 * np.pi * np.outer(np.arange(size), np.arange(size) + 0.5) / (2 * size)


def basis(size):
    return np.concatenate([np.cos(angles(size)), np.sin(angles(size))], axis=1)


def spectrum(values, odd, size):
    if odd:
        trig = 2 * np.sin(angles(size))
    else:
        trig = np.cos(angles(size)) * np.where(np.arange(size) == 0, 1, 2)[:, None]
    return np.tensordot(trig.T / size, values, axes=(1, 0))


def split(matrix):
    high = matrix.astype(ml_dtypes.bfloat16)
    low = (matrix - high.astype(np.float64)).astype(ml_dtypes.bfloat16)
    return high, low


class Layout:
    def __init__(self, parts):
        self.at = {}
        row = 0
        for name, rows in parts:
            self.at[name] = (row, rows)
            row += rows
        self.rows = row


def layout(grid_y, boots):
    return Layout(
        [
            ("base_x", GRID),
            ("base_xt2", 2 * GRID),
            ("station_y2", 4 * grid_y),
            ("spread", 3 * LANES),
            ("table", 5 * DEPTHS // 2 * GRID),
            ("field_y2", 2 * LANES),
            ("field_yt", 2 * LANES),
            ("back", 5 * LANES),
            ("same", LANES),
            ("regroup", boots * LANES * max(1, boots // 2)),
        ]
    )


@functools.lru_cache(maxsize=None)
def constants(grid_y, boots):
    deep = LANES // grid_y // boots
    copies = LANES // grid_y
    table = []
    for values, (odd_x, odd_y) in zip(offset_table(grid_y), PARITY):
        t = spectrum(values, odd_x, GRID)
        t = np.moveaxis(spectrum(np.moveaxis(t, 1, 0), odd_y, grid_y), 0, 1)
        table.append(np.tile(np.moveaxis(t, 2, 0), (1, 1, copies)))
    table = np.stack(table).reshape(5, DEPTHS // 2, 2, GRID, LANES).transpose(0, 1, 3, 2, 4)

    base_x = basis(GRID)
    base_y = basis(grid_y).reshape(grid_y, 2, grid_y)
    field_y = np.einsum("de,ab,yhl->dayehbl", np.eye(deep), np.eye(boots), base_y).reshape(LANES, 2 * LANES)
    odd_y = np.stack([-base_y[:, 1], base_y[:, 0]], axis=1)
    station_y = [np.tile(b[:, :, None], (1, 1, boots, 1)).reshape(grid_y, -1) for b in (base_y, odd_y)]
    spread = np.zeros((5, deep, boots, grid_y, copies, grid_y))
    for c in range(5):
        for copy in range(copies):
            spread[c, 0, copy % boots, c, copy, :] = 1
    spread = spread.reshape(5, LANES, LANES)
    back = spread.transpose(0, 2, 1).reshape(5 * LANES, LANES)
    spread = np.concatenate([spread, np.zeros((1, LANES, LANES))])
    spread = spread.reshape(3, 2, LANES, LANES).transpose(0, 2, 1, 3)
    same = np.einsum("ab,dc,yz->daycbz", np.eye(boots), np.ones((deep, deep)), np.ones((grid_y, grid_y)))
    same = same.reshape(LANES, LANES)
    regroup = np.einsum("st,de,ab,yz->sdaybtez", *[np.eye(n) for n in (boots, deep, boots, grid_y)])
    regroup = regroup.reshape(boots * LANES, boots * LANES)
    if boots > 2:
        regroup = np.concatenate(np.split(regroup, boots // 2, axis=1), axis=0)
    y_high, y_low = split(field_y)
    x_high, x_low = split(base_x.T)
    parts = dict(
        base_x=base_x,
        base_xt2=np.concatenate([x_high, x_low], axis=1),
        field_y2=np.concatenate([y_high, y_low], axis=0),
        field_yt=field_y.T,
        station_y2=np.concatenate([part for b in station_y for part in split(b)]),
        spread=spread.reshape(3 * LANES, 2 * LANES),
        back=back,
        same=same,
        regroup=regroup,
        table=table.reshape(-1, 2 * LANES),
    )
    where = layout(grid_y, boots)
    whole = np.zeros((max(where.rows, 1 << 14), 2 * LANES), ml_dtypes.bfloat16)
    for name, (row, rows) in where.at.items():
        part = parts[name].astype(ml_dtypes.bfloat16)
        assert part.shape[0] == rows
        whole[row : row + rows, : part.shape[1]] = part
    return whole


def dot(a, b):
    return jnp.dot(a, b, preferred_element_type=F32)


def solve_kernel(
    grid_y,
    boots,
    steps,
    slot_ref,
    comp_ref,
    station_ref,
    observed_ref,
    counts_ref,
    source,
    out_ref,
    const,
    copied,
    pick_x,
    pick_xt,
    pick_y,
    weights,
    data,
    pred,
    image,
    values,
    rows,
    table_wide,
    spread_out,
    spec_q,
    spec_i,
    spec_f,
    spec_g,
    picked_in,
    models,
    residual,
    direction,
    penalty,
):
    deep = LANES // grid_y // boots
    slabs = DEPTHS // deep
    where = layout(grid_y, boots)
    table_row, table_rows = where.at["table"]
    wide = 2 * boots * grid_y
    chunks = range(wide // LANES)
    bounds = [0, table_row, table_row + table_rows, where.rows]
    copies = [
        pltpu.make_async_copy(source.at[a:b], const.at[a:b], copied.at[i])
        for i, (a, b) in enumerate(zip(bounds[:-1], bounds[1:]))
    ]

    def once(f):
        if steps == 1:
            f()
        else:
            pl.when(pl.program_id(0) == 0)(f)

    @once
    def _():
        for copy in copies:
            copy.start()

    def held(name, width=2 * LANES):
        row, count = where.at[name]
        return const[row : row + count, :width]

    def table(c, z, at):
        row = table_row + (c * (DEPTHS // 2) + z // 2) * GRID
        return const[row + at.start : row + at.stop, z % 2 * LANES : (z % 2 + 1) * LANES]

    stations = station_ref.shape[1]
    first = (slot_ref[0] * pl.num_programs(0) + pl.program_id(0)) * boots
    halves = [range(half, half + slabs // 2) for half in (0, slabs // 2)]
    half_lanes = slabs // 2 * 2 * LANES

    def pieces(half):
        return [(slab, slice(row, row + ROWS)) for slab in half for row in range(0, GRID, ROWS)]


    rows[...] = jnp.zeros_like(rows)
    for b in range(boots):
        row = b * grid_y
        rows[row : row + 5, :] = observed_ref[...]
        count = counts_ref[pl.ds(first + b, 1), :].astype(F32)
        for c in range(5):
            rows[row + 8 + c : row + 9 + c, :] = count * comp_ref[c]
    rows[16:18, :] = station_ref[...].astype(F32)
    turned = jnp.transpose(rows[...])
    lane = lax.broadcasted_iota(jnp.int32, (1, LANES), 1)
    used = lane % grid_y < 5
    data[...] = jnp.where(used, turned, 0.0)
    weights[...] = jnp.where(used, pltpu.roll(turned, LANES - 8, 1), 0.0)
    values[...] = (weights[...] * data[...]).astype(BF)

    place_x = (lax.broadcasted_iota(jnp.int32, (GRID, stations), 0) == station_ref[0:1, :]).astype(F32).astype(BF)
    place_xt = (turned[:, 16:17] == lane.astype(F32)).astype(F32).astype(BF)
    place_yt = (turned[:, 17:18] == lane.astype(F32)).astype(F32)[:, :grid_y].astype(BF)

    @once
    def _():
        copies[0].wait()

    pick_xt[...] = dot(held("base_xt2", GRID), place_x).astype(BF)
    pick_x[...] = dot(place_xt, held("base_x")).astype(BF)
    station_y2 = held("station_y2", wide)
    for odd in range(2):
        high, low = [station_y2[(2 * odd + i) * grid_y : (2 * odd + i + 1) * grid_y] for i in range(2)]
        pick_y[:, odd * wide : (odd + 1) * wide] = dot(place_yt, high) + dot(place_yt, low)
    no_sum = jnp.zeros((8, LANES), F32)

    def trig(at, odd, chunk):
        lane = odd * wide + chunk * LANES
        return pick_y[at, lane : lane + LANES]

    def station_spectra():
        spread = held("spread")
        spread = jnp.concatenate([spread[i * LANES : (i + 1) * LANES] for i in range(3)], axis=1)
        spreads = dot(values[...], spread[:, : 5 * LANES])
        for row in range(0, stations, ROWS):
            at = slice(row, row + ROWS)
            for c, (_, odd_y) in enumerate(PARITY):
                e = spreads[at, c * LANES : (c + 1) * LANES]
                for chunk in chunks:
                    to = c * wide + chunk * LANES
                    spread_out[at, to : to + LANES] = (e * trig(at, odd_y, chunk)).astype(BF)
        spec = dot(pick_xt[...], spread_out[...])
        for c, (odd_x, _) in enumerate(PARITY):
            for hx in range(2):
                for chunk in chunks:
                    lane = c * wide + chunk * LANES
                    part = spec[hx * GRID : (hx + 1) * GRID, lane : lane + LANES]
                    spec_q[c, hx, chunk] = -part if odd_x * hx else part

    def back_project(receive):
        for half in halves:
            for row in range(0, GRID, 16):
                at = slice(row, row + 16)
                for chunk in chunks:
                    q = [[spec_q[c, hx, chunk, at, :] for hx in range(2)] for c in range(5)]
                    for z in range(half.start * deep, half.stop * deep):
                        t = [table_wide[c, z, at, :] for c in range(5)]
                        lane = z * wide + chunk * LANES
                        for hx in range(2):
                            total = t[0] * q[0][hx]
                            for c in range(1, 5):
                                total = total + t[c] * q[c][hx ^ PARITY[c][0]]
                            spec_g[hx * GRID + row : hx * GRID + row + 16, lane : lane + LANES] = total.astype(BF)
            lane = half.start * 2 * LANES
            along_x = dot(held("base_x"), spec_g[:, lane : lane + half_lanes]).astype(BF)
            along_x = [along_x[:, lane : lane + 2 * LANES] for lane in range(0, half_lanes, 2 * LANES)]
            receive(half, dot(jnp.concatenate(along_x, axis=0), held("field_yt", LANES)))

    def predict():
        for half in halves:
            r = residual[half.start : half.stop].reshape(len(half) * GRID, LANES).astype(BF)
            y = dot(jnp.concatenate([r, r], axis=1), held("field_y2")).astype(BF)
            y = jnp.concatenate([y[i * GRID : (i + 1) * GRID] for i in range(len(half))], axis=1)
            lane = half.start * 2 * LANES
            spec_f[:, lane : lane + half_lanes] = dot(held("base_xt2"), jnp.concatenate([y, y], axis=0)).astype(BF)

            for row in range(0, GRID, 16):
                at = [slice(hx * GRID + row, hx * GRID + row + 16) for hx in range(2)]
                for chunk in chunks:
                    total = [[None] * 2 for _ in range(5)]
                    for z in range(half.start * deep, half.stop * deep):
                        lane = z * wide + chunk * LANES
                        f = [spec_f[at[hx], lane : lane + LANES] for hx in range(2)]
                        for c, (odd_x, _) in enumerate(PARITY):
                            t = table(c, z, at[0])
                            for hx in range(2):
                                term = t * f[hx ^ odd_x]
                                total[c][hx] = term if total[c][hx] is None else total[c][hx] + term
                    for c, (odd_x, _) in enumerate(PARITY):
                        lane = c * wide + chunk * LANES
                        for hx in range(2):
                            part = total[c][hx]
                            if half is not halves[0]:
                                part = part + spec_i[at[hx], lane : lane + LANES]
                                part = -part if odd_x * hx else part
                            spec_i[at[hx], lane : lane + LANES] = part

        picked = dot(pick_x[...], spec_i[...])
        for row in range(0, stations, ROWS):
            at = slice(row, row + ROWS)
            for c, (_, odd_y) in enumerate(PARITY):
                part = None
                for chunk in chunks:
                    lane = c * wide + chunk * LANES
                    term = picked[at, lane : lane + LANES] * trig(at, odd_y, chunk)
                    part = term if part is None else part + term
                picked_in[at, c * LANES : (c + 1) * LANES] = part.astype(BF)
        return dot(picked_in[...], held("back", LANES))

    def fold(a):
        return jnp.sum(a.reshape(a.shape[0] // 8, 8, LANES), axis=0)

    def totals_of(partials):
        rows_of = []
        for partial in partials:
            for _ in range(3):
                part = partial.astype(BF).astype(F32)
                rows_of.append(part)
                partial = partial - part
        if len(rows_of) % 2:
            rows_of.append(no_sum)
        sums = dot(jnp.concatenate(rows_of, axis=0).astype(BF), held("same", LANES))
        return [jnp.sum(sums[i * 24 : (i + 1) * 24], axis=0, keepdims=True) for i in range(len(partials))]

    def depth_weight(z):
        within = lax.broadcasted_iota(jnp.int32, (1, LANES), 1) // (boots * grid_y)
        depth = (within + z * deep).astype(F32) + 0.5 + station_height
        ratio = station_height / depth
        return ratio * ratio * ratio

    def round_of(outer, inner, carry):
        first = outer == 0 and inner == 0
        last = outer == IRLS - 1 and inner == CG_STEPS - 1
        fresh = inner == 0
        old_norm, old_step, old_curve = carry
        sums = [no_sum] * 3

        def penalty_at(slab, at):
            if outer == 0:
                return damping * depth_weight(slab) / (focusing * focusing)
            return penalty[slab, at]

        def receive(half, applied):
            norm, bend, cross = sums
            for slab, at in pieces(half):
                row = (slab - half.start) * GRID + at.start
                r = applied[row : row + ROWS]
                if fresh and outer:
                    m = models[slab, at]
                    p = damping * depth_weight(slab) / (m * m + focusing * focusing)
                    penalty[slab, at] = p
                    r = r - p * m
                else:
                    p = penalty_at(slab, at)
                if not fresh:
                    pd = p * direction[slab, at]
                    r = residual[slab, at] - old_step * (r + pd)
                    cross += fold(pd * r)
                residual[slab, at] = r
                square = r * r
                norm += fold(square)
                bend += fold(p * square)
            sums[:] = [norm, bend, cross]

        back_project(receive)
        here = predict()
        weighted = weights[...] * here
        norm, bend, cross = sums
        if fresh:
            norm, curve = totals_of([norm, bend + fold(weighted * here)])
        else:
            norm, bend, cross = totals_of(
                [norm, bend + fold(weighted * here), cross + fold(weighted * image[...])]
            )
            ratio = norm / old_norm
            curve = bend + ratio * (2.0 * cross + ratio * old_curve)
        step = norm / curve
        if not last:
            if not fresh:
                here = here + ratio * image[...]
            now = step * here if first else pred[...] + step * here
            pred[...] = now
            if fresh:
                image[...] = here
                values[...] = (weights[...] * here).astype(BF)
            else:
                values[...] = (weights[...] * (data[...] - now)).astype(BF)
            station_spectra()
        for half in halves:
            for slab, at in pieces(half):
                d = residual[slab, at]
                if not fresh:
                    d = d + ratio * direction[slab, at]
                if fresh:
                    direction[slab, at] = d
                models[slab, at] = step * d if first else models[slab, at] + step * d
        return norm, step, curve

    station_spectra()

    @once
    def _():
        copies[1].wait()
        copies[2].wait()
        for c in range(5):
            for z in range(DEPTHS):
                table_wide[c, z] = table(c, z, slice(0, GRID)).astype(F32)

    carry = (None, None, None)
    for outer in range(IRLS):
        for inner in range(CG_STEPS):
            carry = round_of(outer, inner, carry)

    for group in range(slabs // boots):
        m = jnp.concatenate([models[group * boots + i].astype(BF) for i in range(boots)], axis=1)
        if boots > 1:
            regroup = held("regroup")
            regroup = [regroup[i * boots * LANES : (i + 1) * boots * LANES] for i in range(boots // 2)]
            m = dot(m, jnp.concatenate(regroup, axis=1)).astype(BF)
        for b in range(boots):
            out_ref[b * GRID : (b + 1) * GRID, group * LANES : (group + 1) * LANES] = (
                m[:, b * LANES : (b + 1) * LANES]
            )


def solve(slot, comp_weight, station_index, observed, counts, mine, grid_y):
    boots = min(mine, LANES // grid_y)
    slabs = DEPTHS * grid_y * boots // LANES
    stations = station_index.shape[1]
    const = jnp.asarray(constants(grid_y, boots))
    vmem = pltpu.VMEM
    whole = lambda a: pl.BlockSpec(a.shape, lambda i, n=a.ndim: (0,) * n)
    smem = pl.BlockSpec(memory_space=pltpu.SMEM)
    field = vmem((slabs, GRID, LANES), F32)
    at_stations = vmem((stations, LANES), F32)
    wide = 2 * boots * grid_y
    inputs = [station_index, observed, counts]
    return pl.pallas_call(
        functools.partial(solve_kernel, grid_y, boots, mine // boots),
        out_shape=jax.ShapeDtypeStruct((mine * GRID, DEPTHS * grid_y), BF),
        grid=(mine // boots,),
        in_specs=[smem, smem] + [whole(a) for a in inputs] + [pl.BlockSpec(memory_space=pl.ANY)],
        out_specs=pl.BlockSpec((boots * GRID, DEPTHS * grid_y), lambda i: (i, 0)),
        scratch_shapes=[
            vmem((layout(grid_y, boots).rows, 2 * LANES), BF),
            pltpu.SemaphoreType.DMA((3,)),
            vmem((stations, 2 * GRID), BF),
            vmem((2 * GRID, stations), BF),
            vmem((stations, 2 * wide), F32),
            at_stations,
            at_stations,
            at_stations,
            at_stations,
            vmem((stations, LANES), BF),
            vmem((LANES, stations), F32),
            vmem((5, DEPTHS, GRID, LANES), F32),
            vmem((stations, 5 * wide), BF),
            vmem((5, 2, wide // LANES, GRID, LANES), F32),
            vmem((2 * GRID, 5 * wide), BF),
            vmem((2 * GRID, slabs * 2 * LANES), BF),
            vmem((2 * GRID, slabs * 2 * LANES), BF),
            vmem((stations, 5 * LANES), BF),
            field,
            field,
            field,
            field,
        ],
        compiler_params=pltpu.CompilerParams(vmem_limit_bytes=56 * 1024 * 1024),
        cost_estimate=pl.CostEstimate(flops=10**10, bytes_accessed=10**7, transcendentals=0),
        name="solve",
    )(slot, comp_weight, *inputs, const)


def pick_kernel(grid_y, boots, count, *refs):
    models_refs, cell_ref, out_ref = refs[:count], refs[count], refs[count + 1]

    @pl.loop(0, cell_ref.shape[1] // CHUNK)
    def _(step):
        at = pl.ds(pl.multiple_of(step * CHUNK, CHUNK), CHUNK)
        place = cell_ref[:, at].astype(F32)
        wide = lambda row, rows: jnp.broadcast_to(row, (rows, CHUNK)).astype(BF)
        count_up = lambda rows: lax.broadcasted_iota(jnp.int32, (rows, CHUNK), 0).astype(F32).astype(BF)
        here_y = count_up(grid_y) == wide(place[1:2], grid_y)
        here_y = jnp.where(here_y, jnp.ones((grid_y, CHUNK), BF), jnp.zeros((grid_y, CHUNK), BF))
        z_row = wide(place[2:3], 16)
        none = jnp.zeros((16, CHUNK), BF)
        chosen = []
        for z in range(DEPTHS):
            here_z = z_row == jnp.full((16, CHUNK), z, BF)
            chosen += [jnp.where(here_z, here_y[i : i + 16], none) for i in range(0, grid_y, 16)]
        models = jnp.concatenate([ref[...] for ref in models_refs], axis=0)
        found = dot(models, jnp.concatenate(chosen, axis=0)).astype(BF)
        at_x = count_up(GRID) == wide(place[0:1], GRID)
        parts = []
        for b in range(boots):
            part = jnp.where(at_x, found[b * GRID : (b + 1) * GRID], jnp.zeros((GRID, CHUNK), BF))
            while part.shape[0] > 16:
                half = part.shape[0] // 2
                part = part[:half] + part[half:]
            parts.append(jnp.sum(part.astype(F32), axis=0, keepdims=True))
        out_ref[:, at] = jnp.concatenate(parts, axis=0).astype(BF)


def pick(models, cells, grid_y):
    rows = sum(m.shape[0] for m in models)
    boots = rows // GRID
    count = cells.shape[1]
    vmem = pl.BlockSpec(memory_space=pltpu.VMEM)
    return pl.pallas_call(
        functools.partial(pick_kernel, grid_y, boots, len(models)),
        out_shape=jax.ShapeDtypeStruct((boots, count), BF),
        in_specs=[vmem] * (len(models) + 1),
        out_specs=vmem,
        compiler_params=pltpu.CompilerParams(vmem_limit_bytes=40 * 1024 * 1024),
        cost_estimate=pl.CostEstimate(
            flops=2 * rows * DEPTHS * grid_y * count, bytes_accessed=10**6, transcendentals=0
        ),
        name="pick",
    )(*models, cells)


def local(wide, cell_index, station_index, observed, comp_weight, counts):
    boots = counts.shape[0]
    grid_y = cell_index.shape[1] * wide // (GRID * DEPTHS)
    team = TEAM if wide % TEAM == 0 and boots % TEAM == 0 else 1
    while 4 * boots * grid_y < team * 2 * LANES:
        team //= 2
    slot = lax.axis_index("wide").astype(jnp.int32) & (team - 1)

    def swap(a, k):
        return lax.ppermute(a, "wide", [(i, i ^ k) for i in range(wide)])

    theirs = [swap(cell_index, k) for k in range(2, team, 2)]
    models = [solve(slot.reshape(1), comp_weight, station_index, observed, counts, boots // team, grid_y)]
    models, theirs = lax.optimization_barrier((models, theirs))
    if team > 1:
        models.append(swap(models[0], 1))
    far = [swap(pick(models, cells, grid_y), 2 * k + 2) for k, cells in enumerate(theirs)]
    found = [pick(models, cell_index, grid_y)] + far
    mine = boots // team
    got = [a[i * mine : (i + 1) * mine] for a in found for i in range(len(models))]
    blocks = []
    for member in range(team):
        block = got[member]
        for other in range(1, team):
            block = jnp.where(slot == other, got[member ^ other], block)
        blocks.append(block.astype(F32))
    return jnp.concatenate(blocks, axis=0)


def solution(mesh):
    in_specs = (P(None, "wide"), P(None, "groups"), P(None, "groups"), P(), P("groups", None))
    out_specs = P("groups", "wide")
    fn = functools.partial(local, mesh.shape["wide"])
    return jax.shard_map(fn, mesh=mesh, in_specs=in_specs, out_specs=out_specs, check_vma=False)
```

```python
import functools

import jax
import jax.numpy as jnp
import ml_dtypes
import numpy as np
from jax import lax
from jax.experimental import pallas as pl
from jax.experimental.pallas import tpu as pltpu
from jax.sharding import PartitionSpec as P

IRLS = 2
CG_STEPS = 2
GRID = 128
DEPTHS = 16
LANES = 128
TEAM = 4
PARTS = 4
CHUNK = 2048
ROWS = 32

station_height = 2.0
focusing = 0.1
damping = 0.0002

PARITY = ((0, 0), (1, 1), (1, 0), (0, 0), (0, 1))
BF = jnp.bfloat16
F32 = jnp.float32


def offset_table(grid_y):
    one = np.float32
    dx = np.arange(GRID, dtype=one)[:, None, None]
    dy = np.arange(grid_y, dtype=one)[None, :, None]
    dz = (np.arange(DEPTHS, dtype=one) + one(0.5) + one(station_height))[None, None, :]
    radius2 = dx * dx + dy * dy + dz * dz
    strength = one(1) / (radius2 * radius2 * np.sqrt(radius2))
    three = one(3)
    kinds = [
        (three * dx * dx - radius2) * strength,
        three * dx * dy * strength,
        three * dx * dz * strength,
        (three * dy * dy - radius2) * strength,
        three * dy * dz * strength,
    ]
    return [k.astype(ml_dtypes.bfloat16).astype(np.float64) for k in kinds]


def angles(size):
    return 2 * np.pi * np.outer(np.arange(size), np.arange(size) + 0.5) / (2 * size)


def basis(size):
    return np.concatenate([np.cos(angles(size)), np.sin(angles(size))], axis=1)


def spectrum(values, odd, size):
    if odd:
        trig = 2 * np.sin(angles(size))
    else:
        trig = np.cos(angles(size)) * np.where(np.arange(size) == 0, 1, 2)[:, None]
    return np.tensordot(trig.T / size, values, axes=(1, 0))


def split(matrix):
    high = matrix.astype(ml_dtypes.bfloat16)
    low = (matrix - high.astype(np.float64)).astype(ml_dtypes.bfloat16)
    return high, low


class Layout:
    def __init__(self, parts):
        self.at = {}
        row = 0
        for name, rows in parts:
            self.at[name] = (row, rows)
            row += rows
        self.rows = row


def layout(grid_y, boots):
    return Layout(
        [
            ("base_x", GRID),
            ("base_xt2", 2 * GRID),
            ("station_y2", 4 * grid_y),
            ("spread", 3 * LANES),
            ("table", 5 * DEPTHS // 2 * GRID),
            ("field_y2", 2 * LANES),
            ("field_yt", 2 * LANES),
            ("back", 5 * LANES),
            ("same", LANES),
            ("regroup", boots * LANES * max(1, boots // 2)),
        ]
    )


@functools.lru_cache(maxsize=None)
def constants(grid_y, boots):
    deep = LANES // grid_y // boots
    copies = LANES // grid_y
    table = []
    for values, (odd_x, odd_y) in zip(offset_table(grid_y), PARITY):
        t = spectrum(values, odd_x, GRID)
        t = np.moveaxis(spectrum(np.moveaxis(t, 1, 0), odd_y, grid_y), 0, 1)
        table.append(np.tile(np.moveaxis(t, 2, 0), (1, 1, copies)))
    table = np.stack(table).reshape(5, DEPTHS // 2, 2, GRID, LANES).transpose(0, 1, 3, 2, 4)

    base_x = basis(GRID)
    base_y = basis(grid_y).reshape(grid_y, 2, grid_y)
    field_y = np.einsum("de,ab,yhl->dayehbl", np.eye(deep), np.eye(boots), base_y).reshape(LANES, 2 * LANES)
    odd_y = np.stack([-base_y[:, 1], base_y[:, 0]], axis=1)
    station_y = [np.tile(b[:, :, None], (1, 1, boots, 1)).reshape(grid_y, -1) for b in (base_y, odd_y)]
    spread = np.zeros((5, deep, boots, grid_y, copies, grid_y))
    for c in range(5):
        for copy in range(copies):
            spread[c, 0, copy % boots, c, copy, :] = 1
    spread = spread.reshape(5, LANES, LANES)
    back = spread.transpose(0, 2, 1).reshape(5 * LANES, LANES)
    spread = np.concatenate([spread, np.zeros((1, LANES, LANES))])
    spread = spread.reshape(3, 2, LANES, LANES).transpose(0, 2, 1, 3)
    same = np.einsum("ab,dc,yz->daycbz", np.eye(boots), np.ones((deep, deep)), np.ones((grid_y, grid_y)))
    same = same.reshape(LANES, LANES)
    regroup = np.einsum("st,de,ab,yz->sdaybtez", *[np.eye(n) for n in (boots, deep, boots, grid_y)])
    regroup = regroup.reshape(boots * LANES, boots * LANES)
    if boots > 2:
        regroup = np.concatenate(np.split(regroup, boots // 2, axis=1), axis=0)
    y_high, y_low = split(field_y)
    x_high, x_low = split(base_x.T)
    parts = dict(
        base_x=base_x,
        base_xt2=np.concatenate([x_high, x_low], axis=1),
        field_y2=np.concatenate([y_high, y_low], axis=0),
        field_yt=field_y.T,
        station_y2=np.concatenate([part for b in station_y for part in split(b)]),
        spread=spread.reshape(3 * LANES, 2 * LANES),
        back=back,
        same=same,
        regroup=regroup,
        table=table.reshape(-1, 2 * LANES),
    )
    where = layout(grid_y, boots)
    whole = np.zeros((max(where.rows, 1 << 14), 2 * LANES), ml_dtypes.bfloat16)
    for name, (row, rows) in where.at.items():
        part = parts[name].astype(ml_dtypes.bfloat16)
        assert part.shape[0] == rows
        whole[row : row + rows, : part.shape[1]] = part
    return whole


def dot(a, b):
    return jnp.dot(a, b, preferred_element_type=F32)


def solve_kernel(
    grid_y,
    boots,
    steps,
    slot_ref,
    comp_ref,
    station_ref,
    observed_ref,
    counts_ref,
    source,
    out_ref,
    const,
    copied,
    pick_x,
    pick_xt,
    pick_y,
    weights,
    data,
    pred,
    image,
    values,
    rows,
    table_wide,
    spread_out,
    spec_q,
    spec_i,
    spec_f,
    spec_g,
    picked_in,
    models,
    residual,
    direction,
    penalty,
):
    deep = LANES // grid_y // boots
    slabs = DEPTHS // deep
    where = layout(grid_y, boots)
    table_row, table_rows = where.at["table"]
    wide = 2 * boots * grid_y
    chunks = range(wide // LANES)
    bounds = [0, table_row, table_row + table_rows, where.rows]
    copies = [
        pltpu.make_async_copy(source.at[a:b], const.at[a:b], copied.at[i])
        for i, (a, b) in enumerate(zip(bounds[:-1], bounds[1:]))
    ]

    def once(f):
        if steps == 1:
            f()
        else:
            pl.when(pl.program_id(0) == 0)(f)

    @once
    def _():
        for copy in copies:
            copy.start()

    def held(name, width=2 * LANES):
        row, count = where.at[name]
        return const[row : row + count, :width]

    def table(c, z, at):
        row = table_row + (c * (DEPTHS // 2) + z // 2) * GRID
        return const[row + at.start : row + at.stop, z % 2 * LANES : (z % 2 + 1) * LANES]

    stations = station_ref.shape[1]
    first = (slot_ref[0] * pl.num_programs(0) + pl.program_id(0)) * boots
    size = slabs // PARTS
    shares = [range(start, start + size) for start in range(0, slabs, size)]
    share_lanes = size * 2 * LANES

    def pieces(share):
        return [(slab, slice(row, row + ROWS)) for slab in share for row in range(0, GRID, ROWS)]


    rows[...] = jnp.zeros_like(rows)
    for b in range(boots):
        row = b * grid_y
        rows[row : row + 5, :] = observed_ref[...]
        count = counts_ref[pl.ds(first + b, 1), :].astype(F32)
        for c in range(5):
            rows[row + 8 + c : row + 9 + c, :] = count * comp_ref[c]
    rows[16:18, :] = station_ref[...].astype(F32)
    turned = jnp.transpose(rows[...])
    lane = lax.broadcasted_iota(jnp.int32, (1, LANES), 1)
    used = lane % grid_y < 5
    data[...] = jnp.where(used, turned, 0.0)
    weights[...] = jnp.where(used, pltpu.roll(turned, LANES - 8, 1), 0.0)
    values[...] = (weights[...] * data[...]).astype(BF)

    place_x = (lax.broadcasted_iota(jnp.int32, (GRID, stations), 0) == station_ref[0:1, :]).astype(F32).astype(BF)
    place_xt = (turned[:, 16:17] == lane.astype(F32)).astype(F32).astype(BF)
    place_yt = (turned[:, 17:18] == lane.astype(F32)).astype(F32)[:, :grid_y].astype(BF)

    @once
    def _():
        copies[0].wait()

    pick_xt[...] = dot(held("base_xt2", GRID), place_x).astype(BF)
    pick_x[...] = dot(place_xt, held("base_x")).astype(BF)
    station_y2 = held("station_y2", wide)
    for odd in range(2):
        high, low = [station_y2[(2 * odd + i) * grid_y : (2 * odd + i + 1) * grid_y] for i in range(2)]
        pick_y[:, odd * wide : (odd + 1) * wide] = dot(place_yt, high) + dot(place_yt, low)
    no_sum = jnp.zeros((8, LANES), F32)

    def trig(at, odd, chunk):
        lane = odd * wide + chunk * LANES
        return pick_y[at, lane : lane + LANES]

    def station_spectra():
        spread = held("spread")
        spread = jnp.concatenate([spread[i * LANES : (i + 1) * LANES] for i in range(3)], axis=1)
        spreads = dot(values[...], spread[:, : 5 * LANES])
        for row in range(0, stations, ROWS):
            at = slice(row, row + ROWS)
            for c, (_, odd_y) in enumerate(PARITY):
                e = spreads[at, c * LANES : (c + 1) * LANES]
                for chunk in chunks:
                    to = c * wide + chunk * LANES
                    spread_out[at, to : to + LANES] = (e * trig(at, odd_y, chunk)).astype(BF)
        spec = dot(pick_xt[...], spread_out[...])
        for c, (odd_x, _) in enumerate(PARITY):
            for hx in range(2):
                for chunk in chunks:
                    lane = c * wide + chunk * LANES
                    part = spec[hx * GRID : (hx + 1) * GRID, lane : lane + LANES]
                    spec_q[c, hx, chunk] = -part if odd_x * hx else part

    def back_project(receive):
        for share in shares:
            for row in range(0, GRID, 16):
                at = slice(row, row + 16)
                for chunk in chunks:
                    q = [[spec_q[c, hx, chunk, at, :] for hx in range(2)] for c in range(5)]
                    for z in range(share.start * deep, share.stop * deep):
                        t = [table_wide[c, z, at, :] for c in range(5)]
                        lane = z * wide + chunk * LANES
                        for hx in range(2):
                            total = t[0] * q[0][hx]
                            for c in range(1, 5):
                                total = total + t[c] * q[c][hx ^ PARITY[c][0]]
                            spec_g[hx * GRID + row : hx * GRID + row + 16, lane : lane + LANES] = total.astype(BF)
            lane = share.start * 2 * LANES
            along_x = dot(held("base_x"), spec_g[:, lane : lane + share_lanes]).astype(BF)
            along_x = [along_x[:, lane : lane + 2 * LANES] for lane in range(0, share_lanes, 2 * LANES)]
            receive(share, dot(jnp.concatenate(along_x, axis=0), held("field_yt", LANES)))

    def predict():
        for share in shares:
            r = residual[share.start : share.stop].reshape(len(share) * GRID, LANES).astype(BF)
            y = dot(jnp.concatenate([r, r], axis=1), held("field_y2")).astype(BF)
            y = jnp.concatenate([y[i * GRID : (i + 1) * GRID] for i in range(len(share))], axis=1)
            lane = share.start * 2 * LANES
            spec_f[:, lane : lane + share_lanes] = dot(held("base_xt2"), jnp.concatenate([y, y], axis=0)).astype(BF)

            for row in range(0, GRID, 16):
                at = [slice(hx * GRID + row, hx * GRID + row + 16) for hx in range(2)]
                for chunk in chunks:
                    total = [[None] * 2 for _ in range(5)]
                    for z in range(share.start * deep, share.stop * deep):
                        lane = z * wide + chunk * LANES
                        f = [spec_f[at[hx], lane : lane + LANES] for hx in range(2)]
                        for c, (odd_x, _) in enumerate(PARITY):
                            t = table(c, z, at[0])
                            for hx in range(2):
                                term = t * f[hx ^ odd_x]
                                total[c][hx] = term if total[c][hx] is None else total[c][hx] + term
                    for c, (odd_x, _) in enumerate(PARITY):
                        lane = c * wide + chunk * LANES
                        for hx in range(2):
                            part = total[c][hx]
                            if share is not shares[0]:
                                part = part + spec_i[at[hx], lane : lane + LANES]
                            if share is shares[-1] and odd_x * hx:
                                part = -part
                            spec_i[at[hx], lane : lane + LANES] = part

        picked = dot(pick_x[...], spec_i[...])
        for row in range(0, stations, ROWS):
            at = slice(row, row + ROWS)
            for c, (_, odd_y) in enumerate(PARITY):
                part = None
                for chunk in chunks:
                    lane = c * wide + chunk * LANES
                    term = picked[at, lane : lane + LANES] * trig(at, odd_y, chunk)
                    part = term if part is None else part + term
                picked_in[at, c * LANES : (c + 1) * LANES] = part.astype(BF)
        return dot(picked_in[...], held("back", LANES))

    def fold(a):
        return jnp.sum(a.reshape(a.shape[0] // 8, 8, LANES), axis=0)

    def totals_of(partials):
        rows_of = []
        for partial in partials:
            for _ in range(3):
                part = partial.astype(BF).astype(F32)
                rows_of.append(part)
                partial = partial - part
        if len(rows_of) % 2:
            rows_of.append(no_sum)
        sums = dot(jnp.concatenate(rows_of, axis=0).astype(BF), held("same", LANES))
        return [jnp.sum(sums[i * 24 : (i + 1) * 24], axis=0, keepdims=True) for i in range(len(partials))]

    def depth_weight(z):
        within = lax.broadcasted_iota(jnp.int32, (1, LANES), 1) // (boots * grid_y)
        depth = (within + z * deep).astype(F32) + 0.5 + station_height
        ratio = station_height / depth
        return ratio * ratio * ratio

    def round_of(outer, inner, carry):
        first = outer == 0 and inner == 0
        last = outer == IRLS - 1 and inner == CG_STEPS - 1
        fresh = inner == 0
        old_norm, old_step, old_curve = carry
        sums = [no_sum] * 3

        def penalty_at(slab, at):
            if outer == 0:
                return damping * depth_weight(slab) / (focusing * focusing)
            return penalty[slab, at]

        def receive(share, applied):
            norm, bend, cross = sums
            for slab, at in pieces(share):
                row = (slab - share.start) * GRID + at.start
                r = applied[row : row + ROWS]
                if fresh and outer:
                    m = models[slab, at]
                    p = damping * depth_weight(slab) / (m * m + focusing * focusing)
                    penalty[slab, at] = p
                    r = r - p * m
                else:
                    p = penalty_at(slab, at)
                if not fresh:
                    pd = p * direction[slab, at]
                    r = residual[slab, at] - old_step * (r + pd)
                    cross += fold(pd * r)
                residual[slab, at] = r
                square = r * r
                norm += fold(square)
                bend += fold(p * square)
            sums[:] = [norm, bend, cross]

        back_project(receive)
        here = predict()
        weighted = weights[...] * here
        norm, bend, cross = sums
        if fresh:
            norm, curve = totals_of([norm, bend + fold(weighted * here)])
        else:
            norm, bend, cross = totals_of(
                [norm, bend + fold(weighted * here), cross + fold(weighted * image[...])]
            )
            ratio = norm / old_norm
            curve = bend + ratio * (2.0 * cross + ratio * old_curve)
        step = norm / curve
        if not last:
            if not fresh:
                here = here + ratio * image[...]
            now = step * here if first else pred[...] + step * here
            pred[...] = now
            if fresh:
                image[...] = here
                values[...] = (weights[...] * here).astype(BF)
            else:
                values[...] = (weights[...] * (data[...] - now)).astype(BF)
            station_spectra()
        for share in shares:
            for slab, at in pieces(share):
                d = residual[slab, at]
                if not fresh:
                    d = d + ratio * direction[slab, at]
                if fresh:
                    direction[slab, at] = d
                models[slab, at] = step * d if first else models[slab, at] + step * d
        return norm, step, curve

    station_spectra()

    @once
    def _():
        copies[1].wait()
        copies[2].wait()
        for c in range(5):
            for z in range(DEPTHS):
                table_wide[c, z] = table(c, z, slice(0, GRID)).astype(F32)

    carry = (None, None, None)
    for outer in range(IRLS):
        for inner in range(CG_STEPS):
            carry = round_of(outer, inner, carry)

    for group in range(slabs // boots):
        m = jnp.concatenate([models[group * boots + i].astype(BF) for i in range(boots)], axis=1)
        if boots > 1:
            regroup = held("regroup")
            regroup = [regroup[i * boots * LANES : (i + 1) * boots * LANES] for i in range(boots // 2)]
            m = dot(m, jnp.concatenate(regroup, axis=1)).astype(BF)
        for b in range(boots):
            out_ref[b * GRID : (b + 1) * GRID, group * LANES : (group + 1) * LANES] = (
                m[:, b * LANES : (b + 1) * LANES]
            )


def solve(slot, comp_weight, station_index, observed, counts, mine, grid_y):
    boots = min(mine, LANES // grid_y)
    slabs = DEPTHS * grid_y * boots // LANES
    stations = station_index.shape[1]
    const = jnp.asarray(constants(grid_y, boots))
    vmem = pltpu.VMEM
    whole = lambda a: pl.BlockSpec(a.shape, lambda i, n=a.ndim: (0,) * n)
    smem = pl.BlockSpec(memory_space=pltpu.SMEM)
    field = vmem((slabs, GRID, LANES), F32)
    at_stations = vmem((stations, LANES), F32)
    wide = 2 * boots * grid_y
    inputs = [station_index, observed, counts]
    return pl.pallas_call(
        functools.partial(solve_kernel, grid_y, boots, mine // boots),
        out_shape=jax.ShapeDtypeStruct((mine * GRID, DEPTHS * grid_y), BF),
        grid=(mine // boots,),
        in_specs=[smem, smem] + [whole(a) for a in inputs] + [pl.BlockSpec(memory_space=pl.ANY)],
        out_specs=pl.BlockSpec((boots * GRID, DEPTHS * grid_y), lambda i: (i, 0)),
        scratch_shapes=[
            vmem((layout(grid_y, boots).rows, 2 * LANES), BF),
            pltpu.SemaphoreType.DMA((3,)),
            vmem((stations, 2 * GRID), BF),
            vmem((2 * GRID, stations), BF),
            vmem((stations, 2 * wide), F32),
            at_stations,
            at_stations,
            at_stations,
            at_stations,
            vmem((stations, LANES), BF),
            vmem((LANES, stations), F32),
            vmem((5, DEPTHS, GRID, LANES), F32),
            vmem((stations, 5 * wide), BF),
            vmem((5, 2, wide // LANES, GRID, LANES), F32),
            vmem((2 * GRID, 5 * wide), BF),
            vmem((2 * GRID, slabs * 2 * LANES), BF),
            vmem((2 * GRID, slabs * 2 * LANES), BF),
            vmem((stations, 5 * LANES), BF),
            field,
            field,
            field,
            field,
        ],
        compiler_params=pltpu.CompilerParams(vmem_limit_bytes=56 * 1024 * 1024),
        cost_estimate=pl.CostEstimate(flops=10**10, bytes_accessed=10**7, transcendentals=0),
        name="solve",
    )(slot, comp_weight, *inputs, const)


def pick_kernel(grid_y, boots, count, models_ref, *refs):
    def pick_chunk(cell_ref, out_ref, at):
        place = cell_ref[:, at].astype(F32)
        wide = lambda row, rows: jnp.broadcast_to(row, (rows, CHUNK)).astype(BF)
        count_up = lambda rows: lax.broadcasted_iota(jnp.int32, (rows, CHUNK), 0).astype(F32).astype(BF)
        here_y = count_up(grid_y) == wide(place[1:2], grid_y)
        here_y = jnp.where(here_y, jnp.ones((grid_y, CHUNK), BF), jnp.zeros((grid_y, CHUNK), BF))
        z_row = wide(place[2:3], 16)
        none = jnp.zeros((16, CHUNK), BF)
        chosen = []
        for z in range(DEPTHS):
            here_z = z_row == jnp.full((16, CHUNK), z, BF)
            chosen += [jnp.where(here_z, here_y[i : i + 16], none) for i in range(0, grid_y, 16)]
        found = dot(models_ref[...], jnp.concatenate(chosen, axis=0)).astype(BF)
        at_x = count_up(GRID) == wide(place[0:1], GRID)
        parts = []
        for b in range(boots):
            part = jnp.where(at_x, found[b * GRID : (b + 1) * GRID], jnp.zeros((GRID, CHUNK), BF))
            while part.shape[0] > 16:
                half = part.shape[0] // 2
                part = part[:half] + part[half:]
            parts.append(jnp.sum(part.astype(F32), axis=0, keepdims=True))
        out_ref[:, at] = jnp.concatenate(parts, axis=0).astype(BF)

    @pl.loop(0, refs[0].shape[1] // CHUNK)
    def _(step):
        at = pl.ds(pl.multiple_of(step * CHUNK, CHUNK), CHUNK)
        for cell_ref, out_ref in zip(refs[:count], refs[count:]):
            pick_chunk(cell_ref, out_ref, at)


def pick(models, cells, grid_y):
    boots = models.shape[0] // GRID
    count = cells[0].shape[1]
    vmem = pl.BlockSpec(memory_space=pltpu.VMEM)
    return pl.pallas_call(
        functools.partial(pick_kernel, grid_y, boots, len(cells)),
        out_shape=[jax.ShapeDtypeStruct((boots, count), BF)] * len(cells),
        in_specs=[vmem] * (1 + len(cells)),
        out_specs=[vmem] * len(cells),
        compiler_params=pltpu.CompilerParams(vmem_limit_bytes=40 * 1024 * 1024),
        cost_estimate=pl.CostEstimate(
            flops=2 * models.size * count * len(cells), bytes_accessed=10**6, transcendentals=0
        ),
        name="pick",
    )(models, *cells)


def local(wide, cell_index, station_index, observed, comp_weight, counts):
    boots = counts.shape[0]
    grid_y = cell_index.shape[1] * wide // (GRID * DEPTHS)
    team = TEAM if wide % TEAM == 0 and boots % TEAM == 0 else 1
    while 4 * boots * grid_y < team * 2 * LANES:
        team //= 2
    slot = lax.axis_index("wide").astype(jnp.int32) & (team - 1)

    def swap(a, k):
        return lax.ppermute(a, "wide", [(i, i ^ k) for i in range(wide)])

    theirs = [swap(cell_index, k) for k in range(2, team, 2)]
    models = solve(slot.reshape(1), comp_weight, station_index, observed, counts, boots // team, grid_y)
    models, theirs = lax.optimization_barrier((models, theirs))
    if team > 1:
        shared = swap(models, 1)
        *ours_far, ours_near = pick(models, [*theirs, cell_index], grid_y)
        ours_far = [swap(a, 2 * k + 2) for k, a in enumerate(ours_far)]
        shared_far = [swap(a, 2 * k + 2) for k, a in enumerate(pick(shared, theirs, grid_y))]
        got = [ours_near, pick(shared, [cell_index], grid_y)[0]]
        for pair in zip(ours_far, shared_far):
            got += pair
    else:
        got = pick(models, [cell_index], grid_y)
    blocks = []
    for member in range(team):
        block = got[member]
        for other in range(1, team):
            block = jnp.where(slot == other, got[member ^ other], block)
        blocks.append(block.astype(F32))
    return jnp.concatenate(blocks, axis=0)


def solution(mesh):
    in_specs = (P(None, "wide"), P(None, "groups"), P(None, "groups"), P(), P("groups", None))
    out_specs = P("groups", "wide")
    fn = functools.partial(local, mesh.shape["wide"])
    return jax.shard_map(fn, mesh=mesh, in_specs=in_specs, out_specs=out_specs, check_vma=False)
```

```python
import functools

import jax
import jax.numpy as jnp
import ml_dtypes
import numpy as np
from jax import lax
from jax.experimental import pallas as pl
from jax.experimental.pallas import tpu as pltpu
from jax.sharding import PartitionSpec as P

IRLS = 2
CG_STEPS = 2
GRID = 128
DEPTHS = 16
LANES = 128
TEAM = 4
PARTS = 2
CHUNK = 2048
ROWS = 32

station_height = 2.0
focusing = 0.1
damping = 0.0002

PARITY = ((0, 0), (1, 1), (1, 0), (0, 0), (0, 1))
BF = jnp.bfloat16
F32 = jnp.float32


def offset_table(grid_y):
    one = np.float32
    dx = np.arange(GRID, dtype=one)[:, None, None]
    dy = np.arange(grid_y, dtype=one)[None, :, None]
    dz = (np.arange(DEPTHS, dtype=one) + one(0.5) + one(station_height))[None, None, :]
    radius2 = dx * dx + dy * dy + dz * dz
    strength = one(1) / (radius2 * radius2 * np.sqrt(radius2))
    three = one(3)
    kinds = [
        (three * dx * dx - radius2) * strength,
        three * dx * dy * strength,
        three * dx * dz * strength,
        (three * dy * dy - radius2) * strength,
        three * dy * dz * strength,
    ]
    return [k.astype(ml_dtypes.bfloat16).astype(np.float64) for k in kinds]


def angles(size):
    return 2 * np.pi * np.outer(np.arange(size), np.arange(size) + 0.5) / (2 * size)


def basis(size):
    return np.concatenate([np.cos(angles(size)), np.sin(angles(size))], axis=1)


def spectrum(values, odd, size):
    if odd:
        trig = 2 * np.sin(angles(size))
    else:
        trig = np.cos(angles(size)) * np.where(np.arange(size) == 0, 1, 2)[:, None]
    return np.tensordot(trig.T / size, values, axes=(1, 0))


def split(matrix):
    high = matrix.astype(ml_dtypes.bfloat16)
    low = (matrix - high.astype(np.float64)).astype(ml_dtypes.bfloat16)
    return high, low


class Layout:
    def __init__(self, parts):
        self.at = {}
        row = 0
        for name, rows in parts:
            self.at[name] = (row, rows)
            row += rows
        self.rows = row


def layout(grid_y, boots):
    return Layout(
        [
            ("base_x", GRID),
            ("base_xt2", 2 * GRID),
            ("station_y2", 4 * grid_y),
            ("spread", 3 * LANES),
            ("table", 5 * DEPTHS // 2 * GRID),
            ("field_y2", 2 * LANES),
            ("field_yt", 2 * LANES),
            ("back", 5 * LANES),
            ("same", LANES),
            ("regroup", boots * LANES * max(1, boots // 2)),
        ]
    )


@functools.lru_cache(maxsize=None)
def constants(grid_y, boots):
    deep = LANES // grid_y // boots
    copies = LANES // grid_y
    table = []
    for values, (odd_x, odd_y) in zip(offset_table(grid_y), PARITY):
        t = spectrum(values, odd_x, GRID)
        t = np.moveaxis(spectrum(np.moveaxis(t, 1, 0), odd_y, grid_y), 0, 1)
        table.append(np.tile(np.moveaxis(t, 2, 0), (1, 1, copies)))
    table = np.stack(table).reshape(5, DEPTHS // 2, 2, GRID, LANES).transpose(0, 1, 3, 2, 4)

    base_x = basis(GRID)
    base_y = basis(grid_y).reshape(grid_y, 2, grid_y)
    field_y = np.einsum("de,ab,yhl->dayehbl", np.eye(deep), np.eye(boots), base_y).reshape(LANES, 2 * LANES)
    odd_y = np.stack([-base_y[:, 1], base_y[:, 0]], axis=1)
    station_y = [np.tile(b[:, :, None], (1, 1, boots, 1)).reshape(grid_y, -1) for b in (base_y, odd_y)]
    spread = np.zeros((5, deep, boots, grid_y, copies, grid_y))
    for c in range(5):
        for copy in range(copies):
            spread[c, 0, copy % boots, c, copy, :] = 1
    spread = spread.reshape(5, LANES, LANES)
    back = spread.transpose(0, 2, 1).reshape(5 * LANES, LANES)
    spread = np.concatenate([spread, np.zeros((1, LANES, LANES))])
    spread = spread.reshape(3, 2, LANES, LANES).transpose(0, 2, 1, 3)
    same = np.einsum("ab,dc,yz->daycbz", np.eye(boots), np.ones((deep, deep)), np.ones((grid_y, grid_y)))
    same = same.reshape(LANES, LANES)
    regroup = np.einsum("st,de,ab,yz->sdaybtez", *[np.eye(n) for n in (boots, deep, boots, grid_y)])
    regroup = regroup.reshape(boots * LANES, boots * LANES)
    if boots > 2:
        regroup = np.concatenate(np.split(regroup, boots // 2, axis=1), axis=0)
    y_high, y_low = split(field_y)
    x_high, x_low = split(base_x.T)
    parts = dict(
        base_x=base_x,
        base_xt2=np.concatenate([x_high, x_low], axis=1),
        field_y2=np.concatenate([y_high, y_low], axis=0),
        field_yt=field_y.T,
        station_y2=np.concatenate([part for b in station_y for part in split(b)]),
        spread=spread.reshape(3 * LANES, 2 * LANES),
        back=back,
        same=same,
        regroup=regroup,
        table=table.reshape(-1, 2 * LANES),
    )
    where = layout(grid_y, boots)
    whole = np.zeros((max(where.rows, 1 << 14), 2 * LANES), ml_dtypes.bfloat16)
    for name, (row, rows) in where.at.items():
        part = parts[name].astype(ml_dtypes.bfloat16)
        assert part.shape[0] == rows
        whole[row : row + rows, : part.shape[1]] = part
    return whole


def dot(a, b):
    return jnp.dot(a, b, preferred_element_type=F32)


def solve_kernel(
    grid_y,
    boots,
    steps,
    slot_ref,
    comp_ref,
    station_ref,
    observed_ref,
    counts_ref,
    source,
    out_ref,
    const,
    copied,
    pick_x,
    pick_xt,
    pick_y,
    weights,
    data,
    pred,
    image,
    values,
    rows,
    table_wide,
    spread_out,
    spec_q,
    spec_i,
    spec_f,
    spec_g,
    picked_in,
    models,
    residual,
    direction,
    penalty,
):
    deep = LANES // grid_y // boots
    slabs = DEPTHS // deep
    where = layout(grid_y, boots)
    table_row, table_rows = where.at["table"]
    wide = 2 * boots * grid_y
    chunks = range(wide // LANES)
    bounds = [0, table_row, table_row + table_rows, where.rows]
    copies = [
        pltpu.make_async_copy(source.at[a:b], const.at[a:b], copied.at[i])
        for i, (a, b) in enumerate(zip(bounds[:-1], bounds[1:]))
    ]

    def once(f):
        if steps == 1:
            f()
        else:
            pl.when(pl.program_id(0) == 0)(f)

    @once
    def _():
        for copy in copies:
            copy.start()

    def held(name, width=2 * LANES):
        row, count = where.at[name]
        return const[row : row + count, :width]

    def table(c, z, at):
        row = table_row + (c * (DEPTHS // 2) + z // 2) * GRID
        return const[row + at.start : row + at.stop, z % 2 * LANES : (z % 2 + 1) * LANES]

    stations = station_ref.shape[1]
    first = (slot_ref[0] * pl.num_programs(0) + pl.program_id(0)) * boots
    size = slabs // PARTS
    shares = [range(start, start + size) for start in range(0, slabs, size)]
    share_lanes = size * 2 * LANES

    def pieces(share):
        return [(slab, slice(row, row + ROWS)) for slab in share for row in range(0, GRID, ROWS)]


    rows[...] = jnp.zeros_like(rows)
    for b in range(boots):
        row = b * grid_y
        rows[row : row + 5, :] = observed_ref[...]
        count = counts_ref[pl.ds(first + b, 1), :].astype(F32)
        for c in range(5):
            rows[row + 8 + c : row + 9 + c, :] = count * comp_ref[c]
    rows[16:18, :] = station_ref[...].astype(F32)
    turned = jnp.transpose(rows[...])
    lane = lax.broadcasted_iota(jnp.int32, (1, LANES), 1)
    used = lane % grid_y < 5
    data[...] = jnp.where(used, turned, 0.0)
    weights[...] = jnp.where(used, pltpu.roll(turned, LANES - 8, 1), 0.0)
    values[...] = (weights[...] * data[...]).astype(BF)

    place_x = (lax.broadcasted_iota(jnp.int32, (GRID, stations), 0) == station_ref[0:1, :]).astype(F32).astype(BF)
    place_xt = (turned[:, 16:17] == lane.astype(F32)).astype(F32).astype(BF)
    place_yt = (turned[:, 17:18] == lane.astype(F32)).astype(F32)[:, :grid_y].astype(BF)

    @once
    def _():
        copies[0].wait()

    pick_xt[...] = dot(held("base_xt2", GRID), place_x).astype(BF)
    pick_x[...] = dot(place_xt, held("base_x")).astype(BF)
    station_y2 = held("station_y2", wide)
    for odd in range(2):
        high, low = [station_y2[(2 * odd + i) * grid_y : (2 * odd + i + 1) * grid_y] for i in range(2)]
        pick_y[:, odd * wide : (odd + 1) * wide] = dot(place_yt, high) + dot(place_yt, low)
    no_sum = jnp.zeros((8, LANES), F32)

    def trig(at, odd, chunk):
        lane = odd * wide + chunk * LANES
        return pick_y[at, lane : lane + LANES]

    def station_spectra():
        spread = held("spread")
        spread = jnp.concatenate([spread[i * LANES : (i + 1) * LANES] for i in range(3)], axis=1)
        spreads = dot(values[...], spread[:, : 5 * LANES])
        for row in range(0, stations, ROWS):
            at = slice(row, row + ROWS)
            for c, (_, odd_y) in enumerate(PARITY):
                e = spreads[at, c * LANES : (c + 1) * LANES]
                for chunk in chunks:
                    to = c * wide + chunk * LANES
                    spread_out[at, to : to + LANES] = (e * trig(at, odd_y, chunk)).astype(BF)
        spec = dot(pick_xt[...], spread_out[...])
        for c, (odd_x, _) in enumerate(PARITY):
            for hx in range(2):
                for chunk in chunks:
                    lane = c * wide + chunk * LANES
                    part = spec[hx * GRID : (hx + 1) * GRID, lane : lane + LANES]
                    spec_q[c, hx, chunk] = -part if odd_x * hx else part

    def back_project(receive):
        for share in shares:
            for row in range(0, GRID, 16):
                at = slice(row, row + 16)
                for chunk in chunks:
                    q = [[spec_q[c, hx, chunk, at, :] for hx in range(2)] for c in range(5)]
                    for z in range(share.start * deep, share.stop * deep):
                        t = [table_wide[c, z, at, :] for c in range(5)]
                        lane = z * wide + chunk * LANES
                        for hx in range(2):
                            total = t[0] * q[0][hx]
                            for c in range(1, 5):
                                total = total + t[c] * q[c][hx ^ PARITY[c][0]]
                            spec_g[hx * GRID + row : hx * GRID + row + 16, lane : lane + LANES] = total.astype(BF)
            lane = share.start * 2 * LANES
            along_x = dot(held("base_x"), spec_g[:, lane : lane + share_lanes]).astype(BF)
            along_x = [along_x[:, lane : lane + 2 * LANES] for lane in range(0, share_lanes, 2 * LANES)]
            receive(share, dot(jnp.concatenate(along_x, axis=0), held("field_yt", LANES)))

    def predict():
        for share in shares:
            r = residual[share.start : share.stop].reshape(len(share) * GRID, LANES).astype(BF)
            y = dot(jnp.concatenate([r, r], axis=1), held("field_y2")).astype(BF)
            y = jnp.concatenate([y[i * GRID : (i + 1) * GRID] for i in range(len(share))], axis=1)
            lane = share.start * 2 * LANES
            spec_f[:, lane : lane + share_lanes] = dot(held("base_xt2"), jnp.concatenate([y, y], axis=0)).astype(BF)

            for row in range(0, GRID, 16):
                at = [slice(hx * GRID + row, hx * GRID + row + 16) for hx in range(2)]
                for chunk in chunks:
                    total = [[None] * 2 for _ in range(5)]
                    for z in range(share.start * deep, share.stop * deep):
                        lane = z * wide + chunk * LANES
                        f = [spec_f[at[hx], lane : lane + LANES] for hx in range(2)]
                        for c, (odd_x, _) in enumerate(PARITY):
                            t = table(c, z, at[0])
                            for hx in range(2):
                                term = t * f[hx ^ odd_x]
                                total[c][hx] = term if total[c][hx] is None else total[c][hx] + term
                    for c, (odd_x, _) in enumerate(PARITY):
                        lane = c * wide + chunk * LANES
                        for hx in range(2):
                            part = total[c][hx]
                            if share is not shares[0]:
                                part = part + spec_i[at[hx], lane : lane + LANES]
                            if share is shares[-1] and odd_x * hx:
                                part = -part
                            spec_i[at[hx], lane : lane + LANES] = part

        picked = dot(pick_x[...], spec_i[...])
        for row in range(0, stations, ROWS):
            at = slice(row, row + ROWS)
            for c, (_, odd_y) in enumerate(PARITY):
                part = None
                for chunk in chunks:
                    lane = c * wide + chunk * LANES
                    term = picked[at, lane : lane + LANES] * trig(at, odd_y, chunk)
                    part = term if part is None else part + term
                picked_in[at, c * LANES : (c + 1) * LANES] = part.astype(BF)
        return dot(picked_in[...], held("back", LANES))

    def fold(a):
        return jnp.sum(a.reshape(a.shape[0] // 8, 8, LANES), axis=0)

    def totals_of(partials):
        rows_of = []
        for partial in partials:
            for _ in range(3):
                part = partial.astype(BF).astype(F32)
                rows_of.append(part)
                partial = partial - part
        if len(rows_of) % 2:
            rows_of.append(no_sum)
        sums = dot(jnp.concatenate(rows_of, axis=0).astype(BF), held("same", LANES))
        return [jnp.sum(sums[i * 24 : (i + 1) * 24], axis=0, keepdims=True) for i in range(len(partials))]

    def depth_weight(z):
        within = lax.broadcasted_iota(jnp.int32, (1, LANES), 1) // (boots * grid_y)
        depth = (within + z * deep).astype(F32) + 0.5 + station_height
        ratio = station_height / depth
        return ratio * ratio * ratio

    def round_of(outer, inner, carry):
        first = outer == 0 and inner == 0
        last = outer == IRLS - 1 and inner == CG_STEPS - 1
        fresh = inner == 0
        old_norm, old_step, old_curve = carry
        sums = [no_sum] * 3

        def penalty_at(slab, at):
            if outer == 0:
                return damping * depth_weight(slab) / (focusing * focusing)
            return penalty[slab, at]

        def receive(share, applied):
            norm, bend, cross = sums
            for slab, at in pieces(share):
                row = (slab - share.start) * GRID + at.start
                r = applied[row : row + ROWS]
                if fresh and outer:
                    m = models[slab, at]
                    p = damping * depth_weight(slab) / (m * m + focusing * focusing)
                    penalty[slab, at] = p
                    r = r - p * m
                else:
                    p = penalty_at(slab, at)
                if not fresh:
                    pd = p * direction[slab, at]
                    r = residual[slab, at] - old_step * (r + pd)
                    cross += fold(pd * r)
                residual[slab, at] = r
                square = r * r
                norm += fold(square)
                bend += fold(p * square)
            sums[:] = [norm, bend, cross]

        back_project(receive)
        here = predict()
        weighted = weights[...] * here
        norm, bend, cross = sums
        if fresh:
            norm, curve = totals_of([norm, bend + fold(weighted * here)])
        else:
            norm, bend, cross = totals_of(
                [norm, bend + fold(weighted * here), cross + fold(weighted * image[...])]
            )
            ratio = norm / old_norm
            curve = bend + ratio * (2.0 * cross + ratio * old_curve)
        step = norm / curve
        if not last:
            if not fresh:
                here = here + ratio * image[...]
            now = step * here if first else pred[...] + step * here
            pred[...] = now
            if fresh:
                image[...] = here
                values[...] = (weights[...] * here).astype(BF)
            else:
                values[...] = (weights[...] * (data[...] - now)).astype(BF)
            station_spectra()
        for share in shares:
            for slab, at in pieces(share):
                d = residual[slab, at]
                if not fresh:
                    d = d + ratio * direction[slab, at]
                if fresh:
                    direction[slab, at] = d
                models[slab, at] = step * d if first else models[slab, at] + step * d
        return norm, step, curve

    @once
    def _():
        copies[1].wait()
        copies[2].wait()
        for c in range(5):
            for z in range(DEPTHS):
                table_wide[c, z] = table(c, z, slice(0, GRID)).astype(F32)

    station_spectra()

    carry = (None, None, None)
    for outer in range(IRLS):
        for inner in range(CG_STEPS):
            carry = round_of(outer, inner, carry)

    for group in range(slabs // boots):
        m = jnp.concatenate([models[group * boots + i].astype(BF) for i in range(boots)], axis=1)
        if boots > 1:
            regroup = held("regroup")
            regroup = [regroup[i * boots * LANES : (i + 1) * boots * LANES] for i in range(boots // 2)]
            m = dot(m, jnp.concatenate(regroup, axis=1)).astype(BF)
        for b in range(boots):
            out_ref[b * GRID : (b + 1) * GRID, group * LANES : (group + 1) * LANES] = (
                m[:, b * LANES : (b + 1) * LANES]
            )


def solve(slot, comp_weight, station_index, observed, counts, mine, grid_y):
    boots = min(mine, LANES // grid_y)
    slabs = DEPTHS * grid_y * boots // LANES
    stations = station_index.shape[1]
    const = jnp.asarray(constants(grid_y, boots))
    vmem = pltpu.VMEM
    whole = lambda a: pl.BlockSpec(a.shape, lambda i, n=a.ndim: (0,) * n)
    smem = pl.BlockSpec(memory_space=pltpu.SMEM)
    field = vmem((slabs, GRID, LANES), F32)
    at_stations = vmem((stations, LANES), F32)
    wide = 2 * boots * grid_y
    inputs = [station_index, observed, counts]
    return pl.pallas_call(
        functools.partial(solve_kernel, grid_y, boots, mine // boots),
        out_shape=jax.ShapeDtypeStruct((mine * GRID, DEPTHS * grid_y), BF),
        grid=(mine // boots,),
        in_specs=[smem, smem] + [whole(a) for a in inputs] + [pl.BlockSpec(memory_space=pl.ANY)],
        out_specs=pl.BlockSpec((boots * GRID, DEPTHS * grid_y), lambda i: (i, 0)),
        scratch_shapes=[
            vmem((layout(grid_y, boots).rows, 2 * LANES), BF),
            pltpu.SemaphoreType.DMA((3,)),
            vmem((stations, 2 * GRID), BF),
            vmem((2 * GRID, stations), BF),
            vmem((stations, 2 * wide), F32),
            at_stations,
            at_stations,
            at_stations,
            at_stations,
            vmem((stations, LANES), BF),
            vmem((LANES, stations), F32),
            vmem((5, DEPTHS, GRID, LANES), F32),
            vmem((stations, 5 * wide), BF),
            vmem((5, 2, wide // LANES, GRID, LANES), F32),
            vmem((2 * GRID, 5 * wide), BF),
            vmem((2 * GRID, slabs * 2 * LANES), BF),
            vmem((2 * GRID, slabs * 2 * LANES), BF),
            vmem((stations, 5 * LANES), BF),
            field,
            field,
            field,
            field,
        ],
        compiler_params=pltpu.CompilerParams(vmem_limit_bytes=56 * 1024 * 1024),
        cost_estimate=pl.CostEstimate(flops=10**10, bytes_accessed=10**7, transcendentals=0),
        name="solve",
    )(slot, comp_weight, *inputs, const)


def pick_kernel(grid_y, n_models, n_before, keep, cell_ref, *refs):
    models_refs, refs = refs[:n_models], refs[n_models:]
    before_refs, refs = refs[:n_before], refs[n_before:]
    if keep:
        refs[1][...] = models_refs[0][...]

    @pl.loop(0, cell_ref.shape[1] // CHUNK)
    def _(step):
        at = pl.ds(pl.multiple_of(step * CHUNK, CHUNK), CHUNK)
        place = cell_ref[:, at].astype(F32)
        wide = lambda row, rows: jnp.broadcast_to(row, (rows, CHUNK)).astype(BF)
        count_up = lambda rows: lax.broadcasted_iota(jnp.int32, (rows, CHUNK), 0).astype(F32).astype(BF)
        here_y = count_up(grid_y) == wide(place[1:2], grid_y)
        here_y = jnp.where(here_y, jnp.ones((grid_y, CHUNK), BF), jnp.zeros((grid_y, CHUNK), BF))
        z_row = wide(place[2:3], 16)
        none = jnp.zeros((16, CHUNK), BF)
        chosen = []
        for z in range(DEPTHS):
            here_z = z_row == jnp.full((16, CHUNK), z, BF)
            chosen += [jnp.where(here_z, here_y[i : i + 16], none) for i in range(0, grid_y, 16)]
        models = jnp.concatenate([ref[...] for ref in models_refs], axis=0)
        found = dot(models, jnp.concatenate(chosen, axis=0)).astype(BF)
        at_x = count_up(GRID) == wide(place[0:1], GRID)
        parts = [ref[:, at].astype(F32) for ref in before_refs]
        for b in range(models.shape[0] // GRID):
            part = jnp.where(at_x, found[b * GRID : (b + 1) * GRID], jnp.zeros((GRID, CHUNK), BF))
            while part.shape[0] > 16:
                half = part.shape[0] // 2
                part = part[:half] + part[half:]
            parts.append(jnp.sum(part.astype(F32), axis=0, keepdims=True))
        refs[0][:, at] = jnp.concatenate(parts, axis=0).astype(BF)


def pick(cells, models, before=(), grid_y=0, keep=False):
    rows = sum(m.shape[0] for m in models)
    boots = rows // GRID + sum(a.shape[0] for a in before)
    count = cells.shape[1]
    vmem = pl.BlockSpec(memory_space=pltpu.VMEM)
    shapes = [jax.ShapeDtypeStruct((boots, count), BF)]
    if keep:
        shapes.append(jax.ShapeDtypeStruct(models[0].shape, BF))
    found = pl.pallas_call(
        functools.partial(pick_kernel, grid_y, len(models), len(before), keep),
        out_shape=shapes,
        in_specs=[vmem] * (1 + len(models) + len(before)),
        out_specs=[vmem] * len(shapes),
        compiler_params=pltpu.CompilerParams(vmem_limit_bytes=40 * 1024 * 1024),
        cost_estimate=pl.CostEstimate(
            flops=2 * rows * DEPTHS * grid_y * count, bytes_accessed=10**6, transcendentals=0
        ),
        name="pick",
    )(cells, *models, *before)
    return found if keep else found[0]


def local(wide, cell_index, station_index, observed, comp_weight, counts):
    boots = counts.shape[0]
    grid_y = cell_index.shape[1] * wide // (GRID * DEPTHS)
    team = TEAM if wide % TEAM == 0 and boots % TEAM == 0 else 1
    while 4 * boots * grid_y < team * 2 * LANES:
        team //= 2
    slot = lax.axis_index("wide").astype(jnp.int32) & (team - 1)

    def swap(a, k):
        return lax.ppermute(a, "wide", [(i, i ^ k) for i in range(wide)])

    theirs = [swap(cell_index, k) for k in range(2, team, 2)]
    models = solve(slot.reshape(1), comp_weight, station_index, observed, counts, boots // team, grid_y)
    models, theirs = lax.optimization_barrier((models, theirs))
    if team > 1:
        shared = swap(models, 1)
        far = []
        for k, cells in enumerate(theirs):
            ours = pick(cells, [models], grid_y=grid_y, keep=k == 0)
            if k == 0:
                ours, models = ours
            far.append(swap(pick(cells, [shared], [ours], grid_y=grid_y), 2 * k + 2))
        found = [pick(cell_index, [models, shared], grid_y=grid_y)] + far
    else:
        found = [pick(cell_index, [models], grid_y=grid_y)]
    mine = boots // team
    got = [a[i * mine : (i + 1) * mine] for a in found for i in range(a.shape[0] // mine)]
    blocks = []
    for member in range(team):
        block = got[member]
        for other in range(1, team):
            block = jnp.where(slot == other, got[member ^ other], block)
        blocks.append(block.astype(F32))
    return jnp.concatenate(blocks, axis=0)


def solution(mesh):
    in_specs = (P(None, "wide"), P(None, "groups"), P(None, "groups"), P(), P("groups", None))
    out_specs = P("groups", "wide")
    fn = functools.partial(local, mesh.shape["wide"])
    return jax.shard_map(fn, mesh=mesh, in_specs=in_specs, out_specs=out_specs, check_vma=False)
```

```python
import functools

import jax
import jax.numpy as jnp
import ml_dtypes
import numpy as np
from jax import lax
from jax.experimental import pallas as pl
from jax.experimental.pallas import tpu as pltpu
from jax.sharding import PartitionSpec as P

IRLS = 2
CG_STEPS = 2
GRID = 128
DEPTHS = 16
LANES = 128
TEAM = 4
PARTS = 2
CHUNK = 2048
ROWS = 32

station_height = 2.0
focusing = 0.1
damping = 0.0002

PARITY = ((0, 0), (1, 1), (1, 0), (0, 0), (0, 1))
BF = jnp.bfloat16
F32 = jnp.float32


def offset_table(grid_y):
    one = np.float32
    dx = np.arange(GRID, dtype=one)[:, None, None]
    dy = np.arange(grid_y, dtype=one)[None, :, None]
    dz = (np.arange(DEPTHS, dtype=one) + one(0.5) + one(station_height))[None, None, :]
    radius2 = dx * dx + dy * dy + dz * dz
    strength = one(1) / (radius2 * radius2 * np.sqrt(radius2))
    three = one(3)
    kinds = [
        (three * dx * dx - radius2) * strength,
        three * dx * dy * strength,
        three * dx * dz * strength,
        (three * dy * dy - radius2) * strength,
        three * dy * dz * strength,
    ]
    return [k.astype(ml_dtypes.bfloat16).astype(np.float64) for k in kinds]


def angles(size):
    return 2 * np.pi * np.outer(np.arange(size), np.arange(size) + 0.5) / (2 * size)


def basis(size):
    return np.concatenate([np.cos(angles(size)), np.sin(angles(size))], axis=1)


def spectrum(values, odd, size):
    if odd:
        trig = 2 * np.sin(angles(size))
    else:
        trig = np.cos(angles(size)) * np.where(np.arange(size) == 0, 1, 2)[:, None]
    return np.tensordot(trig.T / size, values, axes=(1, 0))


def split(matrix):
    high = matrix.astype(ml_dtypes.bfloat16)
    low = (matrix - high.astype(np.float64)).astype(ml_dtypes.bfloat16)
    return high, low


class Layout:
    def __init__(self, parts):
        self.at = {}
        row = 0
        for name, rows in parts:
            self.at[name] = (row, rows)
            row += rows
        self.rows = row


def layout(grid_y, boots):
    return Layout(
        [
            ("base_x", GRID),
            ("base_xt2", 2 * GRID),
            ("station_y2", 4 * grid_y),
            ("spread", 3 * LANES),
            ("widen", LANES * max(1, LANES // grid_y // 2)),
            ("compact", 5 * DEPTHS * grid_y // LANES // 2 * GRID),
            ("field_y2", 2 * LANES),
            ("field_yt", 2 * LANES),
            ("back", 5 * LANES),
            ("same", LANES),
            ("regroup", boots * LANES * max(1, boots // 2)),
            ("table", 5 * DEPTHS // 2 * GRID),
        ]
    )


@functools.lru_cache(maxsize=None)
def constants(grid_y, boots):
    deep = LANES // grid_y // boots
    copies = LANES // grid_y
    table = []
    for values, (odd_x, odd_y) in zip(offset_table(grid_y), PARITY):
        t = spectrum(values, odd_x, GRID)
        t = np.moveaxis(spectrum(np.moveaxis(t, 1, 0), odd_y, grid_y), 0, 1)
        table.append(np.moveaxis(t, 2, 0))
    table = np.stack(table)
    compact = table.reshape(-1, copies, GRID, grid_y).transpose(0, 2, 1, 3).reshape(-1, 2, GRID, LANES)
    compact = compact.transpose(0, 2, 1, 3).reshape(-1, 2 * LANES)
    widen = np.einsum("de,yz,c->dyecz", np.eye(copies), np.eye(grid_y), np.ones(copies)).reshape(LANES, -1)
    if copies > 1:
        widen = np.concatenate(np.split(widen, copies // 2, axis=1), axis=0)
    table = np.tile(table, (1, 1, 1, copies))
    table = table.reshape(5, DEPTHS // 2, 2, GRID, LANES).transpose(0, 1, 3, 2, 4)

    base_x = basis(GRID)
    base_y = basis(grid_y).reshape(grid_y, 2, grid_y)
    field_y = np.einsum("de,ab,yhl->dayehbl", np.eye(deep), np.eye(boots), base_y).reshape(LANES, 2 * LANES)
    odd_y = np.stack([-base_y[:, 1], base_y[:, 0]], axis=1)
    station_y = [np.tile(b[:, :, None], (1, 1, boots, 1)).reshape(grid_y, -1) for b in (base_y, odd_y)]
    spread = np.zeros((5, deep, boots, grid_y, copies, grid_y))
    for c in range(5):
        for copy in range(copies):
            spread[c, 0, copy % boots, c, copy, :] = 1
    spread = spread.reshape(5, LANES, LANES)
    back = spread.transpose(0, 2, 1).reshape(5 * LANES, LANES)
    spread = np.concatenate([spread, np.zeros((1, LANES, LANES))])
    spread = spread.reshape(3, 2, LANES, LANES).transpose(0, 2, 1, 3)
    same = np.einsum("ab,dc,yz->daycbz", np.eye(boots), np.ones((deep, deep)), np.ones((grid_y, grid_y)))
    same = same.reshape(LANES, LANES)
    regroup = np.einsum("st,de,ab,yz->sdaybtez", *[np.eye(n) for n in (boots, deep, boots, grid_y)])
    regroup = regroup.reshape(boots * LANES, boots * LANES)
    if boots > 2:
        regroup = np.concatenate(np.split(regroup, boots // 2, axis=1), axis=0)
    y_high, y_low = split(field_y)
    x_high, x_low = split(base_x.T)
    parts = dict(
        base_x=base_x,
        base_xt2=np.concatenate([x_high, x_low], axis=1),
        field_y2=np.concatenate([y_high, y_low], axis=0),
        field_yt=field_y.T,
        station_y2=np.concatenate([part for b in station_y for part in split(b)]),
        spread=spread.reshape(3 * LANES, 2 * LANES),
        back=back,
        same=same,
        regroup=regroup,
        widen=widen,
        compact=compact,
        table=table.reshape(-1, 2 * LANES),
    )
    where = layout(grid_y, boots)
    whole = np.zeros((max(where.rows, 1 << 14), 2 * LANES), ml_dtypes.bfloat16)
    for name, (row, rows) in where.at.items():
        part = parts[name].astype(ml_dtypes.bfloat16)
        assert part.shape[0] == rows
        whole[row : row + rows, : part.shape[1]] = part
    return whole


def dot(a, b):
    return jnp.dot(a, b, preferred_element_type=F32)


def solve_kernel(
    grid_y,
    boots,
    steps,
    slot_ref,
    comp_ref,
    station_ref,
    observed_ref,
    counts_ref,
    source,
    out_ref,
    const,
    copied,
    pick_x,
    pick_xt,
    pick_y,
    weights,
    data,
    pred,
    image,
    values,
    rows,
    table_wide,
    spread_out,
    spec_q,
    spec_i,
    spec_f,
    spec_g,
    picked_in,
    models,
    residual,
    direction,
    penalty,
):
    deep = LANES // grid_y // boots
    slabs = DEPTHS // deep
    where = layout(grid_y, boots)
    table_row = where.at["table"][0]
    wide = 2 * boots * grid_y
    chunks = range(wide // LANES)
    bounds = [0, where.at["field_y2"][0], table_row, where.rows]
    copies = [
        pltpu.make_async_copy(source.at[a:b], const.at[a:b], copied.at[i])
        for i, (a, b) in enumerate(zip(bounds[:-1], bounds[1:]))
    ]

    def once(f):
        if steps == 1:
            f()
        else:
            pl.when(pl.program_id(0) == 0)(f)

    @once
    def _():
        for copy in copies:
            copy.start()

    def held(name, width=2 * LANES):
        row, count = where.at[name]
        return const[row : row + count, :width]

    def table(c, z, at):
        row = table_row + (c * (DEPTHS // 2) + z // 2) * GRID
        return const[row + at.start : row + at.stop, z % 2 * LANES : (z % 2 + 1) * LANES]

    stations = station_ref.shape[1]
    first = (slot_ref[0] * pl.num_programs(0) + pl.program_id(0)) * boots
    size = slabs // PARTS
    shares = [range(start, start + size) for start in range(0, slabs, size)]
    share_lanes = size * 2 * LANES

    def pieces(share):
        return [(slab, slice(row, row + ROWS)) for slab in share for row in range(0, GRID, ROWS)]


    rows[...] = jnp.zeros_like(rows)
    for b in range(boots):
        row = b * grid_y
        rows[row : row + 5, :] = observed_ref[...]
        count = counts_ref[pl.ds(first + b, 1), :].astype(F32)
        for c in range(5):
            rows[row + 8 + c : row + 9 + c, :] = count * comp_ref[c]
    rows[16:18, :] = station_ref[...].astype(F32)
    turned = jnp.transpose(rows[...])
    lane = lax.broadcasted_iota(jnp.int32, (1, LANES), 1)
    used = lane % grid_y < 5
    data[...] = jnp.where(used, turned, 0.0)
    weights[...] = jnp.where(used, pltpu.roll(turned, LANES - 8, 1), 0.0)
    values[...] = (weights[...] * data[...]).astype(BF)

    place_x = (lax.broadcasted_iota(jnp.int32, (GRID, stations), 0) == station_ref[0:1, :]).astype(F32).astype(BF)
    place_xt = (turned[:, 16:17] == lane.astype(F32)).astype(F32).astype(BF)
    place_yt = (turned[:, 17:18] == lane.astype(F32)).astype(F32)[:, :grid_y].astype(BF)

    @once
    def _():
        copies[0].wait()

    pick_xt[...] = dot(held("base_xt2", GRID), place_x).astype(BF)
    pick_x[...] = dot(place_xt, held("base_x")).astype(BF)
    station_y2 = held("station_y2", wide)
    for odd in range(2):
        high, low = [station_y2[(2 * odd + i) * grid_y : (2 * odd + i + 1) * grid_y] for i in range(2)]
        pick_y[:, odd * wide : (odd + 1) * wide] = dot(place_yt, high) + dot(place_yt, low)
    no_sum = jnp.zeros((8, LANES), F32)

    def trig(at, odd, chunk):
        lane = odd * wide + chunk * LANES
        return pick_y[at, lane : lane + LANES]

    def station_spectra():
        spread = held("spread")
        spread = jnp.concatenate([spread[i * LANES : (i + 1) * LANES] for i in range(3)], axis=1)
        spreads = dot(values[...], spread[:, : 5 * LANES])
        for row in range(0, stations, ROWS):
            at = slice(row, row + ROWS)
            for c, (_, odd_y) in enumerate(PARITY):
                e = spreads[at, c * LANES : (c + 1) * LANES]
                for chunk in chunks:
                    to = c * wide + chunk * LANES
                    spread_out[at, to : to + LANES] = (e * trig(at, odd_y, chunk)).astype(BF)
        spec = dot(pick_xt[...], spread_out[...])
        for c, (odd_x, _) in enumerate(PARITY):
            for hx in range(2):
                for chunk in chunks:
                    lane = c * wide + chunk * LANES
                    part = spec[hx * GRID : (hx + 1) * GRID, lane : lane + LANES]
                    spec_q[c, hx, chunk] = -part if odd_x * hx else part

    def back_project(receive):
        for share in shares:
            for row in range(0, GRID, 16):
                at = slice(row, row + 16)
                for chunk in chunks:
                    q = [[spec_q[c, hx, chunk, at, :] for hx in range(2)] for c in range(5)]
                    for z in range(share.start * deep, share.stop * deep):
                        t = [table_wide[c, z, at, :] for c in range(5)]
                        lane = z * wide + chunk * LANES
                        for hx in range(2):
                            total = t[0] * q[0][hx]
                            for c in range(1, 5):
                                total = total + t[c] * q[c][hx ^ PARITY[c][0]]
                            spec_g[hx * GRID + row : hx * GRID + row + 16, lane : lane + LANES] = total.astype(BF)
            lane = share.start * 2 * LANES
            along_x = dot(held("base_x"), spec_g[:, lane : lane + share_lanes]).astype(BF)
            along_x = [along_x[:, lane : lane + 2 * LANES] for lane in range(0, share_lanes, 2 * LANES)]
            receive(share, dot(jnp.concatenate(along_x, axis=0), held("field_yt", LANES)))

    def predict():
        for share in shares:
            r = residual[share.start : share.stop].reshape(len(share) * GRID, LANES).astype(BF)
            y = dot(jnp.concatenate([r, r], axis=1), held("field_y2")).astype(BF)
            y = jnp.concatenate([y[i * GRID : (i + 1) * GRID] for i in range(len(share))], axis=1)
            lane = share.start * 2 * LANES
            spec_f[:, lane : lane + share_lanes] = dot(held("base_xt2"), jnp.concatenate([y, y], axis=0)).astype(BF)

            for row in range(0, GRID, 16):
                at = [slice(hx * GRID + row, hx * GRID + row + 16) for hx in range(2)]
                for chunk in chunks:
                    total = [[None] * 2 for _ in range(5)]
                    for z in range(share.start * deep, share.stop * deep):
                        lane = z * wide + chunk * LANES
                        f = [spec_f[at[hx], lane : lane + LANES] for hx in range(2)]
                        for c, (odd_x, _) in enumerate(PARITY):
                            t = table(c, z, at[0])
                            for hx in range(2):
                                term = t * f[hx ^ odd_x]
                                total[c][hx] = term if total[c][hx] is None else total[c][hx] + term
                    for c, (odd_x, _) in enumerate(PARITY):
                        lane = c * wide + chunk * LANES
                        for hx in range(2):
                            part = total[c][hx]
                            if share is not shares[0]:
                                part = part + spec_i[at[hx], lane : lane + LANES]
                            if share is shares[-1] and odd_x * hx:
                                part = -part
                            spec_i[at[hx], lane : lane + LANES] = part

        picked = dot(pick_x[...], spec_i[...])
        for row in range(0, stations, ROWS):
            at = slice(row, row + ROWS)
            for c, (_, odd_y) in enumerate(PARITY):
                part = None
                for chunk in chunks:
                    lane = c * wide + chunk * LANES
                    term = picked[at, lane : lane + LANES] * trig(at, odd_y, chunk)
                    part = term if part is None else part + term
                picked_in[at, c * LANES : (c + 1) * LANES] = part.astype(BF)
        return dot(picked_in[...], held("back", LANES))

    def fold(a):
        return jnp.sum(a.reshape(a.shape[0] // 8, 8, LANES), axis=0)

    def totals_of(partials):
        rows_of = []
        for partial in partials:
            for _ in range(3):
                part = partial.astype(BF).astype(F32)
                rows_of.append(part)
                partial = partial - part
        if len(rows_of) % 2:
            rows_of.append(no_sum)
        sums = dot(jnp.concatenate(rows_of, axis=0).astype(BF), held("same", LANES))
        return [jnp.sum(sums[i * 24 : (i + 1) * 24], axis=0, keepdims=True) for i in range(len(partials))]

    def depth_weight(z):
        within = lax.broadcasted_iota(jnp.int32, (1, LANES), 1) // (boots * grid_y)
        depth = (within + z * deep).astype(F32) + 0.5 + station_height
        ratio = station_height / depth
        return ratio * ratio * ratio

    def round_of(outer, inner, carry):
        first = outer == 0 and inner == 0
        last = outer == IRLS - 1 and inner == CG_STEPS - 1
        fresh = inner == 0
        old_norm, old_step, old_curve = carry
        sums = [no_sum] * 3

        def penalty_at(slab, at):
            if outer == 0:
                return damping * depth_weight(slab) / (focusing * focusing)
            return penalty[slab, at]

        def receive(share, applied):
            norm, bend, cross = sums
            for slab, at in pieces(share):
                row = (slab - share.start) * GRID + at.start
                r = applied[row : row + ROWS]
                if fresh and outer:
                    m = models[slab, at]
                    p = damping * depth_weight(slab) / (m * m + focusing * focusing)
                    penalty[slab, at] = p
                    r = r - p * m
                else:
                    p = penalty_at(slab, at)
                if not fresh:
                    pd = p * direction[slab, at]
                    r = residual[slab, at] - old_step * (r + pd)
                    cross += fold(pd * r)
                residual[slab, at] = r
                square = r * r
                norm += fold(square)
                bend += fold(p * square)
            sums[:] = [norm, bend, cross]

        back_project(receive)
        if first:
            once(copies[2].wait)
        here = predict()
        weighted = weights[...] * here
        norm, bend, cross = sums
        if fresh:
            norm, curve = totals_of([norm, bend + fold(weighted * here)])
        else:
            norm, bend, cross = totals_of(
                [norm, bend + fold(weighted * here), cross + fold(weighted * image[...])]
            )
            ratio = norm / old_norm
            curve = bend + ratio * (2.0 * cross + ratio * old_curve)
        step = norm / curve
        if not last:
            if not fresh:
                here = here + ratio * image[...]
            now = step * here if first else pred[...] + step * here
            pred[...] = now
            if fresh:
                image[...] = here
                values[...] = (weights[...] * here).astype(BF)
            else:
                values[...] = (weights[...] * (data[...] - now)).astype(BF)
            station_spectra()
        for share in shares:
            for slab, at in pieces(share):
                d = residual[slab, at]
                if not fresh:
                    d = d + ratio * direction[slab, at]
                if fresh:
                    direction[slab, at] = d
                models[slab, at] = step * d if first else models[slab, at] + step * d
        return norm, step, curve

    @once
    def _():
        per = LANES // grid_y
        widen = held("widen")
        if per > 1:
            widen = jnp.concatenate([widen[i * LANES : (i + 1) * LANES] for i in range(per // 2)], axis=1)
        else:
            widen = widen[:, :LANES]
        compact = held("compact")
        blocks = 5 * DEPTHS // per
        compact = jnp.concatenate(
            [compact[i // 2 * GRID : (i // 2 + 1) * GRID, i % 2 * LANES : (i % 2 + 1) * LANES] for i in range(blocks)],
            axis=0,
        )
        widened = dot(compact, widen)
        for i in range(blocks):
            for z in range(per):
                table_wide[i * per // DEPTHS, i * per % DEPTHS + z] = widened[
                    i * GRID : (i + 1) * GRID, z * LANES : (z + 1) * LANES
                ]

    station_spectra()

    @once
    def _():
        copies[1].wait()

    carry = (None, None, None)
    for outer in range(IRLS):
        for inner in range(CG_STEPS):
            carry = round_of(outer, inner, carry)

    for group in range(slabs // boots):
        m = jnp.concatenate([models[group * boots + i].astype(BF) for i in range(boots)], axis=1)
        if boots > 1:
            regroup = held("regroup")
            regroup = [regroup[i * boots * LANES : (i + 1) * boots * LANES] for i in range(boots // 2)]
            m = dot(m, jnp.concatenate(regroup, axis=1)).astype(BF)
        for b in range(boots):
            out_ref[b * GRID : (b + 1) * GRID, group * LANES : (group + 1) * LANES] = (
                m[:, b * LANES : (b + 1) * LANES]
            )


def solve(slot, comp_weight, station_index, observed, counts, mine, grid_y):
    boots = min(mine, LANES // grid_y)
    slabs = DEPTHS * grid_y * boots // LANES
    stations = station_index.shape[1]
    const = jnp.asarray(constants(grid_y, boots))
    vmem = pltpu.VMEM
    whole = lambda a: pl.BlockSpec(a.shape, lambda i, n=a.ndim: (0,) * n)
    smem = pl.BlockSpec(memory_space=pltpu.SMEM)
    field = vmem((slabs, GRID, LANES), F32)
    at_stations = vmem((stations, LANES), F32)
    wide = 2 * boots * grid_y
    inputs = [station_index, observed, counts]
    return pl.pallas_call(
        functools.partial(solve_kernel, grid_y, boots, mine // boots),
        out_shape=jax.ShapeDtypeStruct((mine * GRID, DEPTHS * grid_y), BF),
        grid=(mine // boots,),
        in_specs=[smem, smem] + [whole(a) for a in inputs] + [pl.BlockSpec(memory_space=pl.ANY)],
        out_specs=pl.BlockSpec((boots * GRID, DEPTHS * grid_y), lambda i: (i, 0)),
        scratch_shapes=[
            vmem((layout(grid_y, boots).rows, 2 * LANES), BF),
            pltpu.SemaphoreType.DMA((3,)),
            vmem((stations, 2 * GRID), BF),
            vmem((2 * GRID, stations), BF),
            vmem((stations, 2 * wide), F32),
            at_stations,
            at_stations,
            at_stations,
            at_stations,
            vmem((stations, LANES), BF),
            vmem((LANES, stations), F32),
            vmem((5, DEPTHS, GRID, LANES), F32),
            vmem((stations, 5 * wide), BF),
            vmem((5, 2, wide // LANES, GRID, LANES), F32),
            vmem((2 * GRID, 5 * wide), BF),
            vmem((2 * GRID, slabs * 2 * LANES), BF),
            vmem((2 * GRID, slabs * 2 * LANES), BF),
            vmem((stations, 5 * LANES), BF),
            field,
            field,
            field,
            field,
        ],
        compiler_params=pltpu.CompilerParams(vmem_limit_bytes=56 * 1024 * 1024),
        cost_estimate=pl.CostEstimate(flops=10**10, bytes_accessed=10**7, transcendentals=0),
        name="solve",
    )(slot, comp_weight, *inputs, const)


def pick_kernel(grid_y, n_models, n_before, keep, cell_ref, *refs):
    models_refs, refs = refs[:n_models], refs[n_models:]
    before_refs, refs = refs[:n_before], refs[n_before:]
    if keep:
        refs[1][...] = models_refs[0][...]

    @pl.loop(0, cell_ref.shape[1] // CHUNK)
    def _(step):
        at = pl.ds(pl.multiple_of(step * CHUNK, CHUNK), CHUNK)
        place = cell_ref[:, at].astype(F32)
        wide = lambda row, rows: jnp.broadcast_to(row, (rows, CHUNK)).astype(BF)
        count_up = lambda rows: lax.broadcasted_iota(jnp.int32, (rows, CHUNK), 0).astype(F32).astype(BF)
        here_y = count_up(grid_y) == wide(place[1:2], grid_y)
        here_y = jnp.where(here_y, jnp.ones((grid_y, CHUNK), BF), jnp.zeros((grid_y, CHUNK), BF))
        z_row = wide(place[2:3], 16)
        none = jnp.zeros((16, CHUNK), BF)
        chosen = []
        for z in range(DEPTHS):
            here_z = z_row == jnp.full((16, CHUNK), z, BF)
            chosen += [jnp.where(here_z, here_y[i : i + 16], none) for i in range(0, grid_y, 16)]
        models = jnp.concatenate([ref[...] for ref in models_refs], axis=0)
        found = dot(models, jnp.concatenate(chosen, axis=0)).astype(BF)
        at_x = count_up(GRID) == wide(place[0:1], GRID)
        parts = [ref[:, at].astype(F32) for ref in before_refs]
        for b in range(models.shape[0] // GRID):
            part = jnp.where(at_x, found[b * GRID : (b + 1) * GRID], jnp.zeros((GRID, CHUNK), BF))
            while part.shape[0] > 16:
                half = part.shape[0] // 2
                part = part[:half] + part[half:]
            parts.append(jnp.sum(part.astype(F32), axis=0, keepdims=True))
        refs[0][:, at] = jnp.concatenate(parts, axis=0).astype(BF)


def pick(cells, models, before=(), grid_y=0, keep=False):
    rows = sum(m.shape[0] for m in models)
    boots = rows // GRID + sum(a.shape[0] for a in before)
    count = cells.shape[1]
    vmem = pl.BlockSpec(memory_space=pltpu.VMEM)
    shapes = [jax.ShapeDtypeStruct((boots, count), BF)]
    if keep:
        shapes.append(jax.ShapeDtypeStruct(models[0].shape, BF))
    found = pl.pallas_call(
        functools.partial(pick_kernel, grid_y, len(models), len(before), keep),
        out_shape=shapes,
        in_specs=[vmem] * (1 + len(models) + len(before)),
        out_specs=[vmem] * len(shapes),
        compiler_params=pltpu.CompilerParams(vmem_limit_bytes=40 * 1024 * 1024),
        cost_estimate=pl.CostEstimate(
            flops=2 * rows * DEPTHS * grid_y * count, bytes_accessed=10**6, transcendentals=0
        ),
        name="pick",
    )(cells, *models, *before)
    return found if keep else found[0]


def local(wide, cell_index, station_index, observed, comp_weight, counts):
    boots = counts.shape[0]
    grid_y = cell_index.shape[1] * wide // (GRID * DEPTHS)
    team = TEAM if wide % TEAM == 0 and boots % TEAM == 0 else 1
    while 4 * boots * grid_y < team * 2 * LANES:
        team //= 2
    slot = lax.axis_index("wide").astype(jnp.int32) & (team - 1)

    def swap(a, k):
        return lax.ppermute(a, "wide", [(i, i ^ k) for i in range(wide)])

    theirs = [swap(cell_index, k) for k in range(2, team, 2)]
    models = solve(slot.reshape(1), comp_weight, station_index, observed, counts, boots // team, grid_y)
    models, theirs = lax.optimization_barrier((models, theirs))
    if team > 1:
        shared = swap(models, 1)
        far = []
        for k, cells in enumerate(theirs):
            ours = pick(cells, [models], grid_y=grid_y, keep=k == 0)
            if k == 0:
                ours, models = ours
            far.append(swap(pick(cells, [shared], [ours], grid_y=grid_y), 2 * k + 2))
        found = [pick(cell_index, [models, shared], grid_y=grid_y)] + far
    else:
        found = [pick(cell_index, [models], grid_y=grid_y)]
    mine = boots // team
    got = [a[i * mine : (i + 1) * mine] for a in found for i in range(a.shape[0] // mine)]
    blocks = []
    for member in range(team):
        block = got[member]
        for other in range(1, team):
            block = jnp.where(slot == other, got[member ^ other], block)
        blocks.append(block.astype(F32))
    return jnp.concatenate(blocks, axis=0)


def solution(mesh):
    in_specs = (P(None, "wide"), P(None, "groups"), P(None, "groups"), P(), P("groups", None))
    out_specs = P("groups", "wide")
    fn = functools.partial(local, mesh.shape["wide"])
    return jax.shard_map(fn, mesh=mesh, in_specs=in_specs, out_specs=out_specs, check_vma=False)
```

```python
import functools

import jax
import jax.numpy as jnp
import ml_dtypes
import numpy as np
from jax import lax
from jax.experimental import pallas as pl
from jax.experimental.pallas import tpu as pltpu
from jax.sharding import PartitionSpec as P

IRLS = 2
CG_STEPS = 2
GRID = 128
DEPTHS = 16
LANES = 128
TEAM = 4
PARTS = 2
CHUNK = 2048
ROWS = 32

station_height = 2.0
focusing = 0.1
damping = 0.0002

PARITY = ((0, 0), (1, 1), (1, 0), (0, 0), (0, 1))
BF = jnp.bfloat16
F32 = jnp.float32


def offset_table(grid_y):
    one = np.float32
    dx = np.arange(GRID, dtype=one)[:, None, None]
    dy = np.arange(grid_y, dtype=one)[None, :, None]
    dz = (np.arange(DEPTHS, dtype=one) + one(0.5) + one(station_height))[None, None, :]
    radius2 = dx * dx + dy * dy + dz * dz
    strength = one(1) / (radius2 * radius2 * np.sqrt(radius2))
    three = one(3)
    kinds = [
        (three * dx * dx - radius2) * strength,
        three * dx * dy * strength,
        three * dx * dz * strength,
        (three * dy * dy - radius2) * strength,
        three * dy * dz * strength,
    ]
    return [k.astype(ml_dtypes.bfloat16).astype(np.float64) for k in kinds]


def angles(size):
    return 2 * np.pi * np.outer(np.arange(size), np.arange(size) + 0.5) / (2 * size)


def basis(size):
    return np.concatenate([np.cos(angles(size)), np.sin(angles(size))], axis=1)


def spectrum(values, odd, size):
    if odd:
        trig = 2 * np.sin(angles(size))
    else:
        trig = np.cos(angles(size)) * np.where(np.arange(size) == 0, 1, 2)[:, None]
    return np.tensordot(trig.T / size, values, axes=(1, 0))


def split(matrix):
    high = matrix.astype(ml_dtypes.bfloat16)
    low = (matrix - high.astype(np.float64)).astype(ml_dtypes.bfloat16)
    return high, low


class Layout:
    def __init__(self, parts):
        self.at = {}
        row = 0
        for name, rows in parts:
            self.at[name] = (row, rows)
            row += rows
        self.rows = row


def layout(grid_y, boots):
    return Layout(
        [
            ("base_x", GRID),
            ("base_xt2", 2 * GRID),
            ("station_y2", 4 * grid_y),
            ("spread", 3 * LANES),
            ("table", 5 * DEPTHS // 2 * GRID),
            ("field_y2", 2 * LANES),
            ("field_yt", 2 * LANES),
            ("back", 5 * LANES),
            ("same", LANES),
            ("regroup", boots * LANES * max(1, boots // 2)),
        ]
    )


@functools.lru_cache(maxsize=None)
def constants(grid_y, boots):
    deep = LANES // grid_y // boots
    copies = LANES // grid_y
    table = []
    for values, (odd_x, odd_y) in zip(offset_table(grid_y), PARITY):
        t = spectrum(values, odd_x, GRID)
        t = np.moveaxis(spectrum(np.moveaxis(t, 1, 0), odd_y, grid_y), 0, 1)
        table.append(np.tile(np.moveaxis(t, 2, 0), (1, 1, copies)))
    table = np.stack(table).reshape(5, DEPTHS // 2, 2, GRID, LANES).transpose(0, 1, 3, 2, 4)

    base_x = basis(GRID)
    base_y = basis(grid_y).reshape(grid_y, 2, grid_y)
    field_y = np.einsum("de,ab,yhl->dayehbl", np.eye(deep), np.eye(boots), base_y).reshape(LANES, 2 * LANES)
    odd_y = np.stack([-base_y[:, 1], base_y[:, 0]], axis=1)
    station_y = [np.tile(b[:, :, None], (1, 1, boots, 1)).reshape(grid_y, -1) for b in (base_y, odd_y)]
    spread = np.zeros((5, deep, boots, grid_y, copies, grid_y))
    for c in range(5):
        for copy in range(copies):
            spread[c, 0, copy % boots, c, copy, :] = 1
    spread = spread.reshape(5, LANES, LANES)
    back = spread.transpose(0, 2, 1).reshape(5 * LANES, LANES)
    spread = np.concatenate([spread, np.zeros((1, LANES, LANES))])
    spread = spread.reshape(3, 2, LANES, LANES).transpose(0, 2, 1, 3)
    same = np.einsum("ab,dc,yz->daycbz", np.eye(boots), np.ones((deep, deep)), np.ones((grid_y, grid_y)))
    same = same.reshape(LANES, LANES)
    regroup = np.einsum("st,de,ab,yz->sdaybtez", *[np.eye(n) for n in (boots, deep, boots, grid_y)])
    regroup = regroup.reshape(boots * LANES, boots * LANES)
    if boots > 2:
        regroup = np.concatenate(np.split(regroup, boots // 2, axis=1), axis=0)
    y_high, y_low = split(field_y)
    x_high, x_low = split(base_x.T)
    parts = dict(
        base_x=base_x,
        base_xt2=np.concatenate([x_high, x_low], axis=1),
        field_y2=np.concatenate([y_high, y_low], axis=0),
        field_yt=field_y.T,
        station_y2=np.concatenate([part for b in station_y for part in split(b)]),
        spread=spread.reshape(3 * LANES, 2 * LANES),
        back=back,
        same=same,
        regroup=regroup,
        table=table.reshape(-1, 2 * LANES),
    )
    where = layout(grid_y, boots)
    whole = np.zeros((max(where.rows, 1 << 14), 2 * LANES), ml_dtypes.bfloat16)
    for name, (row, rows) in where.at.items():
        part = parts[name].astype(ml_dtypes.bfloat16)
        assert part.shape[0] == rows
        whole[row : row + rows, : part.shape[1]] = part
    return whole


def dot(a, b):
    return jnp.dot(a, b, preferred_element_type=F32)


def solve_kernel(
    grid_y,
    boots,
    steps,
    slot_ref,
    comp_ref,
    station_ref,
    observed_ref,
    counts_ref,
    source,
    out_ref,
    const,
    copied,
    pick_x,
    pick_xt,
    pick_y,
    weights,
    data,
    pred,
    image,
    values,
    rows,
    table_wide,
    spread_out,
    spec_q,
    spec_i,
    spec_f,
    spec_g,
    picked_in,
    models,
    residual,
    direction,
    penalty,
):
    deep = LANES // grid_y // boots
    slabs = DEPTHS // deep
    where = layout(grid_y, boots)
    table_row, table_rows = where.at["table"]
    wide = 2 * boots * grid_y
    chunks = range(wide // LANES)
    bounds = [0, table_row, table_row + table_rows, where.rows]
    copies = [
        pltpu.make_async_copy(source.at[a:b], const.at[a:b], copied.at[i])
        for i, (a, b) in enumerate(zip(bounds[:-1], bounds[1:]))
    ]

    def once(f):
        if steps == 1:
            f()
        else:
            pl.when(pl.program_id(0) == 0)(f)

    @once
    def _():
        for copy in copies:
            copy.start()

    def held(name, width=2 * LANES):
        row, count = where.at[name]
        return const[row : row + count, :width]

    def table(c, z, at):
        row = table_row + (c * (DEPTHS // 2) + z // 2) * GRID
        return const[row + at.start : row + at.stop, z % 2 * LANES : (z % 2 + 1) * LANES]

    stations = station_ref.shape[1]
    first = (slot_ref[0] * pl.num_programs(0) + pl.program_id(0)) * boots
    size = slabs // PARTS
    shares = [range(start, start + size) for start in range(0, slabs, size)]
    share_lanes = size * 2 * LANES

    def pieces(share):
        return [(slab, slice(row, row + ROWS)) for slab in share for row in range(0, GRID, ROWS)]


    rows[...] = jnp.zeros_like(rows)
    for b in range(boots):
        row = b * grid_y
        rows[row : row + 5, :] = observed_ref[...]
        count = counts_ref[pl.ds(first + b, 1), :].astype(F32)
        for c in range(5):
            rows[row + 8 + c : row + 9 + c, :] = count * comp_ref[c]
    rows[16:18, :] = station_ref[...].astype(F32)
    turned = jnp.transpose(rows[...])
    lane = lax.broadcasted_iota(jnp.int32, (1, LANES), 1)
    used = lane % grid_y < 5
    data[...] = jnp.where(used, turned, 0.0)
    weights[...] = jnp.where(used, pltpu.roll(turned, LANES - 8, 1), 0.0)
    values[...] = (weights[...] * data[...]).astype(BF)

    place_x = (lax.broadcasted_iota(jnp.int32, (GRID, stations), 0) == station_ref[0:1, :]).astype(F32).astype(BF)
    place_xt = (turned[:, 16:17] == lane.astype(F32)).astype(F32).astype(BF)
    place_yt = (turned[:, 17:18] == lane.astype(F32)).astype(F32)[:, :grid_y].astype(BF)

    @once
    def _():
        copies[0].wait()

    pick_xt[...] = dot(held("base_xt2", GRID), place_x).astype(BF)
    pick_x[...] = dot(place_xt, held("base_x")).astype(BF)
    station_y2 = held("station_y2", wide)
    for odd in range(2):
        high, low = [station_y2[(2 * odd + i) * grid_y : (2 * odd + i + 1) * grid_y] for i in range(2)]
        pick_y[:, odd * wide : (odd + 1) * wide] = dot(place_yt, high) + dot(place_yt, low)
    no_sum = jnp.zeros((8, LANES), F32)

    def trig(at, odd, chunk):
        lane = odd * wide + chunk * LANES
        return pick_y[at, lane : lane + LANES]

    def station_spectra():
        spread = held("spread")
        spread = jnp.concatenate([spread[i * LANES : (i + 1) * LANES] for i in range(3)], axis=1)
        spreads = dot(values[...], spread[:, : 5 * LANES])
        for row in range(0, stations, ROWS):
            at = slice(row, row + ROWS)
            for c, (_, odd_y) in enumerate(PARITY):
                e = spreads[at, c * LANES : (c + 1) * LANES]
                for chunk in chunks:
                    to = c * wide + chunk * LANES
                    spread_out[at, to : to + LANES] = (e * trig(at, odd_y, chunk)).astype(BF)
        spec = dot(pick_xt[...], spread_out[...])
        for c, (odd_x, _) in enumerate(PARITY):
            for hx in range(2):
                for chunk in chunks:
                    lane = c * wide + chunk * LANES
                    part = spec[hx * GRID : (hx + 1) * GRID, lane : lane + LANES]
                    spec_q[c, hx, chunk] = -part if odd_x * hx else part

    def back_project(receive):
        for share in shares:
            for row in range(0, GRID, 16):
                at = slice(row, row + 16)
                for chunk in chunks:
                    q = [[spec_q[c, hx, chunk, at, :] for hx in range(2)] for c in range(5)]
                    for z in range(share.start * deep, share.stop * deep):
                        t = [table_wide[c, z, at, :] for c in range(5)]
                        lane = z * wide + chunk * LANES
                        for hx in range(2):
                            total = t[0] * q[0][hx]
                            for c in range(1, 5):
                                total = total + t[c] * q[c][hx ^ PARITY[c][0]]
                            spec_g[hx * GRID + row : hx * GRID + row + 16, lane : lane + LANES] = total.astype(BF)
            lane = share.start * 2 * LANES
            along_x = dot(held("base_x"), spec_g[:, lane : lane + share_lanes]).astype(BF)
            along_x = [along_x[:, lane : lane + 2 * LANES] for lane in range(0, share_lanes, 2 * LANES)]
            receive(share, dot(jnp.concatenate(along_x, axis=0), held("field_yt", LANES)))

    def predict():
        for share in shares:
            r = residual[share.start : share.stop].reshape(len(share) * GRID, LANES).astype(BF)
            y = dot(jnp.concatenate([r, r], axis=1), held("field_y2")).astype(BF)
            y = jnp.concatenate([y[i * GRID : (i + 1) * GRID] for i in range(len(share))], axis=1)
            lane = share.start * 2 * LANES
            spec_f[:, lane : lane + share_lanes] = dot(held("base_xt2"), jnp.concatenate([y, y], axis=0)).astype(BF)

            for row in range(0, GRID, 16):
                at = [slice(hx * GRID + row, hx * GRID + row + 16) for hx in range(2)]
                for chunk in chunks:
                    total = [[None] * 2 for _ in range(5)]
                    for z in range(share.start * deep, share.stop * deep):
                        lane = z * wide + chunk * LANES
                        f = [spec_f[at[hx], lane : lane + LANES] for hx in range(2)]
                        for c, (odd_x, _) in enumerate(PARITY):
                            t = table(c, z, at[0])
                            for hx in range(2):
                                term = t * f[hx ^ odd_x]
                                total[c][hx] = term if total[c][hx] is None else total[c][hx] + term
                    for c, (odd_x, _) in enumerate(PARITY):
                        lane = c * wide + chunk * LANES
                        for hx in range(2):
                            part = total[c][hx]
                            if share is not shares[0]:
                                part = part + spec_i[at[hx], lane : lane + LANES]
                            if share is shares[-1] and odd_x * hx:
                                part = -part
                            spec_i[at[hx], lane : lane + LANES] = part

        picked = dot(pick_x[...], spec_i[...])
        for row in range(0, stations, ROWS):
            at = slice(row, row + ROWS)
            for c, (_, odd_y) in enumerate(PARITY):
                part = None
                for chunk in chunks:
                    lane = c * wide + chunk * LANES
                    term = picked[at, lane : lane + LANES] * trig(at, odd_y, chunk)
                    part = term if part is None else part + term
                picked_in[at, c * LANES : (c + 1) * LANES] = part.astype(BF)
        return dot(picked_in[...], held("back", LANES))

    def fold(a):
        return jnp.sum(a.reshape(a.shape[0] // 8, 8, LANES), axis=0)

    def totals_of(partials):
        rows_of = []
        for partial in partials:
            for _ in range(3):
                part = partial.astype(BF).astype(F32)
                rows_of.append(part)
                partial = partial - part
        if len(rows_of) % 2:
            rows_of.append(no_sum)
        sums = dot(jnp.concatenate(rows_of, axis=0).astype(BF), held("same", LANES))
        return [jnp.sum(sums[i * 24 : (i + 1) * 24], axis=0, keepdims=True) for i in range(len(partials))]

    def depth_weight(z):
        within = lax.broadcasted_iota(jnp.int32, (1, LANES), 1) // (boots * grid_y)
        depth = (within + z * deep).astype(F32) + 0.5 + station_height
        ratio = station_height / depth
        return ratio * ratio * ratio

    def round_of(outer, inner, carry):
        first = outer == 0 and inner == 0
        last = outer == IRLS - 1 and inner == CG_STEPS - 1
        fresh = inner == 0
        old_norm, old_step, old_curve = carry
        sums = [no_sum] * 3

        def penalty_at(slab, at):
            if outer == 0:
                return damping * depth_weight(slab) / (focusing * focusing)
            return penalty[slab, at]

        def receive(share, applied):
            norm, bend, cross = sums
            for slab, at in pieces(share):
                row = (slab - share.start) * GRID + at.start
                r = applied[row : row + ROWS]
                if fresh and outer:
                    m = models[slab, at]
                    p = damping * depth_weight(slab) / (m * m + focusing * focusing)
                    penalty[slab, at] = p
                    r = r - p * m
                else:
                    p = penalty_at(slab, at)
                if not fresh:
                    pd = p * direction[slab, at]
                    r = residual[slab, at] - old_step * (r + pd)
                    cross += fold(pd * r)
                residual[slab, at] = r
                square = r * r
                norm += fold(square)
                bend += fold(p * square)
            sums[:] = [norm, bend, cross]

        back_project(receive)
        here = predict()
        weighted = weights[...] * here
        norm, bend, cross = sums
        if fresh:
            norm, curve = totals_of([norm, bend + fold(weighted * here)])
        else:
            norm, bend, cross = totals_of(
                [norm, bend + fold(weighted * here), cross + fold(weighted * image[...])]
            )
            ratio = norm / old_norm
            curve = bend + ratio * (2.0 * cross + ratio * old_curve)
        step = norm / curve
        if not last:
            if not fresh:
                here = here + ratio * image[...]
            now = step * here if first else pred[...] + step * here
            pred[...] = now
            if fresh:
                image[...] = here
                values[...] = (weights[...] * here).astype(BF)
            else:
                values[...] = (weights[...] * (data[...] - now)).astype(BF)
            station_spectra()
        for share in shares:
            for slab, at in pieces(share):
                d = residual[slab, at]
                if not fresh:
                    d = d + ratio * direction[slab, at]
                if fresh:
                    direction[slab, at] = d
                models[slab, at] = step * d if first else models[slab, at] + step * d
        return norm, step, curve

    station_spectra()

    @once
    def _():
        copies[1].wait()
        copies[2].wait()
        for c in range(5):
            for z in range(DEPTHS):
                table_wide[c, z] = table(c, z, slice(0, GRID)).astype(F32)

    carry = (None, None, None)
    for outer in range(IRLS):
        for inner in range(CG_STEPS):
            carry = round_of(outer, inner, carry)

    for group in range(slabs // boots):
        m = jnp.concatenate([models[group * boots + i].astype(BF) for i in range(boots)], axis=1)
        if boots > 1:
            regroup = held("regroup")
            regroup = [regroup[i * boots * LANES : (i + 1) * boots * LANES] for i in range(boots // 2)]
            m = dot(m, jnp.concatenate(regroup, axis=1)).astype(BF)
        for b in range(boots):
            out_ref[b * GRID : (b + 1) * GRID, group * LANES : (group + 1) * LANES] = (
                m[:, b * LANES : (b + 1) * LANES]
            )


def solve(slot, comp_weight, station_index, observed, counts, mine, grid_y):
    boots = min(mine, LANES // grid_y)
    slabs = DEPTHS * grid_y * boots // LANES
    stations = station_index.shape[1]
    const = jnp.asarray(constants(grid_y, boots))
    vmem = pltpu.VMEM
    whole = lambda a: pl.BlockSpec(a.shape, lambda i, n=a.ndim: (0,) * n)
    smem = pl.BlockSpec(memory_space=pltpu.SMEM)
    field = vmem((slabs, GRID, LANES), F32)
    at_stations = vmem((stations, LANES), F32)
    wide = 2 * boots * grid_y
    inputs = [station_index, observed, counts]
    return pl.pallas_call(
        functools.partial(solve_kernel, grid_y, boots, mine // boots),
        out_shape=jax.ShapeDtypeStruct((mine * GRID, DEPTHS * grid_y), BF),
        grid=(mine // boots,),
        in_specs=[smem, smem] + [whole(a) for a in inputs] + [pl.BlockSpec(memory_space=pl.ANY)],
        out_specs=pl.BlockSpec((boots * GRID, DEPTHS * grid_y), lambda i: (i, 0)),
        scratch_shapes=[
            vmem((layout(grid_y, boots).rows, 2 * LANES), BF),
            pltpu.SemaphoreType.DMA((3,)),
            vmem((stations, 2 * GRID), BF),
            vmem((2 * GRID, stations), BF),
            vmem((stations, 2 * wide), F32),
            at_stations,
            at_stations,
            at_stations,
            at_stations,
            vmem((stations, LANES), BF),
            vmem((LANES, stations), F32),
            vmem((5, DEPTHS, GRID, LANES), F32),
            vmem((stations, 5 * wide), BF),
            vmem((5, 2, wide // LANES, GRID, LANES), F32),
            vmem((2 * GRID, 5 * wide), BF),
            vmem((2 * GRID, slabs * 2 * LANES), BF),
            vmem((2 * GRID, slabs * 2 * LANES), BF),
            vmem((stations, 5 * LANES), BF),
            field,
            field,
            field,
            field,
        ],
        compiler_params=pltpu.CompilerParams(vmem_limit_bytes=56 * 1024 * 1024),
        cost_estimate=pl.CostEstimate(flops=10**10, bytes_accessed=10**7, transcendentals=0),
        name="solve",
    )(slot, comp_weight, *inputs, const)


def pick_kernel(grid_y, n_models, n_before, keep, cell_ref, *refs):
    models_refs, refs = refs[:n_models], refs[n_models:]
    before_refs, refs = refs[:n_before], refs[n_before:]
    if keep:
        refs[1][...] = models_refs[0][...]

    @pl.loop(0, cell_ref.shape[1] // CHUNK)
    def _(step):
        at = pl.ds(pl.multiple_of(step * CHUNK, CHUNK), CHUNK)
        place = cell_ref[:, at].astype(F32)
        wide = lambda row, rows: jnp.broadcast_to(row, (rows, CHUNK)).astype(BF)
        count_up = lambda rows: lax.broadcasted_iota(jnp.int32, (rows, CHUNK), 0).astype(F32).astype(BF)
        here_y = count_up(grid_y) == wide(place[1:2], grid_y)
        here_y = jnp.where(here_y, jnp.ones((grid_y, CHUNK), BF), jnp.zeros((grid_y, CHUNK), BF))
        z_row = wide(place[2:3], 16)
        none = jnp.zeros((16, CHUNK), BF)
        chosen = []
        for z in range(DEPTHS):
            here_z = z_row == jnp.full((16, CHUNK), z, BF)
            chosen += [jnp.where(here_z, here_y[i : i + 16], none) for i in range(0, grid_y, 16)]
        models = jnp.concatenate([ref[...] for ref in models_refs], axis=0)
        found = dot(models, jnp.concatenate(chosen, axis=0)).astype(BF)
        at_x = count_up(GRID) == wide(place[0:1], GRID)
        parts = [ref[:, at].astype(F32) for ref in before_refs]
        for b in range(models.shape[0] // GRID):
            part = jnp.where(at_x, found[b * GRID : (b + 1) * GRID], jnp.zeros((GRID, CHUNK), BF))
            while part.shape[0] > 16:
                half = part.shape[0] // 2
                part = part[:half] + part[half:]
            parts.append(jnp.sum(part.astype(F32), axis=0, keepdims=True))
        refs[0][:, at] = jnp.concatenate(parts, axis=0).astype(BF)


def pick(cells, models, before=(), grid_y=0, keep=False):
    rows = sum(m.shape[0] for m in models)
    boots = rows // GRID + sum(a.shape[0] for a in before)
    count = cells.shape[1]
    vmem = pl.BlockSpec(memory_space=pltpu.VMEM)
    shapes = [jax.ShapeDtypeStruct((boots, count), BF)]
    if keep:
        shapes.append(jax.ShapeDtypeStruct(models[0].shape, BF))
    found = pl.pallas_call(
        functools.partial(pick_kernel, grid_y, len(models), len(before), keep),
        out_shape=shapes,
        in_specs=[vmem] * (1 + len(models) + len(before)),
        out_specs=[vmem] * len(shapes),
        compiler_params=pltpu.CompilerParams(vmem_limit_bytes=40 * 1024 * 1024),
        cost_estimate=pl.CostEstimate(
            flops=2 * rows * DEPTHS * grid_y * count, bytes_accessed=10**6, transcendentals=0
        ),
        name="pick",
    )(cells, *models, *before)
    return found if keep else found[0]


def local(wide, cell_index, station_index, observed, comp_weight, counts):
    boots = counts.shape[0]
    grid_y = cell_index.shape[1] * wide // (GRID * DEPTHS)
    team = TEAM if wide % TEAM == 0 and boots % TEAM == 0 else 1
    while 4 * boots * grid_y < team * 2 * LANES:
        team //= 2
    slot = lax.axis_index("wide").astype(jnp.int32) & (team - 1)

    def swap(a, k):
        return lax.ppermute(a, "wide", [(i, i ^ k) for i in range(wide)])

    theirs = [swap(cell_index, k) for k in range(2, team, 2)]
    models = solve(slot.reshape(1), comp_weight, station_index, observed, counts, boots // team, grid_y)
    models, theirs = lax.optimization_barrier((models, theirs))
    if team > 1:
        shared = swap(models, 1)
        far = []
        for k, cells in enumerate(theirs):
            ours = pick(cells, [models], grid_y=grid_y, keep=k == 0)
            if k == 0:
                ours, models = ours
            far.append(swap(pick(cells, [shared], [ours], grid_y=grid_y), 2 * k + 2))
        found = [pick(cell_index, [models, shared], grid_y=grid_y)] + far
    else:
        found = [pick(cell_index, [models], grid_y=grid_y)]
    mine = boots // team
    got = [a[i * mine : (i + 1) * mine] for a in found for i in range(a.shape[0] // mine)]
    blocks = []
    for member in range(team):
        block = got[member]
        for other in range(1, team):
            block = jnp.where(slot == other, got[member ^ other], block)
        blocks.append(block.astype(F32))
    return jnp.concatenate(blocks, axis=0)


def solution(mesh):
    in_specs = (P(None, "wide"), P(None, "groups"), P(None, "groups"), P(), P("groups", None))
    out_specs = P("groups", "wide")
    fn = functools.partial(local, mesh.shape["wide"])
    return jax.shard_map(fn, mesh=mesh, in_specs=in_specs, out_specs=out_specs, check_vma=False)
```

```python
import functools

import jax
import jax.numpy as jnp
import ml_dtypes
import numpy as np
from jax import lax
from jax.experimental import pallas as pl
from jax.experimental.pallas import tpu as pltpu
from jax.sharding import PartitionSpec as P

IRLS = 2
CG_STEPS = 2
GRID = 128
DEPTHS = 16
LANES = 128
TEAM = 4
PARTS = 2
CHUNK = 2048
ROWS = 32

station_height = 2.0
focusing = 0.1
damping = 0.0002

PARITY = ((0, 0), (1, 1), (1, 0), (0, 0), (0, 1))
BF = jnp.bfloat16
F32 = jnp.float32


def offset_table(grid_y):
    one = np.float32
    dx = np.arange(GRID, dtype=one)[:, None, None]
    dy = np.arange(grid_y, dtype=one)[None, :, None]
    dz = (np.arange(DEPTHS, dtype=one) + one(0.5) + one(station_height))[None, None, :]
    radius2 = dx * dx + dy * dy + dz * dz
    strength = one(1) / (radius2 * radius2 * np.sqrt(radius2))
    three = one(3)
    kinds = [
        (three * dx * dx - radius2) * strength,
        three * dx * dy * strength,
        three * dx * dz * strength,
        (three * dy * dy - radius2) * strength,
        three * dy * dz * strength,
    ]
    return [k.astype(ml_dtypes.bfloat16).astype(np.float64) for k in kinds]


def angles(size):
    return 2 * np.pi * np.outer(np.arange(size), np.arange(size) + 0.5) / (2 * size)


def basis(size):
    return np.concatenate([np.cos(angles(size)), np.sin(angles(size))], axis=1)


def spectrum(values, odd, size):
    if odd:
        trig = 2 * np.sin(angles(size))
    else:
        trig = np.cos(angles(size)) * np.where(np.arange(size) == 0, 1, 2)[:, None]
    return np.tensordot(trig.T / size, values, axes=(1, 0))


def split(matrix):
    high = matrix.astype(ml_dtypes.bfloat16)
    low = (matrix - high.astype(np.float64)).astype(ml_dtypes.bfloat16)
    return high, low


class Layout:
    def __init__(self, parts):
        self.at = {}
        row = 0
        for name, rows in parts:
            self.at[name] = (row, rows)
            row += rows
        self.rows = row


def layout(grid_y, boots):
    return Layout(
        [
            ("base_x", GRID),
            ("base_xt2", 2 * GRID),
            ("station_y2", 4 * grid_y),
            ("spread", 3 * LANES),
            ("table", 5 * DEPTHS // 2 * GRID),
            ("field_y2", 2 * LANES),
            ("field_yt", 2 * LANES),
            ("back", 5 * LANES),
            ("same", LANES),
            ("regroup", boots * LANES * max(1, boots // 2)),
        ]
    )


@functools.lru_cache(maxsize=None)
def constants(grid_y, boots):
    deep = LANES // grid_y // boots
    copies = LANES // grid_y
    table = []
    for values, (odd_x, odd_y) in zip(offset_table(grid_y), PARITY):
        t = spectrum(values, odd_x, GRID)
        t = np.moveaxis(spectrum(np.moveaxis(t, 1, 0), odd_y, grid_y), 0, 1)
        table.append(np.tile(np.moveaxis(t, 2, 0), (1, 1, copies)))
    table = np.stack(table).reshape(5, DEPTHS // 2, 2, GRID, LANES).transpose(0, 1, 3, 2, 4)

    base_x = basis(GRID)
    base_y = basis(grid_y).reshape(grid_y, 2, grid_y)
    field_y = np.einsum("de,ab,yhl->dayehbl", np.eye(deep), np.eye(boots), base_y).reshape(LANES, 2 * LANES)
    odd_y = np.stack([-base_y[:, 1], base_y[:, 0]], axis=1)
    station_y = [np.tile(b[:, :, None], (1, 1, boots, 1)).reshape(grid_y, -1) for b in (base_y, odd_y)]
    spread = np.zeros((5, deep, boots, grid_y, copies, grid_y))
    for c in range(5):
        for copy in range(copies):
            spread[c, 0, copy % boots, c, copy, :] = 1
    spread = spread.reshape(5, LANES, LANES)
    back = spread.transpose(0, 2, 1).reshape(5 * LANES, LANES)
    spread = np.concatenate([spread, np.zeros((1, LANES, LANES))])
    spread = spread.reshape(3, 2, LANES, LANES).transpose(0, 2, 1, 3)
    same = np.einsum("ab,dc,yz->daycbz", np.eye(boots), np.ones((deep, deep)), np.ones((grid_y, grid_y)))
    same = same.reshape(LANES, LANES)
    regroup = np.einsum("st,de,ab,yz->sdaybtez", *[np.eye(n) for n in (boots, deep, boots, grid_y)])
    regroup = regroup.reshape(boots * LANES, boots * LANES)
    if boots > 2:
        regroup = np.concatenate(np.split(regroup, boots // 2, axis=1), axis=0)
    y_high, y_low = split(field_y)
    x_high, x_low = split(base_x.T)
    parts = dict(
        base_x=base_x,
        base_xt2=np.concatenate([x_high, x_low], axis=1),
        field_y2=np.concatenate([y_high, y_low], axis=0),
        field_yt=field_y.T,
        station_y2=np.concatenate([part for b in station_y for part in split(b)]),
        spread=spread.reshape(3 * LANES, 2 * LANES),
        back=back,
        same=same,
        regroup=regroup,
        table=table.reshape(-1, 2 * LANES),
    )
    where = layout(grid_y, boots)
    whole = np.zeros((max(where.rows, 1 << 14), 2 * LANES), ml_dtypes.bfloat16)
    for name, (row, rows) in where.at.items():
        part = parts[name].astype(ml_dtypes.bfloat16)
        assert part.shape[0] == rows
        whole[row : row + rows, : part.shape[1]] = part
    return whole


def dot(a, b):
    return jnp.dot(a, b, preferred_element_type=F32)


def dot_in_halves(a, b):
    half = a.shape[0] // 2
    return jnp.concatenate([dot(a[:half], b), dot(a[half:], b)], axis=0)


def solve_kernel(
    grid_y,
    boots,
    steps,
    slot_ref,
    comp_ref,
    station_ref,
    observed_ref,
    counts_ref,
    source,
    out_ref,
    const,
    copied,
    pick_x,
    pick_xt,
    pick_y,
    weights,
    data,
    pred,
    image,
    values,
    rows,
    table_wide,
    spread_out,
    spec_q,
    spec_i,
    spec_f,
    spec_g,
    picked_in,
    models,
    residual,
    direction,
    penalty,
):
    deep = LANES // grid_y // boots
    slabs = DEPTHS // deep
    where = layout(grid_y, boots)
    table_row, table_rows = where.at["table"]
    wide = 2 * boots * grid_y
    chunks = range(wide // LANES)
    bounds = [0, table_row, table_row + table_rows, where.rows]
    copies = [
        pltpu.make_async_copy(source.at[a:b], const.at[a:b], copied.at[i])
        for i, (a, b) in enumerate(zip(bounds[:-1], bounds[1:]))
    ]

    def once(f):
        if steps == 1:
            f()
        else:
            pl.when(pl.program_id(0) == 0)(f)

    @once
    def _():
        for copy in copies:
            copy.start()

    def held(name, width=2 * LANES):
        row, count = where.at[name]
        return const[row : row + count, :width]

    def table(c, z, at):
        row = table_row + (c * (DEPTHS // 2) + z // 2) * GRID
        return const[row + at.start : row + at.stop, z % 2 * LANES : (z % 2 + 1) * LANES]

    stations = station_ref.shape[1]
    first = (slot_ref[0] * pl.num_programs(0) + pl.program_id(0)) * boots
    size = slabs // PARTS
    shares = [range(start, start + size) for start in range(0, slabs, size)]
    share_lanes = size * 2 * LANES

    def pieces(share):
        return [(slab, slice(row, row + ROWS)) for slab in share for row in range(0, GRID, ROWS)]


    rows[...] = jnp.zeros_like(rows)
    for b in range(boots):
        row = b * grid_y
        rows[row : row + 5, :] = observed_ref[...]
        count = counts_ref[pl.ds(first + b, 1), :].astype(F32)
        for c in range(5):
            rows[row + 8 + c : row + 9 + c, :] = count * comp_ref[c]
    rows[16:18, :] = station_ref[...].astype(F32)
    turned = jnp.transpose(rows[...])
    lane = lax.broadcasted_iota(jnp.int32, (1, LANES), 1)
    used = lane % grid_y < 5
    data[...] = jnp.where(used, turned, 0.0)
    weights[...] = jnp.where(used, pltpu.roll(turned, LANES - 8, 1), 0.0)
    values[...] = (weights[...] * data[...]).astype(BF)

    place_x = (lax.broadcasted_iota(jnp.int32, (GRID, stations), 0) == station_ref[0:1, :]).astype(F32).astype(BF)
    place_xt = (turned[:, 16:17] == lane.astype(F32)).astype(F32).astype(BF)
    place_yt = (turned[:, 17:18] == lane.astype(F32)).astype(F32)[:, :grid_y].astype(BF)

    @once
    def _():
        copies[0].wait()

    pick_xt[...] = dot(held("base_xt2", GRID), place_x).astype(BF)
    pick_x[...] = dot(place_xt, held("base_x")).astype(BF)
    station_y2 = held("station_y2", wide)
    for odd in range(2):
        high, low = [station_y2[(2 * odd + i) * grid_y : (2 * odd + i + 1) * grid_y] for i in range(2)]
        pick_y[:, odd * wide : (odd + 1) * wide] = dot(place_yt, high) + dot(place_yt, low)
    no_sum = jnp.zeros((8, LANES), F32)

    def trig(at, odd, chunk):
        lane = odd * wide + chunk * LANES
        return pick_y[at, lane : lane + LANES]

    def station_spectra():
        spread = held("spread")
        spread = jnp.concatenate([spread[i * LANES : (i + 1) * LANES] for i in range(3)], axis=1)
        spreads = dot(values[...], spread[:, : 5 * LANES])
        for row in range(0, stations, ROWS):
            at = slice(row, row + ROWS)
            for c, (_, odd_y) in enumerate(PARITY):
                e = spreads[at, c * LANES : (c + 1) * LANES]
                for chunk in chunks:
                    to = c * wide + chunk * LANES
                    spread_out[at, to : to + LANES] = (e * trig(at, odd_y, chunk)).astype(BF)
        spec = dot(pick_xt[...], spread_out[...])
        for c, (odd_x, _) in enumerate(PARITY):
            for hx in range(2):
                for chunk in chunks:
                    lane = c * wide + chunk * LANES
                    part = spec[hx * GRID : (hx + 1) * GRID, lane : lane + LANES]
                    spec_q[c, hx, chunk] = -part if odd_x * hx else part

    def back_project(receive):
        for share in shares:
            for row in range(0, GRID, 16):
                at = slice(row, row + 16)
                for chunk in chunks:
                    q = [[spec_q[c, hx, chunk, at, :] for hx in range(2)] for c in range(5)]
                    for z in range(share.start * deep, share.stop * deep):
                        t = [table_wide[c, z, at, :] for c in range(5)]
                        lane = z * wide + chunk * LANES
                        for hx in range(2):
                            total = t[0] * q[0][hx]
                            for c in range(1, 5):
                                total = total + t[c] * q[c][hx ^ PARITY[c][0]]
                            spec_g[hx * GRID + row : hx * GRID + row + 16, lane : lane + LANES] = total.astype(BF)
            lane = share.start * 2 * LANES
            along_x = dot(held("base_x"), spec_g[:, lane : lane + share_lanes]).astype(BF)
            along_x = [along_x[:, lane : lane + 2 * LANES] for lane in range(0, share_lanes, 2 * LANES)]
            receive(share, dot_in_halves(jnp.concatenate(along_x, axis=0), held("field_yt", LANES)))

    def predict():
        for share in shares:
            r = residual[share.start : share.stop].reshape(len(share) * GRID, LANES).astype(BF)
            y = dot_in_halves(jnp.concatenate([r, r], axis=1), held("field_y2")).astype(BF)
            y = jnp.concatenate([y[i * GRID : (i + 1) * GRID] for i in range(len(share))], axis=1)
            lane = share.start * 2 * LANES
            spec_f[:, lane : lane + share_lanes] = dot(held("base_xt2"), jnp.concatenate([y, y], axis=0)).astype(BF)

            for row in range(0, GRID, 16):
                at = [slice(hx * GRID + row, hx * GRID + row + 16) for hx in range(2)]
                for chunk in chunks:
                    total = [[None] * 2 for _ in range(5)]
                    for z in range(share.start * deep, share.stop * deep):
                        lane = z * wide + chunk * LANES
                        f = [spec_f[at[hx], lane : lane + LANES] for hx in range(2)]
                        for c, (odd_x, _) in enumerate(PARITY):
                            t = table(c, z, at[0])
                            for hx in range(2):
                                term = t * f[hx ^ odd_x]
                                total[c][hx] = term if total[c][hx] is None else total[c][hx] + term
                    for c, (odd_x, _) in enumerate(PARITY):
                        lane = c * wide + chunk * LANES
                        for hx in range(2):
                            part = total[c][hx]
                            if share is not shares[0]:
                                part = part + spec_i[at[hx], lane : lane + LANES]
                            if share is shares[-1] and odd_x * hx:
                                part = -part
                            spec_i[at[hx], lane : lane + LANES] = part

        picked = dot(pick_x[...], spec_i[...])
        for row in range(0, stations, ROWS):
            at = slice(row, row + ROWS)
            for c, (_, odd_y) in enumerate(PARITY):
                part = None
                for chunk in chunks:
                    lane = c * wide + chunk * LANES
                    term = picked[at, lane : lane + LANES] * trig(at, odd_y, chunk)
                    part = term if part is None else part + term
                picked_in[at, c * LANES : (c + 1) * LANES] = part.astype(BF)
        return dot_in_halves(picked_in[...], held("back", LANES))

    def fold(a):
        return jnp.sum(a.reshape(a.shape[0] // 8, 8, LANES), axis=0)

    def totals_of(partials):
        rows_of = []
        for partial in partials:
            for _ in range(3):
                part = partial.astype(BF).astype(F32)
                rows_of.append(part)
                partial = partial - part
        if len(rows_of) % 2:
            rows_of.append(no_sum)
        sums = dot(jnp.concatenate(rows_of, axis=0).astype(BF), held("same", LANES))
        return [jnp.sum(sums[i * 24 : (i + 1) * 24], axis=0, keepdims=True) for i in range(len(partials))]

    def depth_weight(z):
        within = lax.broadcasted_iota(jnp.int32, (1, LANES), 1) // (boots * grid_y)
        depth = (within + z * deep).astype(F32) + 0.5 + station_height
        ratio = station_height / depth
        return ratio * ratio * ratio

    def round_of(outer, inner, carry):
        first = outer == 0 and inner == 0
        last = outer == IRLS - 1 and inner == CG_STEPS - 1
        fresh = inner == 0
        old_norm, old_step, old_curve = carry
        sums = [no_sum] * 3

        def penalty_at(slab, at):
            if outer == 0:
                return damping * depth_weight(slab) / (focusing * focusing)
            return penalty[slab, at]

        def receive(share, applied):
            norm, bend, cross = sums
            for slab, at in pieces(share):
                row = (slab - share.start) * GRID + at.start
                r = applied[row : row + ROWS]
                if fresh and outer:
                    m = models[slab, at]
                    p = damping * depth_weight(slab) / (m * m + focusing * focusing)
                    penalty[slab, at] = p
                    r = r - p * m
                else:
                    p = penalty_at(slab, at)
                if not fresh:
                    pd = p * direction[slab, at]
                    r = residual[slab, at] - old_step * (r + pd)
                    cross += fold(pd * r)
                residual[slab, at] = r
                square = r * r
                norm += fold(square)
                bend += fold(p * square)
            sums[:] = [norm, bend, cross]

        back_project(receive)
        here = predict()
        weighted = weights[...] * here
        norm, bend, cross = sums
        if fresh:
            norm, curve = totals_of([norm, bend + fold(weighted * here)])
        else:
            norm, bend, cross = totals_of(
                [norm, bend + fold(weighted * here), cross + fold(weighted * image[...])]
            )
            ratio = norm / old_norm
            curve = bend + ratio * (2.0 * cross + ratio * old_curve)
        step = norm / curve
        if not last:
            if not fresh:
                here = here + ratio * image[...]
            now = step * here if first else pred[...] + step * here
            pred[...] = now
            if fresh:
                image[...] = here
                values[...] = (weights[...] * here).astype(BF)
            else:
                values[...] = (weights[...] * (data[...] - now)).astype(BF)
            station_spectra()
        for share in shares:
            for slab, at in pieces(share):
                d = residual[slab, at]
                if not fresh:
                    d = d + ratio * direction[slab, at]
                if fresh:
                    direction[slab, at] = d
                models[slab, at] = step * d if first else models[slab, at] + step * d
        return norm, step, curve

    station_spectra()

    @once
    def _():
        copies[1].wait()
        copies[2].wait()
        for c in range(5):
            for z in range(DEPTHS):
                table_wide[c, z] = table(c, z, slice(0, GRID)).astype(F32)

    carry = (None, None, None)
    for outer in range(IRLS):
        for inner in range(CG_STEPS):
            carry = round_of(outer, inner, carry)

    for group in range(slabs // boots):
        m = jnp.concatenate([models[group * boots + i].astype(BF) for i in range(boots)], axis=1)
        if boots > 1:
            regroup = held("regroup")
            regroup = [regroup[i * boots * LANES : (i + 1) * boots * LANES] for i in range(boots // 2)]
            m = dot(m, jnp.concatenate(regroup, axis=1)).astype(BF)
        for b in range(boots):
            out_ref[b * GRID : (b + 1) * GRID, group * LANES : (group + 1) * LANES] = (
                m[:, b * LANES : (b + 1) * LANES]
            )


def solve(slot, comp_weight, station_index, observed, counts, mine, grid_y):
    boots = min(mine, LANES // grid_y)
    slabs = DEPTHS * grid_y * boots // LANES
    stations = station_index.shape[1]
    const = jnp.asarray(constants(grid_y, boots))
    vmem = pltpu.VMEM
    whole = lambda a: pl.BlockSpec(a.shape, lambda i, n=a.ndim: (0,) * n)
    smem = pl.BlockSpec(memory_space=pltpu.SMEM)
    field = vmem((slabs, GRID, LANES), F32)
    at_stations = vmem((stations, LANES), F32)
    wide = 2 * boots * grid_y
    inputs = [station_index, observed, counts]
    return pl.pallas_call(
        functools.partial(solve_kernel, grid_y, boots, mine // boots),
        out_shape=jax.ShapeDtypeStruct((mine * GRID, DEPTHS * grid_y), BF),
        grid=(mine // boots,),
        in_specs=[smem, smem] + [whole(a) for a in inputs] + [pl.BlockSpec(memory_space=pl.ANY)],
        out_specs=pl.BlockSpec((boots * GRID, DEPTHS * grid_y), lambda i: (i, 0)),
        scratch_shapes=[
            vmem((layout(grid_y, boots).rows, 2 * LANES), BF),
            pltpu.SemaphoreType.DMA((3,)),
            vmem((stations, 2 * GRID), BF),
            vmem((2 * GRID, stations), BF),
            vmem((stations, 2 * wide), F32),
            at_stations,
            at_stations,
            at_stations,
            at_stations,
            vmem((stations, LANES), BF),
            vmem((LANES, stations), F32),
            vmem((5, DEPTHS, GRID, LANES), F32),
            vmem((stations, 5 * wide), BF),
            vmem((5, 2, wide // LANES, GRID, LANES), F32),
            vmem((2 * GRID, 5 * wide), BF),
            vmem((2 * GRID, slabs * 2 * LANES), BF),
            vmem((2 * GRID, slabs * 2 * LANES), BF),
            vmem((stations, 5 * LANES), BF),
            field,
            field,
            field,
            field,
        ],
        compiler_params=pltpu.CompilerParams(vmem_limit_bytes=56 * 1024 * 1024),
        cost_estimate=pl.CostEstimate(flops=10**10, bytes_accessed=10**7, transcendentals=0),
        name="solve",
    )(slot, comp_weight, *inputs, const)


def pick_kernel(grid_y, n_models, n_before, keep, cell_ref, *refs):
    models_refs, refs = refs[:n_models], refs[n_models:]
    before_refs, refs = refs[:n_before], refs[n_before:]
    if keep:
        refs[1][...] = models_refs[0][...]

    @pl.loop(0, cell_ref.shape[1] // CHUNK)
    def _(step):
        at = pl.ds(pl.multiple_of(step * CHUNK, CHUNK), CHUNK)
        place = cell_ref[:, at].astype(F32)
        wide = lambda row, rows: jnp.broadcast_to(row, (rows, CHUNK)).astype(BF)
        count_up = lambda rows: lax.broadcasted_iota(jnp.int32, (rows, CHUNK), 0).astype(F32).astype(BF)
        here_y = count_up(grid_y) == wide(place[1:2], grid_y)
        here_y = jnp.where(here_y, jnp.ones((grid_y, CHUNK), BF), jnp.zeros((grid_y, CHUNK), BF))
        z_row = wide(place[2:3], 16)
        none = jnp.zeros((16, CHUNK), BF)
        chosen = []
        for z in range(DEPTHS):
            here_z = z_row == jnp.full((16, CHUNK), z, BF)
            chosen += [jnp.where(here_z, here_y[i : i + 16], none) for i in range(0, grid_y, 16)]
        models = jnp.concatenate([ref[...] for ref in models_refs], axis=0)
        found = dot(models, jnp.concatenate(chosen, axis=0)).astype(BF)
        at_x = count_up(GRID) == wide(place[0:1], GRID)
        parts = [ref[:, at].astype(F32) for ref in before_refs]
        for b in range(models.shape[0] // GRID):
            part = jnp.where(at_x, found[b * GRID : (b + 1) * GRID], jnp.zeros((GRID, CHUNK), BF))
            while part.shape[0] > 16:
                half = part.shape[0] // 2
                part = part[:half] + part[half:]
            parts.append(jnp.sum(part.astype(F32), axis=0, keepdims=True))
        refs[0][:, at] = jnp.concatenate(parts, axis=0).astype(BF)


def pick(cells, models, before=(), grid_y=0, keep=False):
    rows = sum(m.shape[0] for m in models)
    boots = rows // GRID + sum(a.shape[0] for a in before)
    count = cells.shape[1]
    vmem = pl.BlockSpec(memory_space=pltpu.VMEM)
    shapes = [jax.ShapeDtypeStruct((boots, count), BF)]
    if keep:
        shapes.append(jax.ShapeDtypeStruct(models[0].shape, BF))
    found = pl.pallas_call(
        functools.partial(pick_kernel, grid_y, len(models), len(before), keep),
        out_shape=shapes,
        in_specs=[vmem] * (1 + len(models) + len(before)),
        out_specs=[vmem] * len(shapes),
        compiler_params=pltpu.CompilerParams(vmem_limit_bytes=40 * 1024 * 1024),
        cost_estimate=pl.CostEstimate(
            flops=2 * rows * DEPTHS * grid_y * count, bytes_accessed=10**6, transcendentals=0
        ),
        name="pick",
    )(cells, *models, *before)
    return found if keep else found[0]


def local(wide, cell_index, station_index, observed, comp_weight, counts):
    boots = counts.shape[0]
    grid_y = cell_index.shape[1] * wide // (GRID * DEPTHS)
    team = TEAM if wide % TEAM == 0 and boots % TEAM == 0 else 1
    while 4 * boots * grid_y < team * 2 * LANES:
        team //= 2
    slot = lax.axis_index("wide").astype(jnp.int32) & (team - 1)

    def swap(a, k):
        return lax.ppermute(a, "wide", [(i, i ^ k) for i in range(wide)])

    theirs = [swap(cell_index, k) for k in range(2, team, 2)]
    models = solve(slot.reshape(1), comp_weight, station_index, observed, counts, boots // team, grid_y)
    models, theirs = lax.optimization_barrier((models, theirs))
    if team > 1:
        shared = swap(models, 1)
        far = []
        for k, cells in enumerate(theirs):
            ours = pick(cells, [models], grid_y=grid_y, keep=k == 0)
            if k == 0:
                ours, models = ours
            far.append(swap(pick(cells, [shared], [ours], grid_y=grid_y), 2 * k + 2))
        found = [pick(cell_index, [models, shared], grid_y=grid_y)] + far
    else:
        found = [pick(cell_index, [models], grid_y=grid_y)]
    mine = boots // team
    got = [a[i * mine : (i + 1) * mine] for a in found for i in range(a.shape[0] // mine)]
    blocks = []
    for member in range(team):
        block = got[member]
        for other in range(1, team):
            block = jnp.where(slot == other, got[member ^ other], block)
        blocks.append(block.astype(F32))
    return jnp.concatenate(blocks, axis=0)


def solution(mesh):
    in_specs = (P(None, "wide"), P(None, "groups"), P(None, "groups"), P(), P("groups", None))
    out_specs = P("groups", "wide")
    fn = functools.partial(local, mesh.shape["wide"])
    return jax.shard_map(fn, mesh=mesh, in_specs=in_specs, out_specs=out_specs, check_vma=False)
```

```python
import functools

import jax
import jax.numpy as jnp
import ml_dtypes
import numpy as np
from jax import lax
from jax.experimental import pallas as pl
from jax.experimental.pallas import tpu as pltpu
from jax.sharding import PartitionSpec as P

IRLS = 2
CG_STEPS = 2
GRID = 128
DEPTHS = 16
LANES = 128
TEAM = 4
PARTS = 2
CHUNK = 2048
ROWS = 32

station_height = 2.0
focusing = 0.1
damping = 0.0002

PARITY = ((0, 0), (1, 1), (1, 0), (0, 0), (0, 1))
BF = jnp.bfloat16
F32 = jnp.float32


def offset_table(grid_y):
    one = np.float32
    dx = np.arange(GRID, dtype=one)[:, None, None]
    dy = np.arange(grid_y, dtype=one)[None, :, None]
    dz = (np.arange(DEPTHS, dtype=one) + one(0.5) + one(station_height))[None, None, :]
    radius2 = dx * dx + dy * dy + dz * dz
    strength = one(1) / (radius2 * radius2 * np.sqrt(radius2))
    three = one(3)
    kinds = [
        (three * dx * dx - radius2) * strength,
        three * dx * dy * strength,
        three * dx * dz * strength,
        (three * dy * dy - radius2) * strength,
        three * dy * dz * strength,
    ]
    return [k.astype(ml_dtypes.bfloat16).astype(np.float64) for k in kinds]


def angles(size):
    return 2 * np.pi * np.outer(np.arange(size), np.arange(size) + 0.5) / (2 * size)


def basis(size):
    return np.concatenate([np.cos(angles(size)), np.sin(angles(size))], axis=1)


def spectrum(values, odd, size):
    if odd:
        trig = 2 * np.sin(angles(size))
    else:
        trig = np.cos(angles(size)) * np.where(np.arange(size) == 0, 1, 2)[:, None]
    return np.tensordot(trig.T / size, values, axes=(1, 0))


def split(matrix):
    high = matrix.astype(ml_dtypes.bfloat16)
    low = (matrix - high.astype(np.float64)).astype(ml_dtypes.bfloat16)
    return high, low


class Layout:
    def __init__(self, parts):
        self.at = {}
        row = 0
        for name, rows in parts:
            self.at[name] = (row, rows)
            row += rows
        self.rows = row


def layout(grid_y, boots):
    return Layout(
        [
            ("base_x", GRID),
            ("base_xt2", 2 * GRID),
            ("station_y2", 4 * grid_y),
            ("spread", 3 * LANES),
            ("table", 5 * DEPTHS // 2 * GRID),
            ("field_y2", 2 * LANES),
            ("field_yt", 2 * LANES),
            ("back", 5 * LANES),
            ("same", LANES),
            ("regroup", boots * LANES * max(1, boots // 2)),
        ]
    )


@functools.lru_cache(maxsize=None)
def constants(grid_y, boots):
    deep = LANES // grid_y // boots
    copies = LANES // grid_y
    table = []
    for values, (odd_x, odd_y) in zip(offset_table(grid_y), PARITY):
        t = spectrum(values, odd_x, GRID)
        t = np.moveaxis(spectrum(np.moveaxis(t, 1, 0), odd_y, grid_y), 0, 1)
        table.append(np.tile(np.moveaxis(t, 2, 0), (1, 1, copies)))
    table = np.stack(table).reshape(5, DEPTHS // 2, 2, GRID, LANES).transpose(0, 1, 3, 2, 4)

    base_x = basis(GRID)
    base_y = basis(grid_y).reshape(grid_y, 2, grid_y)
    field_y = np.einsum("de,ab,yhl->dayehbl", np.eye(deep), np.eye(boots), base_y).reshape(LANES, 2 * LANES)
    odd_y = np.stack([-base_y[:, 1], base_y[:, 0]], axis=1)
    station_y = [np.tile(b[:, :, None], (1, 1, boots, 1)).reshape(grid_y, -1) for b in (base_y, odd_y)]
    spread = np.zeros((5, deep, boots, grid_y, copies, grid_y))
    for c in range(5):
        for copy in range(copies):
            spread[c, 0, copy % boots, c, copy, :] = 1
    spread = spread.reshape(5, LANES, LANES)
    back = spread.transpose(0, 2, 1).reshape(5 * LANES, LANES)
    spread = np.concatenate([spread, np.zeros((1, LANES, LANES))])
    spread = spread.reshape(3, 2, LANES, LANES).transpose(0, 2, 1, 3)
    same = np.einsum("ab,dc,yz->daycbz", np.eye(boots), np.ones((deep, deep)), np.ones((grid_y, grid_y)))
    same = same.reshape(LANES, LANES)
    regroup = np.einsum("st,de,ab,yz->sdaybtez", *[np.eye(n) for n in (boots, deep, boots, grid_y)])
    regroup = regroup.reshape(boots * LANES, boots * LANES)
    if boots > 2:
        regroup = np.concatenate(np.split(regroup, boots // 2, axis=1), axis=0)
    y_high, y_low = split(field_y)
    x_high, x_low = split(base_x.T)
    parts = dict(
        base_x=base_x,
        base_xt2=np.concatenate([x_high, x_low], axis=1),
        field_y2=np.concatenate([y_high, y_low], axis=0),
        field_yt=field_y.T,
        station_y2=np.concatenate([part for b in station_y for part in split(b)]),
        spread=spread.reshape(3 * LANES, 2 * LANES),
        back=back,
        same=same,
        regroup=regroup,
        table=table.reshape(-1, 2 * LANES),
    )
    where = layout(grid_y, boots)
    whole = np.zeros((max(where.rows, 1 << 14), 2 * LANES), ml_dtypes.bfloat16)
    for name, (row, rows) in where.at.items():
        part = parts[name].astype(ml_dtypes.bfloat16)
        assert part.shape[0] == rows
        whole[row : row + rows, : part.shape[1]] = part
    return whole


def dot(a, b):
    return jnp.dot(a, b, preferred_element_type=F32)


def solve_kernel(
    grid_y,
    boots,
    steps,
    slot_ref,
    comp_ref,
    station_source,
    observed_source,
    counts_source,
    source,
    out_ref,
    station_ref,
    observed_ref,
    counts_ref,
    const,
    copied,
    pick_x,
    pick_xt,
    pick_y,
    weights,
    data,
    pred,
    image,
    values,
    rows,
    table_wide,
    spread_out,
    spec_q,
    spec_i,
    spec_f,
    spec_g,
    picked_in,
    models,
    residual,
    direction,
    penalty,
):
    deep = LANES // grid_y // boots
    slabs = DEPTHS // deep
    where = layout(grid_y, boots)
    table_row, table_rows = where.at["table"]
    wide = 2 * boots * grid_y
    chunks = range(wide // LANES)
    bounds = [0, table_row, table_row + table_rows, where.rows]
    copies = [
        pltpu.make_async_copy(source.at[a:b], const.at[a:b], copied.at[i])
        for i, (a, b) in enumerate(zip(bounds[:-1], bounds[1:]))
    ]

    small = [(station_source, station_ref), (observed_source, observed_ref), (counts_source, counts_ref)]
    small = [pltpu.make_async_copy(a, b, copied.at[len(copies) + i]) for i, (a, b) in enumerate(small)]

    def once(f):
        if steps == 1:
            f()
        else:
            pl.when(pl.program_id(0) == 0)(f)

    @once
    def _():
        for copy in small + copies:
            copy.start()
        for copy in small:
            copy.wait()

    def held(name, width=2 * LANES):
        row, count = where.at[name]
        return const[row : row + count, :width]

    def table(c, z, at):
        row = table_row + (c * (DEPTHS // 2) + z // 2) * GRID
        return const[row + at.start : row + at.stop, z % 2 * LANES : (z % 2 + 1) * LANES]

    stations = station_ref.shape[1]
    first = (slot_ref[0] * pl.num_programs(0) + pl.program_id(0)) * boots
    size = slabs // PARTS
    shares = [range(start, start + size) for start in range(0, slabs, size)]
    share_lanes = size * 2 * LANES

    def pieces(share):
        return [(slab, slice(row, row + ROWS)) for slab in share for row in range(0, GRID, ROWS)]


    rows[...] = jnp.zeros_like(rows)
    for b in range(boots):
        row = b * grid_y
        rows[row : row + 5, :] = observed_ref[...]
        count = counts_ref[pl.ds(first + b, 1), :].astype(F32)
        for c in range(5):
            rows[row + 8 + c : row + 9 + c, :] = count * comp_ref[c]
    rows[16:18, :] = station_ref[...].astype(F32)
    turned = jnp.transpose(rows[...])
    lane = lax.broadcasted_iota(jnp.int32, (1, LANES), 1)
    used = lane % grid_y < 5
    data[...] = jnp.where(used, turned, 0.0)
    weights[...] = jnp.where(used, pltpu.roll(turned, LANES - 8, 1), 0.0)
    values[...] = (weights[...] * data[...]).astype(BF)

    place_x = (lax.broadcasted_iota(jnp.int32, (GRID, stations), 0) == station_ref[0:1, :]).astype(F32).astype(BF)
    place_xt = (turned[:, 16:17] == lane.astype(F32)).astype(F32).astype(BF)
    place_yt = (turned[:, 17:18] == lane.astype(F32)).astype(F32)[:, :grid_y].astype(BF)

    @once
    def _():
        copies[0].wait()

    pick_xt[...] = dot(held("base_xt2", GRID), place_x).astype(BF)
    pick_x[...] = dot(place_xt, held("base_x")).astype(BF)
    station_y2 = held("station_y2", wide)
    for odd in range(2):
        high, low = [station_y2[(2 * odd + i) * grid_y : (2 * odd + i + 1) * grid_y] for i in range(2)]
        pick_y[:, odd * wide : (odd + 1) * wide] = dot(place_yt, high) + dot(place_yt, low)
    no_sum = jnp.zeros((8, LANES), F32)

    def trig(at, odd, chunk):
        lane = odd * wide + chunk * LANES
        return pick_y[at, lane : lane + LANES]

    def station_spectra():
        spread = held("spread")
        spread = jnp.concatenate([spread[i * LANES : (i + 1) * LANES] for i in range(3)], axis=1)
        spreads = dot(values[...], spread[:, : 5 * LANES])
        for row in range(0, stations, ROWS):
            at = slice(row, row + ROWS)
            for c, (_, odd_y) in enumerate(PARITY):
                e = spreads[at, c * LANES : (c + 1) * LANES]
                for chunk in chunks:
                    to = c * wide + chunk * LANES
                    spread_out[at, to : to + LANES] = (e * trig(at, odd_y, chunk)).astype(BF)
        spec = dot(pick_xt[...], spread_out[...])
        for c, (odd_x, _) in enumerate(PARITY):
            for hx in range(2):
                for chunk in chunks:
                    lane = c * wide + chunk * LANES
                    part = spec[hx * GRID : (hx + 1) * GRID, lane : lane + LANES]
                    spec_q[c, hx, chunk] = -part if odd_x * hx else part

    def back_project(receive):
        for share in shares:
            for row in range(0, GRID, 16):
                at = slice(row, row + 16)
                for chunk in chunks:
                    q = [[spec_q[c, hx, chunk, at, :] for hx in range(2)] for c in range(5)]
                    for z in range(share.start * deep, share.stop * deep):
                        t = [table_wide[c, z, at, :] for c in range(5)]
                        lane = z * wide + chunk * LANES
                        for hx in range(2):
                            total = t[0] * q[0][hx]
                            for c in range(1, 5):
                                total = total + t[c] * q[c][hx ^ PARITY[c][0]]
                            spec_g[hx * GRID + row : hx * GRID + row + 16, lane : lane + LANES] = total.astype(BF)
            lane = share.start * 2 * LANES
            along_x = dot(held("base_x"), spec_g[:, lane : lane + share_lanes]).astype(BF)
            along_x = [along_x[:, lane : lane + 2 * LANES] for lane in range(0, share_lanes, 2 * LANES)]
            receive(share, dot(jnp.concatenate(along_x, axis=0), held("field_yt", LANES)))

    def predict():
        for share in shares:
            r = residual[share.start : share.stop].reshape(len(share) * GRID, LANES).astype(BF)
            y = dot(jnp.concatenate([r, r], axis=1), held("field_y2")).astype(BF)
            y = jnp.concatenate([y[i * GRID : (i + 1) * GRID] for i in range(len(share))], axis=1)
            lane = share.start * 2 * LANES
            spec_f[:, lane : lane + share_lanes] = dot(held("base_xt2"), jnp.concatenate([y, y], axis=0)).astype(BF)

            for row in range(0, GRID, 16):
                at = [slice(hx * GRID + row, hx * GRID + row + 16) for hx in range(2)]
                for chunk in chunks:
                    total = [[None] * 2 for _ in range(5)]
                    for z in range(share.start * deep, share.stop * deep):
                        lane = z * wide + chunk * LANES
                        f = [spec_f[at[hx], lane : lane + LANES] for hx in range(2)]
                        for c, (odd_x, _) in enumerate(PARITY):
                            t = table(c, z, at[0])
                            for hx in range(2):
                                term = t * f[hx ^ odd_x]
                                total[c][hx] = term if total[c][hx] is None else total[c][hx] + term
                    for c, (odd_x, _) in enumerate(PARITY):
                        lane = c * wide + chunk * LANES
                        for hx in range(2):
                            part = total[c][hx]
                            if share is not shares[0]:
                                part = part + spec_i[at[hx], lane : lane + LANES]
                            if share is shares[-1] and odd_x * hx:
                                part = -part
                            spec_i[at[hx], lane : lane + LANES] = part

        picked = dot(pick_x[...], spec_i[...])
        for row in range(0, stations, ROWS):
            at = slice(row, row + ROWS)
            for c, (_, odd_y) in enumerate(PARITY):
                part = None
                for chunk in chunks:
                    lane = c * wide + chunk * LANES
                    term = picked[at, lane : lane + LANES] * trig(at, odd_y, chunk)
                    part = term if part is None else part + term
                picked_in[at, c * LANES : (c + 1) * LANES] = part.astype(BF)
        return dot(picked_in[...], held("back", LANES))

    def fold(a):
        return jnp.sum(a.reshape(a.shape[0] // 8, 8, LANES), axis=0)

    def totals_of(partials):
        rows_of = []
        for partial in partials:
            for _ in range(3):
                part = partial.astype(BF).astype(F32)
                rows_of.append(part)
                partial = partial - part
        if len(rows_of) % 2:
            rows_of.append(no_sum)
        sums = dot(jnp.concatenate(rows_of, axis=0).astype(BF), held("same", LANES))
        return [jnp.sum(sums[i * 24 : (i + 1) * 24], axis=0, keepdims=True) for i in range(len(partials))]

    def depth_weight(z):
        within = lax.broadcasted_iota(jnp.int32, (1, LANES), 1) // (boots * grid_y)
        depth = (within + z * deep).astype(F32) + 0.5 + station_height
        ratio = station_height / depth
        return ratio * ratio * ratio

    def round_of(outer, inner, carry):
        first = outer == 0 and inner == 0
        last = outer == IRLS - 1 and inner == CG_STEPS - 1
        fresh = inner == 0
        old_norm, old_step, old_curve = carry
        sums = [no_sum] * 3

        def penalty_at(slab, at):
            if outer == 0:
                return damping * depth_weight(slab) / (focusing * focusing)
            return penalty[slab, at]

        def receive(share, applied):
            norm, bend, cross = sums
            for slab, at in pieces(share):
                row = (slab - share.start) * GRID + at.start
                r = applied[row : row + ROWS]
                if fresh and outer:
                    m = models[slab, at]
                    p = damping * depth_weight(slab) / (m * m + focusing * focusing)
                    penalty[slab, at] = p
                    r = r - p * m
                else:
                    p = penalty_at(slab, at)
                if not fresh:
                    pd = p * direction[slab, at]
                    r = residual[slab, at] - old_step * (r + pd)
                    cross += fold(pd * r)
                residual[slab, at] = r
                square = r * r
                norm += fold(square)
                bend += fold(p * square)
            sums[:] = [norm, bend, cross]

        back_project(receive)
        here = predict()
        weighted = weights[...] * here
        norm, bend, cross = sums
        if fresh:
            norm, curve = totals_of([norm, bend + fold(weighted * here)])
        else:
            norm, bend, cross = totals_of(
                [norm, bend + fold(weighted * here), cross + fold(weighted * image[...])]
            )
            ratio = norm / old_norm
            curve = bend + ratio * (2.0 * cross + ratio * old_curve)
        step = norm / curve
        if not last:
            if not fresh:
                here = here + ratio * image[...]
            now = step * here if first else pred[...] + step * here
            pred[...] = now
            if fresh:
                image[...] = here
                values[...] = (weights[...] * here).astype(BF)
            else:
                values[...] = (weights[...] * (data[...] - now)).astype(BF)
            station_spectra()
        for share in shares:
            for slab, at in pieces(share):
                d = residual[slab, at]
                if not fresh:
                    d = d + ratio * direction[slab, at]
                if fresh:
                    direction[slab, at] = d
                models[slab, at] = step * d if first else models[slab, at] + step * d
        return norm, step, curve

    station_spectra()

    @once
    def _():
        copies[1].wait()
        copies[2].wait()
        for c in range(5):
            for z in range(DEPTHS):
                table_wide[c, z] = table(c, z, slice(0, GRID)).astype(F32)

    carry = (None, None, None)
    for outer in range(IRLS):
        for inner in range(CG_STEPS):
            carry = round_of(outer, inner, carry)

    for group in range(slabs // boots):
        m = jnp.concatenate([models[group * boots + i].astype(BF) for i in range(boots)], axis=1)
        if boots > 1:
            regroup = held("regroup")
            regroup = [regroup[i * boots * LANES : (i + 1) * boots * LANES] for i in range(boots // 2)]
            m = dot(m, jnp.concatenate(regroup, axis=1)).astype(BF)
        for b in range(boots):
            out_ref[b * GRID : (b + 1) * GRID, group * LANES : (group + 1) * LANES] = (
                m[:, b * LANES : (b + 1) * LANES]
            )


def solve(slot, comp_weight, station_index, observed, counts, mine, grid_y):
    boots = min(mine, LANES // grid_y)
    slabs = DEPTHS * grid_y * boots // LANES
    stations = station_index.shape[1]
    const = jnp.asarray(constants(grid_y, boots))
    vmem = pltpu.VMEM
    smem = pl.BlockSpec(memory_space=pltpu.SMEM)
    field = vmem((slabs, GRID, LANES), F32)
    at_stations = vmem((stations, LANES), F32)
    wide = 2 * boots * grid_y
    inputs = [station_index, observed, counts]
    return pl.pallas_call(
        functools.partial(solve_kernel, grid_y, boots, mine // boots),
        out_shape=jax.ShapeDtypeStruct((mine * GRID, DEPTHS * grid_y), BF),
        grid=(mine // boots,),
        in_specs=[smem, smem] + [pl.BlockSpec(memory_space=pl.ANY)] * (len(inputs) + 1),
        out_specs=pl.BlockSpec((boots * GRID, DEPTHS * grid_y), lambda i: (i, 0)),
        scratch_shapes=[vmem(a.shape, a.dtype) for a in inputs]
        + [
            vmem((layout(grid_y, boots).rows, 2 * LANES), BF),
            pltpu.SemaphoreType.DMA((6,)),
            vmem((stations, 2 * GRID), BF),
            vmem((2 * GRID, stations), BF),
            vmem((stations, 2 * wide), F32),
            at_stations,
            at_stations,
            at_stations,
            at_stations,
            vmem((stations, LANES), BF),
            vmem((LANES, stations), F32),
            vmem((5, DEPTHS, GRID, LANES), F32),
            vmem((stations, 5 * wide), BF),
            vmem((5, 2, wide // LANES, GRID, LANES), F32),
            vmem((2 * GRID, 5 * wide), BF),
            vmem((2 * GRID, slabs * 2 * LANES), BF),
            vmem((2 * GRID, slabs * 2 * LANES), BF),
            vmem((stations, 5 * LANES), BF),
            field,
            field,
            field,
            field,
        ],
        compiler_params=pltpu.CompilerParams(vmem_limit_bytes=56 * 1024 * 1024),
        cost_estimate=pl.CostEstimate(flops=10**10, bytes_accessed=10**7, transcendentals=0),
        name="solve",
    )(slot, comp_weight, *inputs, const)


def pick_kernel(grid_y, n_models, n_before, keep, cell_ref, *refs):
    models_refs, refs = refs[:n_models], refs[n_models:]
    before_refs, refs = refs[:n_before], refs[n_before:]
    if keep:
        refs[1][...] = models_refs[0][...]

    @pl.loop(0, cell_ref.shape[1] // CHUNK)
    def _(step):
        at = pl.ds(pl.multiple_of(step * CHUNK, CHUNK), CHUNK)
        place = cell_ref[:, at].astype(F32)
        wide = lambda row, rows: jnp.broadcast_to(row, (rows, CHUNK)).astype(BF)
        count_up = lambda rows: lax.broadcasted_iota(jnp.int32, (rows, CHUNK), 0).astype(F32).astype(BF)
        here_y = count_up(grid_y) == wide(place[1:2], grid_y)
        here_y = jnp.where(here_y, jnp.ones((grid_y, CHUNK), BF), jnp.zeros((grid_y, CHUNK), BF))
        z_row = wide(place[2:3], 16)
        none = jnp.zeros((16, CHUNK), BF)
        chosen = []
        for z in range(DEPTHS):
            here_z = z_row == jnp.full((16, CHUNK), z, BF)
            chosen += [jnp.where(here_z, here_y[i : i + 16], none) for i in range(0, grid_y, 16)]
        models = jnp.concatenate([ref[...] for ref in models_refs], axis=0)
        found = dot(models, jnp.concatenate(chosen, axis=0)).astype(BF)
        at_x = count_up(GRID) == wide(place[0:1], GRID)
        parts = [ref[:, at].astype(F32) for ref in before_refs]
        for b in range(models.shape[0] // GRID):
            part = jnp.where(at_x, found[b * GRID : (b + 1) * GRID], jnp.zeros((GRID, CHUNK), BF))
            while part.shape[0] > 16:
                half = part.shape[0] // 2
                part = part[:half] + part[half:]
            parts.append(jnp.sum(part.astype(F32), axis=0, keepdims=True))
        refs[0][:, at] = jnp.concatenate(parts, axis=0).astype(BF)


def pick(cells, models, before=(), grid_y=0, keep=False):
    rows = sum(m.shape[0] for m in models)
    boots = rows // GRID + sum(a.shape[0] for a in before)
    count = cells.shape[1]
    vmem = pl.BlockSpec(memory_space=pltpu.VMEM)
    shapes = [jax.ShapeDtypeStruct((boots, count), BF)]
    if keep:
        shapes.append(jax.ShapeDtypeStruct(models[0].shape, BF))
    found = pl.pallas_call(
        functools.partial(pick_kernel, grid_y, len(models), len(before), keep),
        out_shape=shapes,
        in_specs=[vmem] * (1 + len(models) + len(before)),
        out_specs=[vmem] * len(shapes),
        compiler_params=pltpu.CompilerParams(vmem_limit_bytes=40 * 1024 * 1024),
        cost_estimate=pl.CostEstimate(
            flops=2 * rows * DEPTHS * grid_y * count, bytes_accessed=10**6, transcendentals=0
        ),
        name="pick",
    )(cells, *models, *before)
    return found if keep else found[0]


def local(wide, cell_index, station_index, observed, comp_weight, counts):
    boots = counts.shape[0]
    grid_y = cell_index.shape[1] * wide // (GRID * DEPTHS)
    team = TEAM if wide % TEAM == 0 and boots % TEAM == 0 else 1
    while 4 * boots * grid_y < team * 2 * LANES:
        team //= 2
    slot = lax.axis_index("wide").astype(jnp.int32) & (team - 1)

    def swap(a, k):
        return lax.ppermute(a, "wide", [(i, i ^ k) for i in range(wide)])

    theirs = [swap(cell_index, k) for k in range(2, team, 2)]
    models = solve(slot.reshape(1), comp_weight, station_index, observed, counts, boots // team, grid_y)
    models, theirs = lax.optimization_barrier((models, theirs))
    if team > 1:
        shared = swap(models, 1)
        far = []
        for k, cells in enumerate(theirs):
            ours = pick(cells, [models], grid_y=grid_y, keep=k == 0)
            if k == 0:
                ours, models = ours
            far.append(swap(pick(cells, [shared], [ours], grid_y=grid_y), 2 * k + 2))
        found = [pick(cell_index, [models, shared], grid_y=grid_y)] + far
    else:
        found = [pick(cell_index, [models], grid_y=grid_y)]
    mine = boots // team
    got = [a[i * mine : (i + 1) * mine] for a in found for i in range(a.shape[0] // mine)]
    blocks = []
    for member in range(team):
        block = got[member]
        for other in range(1, team):
            block = jnp.where(slot == other, got[member ^ other], block)
        blocks.append(block.astype(F32))
    return jnp.concatenate(blocks, axis=0)


def solution(mesh):
    in_specs = (P(None, "wide"), P(None, "groups"), P(None, "groups"), P(), P("groups", None))
    out_specs = P("groups", "wide")
    fn = functools.partial(local, mesh.shape["wide"])
    return jax.shard_map(fn, mesh=mesh, in_specs=in_specs, out_specs=out_specs, check_vma=False)
```

```python
import functools

import jax
import jax.numpy as jnp
import ml_dtypes
import numpy as np
from jax import lax
from jax.experimental import pallas as pl
from jax.experimental.pallas import tpu as pltpu
from jax.sharding import PartitionSpec as P

IRLS = 2
CG_STEPS = 2
GRID = 128
DEPTHS = 16
LANES = 128
TEAM = 4
PARTS = 2
CHUNK = 4096
ROWS = 32

station_height = 2.0
focusing = 0.1
damping = 0.0002

PARITY = ((0, 0), (1, 1), (1, 0), (0, 0), (0, 1))
BF = jnp.bfloat16
F32 = jnp.float32


def offset_table(grid_y):
    one = np.float32
    dx = np.arange(GRID, dtype=one)[:, None, None]
    dy = np.arange(grid_y, dtype=one)[None, :, None]
    dz = (np.arange(DEPTHS, dtype=one) + one(0.5) + one(station_height))[None, None, :]
    radius2 = dx * dx + dy * dy + dz * dz
    strength = one(1) / (radius2 * radius2 * np.sqrt(radius2))
    three = one(3)
    kinds = [
        (three * dx * dx - radius2) * strength,
        three * dx * dy * strength,
        three * dx * dz * strength,
        (three * dy * dy - radius2) * strength,
        three * dy * dz * strength,
    ]
    return [k.astype(ml_dtypes.bfloat16).astype(np.float64) for k in kinds]


def angles(size):
    return 2 * np.pi * np.outer(np.arange(size), np.arange(size) + 0.5) / (2 * size)


def basis(size):
    return np.concatenate([np.cos(angles(size)), np.sin(angles(size))], axis=1)


def spectrum(values, odd, size):
    if odd:
        trig = 2 * np.sin(angles(size))
    else:
        trig = np.cos(angles(size)) * np.where(np.arange(size) == 0, 1, 2)[:, None]
    return np.tensordot(trig.T / size, values, axes=(1, 0))


def split(matrix):
    high = matrix.astype(ml_dtypes.bfloat16)
    low = (matrix - high.astype(np.float64)).astype(ml_dtypes.bfloat16)
    return high, low


class Layout:
    def __init__(self, parts):
        self.at = {}
        row = 0
        for name, rows in parts:
            self.at[name] = (row, rows)
            row += rows
        self.rows = row


def layout(grid_y, boots):
    return Layout(
        [
            ("base_x", GRID),
            ("base_xt2", 2 * GRID),
            ("station_y2", 4 * grid_y),
            ("spread", 3 * LANES),
            ("table", 5 * DEPTHS // 2 * GRID),
            ("field_y2", 2 * LANES),
            ("field_yt", 2 * LANES),
            ("back", 5 * LANES),
            ("same", LANES),
            ("regroup", boots * LANES * max(1, boots // 2)),
        ]
    )


@functools.lru_cache(maxsize=None)
def constants(grid_y, boots):
    deep = LANES // grid_y // boots
    copies = LANES // grid_y
    table = []
    for values, (odd_x, odd_y) in zip(offset_table(grid_y), PARITY):
        t = spectrum(values, odd_x, GRID)
        t = np.moveaxis(spectrum(np.moveaxis(t, 1, 0), odd_y, grid_y), 0, 1)
        table.append(np.tile(np.moveaxis(t, 2, 0), (1, 1, copies)))
    table = np.stack(table).reshape(5, DEPTHS // 2, 2, GRID, LANES).transpose(0, 1, 3, 2, 4)

    base_x = basis(GRID)
    base_y = basis(grid_y).reshape(grid_y, 2, grid_y)
    field_y = np.einsum("de,ab,yhl->dayehbl", np.eye(deep), np.eye(boots), base_y).reshape(LANES, 2 * LANES)
    odd_y = np.stack([-base_y[:, 1], base_y[:, 0]], axis=1)
    station_y = [np.tile(b[:, :, None], (1, 1, boots, 1)).reshape(grid_y, -1) for b in (base_y, odd_y)]
    spread = np.zeros((5, deep, boots, grid_y, copies, grid_y))
    for c in range(5):
        for copy in range(copies):
            spread[c, 0, copy % boots, c, copy, :] = 1
    spread = spread.reshape(5, LANES, LANES)
    back = spread.transpose(0, 2, 1).reshape(5 * LANES, LANES)
    spread = np.concatenate([spread, np.zeros((1, LANES, LANES))])
    spread = spread.reshape(3, 2, LANES, LANES).transpose(0, 2, 1, 3)
    same = np.einsum("ab,dc,yz->daycbz", np.eye(boots), np.ones((deep, deep)), np.ones((grid_y, grid_y)))
    same = same.reshape(LANES, LANES)
    regroup = np.einsum("st,de,ab,yz->sdaybtez", *[np.eye(n) for n in (boots, deep, boots, grid_y)])
    regroup = regroup.reshape(boots * LANES, boots * LANES)
    if boots > 2:
        regroup = np.concatenate(np.split(regroup, boots // 2, axis=1), axis=0)
    y_high, y_low = split(field_y)
    x_high, x_low = split(base_x.T)
    parts = dict(
        base_x=base_x,
        base_xt2=np.concatenate([x_high, x_low], axis=1),
        field_y2=np.concatenate([y_high, y_low], axis=0),
        field_yt=field_y.T,
        station_y2=np.concatenate([part for b in station_y for part in split(b)]),
        spread=spread.reshape(3 * LANES, 2 * LANES),
        back=back,
        same=same,
        regroup=regroup,
        table=table.reshape(-1, 2 * LANES),
    )
    where = layout(grid_y, boots)
    whole = np.zeros((max(where.rows, 1 << 14), 2 * LANES), ml_dtypes.bfloat16)
    for name, (row, rows) in where.at.items():
        part = parts[name].astype(ml_dtypes.bfloat16)
        assert part.shape[0] == rows
        whole[row : row + rows, : part.shape[1]] = part
    return whole


def dot(a, b):
    return jnp.dot(a, b, preferred_element_type=F32)


def solve_kernel(
    grid_y,
    boots,
    steps,
    slot_ref,
    comp_ref,
    station_source,
    observed_source,
    counts_source,
    source,
    out_ref,
    station_ref,
    observed_ref,
    counts_ref,
    const,
    copied,
    pick_x,
    pick_xt,
    pick_y,
    weights,
    data,
    pred,
    image,
    values,
    rows,
    spread_out,
    spec_q,
    spec_i,
    spec_f,
    spec_g,
    picked_in,
    models,
    residual,
    direction,
    penalty,
):
    deep = LANES // grid_y // boots
    slabs = DEPTHS // deep
    where = layout(grid_y, boots)
    table_row, table_rows = where.at["table"]
    wide = 2 * boots * grid_y
    chunks = range(wide // LANES)
    bounds = [0, table_row, table_row + table_rows, where.rows]
    copies = [
        pltpu.make_async_copy(source.at[a:b], const.at[a:b], copied.at[i])
        for i, (a, b) in enumerate(zip(bounds[:-1], bounds[1:]))
    ]

    small = [(station_source, station_ref), (observed_source, observed_ref), (counts_source, counts_ref)]
    small = [pltpu.make_async_copy(a, b, copied.at[len(copies) + i]) for i, (a, b) in enumerate(small)]

    def once(f):
        if steps == 1:
            f()
        else:
            pl.when(pl.program_id(0) == 0)(f)

    @once
    def _():
        for copy in small + copies:
            copy.start()
        for copy in small:
            copy.wait()

    def held(name, width=2 * LANES):
        row, count = where.at[name]
        return const[row : row + count, :width]

    def table(c, z, at):
        row = table_row + (c * (DEPTHS // 2) + z // 2) * GRID
        return const[row + at.start : row + at.stop, z % 2 * LANES : (z % 2 + 1) * LANES]

    stations = station_ref.shape[1]
    first = (slot_ref[0] * pl.num_programs(0) + pl.program_id(0)) * boots
    size = slabs // PARTS
    shares = [range(start, start + size) for start in range(0, slabs, size)]
    share_lanes = size * 2 * LANES

    def pieces(share):
        return [(slab, slice(row, row + ROWS)) for slab in share for row in range(0, GRID, ROWS)]


    rows[...] = jnp.zeros_like(rows)
    for b in range(boots):
        row = b * grid_y
        rows[row : row + 5, :] = observed_ref[...]
        count = counts_ref[pl.ds(first + b, 1), :].astype(F32)
        for c in range(5):
            rows[row + 8 + c : row + 9 + c, :] = count * comp_ref[c]
    rows[16:18, :] = station_ref[...].astype(F32)
    turned = jnp.transpose(rows[...])
    lane = lax.broadcasted_iota(jnp.int32, (1, LANES), 1)
    used = lane % grid_y < 5
    data[...] = jnp.where(used, turned, 0.0)
    weights[...] = jnp.where(used, pltpu.roll(turned, LANES - 8, 1), 0.0)
    values[...] = (weights[...] * data[...]).astype(BF)

    place_x = (lax.broadcasted_iota(jnp.int32, (GRID, stations), 0) == station_ref[0:1, :]).astype(F32).astype(BF)
    place_xt = (turned[:, 16:17] == lane.astype(F32)).astype(F32).astype(BF)
    place_yt = (turned[:, 17:18] == lane.astype(F32)).astype(F32)[:, :grid_y].astype(BF)

    @once
    def _():
        copies[0].wait()

    pick_xt[...] = dot(held("base_xt2", GRID), place_x).astype(BF)
    pick_x[...] = dot(place_xt, held("base_x")).astype(BF)
    station_y2 = held("station_y2", wide)
    for odd in range(2):
        high, low = [station_y2[(2 * odd + i) * grid_y : (2 * odd + i + 1) * grid_y] for i in range(2)]
        pick_y[:, odd * wide : (odd + 1) * wide] = dot(place_yt, high) + dot(place_yt, low)
    no_sum = jnp.zeros((8, LANES), F32)

    def trig(at, odd, chunk):
        lane = odd * wide + chunk * LANES
        return pick_y[at, lane : lane + LANES]

    def station_spectra():
        spread = held("spread")
        spread = jnp.concatenate([spread[i * LANES : (i + 1) * LANES] for i in range(3)], axis=1)
        spreads = dot(values[...], spread[:, : 5 * LANES])
        for row in range(0, stations, ROWS):
            at = slice(row, row + ROWS)
            for c, (_, odd_y) in enumerate(PARITY):
                e = spreads[at, c * LANES : (c + 1) * LANES]
                for chunk in chunks:
                    to = c * wide + chunk * LANES
                    spread_out[at, to : to + LANES] = (e * trig(at, odd_y, chunk)).astype(BF)
        spec = dot(pick_xt[...], spread_out[...])
        for c, (odd_x, _) in enumerate(PARITY):
            for hx in range(2):
                for chunk in chunks:
                    lane = c * wide + chunk * LANES
                    part = spec[hx * GRID : (hx + 1) * GRID, lane : lane + LANES]
                    spec_q[c, hx, chunk] = -part if odd_x * hx else part

    def back_project(receive):
        for share in shares:
            for row in range(0, GRID, 16):
                at = slice(row, row + 16)
                for chunk in chunks:
                    q = [[spec_q[c, hx, chunk, at, :] for hx in range(2)] for c in range(5)]
                    for z in range(share.start * deep, share.stop * deep):
                        t = [table(c, z, at).astype(F32) for c in range(5)]
                        lane = z * wide + chunk * LANES
                        for hx in range(2):
                            total = t[0] * q[0][hx]
                            for c in range(1, 5):
                                total = total + t[c] * q[c][hx ^ PARITY[c][0]]
                            spec_g[hx * GRID + row : hx * GRID + row + 16, lane : lane + LANES] = total.astype(BF)
            lane = share.start * 2 * LANES
            along_x = dot(held("base_x"), spec_g[:, lane : lane + share_lanes]).astype(BF)
            along_x = [along_x[:, lane : lane + 2 * LANES] for lane in range(0, share_lanes, 2 * LANES)]
            receive(share, dot(jnp.concatenate(along_x, axis=0), held("field_yt", LANES)))

    def predict():
        for share in shares:
            r = residual[share.start : share.stop].reshape(len(share) * GRID, LANES).astype(BF)
            y = dot(jnp.concatenate([r, r], axis=1), held("field_y2")).astype(BF)
            y = jnp.concatenate([y[i * GRID : (i + 1) * GRID] for i in range(len(share))], axis=1)
            lane = share.start * 2 * LANES
            spec_f[:, lane : lane + share_lanes] = dot(held("base_xt2"), jnp.concatenate([y, y], axis=0)).astype(BF)

            for row in range(0, GRID, 16):
                at = [slice(hx * GRID + row, hx * GRID + row + 16) for hx in range(2)]
                for chunk in chunks:
                    total = [[None] * 2 for _ in range(5)]
                    for z in range(share.start * deep, share.stop * deep):
                        lane = z * wide + chunk * LANES
                        f = [spec_f[at[hx], lane : lane + LANES] for hx in range(2)]
                        for c, (odd_x, _) in enumerate(PARITY):
                            t = table(c, z, at[0])
                            for hx in range(2):
                                term = t * f[hx ^ odd_x]
                                total[c][hx] = term if total[c][hx] is None else total[c][hx] + term
                    for c, (odd_x, _) in enumerate(PARITY):
                        lane = c * wide + chunk * LANES
                        for hx in range(2):
                            part = total[c][hx]
                            if share is not shares[0]:
                                part = part + spec_i[at[hx], lane : lane + LANES]
                            if share is shares[-1] and odd_x * hx:
                                part = -part
                            spec_i[at[hx], lane : lane + LANES] = part

        picked = dot(pick_x[...], spec_i[...])
        for row in range(0, stations, ROWS):
            at = slice(row, row + ROWS)
            for c, (_, odd_y) in enumerate(PARITY):
                part = None
                for chunk in chunks:
                    lane = c * wide + chunk * LANES
                    term = picked[at, lane : lane + LANES] * trig(at, odd_y, chunk)
                    part = term if part is None else part + term
                picked_in[at, c * LANES : (c + 1) * LANES] = part.astype(BF)
        return dot(picked_in[...], held("back", LANES))

    def fold(a):
        return jnp.sum(a.reshape(a.shape[0] // 8, 8, LANES), axis=0)

    def totals_of(partials):
        rows_of = []
        for partial in partials:
            for _ in range(3):
                part = partial.astype(BF).astype(F32)
                rows_of.append(part)
                partial = partial - part
        if len(rows_of) % 2:
            rows_of.append(no_sum)
        sums = dot(jnp.concatenate(rows_of, axis=0).astype(BF), held("same", LANES))
        return [jnp.sum(sums[i * 24 : (i + 1) * 24], axis=0, keepdims=True) for i in range(len(partials))]

    def depth_weight(z):
        within = lax.broadcasted_iota(jnp.int32, (1, LANES), 1) // (boots * grid_y)
        depth = (within + z * deep).astype(F32) + 0.5 + station_height
        ratio = station_height / depth
        return ratio * ratio * ratio

    def round_of(outer, inner, carry):
        first = outer == 0 and inner == 0
        last = outer == IRLS - 1 and inner == CG_STEPS - 1
        fresh = inner == 0
        old_norm, old_step, old_curve = carry
        sums = [no_sum] * 3

        def penalty_at(slab, at):
            if outer == 0:
                return damping * depth_weight(slab) / (focusing * focusing)
            return penalty[slab, at]

        def receive(share, applied):
            norm, bend, cross = sums
            for slab, at in pieces(share):
                row = (slab - share.start) * GRID + at.start
                r = applied[row : row + ROWS]
                if fresh and outer:
                    m = models[slab, at]
                    p = damping * depth_weight(slab) / (m * m + focusing * focusing)
                    penalty[slab, at] = p
                    r = r - p * m
                else:
                    p = penalty_at(slab, at)
                if not fresh:
                    pd = p * direction[slab, at]
                    r = residual[slab, at] - old_step * (r + pd)
                    cross += fold(pd * r)
                residual[slab, at] = r
                square = r * r
                norm += fold(square)
                bend += fold(p * square)
            sums[:] = [norm, bend, cross]

        back_project(receive)
        here = predict()
        weighted = weights[...] * here
        norm, bend, cross = sums
        if fresh:
            norm, curve = totals_of([norm, bend + fold(weighted * here)])
        else:
            norm, bend, cross = totals_of(
                [norm, bend + fold(weighted * here), cross + fold(weighted * image[...])]
            )
            ratio = norm / old_norm
            curve = bend + ratio * (2.0 * cross + ratio * old_curve)
        step = norm / curve
        if not last:
            if not fresh:
                here = here + ratio * image[...]
            now = step * here if first else pred[...] + step * here
            pred[...] = now
            if fresh:
                image[...] = here
                values[...] = (weights[...] * here).astype(BF)
            else:
                values[...] = (weights[...] * (data[...] - now)).astype(BF)
            station_spectra()
        for share in shares:
            for slab, at in pieces(share):
                d = residual[slab, at]
                if not fresh:
                    d = d + ratio * direction[slab, at]
                if fresh:
                    direction[slab, at] = d
                models[slab, at] = step * d if first else models[slab, at] + step * d
        return norm, step, curve

    station_spectra()

    @once
    def _():
        copies[1].wait()
        copies[2].wait()

    carry = (None, None, None)
    for outer in range(IRLS):
        for inner in range(CG_STEPS):
            carry = round_of(outer, inner, carry)

    for group in range(slabs // boots):
        m = jnp.concatenate([models[group * boots + i].astype(BF) for i in range(boots)], axis=1)
        if boots > 1:
            regroup = held("regroup")
            regroup = [regroup[i * boots * LANES : (i + 1) * boots * LANES] for i in range(boots // 2)]
            m = dot(m, jnp.concatenate(regroup, axis=1)).astype(BF)
        for b in range(boots):
            out_ref[b * GRID : (b + 1) * GRID, group * LANES : (group + 1) * LANES] = (
                m[:, b * LANES : (b + 1) * LANES]
            )


def solve(slot, comp_weight, station_index, observed, counts, mine, grid_y):
    boots = min(mine, LANES // grid_y)
    slabs = DEPTHS * grid_y * boots // LANES
    stations = station_index.shape[1]
    const = jnp.asarray(constants(grid_y, boots))
    vmem = pltpu.VMEM
    smem = pl.BlockSpec(memory_space=pltpu.SMEM)
    field = vmem((slabs, GRID, LANES), F32)
    at_stations = vmem((stations, LANES), F32)
    wide = 2 * boots * grid_y
    inputs = [station_index, observed, counts]
    return pl.pallas_call(
        functools.partial(solve_kernel, grid_y, boots, mine // boots),
        out_shape=jax.ShapeDtypeStruct((mine * GRID, DEPTHS * grid_y), BF),
        grid=(mine // boots,),
        in_specs=[smem, smem] + [pl.BlockSpec(memory_space=pl.ANY)] * (len(inputs) + 1),
        out_specs=pl.BlockSpec((boots * GRID, DEPTHS * grid_y), lambda i: (i, 0)),
        scratch_shapes=[vmem(a.shape, a.dtype) for a in inputs]
        + [
            vmem((layout(grid_y, boots).rows, 2 * LANES), BF),
            pltpu.SemaphoreType.DMA((6,)),
            vmem((stations, 2 * GRID), BF),
            vmem((2 * GRID, stations), BF),
            vmem((stations, 2 * wide), F32),
            at_stations,
            at_stations,
            at_stations,
            at_stations,
            vmem((stations, LANES), BF),
            vmem((LANES, stations), F32),
            vmem((stations, 5 * wide), BF),
            vmem((5, 2, wide // LANES, GRID, LANES), F32),
            vmem((2 * GRID, 5 * wide), BF),
            vmem((2 * GRID, slabs * 2 * LANES), BF),
            vmem((2 * GRID, slabs * 2 * LANES), BF),
            vmem((stations, 5 * LANES), BF),
            field,
            field,
            field,
            field,
        ],
        compiler_params=pltpu.CompilerParams(vmem_limit_bytes=56 * 1024 * 1024),
        cost_estimate=pl.CostEstimate(flops=10**10, bytes_accessed=10**7, transcendentals=0),
        name="solve",
    )(slot, comp_weight, *inputs, const)


def pick_kernel(grid_y, n_models, n_before, keep, cell_ref, *refs):
    models_refs, refs = refs[:n_models], refs[n_models:]
    before_refs, refs = refs[:n_before], refs[n_before:]
    if keep:
        refs[1][...] = models_refs[0][...]

    @pl.loop(0, cell_ref.shape[1] // CHUNK)
    def _(step):
        at = pl.ds(pl.multiple_of(step * CHUNK, CHUNK), CHUNK)
        place = cell_ref[:, at].astype(F32)
        wide = lambda row, rows: jnp.broadcast_to(row, (rows, CHUNK)).astype(BF)
        count_up = lambda rows: lax.broadcasted_iota(jnp.int32, (rows, CHUNK), 0).astype(F32).astype(BF)
        here_y = count_up(grid_y) == wide(place[1:2], grid_y)
        here_y = jnp.where(here_y, jnp.ones((grid_y, CHUNK), BF), jnp.zeros((grid_y, CHUNK), BF))
        z_row = wide(place[2:3], 16)
        none = jnp.zeros((16, CHUNK), BF)
        chosen = []
        for z in range(DEPTHS):
            here_z = z_row == jnp.full((16, CHUNK), z, BF)
            chosen += [jnp.where(here_z, here_y[i : i + 16], none) for i in range(0, grid_y, 16)]
        models = jnp.concatenate([ref[...] for ref in models_refs], axis=0)
        found = dot(models, jnp.concatenate(chosen, axis=0)).astype(BF)
        at_x = count_up(GRID) == wide(place[0:1], GRID)
        parts = [ref[:, at].astype(F32) for ref in before_refs]
        for b in range(models.shape[0] // GRID):
            part = jnp.where(at_x, found[b * GRID : (b + 1) * GRID], jnp.zeros((GRID, CHUNK), BF))
            while part.shape[0] > 16:
                half = part.shape[0] // 2
                part = part[:half] + part[half:]
            parts.append(jnp.sum(part.astype(F32), axis=0, keepdims=True))
        refs[0][:, at] = jnp.concatenate(parts, axis=0).astype(BF)


def pick(cells, models, before=(), grid_y=0, keep=False):
    rows = sum(m.shape[0] for m in models)
    boots = rows // GRID + sum(a.shape[0] for a in before)
    count = cells.shape[1]
    vmem = pl.BlockSpec(memory_space=pltpu.VMEM)
    shapes = [jax.ShapeDtypeStruct((boots, count), BF)]
    if keep:
        shapes.append(jax.ShapeDtypeStruct(models[0].shape, BF))
    found = pl.pallas_call(
        functools.partial(pick_kernel, grid_y, len(models), len(before), keep),
        out_shape=shapes,
        in_specs=[vmem] * (1 + len(models) + len(before)),
        out_specs=[vmem] * len(shapes),
        compiler_params=pltpu.CompilerParams(vmem_limit_bytes=40 * 1024 * 1024),
        cost_estimate=pl.CostEstimate(
            flops=2 * rows * DEPTHS * grid_y * count, bytes_accessed=10**6, transcendentals=0
        ),
        name="pick",
    )(cells, *models, *before)
    return found if keep else found[0]


def local(wide, cell_index, station_index, observed, comp_weight, counts):
    boots = counts.shape[0]
    grid_y = cell_index.shape[1] * wide // (GRID * DEPTHS)
    team = TEAM if wide % TEAM == 0 and boots % TEAM == 0 else 1
    while 4 * boots * grid_y < team * 2 * LANES:
        team //= 2
    slot = lax.axis_index("wide").astype(jnp.int32) & (team - 1)

    def swap(a, k):
        return lax.ppermute(a, "wide", [(i, i ^ k) for i in range(wide)])

    theirs = [swap(cell_index, k) for k in range(2, team, 2)]
    models = solve(slot.reshape(1), comp_weight, station_index, observed, counts, boots // team, grid_y)
    models, theirs = lax.optimization_barrier((models, theirs))
    if team > 1:
        shared = swap(models, 1)
        far = []
        for k, cells in enumerate(theirs):
            ours = pick(cells, [models], grid_y=grid_y, keep=k == 0)
            if k == 0:
                ours, models = ours
            far.append(swap(pick(cells, [shared], [ours], grid_y=grid_y), 2 * k + 2))
        found = [pick(cell_index, [models, shared], grid_y=grid_y)] + far
    else:
        found = [pick(cell_index, [models], grid_y=grid_y)]
    mine = boots // team
    got = [a[i * mine : (i + 1) * mine] for a in found for i in range(a.shape[0] // mine)]
    blocks = []
    for member in range(team):
        block = got[member]
        for other in range(1, team):
            block = jnp.where(slot == other, got[member ^ other], block)
        blocks.append(block.astype(F32))
    return jnp.concatenate(blocks, axis=0)


def solution(mesh):
    in_specs = (P(None, "wide"), P(None, "groups"), P(None, "groups"), P(), P("groups", None))
    out_specs = P("groups", "wide")
    fn = functools.partial(local, mesh.shape["wide"])
    return jax.shard_map(fn, mesh=mesh, in_specs=in_specs, out_specs=out_specs, check_vma=False)
```

```python
import functools

import jax
import jax.numpy as jnp
import ml_dtypes
import numpy as np
from jax import lax
from jax.experimental import pallas as pl
from jax.experimental.pallas import tpu as pltpu
from jax.sharding import PartitionSpec as P

IRLS = 2
CG_STEPS = 2
GRID = 128
DEPTHS = 16
LANES = 128
TEAM = 4
PARTS = 2
CHUNK = 4096
ROWS = 32

station_height = 2.0
focusing = 0.1
damping = 0.0002

PARITY = ((0, 0), (1, 1), (1, 0), (0, 0), (0, 1))
BF = jnp.bfloat16
F32 = jnp.float32


def offset_table(grid_y):
    one = np.float32
    dx = np.arange(GRID, dtype=one)[:, None, None]
    dy = np.arange(grid_y, dtype=one)[None, :, None]
    dz = (np.arange(DEPTHS, dtype=one) + one(0.5) + one(station_height))[None, None, :]
    radius2 = dx * dx + dy * dy + dz * dz
    strength = one(1) / (radius2 * radius2 * np.sqrt(radius2))
    three = one(3)
    kinds = [
        (three * dx * dx - radius2) * strength,
        three * dx * dy * strength,
        three * dx * dz * strength,
        (three * dy * dy - radius2) * strength,
        three * dy * dz * strength,
    ]
    return [k.astype(ml_dtypes.bfloat16).astype(np.float64) for k in kinds]


def angles(size):
    return 2 * np.pi * np.outer(np.arange(size), np.arange(size) + 0.5) / (2 * size)


def basis(size):
    return np.concatenate([np.cos(angles(size)), np.sin(angles(size))], axis=1)


def spectrum(values, odd, size):
    if odd:
        trig = 2 * np.sin(angles(size))
    else:
        trig = np.cos(angles(size)) * np.where(np.arange(size) == 0, 1, 2)[:, None]
    return np.tensordot(trig.T / size, values, axes=(1, 0))


def split(matrix):
    high = matrix.astype(ml_dtypes.bfloat16)
    low = (matrix - high.astype(np.float64)).astype(ml_dtypes.bfloat16)
    return high, low


class Layout:
    def __init__(self, parts):
        self.at = {}
        row = 0
        for name, rows in parts:
            self.at[name] = (row, rows)
            row += rows
        self.rows = row


def layout(grid_y, boots):
    return Layout(
        [
            ("base_x", GRID),
            ("base_xt2", 2 * GRID),
            ("station_y2", 4 * grid_y),
            ("spread", 3 * LANES),
            ("table", 5 * DEPTHS // 2 * GRID),
            ("field_y2", 2 * LANES),
            ("field_yt", 2 * LANES),
            ("back", 5 * LANES),
            ("same", LANES),
            ("regroup", boots * LANES * max(1, boots // 2)),
        ]
    )


@functools.lru_cache(maxsize=None)
def constants(grid_y, boots):
    deep = LANES // grid_y // boots
    copies = LANES // grid_y
    table = []
    for values, (odd_x, odd_y) in zip(offset_table(grid_y), PARITY):
        t = spectrum(values, odd_x, GRID)
        t = np.moveaxis(spectrum(np.moveaxis(t, 1, 0), odd_y, grid_y), 0, 1)
        table.append(np.tile(np.moveaxis(t, 2, 0), (1, 1, copies)))
    table = np.stack(table).reshape(5, DEPTHS // 2, 2, GRID, LANES).transpose(0, 1, 3, 2, 4)

    base_x = basis(GRID)
    base_y = basis(grid_y).reshape(grid_y, 2, grid_y)
    field_y = np.einsum("de,ab,yhl->dayehbl", np.eye(deep), np.eye(boots), base_y).reshape(LANES, 2 * LANES)
    odd_y = np.stack([-base_y[:, 1], base_y[:, 0]], axis=1)
    station_y = [np.tile(b[:, :, None], (1, 1, boots, 1)).reshape(grid_y, -1) for b in (base_y, odd_y)]
    spread = np.zeros((5, deep, boots, grid_y, copies, grid_y))
    for c in range(5):
        for copy in range(copies):
            spread[c, 0, copy % boots, c, copy, :] = 1
    spread = spread.reshape(5, LANES, LANES)
    back = spread.transpose(0, 2, 1).reshape(5 * LANES, LANES)
    spread = np.concatenate([spread, np.zeros((1, LANES, LANES))])
    spread = spread.reshape(3, 2, LANES, LANES).transpose(0, 2, 1, 3)
    same = np.einsum("ab,dc,yz->daycbz", np.eye(boots), np.ones((deep, deep)), np.ones((grid_y, grid_y)))
    same = same.reshape(LANES, LANES)
    regroup = np.einsum("st,de,ab,yz->sdaybtez", *[np.eye(n) for n in (boots, deep, boots, grid_y)])
    regroup = regroup.reshape(boots * LANES, boots * LANES)
    if boots > 2:
        regroup = np.concatenate(np.split(regroup, boots // 2, axis=1), axis=0)
    y_high, y_low = split(field_y)
    x_high, x_low = split(base_x.T)
    parts = dict(
        base_x=base_x,
        base_xt2=np.concatenate([x_high, x_low], axis=1),
        field_y2=np.concatenate([y_high, y_low], axis=0),
        field_yt=field_y.T,
        station_y2=np.concatenate([part for b in station_y for part in split(b)]),
        spread=spread.reshape(3 * LANES, 2 * LANES),
        back=back,
        same=same,
        regroup=regroup,
        table=table.reshape(-1, 2 * LANES),
    )
    where = layout(grid_y, boots)
    whole = np.zeros((max(where.rows, 1 << 14), 2 * LANES), ml_dtypes.bfloat16)
    for name, (row, rows) in where.at.items():
        part = parts[name].astype(ml_dtypes.bfloat16)
        assert part.shape[0] == rows
        whole[row : row + rows, : part.shape[1]] = part
    return whole


def dot(a, b):
    return jnp.dot(a, b, preferred_element_type=F32)


def solve_kernel(
    grid_y,
    boots,
    steps,
    slot_ref,
    comp_ref,
    station_source,
    observed_source,
    counts_source,
    source,
    out_ref,
    station_ref,
    observed_ref,
    counts_ref,
    const,
    copied,
    pick_x,
    pick_xt,
    pick_y,
    weights,
    data,
    image,
    values,
    rows,
    table_wide,
    spread_out,
    spec_q,
    spec_i,
    spec_f,
    spec_g,
    picked_in,
    models,
    residual,
    direction,
    penalty,
):
    deep = LANES // grid_y // boots
    slabs = DEPTHS // deep
    where = layout(grid_y, boots)
    table_row, table_rows = where.at["table"]
    wide = 2 * boots * grid_y
    chunks = range(wide // LANES)
    bounds = [0, table_row, table_row + table_rows, where.rows]
    copies = [
        pltpu.make_async_copy(source.at[a:b], const.at[a:b], copied.at[i])
        for i, (a, b) in enumerate(zip(bounds[:-1], bounds[1:]))
    ]

    small = [(station_source, station_ref), (observed_source, observed_ref), (counts_source, counts_ref)]
    small = [pltpu.make_async_copy(a, b, copied.at[len(copies) + i]) for i, (a, b) in enumerate(small)]

    def once(f):
        if steps == 1:
            f()
        else:
            pl.when(pl.program_id(0) == 0)(f)

    @once
    def _():
        for copy in small + copies:
            copy.start()
        for copy in small:
            copy.wait()

    def held(name, width=2 * LANES):
        row, count = where.at[name]
        return const[row : row + count, :width]

    def table(c, z, at):
        row = table_row + (c * (DEPTHS // 2) + z // 2) * GRID
        return const[row + at.start : row + at.stop, z % 2 * LANES : (z % 2 + 1) * LANES]

    stations = station_ref.shape[1]
    first = (slot_ref[0] * pl.num_programs(0) + pl.program_id(0)) * boots
    size = slabs // PARTS
    shares = [range(start, start + size) for start in range(0, slabs, size)]
    share_lanes = size * 2 * LANES

    def pieces(share):
        return [(slab, slice(row, row + ROWS)) for slab in share for row in range(0, GRID, ROWS)]


    rows[...] = jnp.zeros_like(rows)
    for b in range(boots):
        row = b * grid_y
        rows[row : row + 5, :] = observed_ref[...]
        count = counts_ref[pl.ds(first + b, 1), :].astype(F32)
        for c in range(5):
            rows[row + 8 + c : row + 9 + c, :] = count * comp_ref[c]
    rows[16:18, :] = station_ref[...].astype(F32)
    turned = jnp.transpose(rows[...])
    lane = lax.broadcasted_iota(jnp.int32, (1, LANES), 1)
    used = lane % grid_y < 5
    data[...] = jnp.where(used, turned, 0.0)
    weights[...] = jnp.where(used, pltpu.roll(turned, LANES - 8, 1), 0.0)
    values[...] = (weights[...] * data[...]).astype(BF)

    place_x = (lax.broadcasted_iota(jnp.int32, (GRID, stations), 0) == station_ref[0:1, :]).astype(F32).astype(BF)
    place_xt = (turned[:, 16:17] == lane.astype(F32)).astype(F32).astype(BF)
    place_yt = (turned[:, 17:18] == lane.astype(F32)).astype(F32)[:, :grid_y].astype(BF)

    @once
    def _():
        copies[0].wait()

    pick_xt[...] = dot(held("base_xt2", GRID), place_x).astype(BF)
    pick_x[...] = dot(place_xt, held("base_x")).astype(BF)
    station_y2 = held("station_y2", wide)
    for odd in range(2):
        high, low = [station_y2[(2 * odd + i) * grid_y : (2 * odd + i + 1) * grid_y] for i in range(2)]
        pick_y[:, odd * wide : (odd + 1) * wide] = dot(place_yt, high) + dot(place_yt, low)
    no_sum = jnp.zeros((8, LANES), F32)

    def trig(at, odd, chunk):
        lane = odd * wide + chunk * LANES
        return pick_y[at, lane : lane + LANES]

    def station_spectra():
        spread = held("spread")
        spread = jnp.concatenate([spread[i * LANES : (i + 1) * LANES] for i in range(3)], axis=1)
        spreads = dot(values[...], spread[:, : 5 * LANES])
        for row in range(0, stations, ROWS):
            at = slice(row, row + ROWS)
            for c, (_, odd_y) in enumerate(PARITY):
                e = spreads[at, c * LANES : (c + 1) * LANES]
                for chunk in chunks:
                    to = c * wide + chunk * LANES
                    spread_out[at, to : to + LANES] = (e * trig(at, odd_y, chunk)).astype(BF)
        spec = dot(pick_xt[...], spread_out[...])
        for c, (odd_x, _) in enumerate(PARITY):
            for hx in range(2):
                for chunk in chunks:
                    lane = c * wide + chunk * LANES
                    part = spec[hx * GRID : (hx + 1) * GRID, lane : lane + LANES]
                    spec_q[c, hx, chunk] = -part if odd_x * hx else part

    def back_project(receive):
        for share in shares:
            for row in range(0, GRID, 16):
                at = slice(row, row + 16)
                for chunk in chunks:
                    q = [[spec_q[c, hx, chunk, at, :] for hx in range(2)] for c in range(5)]
                    for z in range(share.start * deep, share.stop * deep):
                        t = [table_wide[c, z, at, :] for c in range(5)]
                        lane = z * wide + chunk * LANES
                        for hx in range(2):
                            total = t[0] * q[0][hx]
                            for c in range(1, 5):
                                total = total + t[c] * q[c][hx ^ PARITY[c][0]]
                            spec_g[hx * GRID + row : hx * GRID + row + 16, lane : lane + LANES] = total.astype(BF)
            lane = share.start * 2 * LANES
            along_x = dot(held("base_x"), spec_g[:, lane : lane + share_lanes]).astype(BF)
            along_x = [along_x[:, lane : lane + 2 * LANES] for lane in range(0, share_lanes, 2 * LANES)]
            receive(share, dot(jnp.concatenate(along_x, axis=0), held("field_yt", LANES)))

    def predict(field):
        for share in shares:
            r = field[share.start : share.stop].reshape(len(share) * GRID, LANES).astype(BF)
            y = dot(jnp.concatenate([r, r], axis=1), held("field_y2")).astype(BF)
            y = jnp.concatenate([y[i * GRID : (i + 1) * GRID] for i in range(len(share))], axis=1)
            lane = share.start * 2 * LANES
            spec_f[:, lane : lane + share_lanes] = dot(held("base_xt2"), jnp.concatenate([y, y], axis=0)).astype(BF)

            for row in range(0, GRID, 16):
                at = [slice(hx * GRID + row, hx * GRID + row + 16) for hx in range(2)]
                for chunk in chunks:
                    total = [[None] * 2 for _ in range(5)]
                    for z in range(share.start * deep, share.stop * deep):
                        lane = z * wide + chunk * LANES
                        f = [spec_f[at[hx], lane : lane + LANES] for hx in range(2)]
                        for c, (odd_x, _) in enumerate(PARITY):
                            t = table(c, z, at[0])
                            for hx in range(2):
                                term = t * f[hx ^ odd_x]
                                total[c][hx] = term if total[c][hx] is None else total[c][hx] + term
                    for c, (odd_x, _) in enumerate(PARITY):
                        lane = c * wide + chunk * LANES
                        for hx in range(2):
                            part = total[c][hx]
                            if share is not shares[0]:
                                part = part + spec_i[at[hx], lane : lane + LANES]
                            if share is shares[-1] and odd_x * hx:
                                part = -part
                            spec_i[at[hx], lane : lane + LANES] = part

        picked = dot(pick_x[...], spec_i[...])
        for row in range(0, stations, ROWS):
            at = slice(row, row + ROWS)
            for c, (_, odd_y) in enumerate(PARITY):
                part = None
                for chunk in chunks:
                    lane = c * wide + chunk * LANES
                    term = picked[at, lane : lane + LANES] * trig(at, odd_y, chunk)
                    part = term if part is None else part + term
                picked_in[at, c * LANES : (c + 1) * LANES] = part.astype(BF)
        return dot(picked_in[...], held("back", LANES))

    def fold(a):
        return jnp.sum(a.reshape(a.shape[0] // 8, 8, LANES), axis=0)

    def totals_of(partials):
        rows_of = []
        for partial in partials:
            for _ in range(3):
                part = partial.astype(BF).astype(F32)
                rows_of.append(part)
                partial = partial - part
        if len(rows_of) % 2:
            rows_of.append(no_sum)
        sums = dot(jnp.concatenate(rows_of, axis=0).astype(BF), held("same", LANES))
        return [jnp.sum(sums[i * 24 : (i + 1) * 24], axis=0, keepdims=True) for i in range(len(partials))]

    def depth_weight(z):
        within = lax.broadcasted_iota(jnp.int32, (1, LANES), 1) // (boots * grid_y)
        depth = (within + z * deep).astype(F32) + 0.5 + station_height
        ratio = station_height / depth
        return ratio * ratio * ratio

    def round_of(outer, inner, carry):
        last = outer == IRLS - 1 and inner == CG_STEPS - 1
        fresh = inner == 0
        old_norm, old_step, old_curve = carry
        sums = [no_sum] * 3

        def receive(share, applied):
            norm, bend, cross = sums
            for slab in share:
                if outer == 0:
                    p = damping * depth_weight(slab) / (focusing * focusing)
                squares = products = no_sum
                for at in (slice(row, row + ROWS) for row in range(0, GRID, ROWS)):
                    row = (slab - share.start) * GRID + at.start
                    r = applied[row : row + ROWS]
                    if fresh and outer:
                        m = models[slab, at]
                        p = damping * depth_weight(slab) / (m * m + focusing * focusing)
                        penalty[slab, at] = p
                        r = r - p * m
                    elif outer:
                        p = penalty[slab, at]
                    if fresh:
                        direction[slab, at] = r
                    else:
                        d = direction[slab, at]
                        pd = p * d
                        r = d - old_step * (r + pd)
                        residual[slab, at] = r
                        if outer:
                            cross += fold(pd * r)
                        else:
                            products += fold(d * r)
                    square = r * r
                    squares += fold(square)
                    if outer:
                        bend += fold(p * square)
                norm += squares
                if outer == 0:
                    bend += p * squares
                    cross += p * products
            sums[:] = [norm, bend, cross]

        back_project(receive)
        here = predict(direction if fresh else residual)
        weighted = weights[...] * here
        norm, bend, cross = sums
        if fresh:
            norm, curve = totals_of([norm, bend + fold(weighted * here)])
            step = norm / curve
            image[...] = here
            values[...] = weighted.astype(BF)
            station_spectra()
            return norm, step, curve
        norm, bend, cross = totals_of(
            [norm, bend + fold(weighted * here), cross + fold(weighted * image[...])]
        )
        ratio = norm / old_norm
        curve = bend + ratio * (2.0 * cross + ratio * old_curve)
        step = norm / curve
        along = old_step + step * ratio
        if not last:
            left = data[...] - (along * image[...] + step * here)
            data[...] = left
            values[...] = (weights[...] * left).astype(BF)
            station_spectra()
        for share in shares:
            for slab, at in pieces(share):
                move = along * direction[slab, at] + step * residual[slab, at]
                models[slab, at] = models[slab, at] + move if outer else move
        return norm, step, curve

    station_spectra()

    @once
    def _():
        copies[1].wait()
        copies[2].wait()
        for c in range(5):
            for z in range(DEPTHS):
                table_wide[c, z] = table(c, z, slice(0, GRID)).astype(F32)

    carry = (None, None, None)
    for outer in range(IRLS):
        for inner in range(CG_STEPS):
            carry = round_of(outer, inner, carry)

    for group in range(slabs // boots):
        m = jnp.concatenate([models[group * boots + i].astype(BF) for i in range(boots)], axis=1)
        if boots > 1:
            regroup = held("regroup")
            regroup = [regroup[i * boots * LANES : (i + 1) * boots * LANES] for i in range(boots // 2)]
            m = dot(m, jnp.concatenate(regroup, axis=1)).astype(BF)
        for b in range(boots):
            out_ref[b * GRID : (b + 1) * GRID, group * LANES : (group + 1) * LANES] = (
                m[:, b * LANES : (b + 1) * LANES]
            )


def solve(slot, comp_weight, station_index, observed, counts, mine, grid_y):
    boots = min(mine, LANES // grid_y)
    slabs = DEPTHS * grid_y * boots // LANES
    stations = station_index.shape[1]
    const = jnp.asarray(constants(grid_y, boots))
    vmem = pltpu.VMEM
    smem = pl.BlockSpec(memory_space=pltpu.SMEM)
    field = vmem((slabs, GRID, LANES), F32)
    at_stations = vmem((stations, LANES), F32)
    wide = 2 * boots * grid_y
    inputs = [station_index, observed, counts]
    return pl.pallas_call(
        functools.partial(solve_kernel, grid_y, boots, mine // boots),
        out_shape=jax.ShapeDtypeStruct((mine * GRID, DEPTHS * grid_y), BF),
        grid=(mine // boots,),
        in_specs=[smem, smem] + [pl.BlockSpec(memory_space=pl.ANY)] * (len(inputs) + 1),
        out_specs=pl.BlockSpec((boots * GRID, DEPTHS * grid_y), lambda i: (i, 0)),
        scratch_shapes=[vmem(a.shape, a.dtype) for a in inputs]
        + [
            vmem((layout(grid_y, boots).rows, 2 * LANES), BF),
            pltpu.SemaphoreType.DMA((6,)),
            vmem((stations, 2 * GRID), BF),
            vmem((2 * GRID, stations), BF),
            vmem((stations, 2 * wide), F32),
            at_stations,
            at_stations,
            at_stations,
            vmem((stations, LANES), BF),
            vmem((LANES, stations), F32),
            vmem((5, DEPTHS, GRID, LANES), F32),
            vmem((stations, 5 * wide), BF),
            vmem((5, 2, wide // LANES, GRID, LANES), F32),
            vmem((2 * GRID, 5 * wide), BF),
            vmem((2 * GRID, slabs * 2 * LANES), BF),
            vmem((2 * GRID, slabs * 2 * LANES), BF),
            vmem((stations, 5 * LANES), BF),
            field,
            field,
            field,
            field,
        ],
        compiler_params=pltpu.CompilerParams(vmem_limit_bytes=56 * 1024 * 1024),
        cost_estimate=pl.CostEstimate(flops=10**10, bytes_accessed=10**7, transcendentals=0),
        name="solve",
    )(slot, comp_weight, *inputs, const)


def pick_kernel(grid_y, n_models, n_before, keep, cell_ref, *refs):
    models_refs, refs = refs[:n_models], refs[n_models:]
    before_refs, refs = refs[:n_before], refs[n_before:]
    if keep:
        refs[1][...] = models_refs[0][...]

    @pl.loop(0, cell_ref.shape[1] // CHUNK)
    def _(step):
        at = pl.ds(pl.multiple_of(step * CHUNK, CHUNK), CHUNK)
        place = cell_ref[:, at].astype(F32)
        wide = lambda row, rows: jnp.broadcast_to(row, (rows, CHUNK)).astype(BF)
        count_up = lambda rows: lax.broadcasted_iota(jnp.int32, (rows, CHUNK), 0).astype(F32).astype(BF)
        here_y = count_up(grid_y) == wide(place[1:2], grid_y)
        here_y = jnp.where(here_y, jnp.ones((grid_y, CHUNK), BF), jnp.zeros((grid_y, CHUNK), BF))
        z_row = wide(place[2:3], 16)
        none = jnp.zeros((16, CHUNK), BF)
        chosen = []
        for z in range(DEPTHS):
            here_z = z_row == jnp.full((16, CHUNK), z, BF)
            chosen += [jnp.where(here_z, here_y[i : i + 16], none) for i in range(0, grid_y, 16)]
        models = jnp.concatenate([ref[...] for ref in models_refs], axis=0)
        found = dot(models, jnp.concatenate(chosen, axis=0)).astype(BF)
        at_x = count_up(GRID) == wide(place[0:1], GRID)
        parts = [ref[:, at].astype(F32) for ref in before_refs]
        for b in range(models.shape[0] // GRID):
            part = jnp.where(at_x, found[b * GRID : (b + 1) * GRID], jnp.zeros((GRID, CHUNK), BF))
            while part.shape[0] > 16:
                half = part.shape[0] // 2
                part = part[:half] + part[half:]
            parts.append(jnp.sum(part.astype(F32), axis=0, keepdims=True))
        refs[0][:, at] = jnp.concatenate(parts, axis=0).astype(BF)


def pick(cells, models, before=(), grid_y=0, keep=False):
    rows = sum(m.shape[0] for m in models)
    boots = rows // GRID + sum(a.shape[0] for a in before)
    count = cells.shape[1]
    vmem = pl.BlockSpec(memory_space=pltpu.VMEM)
    shapes = [jax.ShapeDtypeStruct((boots, count), BF)]
    if keep:
        shapes.append(jax.ShapeDtypeStruct(models[0].shape, BF))
    found = pl.pallas_call(
        functools.partial(pick_kernel, grid_y, len(models), len(before), keep),
        out_shape=shapes,
        in_specs=[vmem] * (1 + len(models) + len(before)),
        out_specs=[vmem] * len(shapes),
        compiler_params=pltpu.CompilerParams(vmem_limit_bytes=40 * 1024 * 1024),
        cost_estimate=pl.CostEstimate(
            flops=2 * rows * DEPTHS * grid_y * count, bytes_accessed=10**6, transcendentals=0
        ),
        name="pick",
    )(cells, *models, *before)
    return found if keep else found[0]


def local(wide, cell_index, station_index, observed, comp_weight, counts):
    boots = counts.shape[0]
    grid_y = cell_index.shape[1] * wide // (GRID * DEPTHS)
    team = TEAM if wide % TEAM == 0 and boots % TEAM == 0 else 1
    while 4 * boots * grid_y < team * 2 * LANES:
        team //= 2
    slot = lax.axis_index("wide").astype(jnp.int32) & (team - 1)

    def swap(a, k):
        return lax.ppermute(a, "wide", [(i, i ^ k) for i in range(wide)])

    theirs = [swap(cell_index, k) for k in range(2, team, 2)]
    models = solve(slot.reshape(1), comp_weight, station_index, observed, counts, boots // team, grid_y)
    models, theirs = lax.optimization_barrier((models, theirs))
    if team > 1:
        shared = swap(models, 1)
        far = []
        for k, cells in enumerate(theirs):
            ours = pick(cells, [models], grid_y=grid_y, keep=k == 0)
            if k == 0:
                ours, models = ours
            far.append(swap(pick(cells, [shared], [ours], grid_y=grid_y), 2 * k + 2))
        found = [pick(cell_index, [models, shared], grid_y=grid_y)] + far
    else:
        found = [pick(cell_index, [models], grid_y=grid_y)]
    mine = boots // team
    got = [a[i * mine : (i + 1) * mine] for a in found for i in range(a.shape[0] // mine)]
    blocks = []
    for member in range(team):
        block = got[member]
        for other in range(1, team):
            block = jnp.where(slot == other, got[member ^ other], block)
        blocks.append(block.astype(F32))
    return jnp.concatenate(blocks, axis=0)


def solution(mesh):
    in_specs = (P(None, "wide"), P(None, "groups"), P(None, "groups"), P(), P("groups", None))
    out_specs = P("groups", "wide")
    fn = functools.partial(local, mesh.shape["wide"])
    return jax.shard_map(fn, mesh=mesh, in_specs=in_specs, out_specs=out_specs, check_vma=False)
```

```python
import functools

import jax
import jax.numpy as jnp
import ml_dtypes
import numpy as np
from jax import lax
from jax.experimental import pallas as pl
from jax.experimental.pallas import tpu as pltpu
from jax.sharding import PartitionSpec as P

IRLS = 2
CG_STEPS = 2
GRID = 128
DEPTHS = 16
LANES = 128
TEAM = 4
PARTS = 1
CHUNK = 4096
ROWS = 32

station_height = 2.0
focusing = 0.1
damping = 0.0002

PARITY = ((0, 0), (1, 1), (1, 0), (0, 0), (0, 1))
BF = jnp.bfloat16
F32 = jnp.float32


def offset_table(grid_y):
    one = np.float32
    dx = np.arange(GRID, dtype=one)[:, None, None]
    dy = np.arange(grid_y, dtype=one)[None, :, None]
    dz = (np.arange(DEPTHS, dtype=one) + one(0.5) + one(station_height))[None, None, :]
    radius2 = dx * dx + dy * dy + dz * dz
    strength = one(1) / (radius2 * radius2 * np.sqrt(radius2))
    three = one(3)
    kinds = [
        (three * dx * dx - radius2) * strength,
        three * dx * dy * strength,
        three * dx * dz * strength,
        (three * dy * dy - radius2) * strength,
        three * dy * dz * strength,
    ]
    return [k.astype(ml_dtypes.bfloat16).astype(np.float64) for k in kinds]


def angles(size):
    return 2 * np.pi * np.outer(np.arange(size), np.arange(size) + 0.5) / (2 * size)


def basis(size):
    return np.concatenate([np.cos(angles(size)), np.sin(angles(size))], axis=1)


def spectrum(values, odd, size):
    if odd:
        trig = 2 * np.sin(angles(size))
    else:
        trig = np.cos(angles(size)) * np.where(np.arange(size) == 0, 1, 2)[:, None]
    return np.tensordot(trig.T / size, values, axes=(1, 0))


def split(matrix):
    high = matrix.astype(ml_dtypes.bfloat16)
    low = (matrix - high.astype(np.float64)).astype(ml_dtypes.bfloat16)
    return high, low


class Layout:
    def __init__(self, parts):
        self.at = {}
        row = 0
        for name, rows in parts:
            self.at[name] = (row, rows)
            row += rows
        self.rows = row


def layout(grid_y, boots):
    return Layout(
        [
            ("base_x", GRID),
            ("base_xt2", 2 * GRID),
            ("station_y2", 4 * grid_y),
            ("spread", 3 * LANES),
            ("table", 5 * DEPTHS // 2 * GRID),
            ("field_y2", 2 * LANES),
            ("field_yt", 2 * LANES),
            ("back", 5 * LANES),
            ("same", LANES),
            ("regroup", boots * LANES * max(1, boots // 2)),
        ]
    )


@functools.lru_cache(maxsize=None)
def constants(grid_y, boots):
    deep = LANES // grid_y // boots
    copies = LANES // grid_y
    table = []
    for values, (odd_x, odd_y) in zip(offset_table(grid_y), PARITY):
        t = spectrum(values, odd_x, GRID)
        t = np.moveaxis(spectrum(np.moveaxis(t, 1, 0), odd_y, grid_y), 0, 1)
        table.append(np.tile(np.moveaxis(t, 2, 0), (1, 1, copies)))
    table = np.stack(table).reshape(5, DEPTHS // 2, 2, GRID, LANES).transpose(0, 1, 3, 2, 4)

    base_x = basis(GRID)
    base_y = basis(grid_y).reshape(grid_y, 2, grid_y)
    field_y = np.einsum("de,ab,yhl->dayehbl", np.eye(deep), np.eye(boots), base_y).reshape(LANES, 2 * LANES)
    odd_y = np.stack([-base_y[:, 1], base_y[:, 0]], axis=1)
    station_y = [np.tile(b[:, :, None], (1, 1, boots, 1)).reshape(grid_y, -1) for b in (base_y, odd_y)]
    spread = np.zeros((5, deep, boots, grid_y, copies, grid_y))
    for c in range(5):
        for copy in range(copies):
            spread[c, 0, copy % boots, c, copy, :] = 1
    spread = spread.reshape(5, LANES, LANES)
    back = spread.transpose(0, 2, 1).reshape(5 * LANES, LANES)
    spread = np.concatenate([spread, np.zeros((1, LANES, LANES))])
    spread = spread.reshape(3, 2, LANES, LANES).transpose(0, 2, 1, 3)
    same = np.einsum("ab,dc,yz->daycbz", np.eye(boots), np.ones((deep, deep)), np.ones((grid_y, grid_y)))
    same = same.reshape(LANES, LANES)
    regroup = np.einsum("st,de,ab,yz->sdaybtez", *[np.eye(n) for n in (boots, deep, boots, grid_y)])
    regroup = regroup.reshape(boots * LANES, boots * LANES)
    if boots > 2:
        regroup = np.concatenate(np.split(regroup, boots // 2, axis=1), axis=0)
    y_high, y_low = split(field_y)
    x_high, x_low = split(base_x.T)
    parts = dict(
        base_x=base_x,
        base_xt2=np.concatenate([x_high, x_low], axis=1),
        field_y2=np.concatenate([y_high, y_low], axis=0),
        field_yt=field_y.T,
        station_y2=np.concatenate([part for b in station_y for part in split(b)]),
        spread=spread.reshape(3 * LANES, 2 * LANES),
        back=back,
        same=same,
        regroup=regroup,
        table=table.reshape(-1, 2 * LANES),
    )
    where = layout(grid_y, boots)
    whole = np.zeros((max(where.rows, 1 << 14), 2 * LANES), ml_dtypes.bfloat16)
    for name, (row, rows) in where.at.items():
        part = parts[name].astype(ml_dtypes.bfloat16)
        assert part.shape[0] == rows
        whole[row : row + rows, : part.shape[1]] = part
    return whole


def dot(a, b):
    return jnp.dot(a, b, preferred_element_type=F32)


def solve_kernel(
    grid_y,
    boots,
    steps,
    slot_ref,
    comp_ref,
    station_source,
    observed_source,
    counts_source,
    source,
    out_ref,
    station_ref,
    observed_ref,
    counts_ref,
    const,
    copied,
    pick_x,
    pick_xt,
    pick_y,
    weights,
    data,
    image,
    values,
    rows,
    table_wide,
    spread_out,
    spec_q,
    spec_i,
    spec_f,
    spec_g,
    picked_in,
    models,
    residual,
    direction,
    penalty,
):
    deep = LANES // grid_y // boots
    slabs = DEPTHS // deep
    where = layout(grid_y, boots)
    table_row, table_rows = where.at["table"]
    wide = 2 * boots * grid_y
    chunks = range(wide // LANES)
    bounds = [0, table_row, table_row + table_rows, where.rows]
    copies = [
        pltpu.make_async_copy(source.at[a:b], const.at[a:b], copied.at[i])
        for i, (a, b) in enumerate(zip(bounds[:-1], bounds[1:]))
    ]

    small = [(station_source, station_ref), (observed_source, observed_ref), (counts_source, counts_ref)]
    small = [pltpu.make_async_copy(a, b, copied.at[len(copies) + i]) for i, (a, b) in enumerate(small)]

    def once(f):
        if steps == 1:
            f()
        else:
            pl.when(pl.program_id(0) == 0)(f)

    @once
    def _():
        for copy in small + copies:
            copy.start()
        for copy in small:
            copy.wait()

    def held(name, width=2 * LANES):
        row, count = where.at[name]
        return const[row : row + count, :width]

    def table(c, z, at):
        row = table_row + (c * (DEPTHS // 2) + z // 2) * GRID
        return const[row + at.start : row + at.stop, z % 2 * LANES : (z % 2 + 1) * LANES]

    stations = station_ref.shape[1]
    first = (slot_ref[0] * pl.num_programs(0) + pl.program_id(0)) * boots
    size = slabs // PARTS
    shares = [range(start, start + size) for start in range(0, slabs, size)]
    share_lanes = size * 2 * LANES

    def pieces(share):
        return [(slab, slice(row, row + ROWS)) for slab in share for row in range(0, GRID, ROWS)]


    rows[...] = jnp.zeros_like(rows)
    for b in range(boots):
        row = b * grid_y
        rows[row : row + 5, :] = observed_ref[...]
        count = counts_ref[pl.ds(first + b, 1), :].astype(F32)
        for c in range(5):
            rows[row + 8 + c : row + 9 + c, :] = count * comp_ref[c]
    rows[16:18, :] = station_ref[...].astype(F32)
    turned = jnp.transpose(rows[...])
    lane = lax.broadcasted_iota(jnp.int32, (1, LANES), 1)
    used = lane % grid_y < 5
    data[...] = jnp.where(used, turned, 0.0)
    weights[...] = jnp.where(used, pltpu.roll(turned, LANES - 8, 1), 0.0)
    values[...] = (weights[...] * data[...]).astype(BF)

    place_x = (lax.broadcasted_iota(jnp.int32, (GRID, stations), 0) == station_ref[0:1, :]).astype(F32).astype(BF)
    place_xt = (turned[:, 16:17] == lane.astype(F32)).astype(F32).astype(BF)
    place_yt = (turned[:, 17:18] == lane.astype(F32)).astype(F32)[:, :grid_y].astype(BF)

    @once
    def _():
        copies[0].wait()

    pick_xt[...] = dot(held("base_xt2", GRID), place_x).astype(BF)
    pick_x[...] = dot(place_xt, held("base_x")).astype(BF)
    station_y2 = held("station_y2", wide)
    for odd in range(2):
        high, low = [station_y2[(2 * odd + i) * grid_y : (2 * odd + i + 1) * grid_y] for i in range(2)]
        pick_y[:, odd * wide : (odd + 1) * wide] = dot(place_yt, high) + dot(place_yt, low)
    no_sum = jnp.zeros((8, LANES), F32)

    def trig(at, odd, chunk):
        lane = odd * wide + chunk * LANES
        return pick_y[at, lane : lane + LANES]

    def station_spectra():
        spread = held("spread")
        spread = jnp.concatenate([spread[i * LANES : (i + 1) * LANES] for i in range(3)], axis=1)
        spreads = dot(values[...], spread[:, : 5 * LANES])
        for row in range(0, stations, ROWS):
            at = slice(row, row + ROWS)
            for c, (_, odd_y) in enumerate(PARITY):
                e = spreads[at, c * LANES : (c + 1) * LANES]
                for chunk in chunks:
                    to = c * wide + chunk * LANES
                    spread_out[at, to : to + LANES] = (e * trig(at, odd_y, chunk)).astype(BF)
        spec = dot(pick_xt[...], spread_out[...])
        for c, (odd_x, _) in enumerate(PARITY):
            for hx in range(2):
                for chunk in chunks:
                    lane = c * wide + chunk * LANES
                    part = spec[hx * GRID : (hx + 1) * GRID, lane : lane + LANES]
                    spec_q[c, hx, chunk] = -part if odd_x * hx else part

    def back_project(receive):
        for share in shares:
            for row in range(0, GRID, 16):
                at = slice(row, row + 16)
                for chunk in chunks:
                    q = [[spec_q[c, hx, chunk, at, :] for hx in range(2)] for c in range(5)]
                    for z in range(share.start * deep, share.stop * deep):
                        t = [table_wide[c, z, at, :] for c in range(5)]
                        lane = z * wide + chunk * LANES
                        for hx in range(2):
                            total = t[0] * q[0][hx]
                            for c in range(1, 5):
                                total = total + t[c] * q[c][hx ^ PARITY[c][0]]
                            spec_g[hx * GRID + row : hx * GRID + row + 16, lane : lane + LANES] = total.astype(BF)
            lane = share.start * 2 * LANES
            along_x = dot(held("base_x"), spec_g[:, lane : lane + share_lanes]).astype(BF)
            along_x = [along_x[:, lane : lane + 2 * LANES] for lane in range(0, share_lanes, 2 * LANES)]
            receive(share, dot(jnp.concatenate(along_x, axis=0), held("field_yt", LANES)))

    def predict(field):
        for share in shares:
            r = field[share.start : share.stop].reshape(len(share) * GRID, LANES).astype(BF)
            y = dot(jnp.concatenate([r, r], axis=1), held("field_y2")).astype(BF)
            y = jnp.concatenate([y[i * GRID : (i + 1) * GRID] for i in range(len(share))], axis=1)
            lane = share.start * 2 * LANES
            spec_f[:, lane : lane + share_lanes] = dot(held("base_xt2"), jnp.concatenate([y, y], axis=0)).astype(BF)

            for row in range(0, GRID, 16):
                at = [slice(hx * GRID + row, hx * GRID + row + 16) for hx in range(2)]
                for chunk in chunks:
                    total = [[None] * 2 for _ in range(5)]
                    for eight in range(share.start * deep, share.stop * deep, 8):
                        some = [[None] * 2 for _ in range(5)]
                        for z in range(eight, eight + 8):
                            lane = z * wide + chunk * LANES
                            f = [spec_f[at[hx], lane : lane + LANES] for hx in range(2)]
                            for c, (odd_x, _) in enumerate(PARITY):
                                t = table(c, z, at[0])
                                for hx in range(2):
                                    term = t * f[hx ^ odd_x]
                                    some[c][hx] = term if z == eight else some[c][hx] + term
                        for c in range(5):
                            for hx in range(2):
                                old = total[c][hx]
                                total[c][hx] = some[c][hx] if old is None else old + some[c][hx]
                    for c, (odd_x, _) in enumerate(PARITY):
                        lane = c * wide + chunk * LANES
                        for hx in range(2):
                            part = total[c][hx]
                            if share is not shares[0]:
                                part = part + spec_i[at[hx], lane : lane + LANES]
                            if share is shares[-1] and odd_x * hx:
                                part = -part
                            spec_i[at[hx], lane : lane + LANES] = part

        picked = dot(pick_x[...], spec_i[...])
        for row in range(0, stations, ROWS):
            at = slice(row, row + ROWS)
            for c, (_, odd_y) in enumerate(PARITY):
                part = None
                for chunk in chunks:
                    lane = c * wide + chunk * LANES
                    term = picked[at, lane : lane + LANES] * trig(at, odd_y, chunk)
                    part = term if part is None else part + term
                picked_in[at, c * LANES : (c + 1) * LANES] = part.astype(BF)
        return dot(picked_in[...], held("back", LANES))

    def fold(a):
        return jnp.sum(a.reshape(a.shape[0] // 8, 8, LANES), axis=0)

    def totals_of(partials):
        rows_of = []
        for partial in partials:
            for _ in range(3):
                part = partial.astype(BF).astype(F32)
                rows_of.append(part)
                partial = partial - part
        if len(rows_of) % 2:
            rows_of.append(no_sum)
        sums = dot(jnp.concatenate(rows_of, axis=0).astype(BF), held("same", LANES))
        return [jnp.sum(sums[i * 24 : (i + 1) * 24], axis=0, keepdims=True) for i in range(len(partials))]

    def depth_weight(z):
        within = lax.broadcasted_iota(jnp.int32, (1, LANES), 1) // (boots * grid_y)
        depth = (within + z * deep).astype(F32) + 0.5 + station_height
        ratio = station_height / depth
        return ratio * ratio * ratio

    def round_of(outer, inner, carry):
        last = outer == IRLS - 1 and inner == CG_STEPS - 1
        fresh = inner == 0
        old_norm, old_step, old_curve = carry
        sums = [no_sum] * 3

        def receive(share, applied):
            norm, bend, cross = sums
            for slab in share:
                if outer == 0:
                    p = damping * depth_weight(slab) / (focusing * focusing)
                squares = products = no_sum
                for at in (slice(row, row + ROWS) for row in range(0, GRID, ROWS)):
                    row = (slab - share.start) * GRID + at.start
                    r = applied[row : row + ROWS]
                    if fresh and outer:
                        m = models[slab, at]
                        p = damping * depth_weight(slab) / (m * m + focusing * focusing)
                        penalty[slab, at] = p
                        r = r - p * m
                    elif outer:
                        p = penalty[slab, at]
                    if fresh:
                        direction[slab, at] = r
                    else:
                        d = direction[slab, at]
                        pd = p * d
                        r = d - old_step * (r + pd)
                        residual[slab, at] = r
                        if outer:
                            cross += fold(pd * r)
                        else:
                            products += fold(d * r)
                    square = r * r
                    squares += fold(square)
                    if outer:
                        bend += fold(p * square)
                norm += squares
                if outer == 0:
                    bend += p * squares
                    cross += p * products
            sums[:] = [norm, bend, cross]

        back_project(receive)
        here = predict(direction if fresh else residual)
        weighted = weights[...] * here
        norm, bend, cross = sums
        if fresh:
            norm, curve = totals_of([norm, bend + fold(weighted * here)])
            step = norm / curve
            image[...] = here
            values[...] = weighted.astype(BF)
            station_spectra()
            return norm, step, curve
        norm, bend, cross = totals_of(
            [norm, bend + fold(weighted * here), cross + fold(weighted * image[...])]
        )
        ratio = norm / old_norm
        curve = bend + ratio * (2.0 * cross + ratio * old_curve)
        step = norm / curve
        along = old_step + step * ratio
        if not last:
            left = data[...] - (along * image[...] + step * here)
            data[...] = left
            values[...] = (weights[...] * left).astype(BF)
            station_spectra()
        for share in shares:
            for slab, at in pieces(share):
                move = along * direction[slab, at] + step * residual[slab, at]
                models[slab, at] = models[slab, at] + move if outer else move
        return norm, step, curve

    station_spectra()

    @once
    def _():
        copies[1].wait()
        copies[2].wait()
        for c in range(5):
            for z in range(DEPTHS):
                table_wide[c, z] = table(c, z, slice(0, GRID)).astype(F32)

    carry = (None, None, None)
    for outer in range(IRLS):
        for inner in range(CG_STEPS):
            carry = round_of(outer, inner, carry)

    for group in range(slabs // boots):
        m = jnp.concatenate([models[group * boots + i].astype(BF) for i in range(boots)], axis=1)
        if boots > 1:
            regroup = held("regroup")
            regroup = [regroup[i * boots * LANES : (i + 1) * boots * LANES] for i in range(boots // 2)]
            m = dot(m, jnp.concatenate(regroup, axis=1)).astype(BF)
        for b in range(boots):
            out_ref[b * GRID : (b + 1) * GRID, group * LANES : (group + 1) * LANES] = (
                m[:, b * LANES : (b + 1) * LANES]
            )


def solve(slot, comp_weight, station_index, observed, counts, mine, grid_y):
    boots = min(mine, LANES // grid_y)
    slabs = DEPTHS * grid_y * boots // LANES
    stations = station_index.shape[1]
    const = jnp.asarray(constants(grid_y, boots))
    vmem = pltpu.VMEM
    smem = pl.BlockSpec(memory_space=pltpu.SMEM)
    field = vmem((slabs, GRID, LANES), F32)
    at_stations = vmem((stations, LANES), F32)
    wide = 2 * boots * grid_y
    inputs = [station_index, observed, counts]
    return pl.pallas_call(
        functools.partial(solve_kernel, grid_y, boots, mine // boots),
        out_shape=jax.ShapeDtypeStruct((mine * GRID, DEPTHS * grid_y), BF),
        grid=(mine // boots,),
        in_specs=[smem, smem] + [pl.BlockSpec(memory_space=pl.ANY)] * (len(inputs) + 1),
        out_specs=pl.BlockSpec((boots * GRID, DEPTHS * grid_y), lambda i: (i, 0)),
        scratch_shapes=[vmem(a.shape, a.dtype) for a in inputs]
        + [
            vmem((layout(grid_y, boots).rows, 2 * LANES), BF),
            pltpu.SemaphoreType.DMA((6,)),
            vmem((stations, 2 * GRID), BF),
            vmem((2 * GRID, stations), BF),
            vmem((stations, 2 * wide), F32),
            at_stations,
            at_stations,
            at_stations,
            vmem((stations, LANES), BF),
            vmem((LANES, stations), F32),
            vmem((5, DEPTHS, GRID, LANES), F32),
            vmem((stations, 5 * wide), BF),
            vmem((5, 2, wide // LANES, GRID, LANES), F32),
            vmem((2 * GRID, 5 * wide), BF),
            vmem((2 * GRID, slabs * 2 * LANES), BF),
            vmem((2 * GRID, slabs * 2 * LANES), BF),
            vmem((stations, 5 * LANES), BF),
            field,
            field,
            field,
            field,
        ],
        compiler_params=pltpu.CompilerParams(vmem_limit_bytes=56 * 1024 * 1024),
        cost_estimate=pl.CostEstimate(flops=10**10, bytes_accessed=10**7, transcendentals=0),
        name="solve",
    )(slot, comp_weight, *inputs, const)


def pick_kernel(grid_y, n_models, n_before, keep, cell_ref, *refs):
    models_refs, refs = refs[:n_models], refs[n_models:]
    before_refs, refs = refs[:n_before], refs[n_before:]
    if keep:
        refs[1][...] = models_refs[0][...]

    @pl.loop(0, cell_ref.shape[1] // CHUNK)
    def _(step):
        at = pl.ds(pl.multiple_of(step * CHUNK, CHUNK), CHUNK)
        place = cell_ref[:, at].astype(F32)
        wide = lambda row, rows: jnp.broadcast_to(row, (rows, CHUNK)).astype(BF)
        count_up = lambda rows: lax.broadcasted_iota(jnp.int32, (rows, CHUNK), 0).astype(F32).astype(BF)
        here_y = count_up(grid_y) == wide(place[1:2], grid_y)
        here_y = jnp.where(here_y, jnp.ones((grid_y, CHUNK), BF), jnp.zeros((grid_y, CHUNK), BF))
        z_row = wide(place[2:3], 16)
        none = jnp.zeros((16, CHUNK), BF)
        chosen = []
        for z in range(DEPTHS):
            here_z = z_row == jnp.full((16, CHUNK), z, BF)
            chosen += [jnp.where(here_z, here_y[i : i + 16], none) for i in range(0, grid_y, 16)]
        models = jnp.concatenate([ref[...] for ref in models_refs], axis=0)
        found = dot(models, jnp.concatenate(chosen, axis=0)).astype(BF)
        at_x = count_up(GRID) == wide(place[0:1], GRID)
        parts = [ref[:, at].astype(F32) for ref in before_refs]
        for b in range(models.shape[0] // GRID):
            part = jnp.where(at_x, found[b * GRID : (b + 1) * GRID], jnp.zeros((GRID, CHUNK), BF))
            while part.shape[0] > 16:
                half = part.shape[0] // 2
                part = part[:half] + part[half:]
            parts.append(jnp.sum(part.astype(F32), axis=0, keepdims=True))
        refs[0][:, at] = jnp.concatenate(parts, axis=0).astype(BF)


def pick(cells, models, before=(), grid_y=0, keep=False):
    rows = sum(m.shape[0] for m in models)
    boots = rows // GRID + sum(a.shape[0] for a in before)
    count = cells.shape[1]
    vmem = pl.BlockSpec(memory_space=pltpu.VMEM)
    shapes = [jax.ShapeDtypeStruct((boots, count), BF)]
    if keep:
        shapes.append(jax.ShapeDtypeStruct(models[0].shape, BF))
    found = pl.pallas_call(
        functools.partial(pick_kernel, grid_y, len(models), len(before), keep),
        out_shape=shapes,
        in_specs=[vmem] * (1 + len(models) + len(before)),
        out_specs=[vmem] * len(shapes),
        compiler_params=pltpu.CompilerParams(vmem_limit_bytes=40 * 1024 * 1024),
        cost_estimate=pl.CostEstimate(
            flops=2 * rows * DEPTHS * grid_y * count, bytes_accessed=10**6, transcendentals=0
        ),
        name="pick",
    )(cells, *models, *before)
    return found if keep else found[0]


def local(wide, cell_index, station_index, observed, comp_weight, counts):
    boots = counts.shape[0]
    grid_y = cell_index.shape[1] * wide // (GRID * DEPTHS)
    team = TEAM if wide % TEAM == 0 and boots % TEAM == 0 else 1
    while 4 * boots * grid_y < team * 2 * LANES:
        team //= 2
    slot = lax.axis_index("wide").astype(jnp.int32) & (team - 1)

    def swap(a, k):
        return lax.ppermute(a, "wide", [(i, i ^ k) for i in range(wide)])

    theirs = [swap(cell_index, k) for k in range(2, team, 2)]
    models = solve(slot.reshape(1), comp_weight, station_index, observed, counts, boots // team, grid_y)
    models, theirs = lax.optimization_barrier((models, theirs))
    if team > 1:
        shared = swap(models, 1)
        far = []
        for k, cells in enumerate(theirs):
            ours = pick(cells, [models], grid_y=grid_y, keep=k == 0)
            if k == 0:
                ours, models = ours
            far.append(swap(pick(cells, [shared], [ours], grid_y=grid_y), 2 * k + 2))
        found = [pick(cell_index, [models, shared], grid_y=grid_y)] + far
    else:
        found = [pick(cell_index, [models], grid_y=grid_y)]
    mine = boots // team
    got = [a[i * mine : (i + 1) * mine] for a in found for i in range(a.shape[0] // mine)]
    blocks = []
    for member in range(team):
        block = got[member]
        for other in range(1, team):
            block = jnp.where(slot == other, got[member ^ other], block)
        blocks.append(block.astype(F32))
    return jnp.concatenate(blocks, axis=0)


def solution(mesh):
    in_specs = (P(None, "wide"), P(None, "groups"), P(None, "groups"), P(), P("groups", None))
    out_specs = P("groups", "wide")
    fn = functools.partial(local, mesh.shape["wide"])
    return jax.shard_map(fn, mesh=mesh, in_specs=in_specs, out_specs=out_specs, check_vma=False)
```

```python
import functools

import jax
import jax.numpy as jnp
import ml_dtypes
import numpy as np
from jax import lax
from jax.experimental import pallas as pl
from jax.experimental.pallas import tpu as pltpu
from jax.sharding import PartitionSpec as P

IRLS = 2
CG_STEPS = 2
GRID = 128
DEPTHS = 16
LANES = 128
TEAM = 4
PARTS = 1
CHUNK = 4096
ROWS = 64

station_height = 2.0
focusing = 0.1
damping = 0.0002

PARITY = ((0, 0), (1, 1), (1, 0), (0, 0), (0, 1))
BF = jnp.bfloat16
F32 = jnp.float32


def offset_table(grid_y):
    one = np.float32
    dx = np.arange(GRID, dtype=one)[:, None, None]
    dy = np.arange(grid_y, dtype=one)[None, :, None]
    dz = (np.arange(DEPTHS, dtype=one) + one(0.5) + one(station_height))[None, None, :]
    radius2 = dx * dx + dy * dy + dz * dz
    strength = one(1) / (radius2 * radius2 * np.sqrt(radius2))
    three = one(3)
    kinds = [
        (three * dx * dx - radius2) * strength,
        three * dx * dy * strength,
        three * dx * dz * strength,
        (three * dy * dy - radius2) * strength,
        three * dy * dz * strength,
    ]
    return [k.astype(ml_dtypes.bfloat16).astype(np.float64) for k in kinds]


def angles(size):
    return 2 * np.pi * np.outer(np.arange(size), np.arange(size) + 0.5) / (2 * size)


def basis(size):
    return np.concatenate([np.cos(angles(size)), np.sin(angles(size))], axis=1)


def spectrum(values, odd, size):
    if odd:
        trig = 2 * np.sin(angles(size))
    else:
        trig = np.cos(angles(size)) * np.where(np.arange(size) == 0, 1, 2)[:, None]
    return np.tensordot(trig.T / size, values, axes=(1, 0))


def split(matrix):
    high = matrix.astype(ml_dtypes.bfloat16)
    low = (matrix - high.astype(np.float64)).astype(ml_dtypes.bfloat16)
    return high, low


class Layout:
    def __init__(self, parts):
        self.at = {}
        row = 0
        for name, rows in parts:
            self.at[name] = (row, rows)
            row += rows
        self.rows = row


def layout(grid_y, boots):
    return Layout(
        [
            ("base_x", GRID),
            ("base_xt2", 2 * GRID),
            ("station_y2", 4 * grid_y),
            ("spread", 3 * LANES),
            ("table", 5 * DEPTHS // 2 * GRID),
            ("field_y2", 2 * LANES),
            ("field_yt", 2 * LANES),
            ("back", 5 * LANES),
            ("same", LANES),
            ("regroup", boots * LANES * max(1, boots // 2)),
        ]
    )


@functools.lru_cache(maxsize=None)
def constants(grid_y, boots):
    deep = LANES // grid_y // boots
    copies = LANES // grid_y
    table = []
    for values, (odd_x, odd_y) in zip(offset_table(grid_y), PARITY):
        t = spectrum(values, odd_x, GRID)
        t = np.moveaxis(spectrum(np.moveaxis(t, 1, 0), odd_y, grid_y), 0, 1)
        table.append(np.tile(np.moveaxis(t, 2, 0), (1, 1, copies)))
    table = np.stack(table).reshape(5, DEPTHS // 2, 2, GRID, LANES).transpose(0, 1, 3, 2, 4)

    base_x = basis(GRID)
    base_y = basis(grid_y).reshape(grid_y, 2, grid_y)
    field_y = np.einsum("de,ab,yhl->dayehbl", np.eye(deep), np.eye(boots), base_y).reshape(LANES, 2 * LANES)
    odd_y = np.stack([-base_y[:, 1], base_y[:, 0]], axis=1)
    station_y = [np.tile(b[:, :, None], (1, 1, boots, 1)).reshape(grid_y, -1) for b in (base_y, odd_y)]
    spread = np.zeros((5, deep, boots, grid_y, copies, grid_y))
    for c in range(5):
        for copy in range(copies):
            spread[c, 0, copy % boots, c, copy, :] = 1
    spread = spread.reshape(5, LANES, LANES)
    back = spread.transpose(0, 2, 1).reshape(5 * LANES, LANES)
    spread = np.concatenate([spread, np.zeros((1, LANES, LANES))])
    spread = spread.reshape(3, 2, LANES, LANES).transpose(0, 2, 1, 3)
    same = np.einsum("ab,dc,yz->daycbz", np.eye(boots), np.ones((deep, deep)), np.ones((grid_y, grid_y)))
    same = same.reshape(LANES, LANES)
    regroup = np.einsum("st,de,ab,yz->sdaybtez", *[np.eye(n) for n in (boots, deep, boots, grid_y)])
    regroup = regroup.reshape(boots * LANES, boots * LANES)
    if boots > 2:
        regroup = np.concatenate(np.split(regroup, boots // 2, axis=1), axis=0)
    y_high, y_low = split(field_y)
    x_high, x_low = split(base_x.T)
    parts = dict(
        base_x=base_x,
        base_xt2=np.concatenate([x_high, x_low], axis=1),
        field_y2=np.concatenate([y_high, y_low], axis=0),
        field_yt=field_y.T,
        station_y2=np.concatenate([part for b in station_y for part in split(b)]),
        spread=spread.reshape(3 * LANES, 2 * LANES),
        back=back,
        same=same,
        regroup=regroup,
        table=table.reshape(-1, 2 * LANES),
    )
    where = layout(grid_y, boots)
    whole = np.zeros((max(where.rows, 1 << 14), 2 * LANES), ml_dtypes.bfloat16)
    for name, (row, rows) in where.at.items():
        part = parts[name].astype(ml_dtypes.bfloat16)
        assert part.shape[0] == rows
        whole[row : row + rows, : part.shape[1]] = part
    return whole


def dot(a, b):
    return jnp.dot(a, b, preferred_element_type=F32)


def solve_kernel(
    grid_y,
    boots,
    steps,
    slot_ref,
    comp_ref,
    station_source,
    observed_source,
    counts_source,
    source,
    out_ref,
    station_ref,
    observed_ref,
    counts_ref,
    const,
    copied,
    pick_x,
    pick_xt,
    pick_y,
    weights,
    data,
    image,
    values,
    rows,
    table_wide,
    spread_out,
    spec_q,
    spec_i,
    spec_f,
    spec_g,
    picked_in,
    models,
    residual,
    direction,
    penalty,
):
    deep = LANES // grid_y // boots
    slabs = DEPTHS // deep
    where = layout(grid_y, boots)
    table_row, table_rows = where.at["table"]
    wide = 2 * boots * grid_y
    chunks = range(wide // LANES)
    bounds = [0, table_row, table_row + table_rows, where.rows]
    copies = [
        pltpu.make_async_copy(source.at[a:b], const.at[a:b], copied.at[i])
        for i, (a, b) in enumerate(zip(bounds[:-1], bounds[1:]))
    ]

    small = [(station_source, station_ref), (observed_source, observed_ref), (counts_source, counts_ref)]
    small = [pltpu.make_async_copy(a, b, copied.at[len(copies) + i]) for i, (a, b) in enumerate(small)]

    def once(f):
        if steps == 1:
            f()
        else:
            pl.when(pl.program_id(0) == 0)(f)

    @once
    def _():
        for copy in small + copies:
            copy.start()
        for copy in small:
            copy.wait()

    def held(name, width=2 * LANES):
        row, count = where.at[name]
        return const[row : row + count, :width]

    def table(c, z, at):
        row = table_row + (c * (DEPTHS // 2) + z // 2) * GRID
        return const[row + at.start : row + at.stop, z % 2 * LANES : (z % 2 + 1) * LANES]

    stations = station_ref.shape[1]
    first = (slot_ref[0] * pl.num_programs(0) + pl.program_id(0)) * boots
    size = slabs // PARTS
    shares = [range(start, start + size) for start in range(0, slabs, size)]
    share_lanes = size * 2 * LANES

    def pieces(share):
        return [(slab, slice(row, row + ROWS)) for slab in share for row in range(0, GRID, ROWS)]


    rows[...] = jnp.zeros_like(rows)
    for b in range(boots):
        row = b * grid_y
        rows[row : row + 5, :] = observed_ref[...]
        count = counts_ref[pl.ds(first + b, 1), :].astype(F32)
        for c in range(5):
            rows[row + 8 + c : row + 9 + c, :] = count * comp_ref[c]
    rows[16:18, :] = station_ref[...].astype(F32)
    turned = jnp.transpose(rows[...])
    lane = lax.broadcasted_iota(jnp.int32, (1, LANES), 1)
    used = lane % grid_y < 5
    data[...] = jnp.where(used, turned, 0.0)
    weights[...] = jnp.where(used, pltpu.roll(turned, LANES - 8, 1), 0.0)
    values[...] = (weights[...] * data[...]).astype(BF)

    place_x = (lax.broadcasted_iota(jnp.int32, (GRID, stations), 0) == station_ref[0:1, :]).astype(F32).astype(BF)
    place_xt = (turned[:, 16:17] == lane.astype(F32)).astype(F32).astype(BF)
    place_yt = (turned[:, 17:18] == lane.astype(F32)).astype(F32)[:, :grid_y].astype(BF)

    @once
    def _():
        copies[0].wait()

    pick_xt[...] = dot(held("base_xt2", GRID), place_x).astype(BF)
    pick_x[...] = dot(place_xt, held("base_x")).astype(BF)
    station_y2 = held("station_y2", wide)
    for odd in range(2):
        high, low = [station_y2[(2 * odd + i) * grid_y : (2 * odd + i + 1) * grid_y] for i in range(2)]
        pick_y[:, odd * wide : (odd + 1) * wide] = dot(place_yt, high) + dot(place_yt, low)
    no_sum = jnp.zeros((8, LANES), F32)

    def trig(at, odd, chunk):
        lane = odd * wide + chunk * LANES
        return pick_y[at, lane : lane + LANES]

    def station_spectra():
        spread = held("spread")
        spread = jnp.concatenate([spread[i * LANES : (i + 1) * LANES] for i in range(3)], axis=1)
        spreads = dot(values[...], spread[:, : 5 * LANES])
        for row in range(0, stations, ROWS):
            at = slice(row, row + ROWS)
            for c, (_, odd_y) in enumerate(PARITY):
                e = spreads[at, c * LANES : (c + 1) * LANES]
                for chunk in chunks:
                    to = c * wide + chunk * LANES
                    spread_out[at, to : to + LANES] = (e * trig(at, odd_y, chunk)).astype(BF)
        spec = dot(pick_xt[...], spread_out[...])
        for c, (odd_x, _) in enumerate(PARITY):
            for hx in range(2):
                for chunk in chunks:
                    lane = c * wide + chunk * LANES
                    part = spec[hx * GRID : (hx + 1) * GRID, lane : lane + LANES]
                    spec_q[c, hx, chunk] = -part if odd_x * hx else part

    def back_project(receive):
        for share in shares:
            for row in range(0, GRID, 16):
                at = slice(row, row + 16)
                for chunk in chunks:
                    q = [[spec_q[c, hx, chunk, at, :] for hx in range(2)] for c in range(5)]
                    for z in range(share.start * deep, share.stop * deep):
                        t = [table_wide[c, z, at, :] for c in range(5)]
                        lane = z * wide + chunk * LANES
                        for hx in range(2):
                            total = t[0] * q[0][hx]
                            for c in range(1, 5):
                                total = total + t[c] * q[c][hx ^ PARITY[c][0]]
                            spec_g[hx * GRID + row : hx * GRID + row + 16, lane : lane + LANES] = total.astype(BF)
            lane = share.start * 2 * LANES
            along_x = dot(held("base_x"), spec_g[:, lane : lane + share_lanes]).astype(BF)
            along_x = [along_x[:, lane : lane + 2 * LANES] for lane in range(0, share_lanes, 2 * LANES)]
            receive(share, dot(jnp.concatenate(along_x, axis=0), held("field_yt", LANES)))

    def predict(field):
        for share in shares:
            r = field[share.start : share.stop].reshape(len(share) * GRID, LANES).astype(BF)
            y = dot(jnp.concatenate([r, r], axis=1), held("field_y2")).astype(BF)
            y = jnp.concatenate([y[i * GRID : (i + 1) * GRID] for i in range(len(share))], axis=1)
            lane = share.start * 2 * LANES
            spec_f[:, lane : lane + share_lanes] = dot(held("base_xt2"), jnp.concatenate([y, y], axis=0)).astype(BF)

            for row in range(0, GRID, 16):
                at = [slice(hx * GRID + row, hx * GRID + row + 16) for hx in range(2)]
                for chunk in chunks:
                    total = [[None] * 2 for _ in range(5)]
                    for eight in range(share.start * deep, share.stop * deep, 8):
                        some = [[None] * 2 for _ in range(5)]
                        for z in range(eight, eight + 8):
                            lane = z * wide + chunk * LANES
                            f = [spec_f[at[hx], lane : lane + LANES] for hx in range(2)]
                            for c, (odd_x, _) in enumerate(PARITY):
                                t = table(c, z, at[0])
                                for hx in range(2):
                                    term = t * f[hx ^ odd_x]
                                    some[c][hx] = term if z == eight else some[c][hx] + term
                        for c in range(5):
                            for hx in range(2):
                                old = total[c][hx]
                                total[c][hx] = some[c][hx] if old is None else old + some[c][hx]
                    for c, (odd_x, _) in enumerate(PARITY):
                        lane = c * wide + chunk * LANES
                        for hx in range(2):
                            part = total[c][hx]
                            if share is not shares[0]:
                                part = part + spec_i[at[hx], lane : lane + LANES]
                            if share is shares[-1] and odd_x * hx:
                                part = -part
                            spec_i[at[hx], lane : lane + LANES] = part

        picked = dot(pick_x[...], spec_i[...])
        for row in range(0, stations, ROWS):
            at = slice(row, row + ROWS)
            for c, (_, odd_y) in enumerate(PARITY):
                part = None
                for chunk in chunks:
                    lane = c * wide + chunk * LANES
                    term = picked[at, lane : lane + LANES] * trig(at, odd_y, chunk)
                    part = term if part is None else part + term
                picked_in[at, c * LANES : (c + 1) * LANES] = part.astype(BF)
        return dot(picked_in[...], held("back", LANES))

    def fold(a):
        return jnp.sum(a.reshape(a.shape[0] // 8, 8, LANES), axis=0)

    def totals_of(partials):
        rows_of = []
        for partial in partials:
            for _ in range(3):
                part = partial.astype(BF).astype(F32)
                rows_of.append(part)
                partial = partial - part
        if len(rows_of) % 2:
            rows_of.append(no_sum)
        sums = dot(jnp.concatenate(rows_of, axis=0).astype(BF), held("same", LANES))
        return [jnp.sum(sums[i * 24 : (i + 1) * 24], axis=0, keepdims=True) for i in range(len(partials))]

    def depth_weight(z):
        within = lax.broadcasted_iota(jnp.int32, (1, LANES), 1) // (boots * grid_y)
        depth = (within + z * deep).astype(F32) + 0.5 + station_height
        ratio = station_height / depth
        return ratio * ratio * ratio

    def round_of(outer, inner, carry):
        last = outer == IRLS - 1 and inner == CG_STEPS - 1
        fresh = inner == 0
        old_norm, old_step, old_curve = carry
        sums = [no_sum] * 3

        def receive(share, applied):
            norm, bend, cross = sums
            for slab in share:
                if outer == 0:
                    p = damping * depth_weight(slab) / (focusing * focusing)
                squares = products = no_sum
                for at in (slice(row, row + ROWS) for row in range(0, GRID, ROWS)):
                    row = (slab - share.start) * GRID + at.start
                    r = applied[row : row + ROWS]
                    if fresh and outer:
                        m = models[slab, at]
                        p = damping * depth_weight(slab) / (m * m + focusing * focusing)
                        penalty[slab, at] = p
                        r = r - p * m
                    elif outer:
                        p = penalty[slab, at]
                    if fresh:
                        direction[slab, at] = r
                    else:
                        d = direction[slab, at]
                        pd = p * d
                        r = d - old_step * (r + pd)
                        residual[slab, at] = r
                        if outer:
                            cross += fold(pd * r)
                        else:
                            products += fold(d * r)
                    square = r * r
                    squares += fold(square)
                    if outer:
                        bend += fold(p * square)
                norm += squares
                if outer == 0:
                    bend += p * squares
                    cross += p * products
            sums[:] = [norm, bend, cross]

        back_project(receive)
        here = predict(direction if fresh else residual)
        weighted = weights[...] * here
        norm, bend, cross = sums
        if fresh:
            norm, curve = totals_of([norm, bend + fold(weighted * here)])
            step = norm / curve
            image[...] = here
            values[...] = weighted.astype(BF)
            station_spectra()
            return norm, step, curve
        norm, bend, cross = totals_of(
            [norm, bend + fold(weighted * here), cross + fold(weighted * image[...])]
        )
        ratio = norm / old_norm
        curve = bend + ratio * (2.0 * cross + ratio * old_curve)
        step = norm / curve
        along = old_step + step * ratio
        if not last:
            left = data[...] - (along * image[...] + step * here)
            data[...] = left
            values[...] = (weights[...] * left).astype(BF)
            station_spectra()
        for share in shares:
            for slab, at in pieces(share):
                move = along * direction[slab, at] + step * residual[slab, at]
                models[slab, at] = models[slab, at] + move if outer else move
        return norm, step, curve

    station_spectra()

    @once
    def _():
        copies[1].wait()
        copies[2].wait()
        for c in range(5):
            for z in range(DEPTHS):
                table_wide[c, z] = table(c, z, slice(0, GRID)).astype(F32)

    carry = (None, None, None)
    for outer in range(IRLS):
        for inner in range(CG_STEPS):
            carry = round_of(outer, inner, carry)

    for group in range(slabs // boots):
        m = jnp.concatenate([models[group * boots + i].astype(BF) for i in range(boots)], axis=1)
        if boots > 1:
            regroup = held("regroup")
            regroup = [regroup[i * boots * LANES : (i + 1) * boots * LANES] for i in range(boots // 2)]
            m = dot(m, jnp.concatenate(regroup, axis=1)).astype(BF)
        for b in range(boots):
            out_ref[b * GRID : (b + 1) * GRID, group * LANES : (group + 1) * LANES] = (
                m[:, b * LANES : (b + 1) * LANES]
            )


def solve(slot, comp_weight, station_index, observed, counts, mine, grid_y):
    boots = min(mine, LANES // grid_y)
    slabs = DEPTHS * grid_y * boots // LANES
    stations = station_index.shape[1]
    const = jnp.asarray(constants(grid_y, boots))
    vmem = pltpu.VMEM
    smem = pl.BlockSpec(memory_space=pltpu.SMEM)
    field = vmem((slabs, GRID, LANES), F32)
    at_stations = vmem((stations, LANES), F32)
    wide = 2 * boots * grid_y
    inputs = [station_index, observed, counts]
    return pl.pallas_call(
        functools.partial(solve_kernel, grid_y, boots, mine // boots),
        out_shape=jax.ShapeDtypeStruct((mine * GRID, DEPTHS * grid_y), BF),
        grid=(mine // boots,),
        in_specs=[smem, smem] + [pl.BlockSpec(memory_space=pl.ANY)] * (len(inputs) + 1),
        out_specs=pl.BlockSpec((boots * GRID, DEPTHS * grid_y), lambda i: (i, 0)),
        scratch_shapes=[vmem(a.shape, a.dtype) for a in inputs]
        + [
            vmem((layout(grid_y, boots).rows, 2 * LANES), BF),
            pltpu.SemaphoreType.DMA((6,)),
            vmem((stations, 2 * GRID), BF),
            vmem((2 * GRID, stations), BF),
            vmem((stations, 2 * wide), F32),
            at_stations,
            at_stations,
            at_stations,
            vmem((stations, LANES), BF),
            vmem((LANES, stations), F32),
            vmem((5, DEPTHS, GRID, LANES), F32),
            vmem((stations, 5 * wide), BF),
            vmem((5, 2, wide // LANES, GRID, LANES), F32),
            vmem((2 * GRID, 5 * wide), BF),
            vmem((2 * GRID, slabs * 2 * LANES), BF),
            vmem((2 * GRID, slabs * 2 * LANES), BF),
            vmem((stations, 5 * LANES), BF),
            field,
            field,
            field,
            field,
        ],
        compiler_params=pltpu.CompilerParams(vmem_limit_bytes=56 * 1024 * 1024),
        cost_estimate=pl.CostEstimate(flops=10**10, bytes_accessed=10**7, transcendentals=0),
        name="solve",
    )(slot, comp_weight, *inputs, const)


def pick_kernel(grid_y, n_models, n_before, keep, cell_ref, *refs):
    models_refs, refs = refs[:n_models], refs[n_models:]
    before_refs, refs = refs[:n_before], refs[n_before:]
    if keep:
        refs[1][...] = models_refs[0][...]

    @pl.loop(0, cell_ref.shape[1] // CHUNK)
    def _(step):
        at = pl.ds(pl.multiple_of(step * CHUNK, CHUNK), CHUNK)
        place = cell_ref[:, at].astype(F32)
        wide = lambda row, rows: jnp.broadcast_to(row, (rows, CHUNK)).astype(BF)
        count_up = lambda rows: lax.broadcasted_iota(jnp.int32, (rows, CHUNK), 0).astype(F32).astype(BF)
        here_y = count_up(grid_y) == wide(place[1:2], grid_y)
        here_y = jnp.where(here_y, jnp.ones((grid_y, CHUNK), BF), jnp.zeros((grid_y, CHUNK), BF))
        z_row = wide(place[2:3], 16)
        none = jnp.zeros((16, CHUNK), BF)
        chosen = []
        for z in range(DEPTHS):
            here_z = z_row == jnp.full((16, CHUNK), z, BF)
            chosen += [jnp.where(here_z, here_y[i : i + 16], none) for i in range(0, grid_y, 16)]
        models = jnp.concatenate([ref[...] for ref in models_refs], axis=0)
        found = dot(models, jnp.concatenate(chosen, axis=0)).astype(BF)
        at_x = count_up(GRID) == wide(place[0:1], GRID)
        parts = [ref[:, at].astype(F32) for ref in before_refs]
        for b in range(models.shape[0] // GRID):
            part = jnp.where(at_x, found[b * GRID : (b + 1) * GRID], jnp.zeros((GRID, CHUNK), BF))
            while part.shape[0] > 16:
                half = part.shape[0] // 2
                part = part[:half] + part[half:]
            parts.append(jnp.sum(part.astype(F32), axis=0, keepdims=True))
        refs[0][:, at] = jnp.concatenate(parts, axis=0).astype(BF)


def pick(cells, models, before=(), grid_y=0, keep=False):
    rows = sum(m.shape[0] for m in models)
    boots = rows // GRID + sum(a.shape[0] for a in before)
    count = cells.shape[1]
    vmem = pl.BlockSpec(memory_space=pltpu.VMEM)
    shapes = [jax.ShapeDtypeStruct((boots, count), BF)]
    if keep:
        shapes.append(jax.ShapeDtypeStruct(models[0].shape, BF))
    found = pl.pallas_call(
        functools.partial(pick_kernel, grid_y, len(models), len(before), keep),
        out_shape=shapes,
        in_specs=[vmem] * (1 + len(models) + len(before)),
        out_specs=[vmem] * len(shapes),
        compiler_params=pltpu.CompilerParams(vmem_limit_bytes=40 * 1024 * 1024),
        cost_estimate=pl.CostEstimate(
            flops=2 * rows * DEPTHS * grid_y * count, bytes_accessed=10**6, transcendentals=0
        ),
        name="pick",
    )(cells, *models, *before)
    return found if keep else found[0]


def local(wide, cell_index, station_index, observed, comp_weight, counts):
    boots = counts.shape[0]
    grid_y = cell_index.shape[1] * wide // (GRID * DEPTHS)
    team = TEAM if wide % TEAM == 0 and boots % TEAM == 0 else 1
    while 4 * boots * grid_y < team * 2 * LANES:
        team //= 2
    slot = lax.axis_index("wide").astype(jnp.int32) & (team - 1)

    def swap(a, k):
        return lax.ppermute(a, "wide", [(i, i ^ k) for i in range(wide)])

    theirs = [swap(cell_index, k) for k in range(2, team, 2)]
    models = solve(slot.reshape(1), comp_weight, station_index, observed, counts, boots // team, grid_y)
    models, theirs = lax.optimization_barrier((models, theirs))
    if team > 1:
        shared = swap(models, 1)
        far = []
        for k, cells in enumerate(theirs):
            ours = pick(cells, [models], grid_y=grid_y, keep=k == 0)
            if k == 0:
                ours, models = ours
            far.append(swap(pick(cells, [shared], [ours], grid_y=grid_y), 2 * k + 2))
        found = [pick(cell_index, [models, shared], grid_y=grid_y)] + far
    else:
        found = [pick(cell_index, [models], grid_y=grid_y)]
    mine = boots // team
    got = [a[i * mine : (i + 1) * mine] for a in found for i in range(a.shape[0] // mine)]
    blocks = []
    for member in range(team):
        block = got[member]
        for other in range(1, team):
            block = jnp.where(slot == other, got[member ^ other], block)
        blocks.append(block.astype(F32))
    return jnp.concatenate(blocks, axis=0)


def solution(mesh):
    in_specs = (P(None, "wide"), P(None, "groups"), P(None, "groups"), P(), P("groups", None))
    out_specs = P("groups", "wide")
    fn = functools.partial(local, mesh.shape["wide"])
    return jax.shard_map(fn, mesh=mesh, in_specs=in_specs, out_specs=out_specs, check_vma=False)
```
